32 devices in a mesh: sub: 8 (over y, x, core), rep: 4 (over z).
Axes of the slice: x: 2, y: 2, z: 4, core: 2. Of those that a mesh axis runs over, the one named last changes fastest.
Arguments:
- dual_ops: bfloat16 [32, 1024, 1024], P(('sub', 'rep'))
- mode_traces: float32 [32, 6, 1024], P(('sub', 'rep')), may hold values from -0.046875 to 0.046875
- route: int32 [32, 1024], P(('sub', 'rep')), may hold values from 0 to 1023, each once within a row
- mode_block: int32 [32, 1], replicated, may hold values from 0 to 1
- local_gap: float32 [32, 32768], P(None, ('sub', 'rep')), may hold values from -6 to 6
Outputs:
- multipliers: float32 [32, 32768], P(None, ('sub', 'rep'))
- amplitudes: float32 [32, 12], replicated
The draws below stay inside these ranges and needn't reach their ends.
Inputs may be any that keep to these rules, and one draw needn't show every extreme that they name: Each row of route lists every number below 1024 once. `mode_block`: every aggregate holds at least one subdomain.
All inputs are finite; a program needn't handle non-finite values.
Results may differ from the reference program's by a relative error of at most 0.003.
Values sent between devices are 32-bit elements; how exact they have to be, the bound alone decides.
No kernel may reach another device: no remote copies, remote signals or barrier semaphores. Data moves between devices by JAX's collectives and lax.ppermute only.
A program may use at most 64 MiB of HBM per device.

```python
import math
import jax
import jax.numpy as jnp
from jax import lax

B = 1024
R = 32
MODES = 6
AGG_SUBS = 16
ITERS = 2
SUBS = 32
ROWS = 32768
MODE_BLOCKS = 2
NC = 12
N_SUB = 8
N_REP = 4


def draw_dual_ops(key, part):
    noise_key, diag_key, scale_key = jax.random.split(key, 3)
    noise_draw = jax.random.uniform(noise_key, (SUBS, B, B), jnp.float32, -1.0, 1.0)
    symmetric = 0.5 * (noise_draw + jnp.swapaxes(noise_draw, 1, 2))
    diagonal = jnp.exp(jax.random.uniform(diag_key, (SUBS, B), jnp.float32, math.log(2.0), math.log(4.0)))
    stiffness = jnp.exp(jax.random.uniform(scale_key, (SUBS, 1, 1), jnp.float32, math.log(0.5), math.log(2.0)))
    identity = jnp.eye(B, dtype=jnp.float32)
    matrix = symmetric * (1.8 / math.sqrt(B)) * (1.0 - identity) + identity * diagonal[:, None, :]
    return (stiffness * matrix).astype(jnp.bfloat16)


def shard_levels(stream_key, extent, cuts, low, largest):
    level, own = 1.0, jax.random.fold_in(stream_key, 6)
    for axis_at, blocks in cuts:
        heights = jnp.exp(jax.random.uniform(jax.random.fold_in(own, axis_at), (blocks,), jnp.float32, low / len(cuts), largest / len(cuts)))
        level = level * jnp.repeat(heights, extent[axis_at] // blocks).reshape([-1 if axis == axis_at else 1 for axis in range(len(extent))])
    return level


def distinct(rng, rows, amount, top, lift):
    order = jax.random.permutation(jax.random.fold_in(rng, 1), amount)
    pull = order
    for power in range(3):
        pull = pull * pull // amount
    pull = pull * lift // amount
    lots = jax.random.randint(jax.random.fold_in(rng, 2), (rows, amount), 0, 4096) + pull
    sure = jax.random.permutation(jax.random.fold_in(rng, 3), rows)[jnp.arange(amount) % rows]
    lots = jnp.where(jnp.arange(rows)[:, None] == sure[None, :], 1 << 14, lots)
    merit = lots * amount + jnp.arange(amount)
    return lax.top_k(merit.astype(jnp.int32), top)[1].astype(jnp.int32)


def gaussian(own_key, dims, scale, reach, cuts=(), kind=jnp.bfloat16):
    entries = scale * jax.random.normal(own_key, dims, jnp.float32)
    if cuts:
        entries = entries * shard_levels(own_key, dims, cuts, -0.22, 0.18)
    return jnp.clip(entries, -reach, reach).astype(kind)


def setup_inputs(seed: int = 0) -> dict:
    key_of = jax.random.split(jax.random.key(seed), 6)
    return {
        "dual_ops": draw_dual_ops(jax.random.fold_in(key_of[5], 71), 0),
        "mode_traces": gaussian(key_of[1], (SUBS, MODES, B), (AGG_SUBS * B) ** -0.5, 0.046875, ((0, 32),), jnp.float32),
        "route": jax.vmap(lambda own: jax.random.permutation(own, B))(jax.random.split(key_of[2], SUBS)).reshape((SUBS, B)).astype(jnp.int32),
        "mode_block": distinct(key_of[3], SUBS, MODE_BLOCKS, 1, 0),
        "local_gap": gaussian(key_of[4], (R, ROWS), 1.0, 6.0, ((1, 32),), jnp.float32),
    }


HIGHEST = lax.Precision.HIGHEST

def reference(dual_ops, mode_traces, route, mode_block, local_gap):
    per_peer = B // N_SUB
    slot_local = route.reshape(N_SUB, N_REP, N_SUB, per_peer)
    row_base = (jnp.arange(N_SUB, dtype=jnp.int32)[:, None] * N_REP + jnp.arange(N_REP, dtype=jnp.int32)[None, :]) * B
    rows_at = (slot_local + row_base[:, :, None, None]).astype(jnp.int32)
    swapped = jnp.transpose(rows_at, (2, 1, 0, 3))
    on_diagonal = (jnp.arange(N_SUB)[:, None] == jnp.arange(N_SUB)[None, :])[:, None, :, None]
    partner_at = jnp.where(on_diagonal, jnp.flip(swapped, 3), swapped).astype(jnp.int32)
    partner = jnp.zeros((ROWS,), jnp.int32).at[rows_at.reshape(-1)].set(partner_at.reshape(-1))

    def jump_of(values):
        return values - values[:, partner]
    blocks = mode_block[:, 0]
    labels = jnp.arange(MODE_BLOCKS, dtype=jnp.int32)
    onehot = (blocks[:, None] == labels[None, :]).astype(jnp.float32)

    def coarse_term(values):
        shaped = values.reshape(R, SUBS, B)
        per_sub = 2.0 * jnp.einsum('nkb,rnb->rnk', mode_traces, shaped, precision=HIGHEST)
        return jnp.einsum('na,rnk->rak', onehot, per_sub, precision=HIGHEST).reshape(R, NC)

    def expand(amounts):
        per_sub = jnp.einsum('na,rak->rnk', onehot, amounts.reshape(R, MODE_BLOCKS, MODES), precision=HIGHEST)
        spread = jnp.einsum('nkb,rnk->rnb', mode_traces, per_sub, precision=HIGHEST)
        return jump_of(spread.reshape(R, ROWS))
    row_traces = jnp.transpose(mode_traces, (0, 2, 1)).reshape(ROWS, MODES)
    row_blocks = jnp.repeat(blocks, B)
    far_traces = row_traces[partner].reshape(SUBS, B, MODES)
    far_blocks = row_blocks[partner].reshape(SUBS, B)

    def cross_row(pieces):
        traces_one, far_traces_one, far_blocks_one = pieces
        hits = (far_blocks_one[:, None] == labels[None, :]).astype(jnp.float32)
        embedded = (hits[:, :, None] * far_traces_one[:, None, :]).reshape(B, NC)
        return jnp.dot(traces_one, embedded, precision=HIGHEST)
    cross_terms = lax.map(cross_row, (mode_traces, far_traces, far_blocks))
    own_gram = jnp.einsum('nkb,nlb->nkl', mode_traces, mode_traces, precision=HIGHEST)
    own_rows = (own_gram[:, :, None, :] * onehot[:, None, :, None]).reshape(SUBS, MODES, NC)
    gram_matrix = jnp.einsum('na,nkc->akc', onehot, 2.0 * (own_rows - cross_terms), precision=HIGHEST).reshape(NC, NC)
    factor = jnp.linalg.cholesky(gram_matrix)

    def solve_coarse(right):
        return jax.scipy.linalg.cho_solve((factor, True), right.T).T

    def product_one(pieces):
        return lax.dot_general(pieces[1].astype(jnp.float32), pieces[0].astype(jnp.float32), (((1,), (1,)), ((), ())), preferred_element_type=jnp.float32)

    def apply_ops(values):
        shaped = jnp.transpose(values.reshape(R, SUBS, B).astype(jnp.bfloat16), (1, 0, 2))
        result = lax.map(product_one, (dual_ops, shaped))
        return jnp.transpose(result, (1, 0, 2)).reshape(R, ROWS)
    residual = jump_of(local_gap)
    amplitudes = solve_coarse(coarse_term(residual))
    projected = residual - expand(amplitudes)
    inner_sum = jnp.sum(projected * projected, axis=1)
    direction = projected
    multipliers = jnp.zeros_like(residual)
    for iteration in range(ITERS):
        product = apply_ops(direction)
        image_jump = jump_of(product)
        step_size = inner_sum / jnp.sum(direction * image_jump, axis=1)
        multipliers = multipliers + step_size[:, None] * direction
        residual = residual - step_size[:, None] * image_jump
        amplitudes = solve_coarse(coarse_term(residual))
        if iteration + 1 < ITERS:
            projected = residual - expand(amplitudes)
            renewed = jnp.sum(projected * projected, axis=1)
            direction = projected + (renewed / inner_sum)[:, None] * direction
            inner_sum = renewed
    return (multipliers, amplitudes)
```

```python
import functools

import jax
import jax.numpy as jnp
from jax import lax
from jax.experimental import pallas as pl
from jax.experimental.pallas import tpu as pltpu
from jax.sharding import PartitionSpec as P

MODES = 6
AGG_SUBS = 16
ITERS = 2
GROUP = 8

HIGHEST = lax.Precision.HIGHEST
VMEM = pl.BlockSpec(memory_space=pltpu.VMEM)
SMEM = pl.BlockSpec(memory_space=pltpu.SMEM)
NN = (((1,), (0,)), ((), ()))
NT = (((1,), (1,)), ((), ()))


def split(values):
    high = values.astype(jnp.bfloat16).astype(jnp.float32)
    return jnp.concatenate([high, values - high], axis=0).astype(jnp.bfloat16)


def split_dot(values, matrix, dims):
    rows = values.shape[0]
    both = lax.dot_general(split(values), matrix, dims, preferred_element_type=jnp.float32)
    return both[:rows] + both[rows:]


def small_dot(left, right):
    return jnp.dot(left, right, precision=HIGHEST, preferred_element_type=jnp.float32)


def place_kernel(peers, route_ref, gap_ref, traces_ref, place_ref, own_ref, *send_refs):
    own_index = lax.axis_index("sub")
    rows = gap_ref.shape[1]
    per_peer = rows // peers
    row_ids = lax.broadcasted_iota(jnp.int32, (rows, per_peer), 0)
    for offset in range(peers):
        start = pl.multiple_of((own_index ^ offset) * per_peer, per_peer)
        hits = row_ids == route_ref[:, pl.ds(start, per_peer)]
        at = offset if offset else peers
        place_ref[:, at * per_peer : (at + 1) * per_peer] = jnp.where(hits, 1.0, 0.0).astype(jnp.bfloat16)
    low = lax.broadcasted_iota(jnp.int32, (per_peer, per_peer), 0)
    high = lax.broadcasted_iota(jnp.int32, (per_peer, per_peer), 1)
    reverse = jnp.where(low + high == per_peer - 1, 1.0, 0.0).astype(jnp.bfloat16)
    place_ref[:, :per_peer] = jnp.dot(
        place_ref[:, rows:], reverse, preferred_element_type=jnp.float32
    ).astype(jnp.bfloat16)
    traces = traces_ref[0]
    padding = jnp.zeros((GROUP - traces.shape[0], rows), jnp.float32)
    values = jnp.concatenate([gap_ref[...], traces, padding], axis=0)
    slots = split_dot(values, place_ref[:, :rows], NN)
    for offset, ref in enumerate((own_ref, *send_refs)):
        ref[...] = slots[:, offset * per_peer : (offset + 1) * per_peer]


def first_kernel(peers, planes, groups, block_ref, place_ref, operator_ref, gap_ref, traces_ref, own_ref, *refs):
    got_refs, (basis_ref, image_ref, back_ref, *send_refs) = refs[: peers - 1], refs[peers - 1 :]
    own_index = lax.axis_index("sub")
    plane_index = lax.axis_index("rep")
    rows = gap_ref.shape[1]
    loads = gap_ref.shape[0]
    per_peer = rows // peers

    def spread(traces, peer):
        block = block_ref[peer * planes + plane_index, 0]
        return [traces * jnp.where(block == label, 1.0, 0.0) for label in range(groups)]

    pieces = []
    for offset, ref in zip((*range(1, peers), 0), (*got_refs, own_ref)):
        got = ref[...]
        pieces.append(jnp.concatenate([got[:loads], *spread(got[loads:], own_index ^ offset)], axis=0))
    partner = split_dot(jnp.concatenate(pieces, axis=1), place_ref[:, per_peer:], NT)
    traces = traces_ref[0]
    padding = jnp.zeros((GROUP - traces.shape[0], rows), jnp.float32)
    traces = jnp.concatenate([traces, padding], axis=0)
    basis = jnp.concatenate([gap_ref[...], *spread(traces, own_index)], axis=0) - partner
    basis_ref[...] = basis
    image = split_dot(basis, operator_ref[0], NT)
    image_ref[...] = image
    slots = split_dot(image, place_ref[:, :rows], NN)
    for offset, ref in enumerate((back_ref, *send_refs)):
        ref[...] = slots[:, offset * per_peer : (offset + 1) * per_peer]


def second_kernel(peers, place_ref, operator_ref, basis_ref, image_ref, back_ref, *refs):
    got_refs, (jump_ref, terms_ref) = refs[: peers - 1], refs[peers - 1 :]
    rows = basis_ref.shape[1]
    per_peer = rows // peers
    coarse = terms_ref.shape[1] // 8
    loads = basis_ref.shape[0] - coarse
    got = jnp.concatenate([ref[...] for ref in (*got_refs, back_ref)], axis=1)
    image = image_ref[...]
    jump = image - split_dot(got, place_ref[:, per_peer:], NT)
    jump_ref[...] = jump
    basis = basis_ref[...]
    second = split_dot(jump, operator_ref[0], NT)
    left = jnp.concatenate([basis[:loads], jump[:loads], image[:loads], second[:loads], basis[loads:], jump[loads:]])
    right = jnp.concatenate([basis[loads:], image[loads:], jump[loads:], second[loads:]])
    both = lax.dot_general(split(left), split(right), NT, preferred_element_type=jnp.float32)
    both = both[: left.shape[0]] + both[left.shape[0] :]
    both = both + pltpu.roll(both, 4 * coarse, 1)
    along, jumped, imaged, doubled = (both[at * loads : (at + 1) * loads] for at in range(4))
    base, far = both[4 * loads : 4 * loads + coarse], both[4 * loads + coarse :]
    lane = lax.broadcasted_iota(jnp.int32, (loads, 8 * coarse), 1)
    strip = lane // coarse
    top = jnp.where(strip == 2, doubled, along)
    top = jnp.where(strip == 4, imaged, top)
    top = jnp.where(strip == 5, pltpu.roll(doubled, coarse, 1), top)
    top = jnp.where(strip >= 6, jumped, top)
    residual, jump_loads = basis[:loads], jump[:loads]
    scalars = (
        residual * residual,
        residual * image[:loads],
        jump_loads * jump_loads,
        jump_loads * second[:loads],
        residual * second[:loads],
    )
    for at, product in zip(SCALAR_LANES, scalars):
        top = jnp.where(lane == at, jnp.sum(product, axis=1, keepdims=True), top)
    lane = lax.broadcasted_iota(jnp.int32, (coarse, 8 * coarse), 1)
    terms_ref[...] = jnp.concatenate([top, jnp.where(lane < 4 * coarse, base, far)], axis=0)


SCALAR_LANES = (MODES, MODES + 1, GROUP + MODES, GROUP + MODES + 1, 2 * GROUP + MODES)


def tree_sum(values):
    while len(values) > 1:
        values = [low + high for low, high in zip(values[::2], values[1::2])]
    return values[0]


def inverse_of(gram, coarse):
    row = lax.broadcasted_iota(jnp.int32, (coarse, 2 * coarse), 0)
    lane = lax.broadcasted_iota(jnp.int32, (coarse, 2 * coarse), 1)
    unit = jnp.where(lane - coarse == row, 1.0, 0.0)
    work = jnp.concatenate([gram, unit[:, coarse:]], axis=1)
    work = jnp.where((lane < coarse) & (row % GROUP >= MODES), jnp.where(lane == row, 1.0, 0.0), work)
    work = jnp.where((lane < coarse) & (lane % GROUP >= MODES), jnp.where(lane == row, 1.0, 0.0), work)
    for pivot in range(coarse):
        if pivot % GROUP >= MODES:
            continue
        scaled = work[pivot : pivot + 1] / work[pivot : pivot + 1, pivot : pivot + 1]
        work = jnp.where(row == pivot, scaled, work - work[:, pivot : pivot + 1] * scaled)
    return work[:, coarse:]


def final_kernel(basis_ref, jump_ref, *refs):
    terms_refs, (multipliers_ref, amplitudes_ref) = refs[:-2], refs[-2:]
    terms = tree_sum([ref[...] for ref in terms_refs])
    coarse = terms.shape[1] // 8
    loads = terms.shape[0] - coarse
    groups = coarse // GROUP

    def scalar(at):
        lane = SCALAR_LANES[at]
        return terms[:loads, lane : lane + 1]

    def total(values):
        return jnp.sum(values, axis=1, keepdims=True)

    used = lax.broadcasted_iota(jnp.int32, (loads, coarse), 1) % GROUP < MODES

    def strip(at):
        return jnp.where(used, terms[:loads, at * coarse : (at + 1) * coarse], 0.0)

    def block(at):
        return terms[loads:, at * coarse : (at + 1) * coarse]

    res_res, res_image, jump_jump, jump_second, res_second = (scalar(at) for at in range(5))
    coarse_res, res_h, second_z, res_dz, image_g, second_g, jump_z, jump_dz = (strip(at) for at in range(8))
    gram, g_h, g_dz, z_z, z_dz = block(0), block(1), block(3), block(6), block(7)
    inverse = inverse_of(gram, coarse)
    amounts = small_dot(coarse_res, inverse)
    inner = res_res - total(amounts * coarse_res)
    products = small_dot(amounts, jnp.concatenate([g_h.T, z_z], axis=1))
    coarse_image = image_g - products[:, :coarse]
    res_along = 2.0 * (res_image - total(amounts * res_h))
    curvature = res_along - 2.0 * total(amounts * coarse_image)
    step = inner / curvature
    along_along = jump_jump - total(amounts * (2.0 * jump_z - products[:, coarse:]))
    norm = res_res - 2.0 * step * res_along + step * step * along_along
    coarse_next = coarse_res - 2.0 * step * coarse_image
    amounts_next = small_dot(coarse_next, inverse)
    renewed = norm - total(amounts_next * coarse_next)
    ratio = renewed / inner
    on_res = 1.0 + ratio
    on_jump = -step
    on_z = step * amounts
    on_g = -(amounts_next + ratio * amounts)
    spread = small_dot(
        jnp.concatenate([on_z, on_g], axis=1),
        jnp.concatenate(
            [
                jnp.concatenate([z_dz.T, g_dz.T], axis=1),
                jnp.concatenate([0.5 * z_z, g_h.T], axis=1),
            ],
            axis=0,
        ),
    )
    at_z = 0.5 * on_res * jump_z + on_jump * second_z + spread[:, :coarse]
    at_g = on_res * image_g + on_jump * second_g + spread[:, coarse:]
    at_res = on_res * res_image + on_jump * res_second + total(on_z * res_dz + on_g * res_h)
    at_jump = 0.5 * on_res * jump_jump + on_jump * jump_second + total(on_z * jump_dz + 0.5 * on_g * jump_z)
    curvature = 2.0 * (on_res * at_res + on_jump * at_jump + total(on_z * at_z + on_g * at_g))
    second_step = renewed / curvature
    amplitudes = small_dot(coarse_next - 2.0 * second_step * at_g, inverse)
    amplitudes_ref[...] = jnp.concatenate(
        [amplitudes[:, label * GROUP : label * GROUP + MODES] for label in range(groups)], axis=1
    )
    weights = jnp.concatenate([second_step * on_g - step * amounts, second_step * on_z], axis=1)
    columns = jnp.concatenate([basis_ref[loads:], jump_ref[loads:]], axis=0)
    multipliers_ref[...] = (
        (step + second_step * on_res) * basis_ref[:loads]
        + (second_step * on_jump) * jump_ref[:loads]
        + small_dot(weights, columns)
    )


def call(kernel, shapes, in_specs, name):
    out_shape = [jax.ShapeDtypeStruct(*shape) for shape in shapes]
    return pl.pallas_call(
        kernel,
        out_shape=out_shape,
        in_specs=in_specs,
        out_specs=[VMEM] * len(shapes),
        compiler_params=pltpu.CompilerParams(vmem_limit_bytes=24 * 1024 * 1024),
        name=name,
    )


def permute(values, axis, offset):
    size = lax.axis_size(axis)
    return lax.ppermute(values, axis, [(at, at ^ offset) for at in range(size)])


def fused_body(dual_ops, mode_traces, route, mode_block, local_gap):
    peers = lax.axis_size("sub")
    planes = lax.axis_size("rep")
    loads, rows = local_gap.shape
    per_peer = rows // peers
    groups = mode_block.shape[0] // AGG_SUBS
    coarse = GROUP * groups
    f32 = jnp.float32

    def blocks(height):
        return [((height, per_peer), f32)] * peers

    def exchange(values):
        return [permute(value, "sub", offset + 1) for offset, value in enumerate(values)]

    place, own, *send = call(
        functools.partial(place_kernel, peers),
        [((rows, rows + per_peer), jnp.bfloat16), *blocks(loads + GROUP)],
        [VMEM] * 3,
        "place",
    )(route, local_gap, mode_traces)
    got = exchange(send)
    tall = (loads + coarse, rows)
    basis, image, back, *send = call(
        functools.partial(first_kernel, peers, planes, groups),
        [(tall, f32), (tall, f32), *blocks(loads + coarse)],
        [SMEM] + [VMEM] * (4 + peers),
        "first",
    )(mode_block, place, dual_ops, local_gap, mode_traces, own, *got)
    got = exchange(send)
    jump, terms = call(
        functools.partial(second_kernel, peers),
        [(tall, f32), ((loads + coarse, 8 * coarse), f32)],
        [VMEM] * (4 + peers),
        "second",
    )(place, dual_ops, basis, image, back, *got)
    terms = tree_sum([terms, *(permute(terms, "rep", offset) for offset in range(1, planes))])
    parts = [terms, *(permute(terms, "sub", offset) for offset in range(1, peers))]
    return call(
        final_kernel,
        [((loads, rows), f32), ((loads, MODES * groups), f32)],
        [VMEM] * (2 + peers),
        "final",
    )(basis, jump, *parts)


def general_body(dual_ops, mode_traces, route, mode_block, local_gap):
    own_index = lax.axis_index("sub")
    plane_index = lax.axis_index("rep")
    peer_count = lax.axis_size("sub")
    plane_count = lax.axis_size("rep")
    operator = dual_ops[0]
    traces = mode_traces[0]
    slot_rows = route[0]
    rows_here = operator.shape[0]
    load_cases = local_gap.shape[0]
    per_peer = rows_here // peer_count
    blocks = mode_block[:, 0]
    block_count = blocks.shape[0] // AGG_SUBS
    coarse = block_count * MODES
    positions = jnp.arange(rows_here, dtype=jnp.int32)
    inverse = jnp.zeros((rows_here,), jnp.int32).at[slot_rows].set(positions)
    slot_peer = positions // per_peer
    within = positions % per_peer
    flip_index = jnp.where(
        slot_peer == own_index, slot_peer * per_peer + per_peer - 1 - within, positions
    )
    peer_ids = jnp.arange(peer_count, dtype=jnp.int32)
    peer_blocks = blocks[peer_ids * plane_count + plane_index]
    own_block = blocks[own_index * plane_count + plane_index]
    labels = jnp.arange(block_count, dtype=jnp.int32)
    peer_onehot = (peer_blocks[:, None] == labels[None, :]).astype(jnp.float32)
    own_onehot = (labels == own_block).astype(jnp.float32)
    trace_slots = traces[:, slot_rows]
    receive_index = flip_index[inverse]

    def to_peers(values):
        return values[:, slot_rows]

    def from_peers(values):
        return values[:, inverse]

    gap_peers = to_peers(local_gap)
    got_traces = lax.all_to_all(trace_slots, "sub", split_axis=1, concat_axis=1, tiled=True)
    got_gap = lax.all_to_all(gap_peers, "sub", split_axis=1, concat_axis=1, tiled=True)
    partner_traces = got_traces[:, flip_index]
    residual = local_gap - got_gap[:, receive_index]
    own_gram = jnp.dot(traces, traces.T, precision=HIGHEST)
    paired = (trace_slots[:, None, :] * partner_traces[None, :, :]).reshape(
        MODES, MODES, peer_count, per_peer
    )
    cross_terms = jnp.sum(paired, axis=3)
    cross_blocks = jnp.einsum("klq,qb->kbl", cross_terms, peer_onehot, precision=HIGHEST)
    own_blocks = own_gram[:, None, :] * own_onehot[None, :, None]
    row_term = 2.0 * (own_blocks - cross_blocks).reshape(MODES, coarse)
    gram_term = (own_onehot[:, None, None] * row_term[None]).reshape(coarse, coarse)

    def coarse_term(values):
        own_part = 2.0 * jnp.dot(values, traces.T, precision=HIGHEST)
        return (own_part[:, None, :] * own_onehot[None, :, None]).reshape(load_cases, coarse)

    def expand(amounts):
        grouped = amounts.reshape(load_cases, block_count, MODES)
        own_amounts = lax.dynamic_index_in_dim(grouped, own_block, 1, keepdims=False)
        own_part = jnp.dot(own_amounts, traces, precision=HIGHEST)
        peer_amounts = jnp.einsum("qb,rbk->rkq", peer_onehot, grouped, precision=HIGHEST)
        spread = jnp.repeat(peer_amounts, per_peer, axis=2)
        peer_part = jnp.sum(spread * partner_traces[None, :, :], axis=1)
        return own_part - from_peers(peer_part)

    squares = jnp.sum(residual * residual, axis=1)
    gram_matrix, coarse_res, norm_res = lax.psum(
        (gram_term, coarse_term(residual), squares), ("sub", "rep")
    )
    factor = jnp.linalg.cholesky(gram_matrix)

    def solve_coarse(right):
        return jax.scipy.linalg.cho_solve((factor, True), right.T).T

    amplitudes = solve_coarse(coarse_res)
    projected = residual - expand(amplitudes)
    inner_sum = norm_res - jnp.sum(amplitudes * coarse_res, axis=1)
    direction = projected
    multipliers = jnp.zeros_like(residual)
    for iteration in range(ITERS):
        product = lax.dot_general(
            direction.astype(jnp.bfloat16),
            operator,
            (((1,), (1,)), ((), ())),
            preferred_element_type=jnp.float32,
        )
        got_product = lax.all_to_all(
            to_peers(product), "sub", split_axis=1, concat_axis=1, tiled=True
        )
        image_jump = product - got_product[:, receive_index]
        coarse_jump, jump_squares, residual_cross, curvature = lax.psum(
            (
                coarse_term(image_jump),
                jnp.sum(image_jump * image_jump, axis=1),
                jnp.sum(residual * image_jump, axis=1),
                jnp.sum(direction * image_jump, axis=1),
            ),
            ("sub", "rep"),
        )
        step_size = inner_sum / curvature
        multipliers = multipliers + step_size[:, None] * direction
        residual = residual - step_size[:, None] * image_jump
        coarse_res = coarse_res - step_size[:, None] * coarse_jump
        norm_res = (
            norm_res - 2.0 * step_size * residual_cross + step_size * step_size * jump_squares
        )
        amplitudes = solve_coarse(coarse_res)
        if iteration + 1 < ITERS:
            projected = residual - expand(amplitudes)
            renewed = norm_res - jnp.sum(amplitudes * coarse_res, axis=1)
            direction = projected + (renewed / inner_sum)[:, None] * direction
            inner_sum = renewed
    return (multipliers, amplitudes)


def fits(mesh, dual_ops, mode_block, local_gap):
    peers, planes = mesh.shape["sub"], mesh.shape["rep"]
    powers = all(size & (size - 1) == 0 for size in (peers, planes))
    whole = dual_ops.shape[1] % (128 * peers) == 0 and local_gap.shape[0] % 16 == 0
    return powers and whole and 8 * GROUP * (mode_block.shape[0] // AGG_SUBS) == 128


def solution(mesh):
    placed = (
        P(("sub", "rep"), None, None),
        P(("sub", "rep"), None, None),
        P(("sub", "rep"), None),
        P(),
        P(None, ("sub", "rep")),
    )

    def run(dual_ops, mode_traces, route, mode_block, local_gap):
        body = fused_body if fits(mesh, dual_ops, mode_block, local_gap) else general_body
        return jax.shard_map(
            body, mesh=mesh, in_specs=placed, out_specs=(P(None, ("sub", "rep")), P()), check_vma=False
        )(dual_ops, mode_traces, route, mode_block, local_gap)

    return run
```

```python
import functools

import jax
import jax.numpy as jnp
from jax import lax
from jax.experimental import pallas as pl
from jax.experimental.pallas import tpu as pltpu
from jax.sharding import PartitionSpec as P

MODES = 6
AGG_SUBS = 16
ITERS = 2
GROUP = 8
SCALAR_LANES = (MODES, MODES + 1, GROUP + MODES, GROUP + MODES + 1, 2 * GROUP + MODES)

HIGHEST = lax.Precision.HIGHEST
VMEM = pl.BlockSpec(memory_space=pltpu.VMEM)
HBM = pl.BlockSpec(memory_space=pltpu.HBM)
NN = (((1,), (0,)), ((), ()))
NT = (((1,), (1,)), ((), ()))


def split(values):
    high = values.astype(jnp.bfloat16).astype(jnp.float32)
    return jnp.concatenate([high, values - high], axis=0).astype(jnp.bfloat16)


def split_dot(values, matrix, dims):
    rows = values.shape[0]
    both = lax.dot_general(split(values), matrix, dims, preferred_element_type=jnp.float32)
    return both[:rows] + both[rows:]


def small_dot(left, right):
    return jnp.dot(left, right, precision=HIGHEST, preferred_element_type=jnp.float32)


def send_blocks(values, place_ref, send_ref):
    peers, _, per_peer = send_ref.shape
    slots = split_dot(values, place_ref[...], NN)
    for peer in range(peers):
        send_ref[peer] = slots[:, peer * per_peer : (peer + 1) * per_peer]
    send_ref[lax.axis_index("sub")] = slots[:, peers * per_peer :]


def jump_of(values, got_ref, place_ref):
    got = jnp.concatenate([got_ref[peer] for peer in range(got_ref.shape[0])], axis=1)
    return values - split_dot(got, place_ref[:, : values.shape[1]], NT)


def place_kernel(
    route_hbm, block_hbm, gap_hbm, traces_hbm, operator_hbm,
    place_ref, operator_ref, own_ref, send_ref,
    route_ref, block_ref, traces_ref, sems,
):
    loads, rows = gap_hbm.shape
    peers, _, per_peer = send_ref.shape
    copies = [
        pltpu.make_async_copy(source, target, sems.at[at])
        for at, (source, target) in enumerate(
            (
                (route_hbm, route_ref),
                (block_hbm, block_ref),
                (traces_hbm, traces_ref),
                (gap_hbm, own_ref.at[pl.ds(0, loads)]),
                (operator_hbm, operator_ref),
            )
        )
    ]
    for copy in copies:
        copy.start()
    own_index = lax.axis_index("sub")
    device = own_index * lax.axis_size("rep") + lax.axis_index("rep")
    copies[0].wait()
    row_ids = lax.broadcasted_iota(jnp.int32, (rows, per_peer), 0)
    for peer in range(peers):
        columns = slice(peer * per_peer, (peer + 1) * per_peer)
        place_ref[:, columns] = jnp.where(row_ids == route_ref[:, columns], 1.0, 0.0).astype(jnp.bfloat16)
    low = lax.broadcasted_iota(jnp.int32, (per_peer, per_peer), 0)
    high = lax.broadcasted_iota(jnp.int32, (per_peer, per_peer), 1)
    reverse = jnp.where(low + high == per_peer - 1, 1.0, 0.0).astype(jnp.bfloat16)
    own_columns = pl.ds(pl.multiple_of(own_index * per_peer, per_peer), per_peer)
    place_ref[:, rows:] = jnp.dot(
        place_ref[:, own_columns], reverse, preferred_element_type=jnp.float32
    ).astype(jnp.bfloat16)
    copies[1].wait()
    copies[2].wait()
    blocks = block_ref[...]
    lane = lax.broadcasted_iota(jnp.int32, blocks.shape, 1)
    own_block = jnp.sum(jnp.where(lane == device, blocks, 0), axis=1, keepdims=True)
    modes = traces_ref.shape[0]
    traces = jnp.concatenate(
        [traces_ref[mode] for mode in range(modes)] + [jnp.zeros((GROUP - modes, rows), jnp.float32)], axis=0
    )
    for label in range((own_ref.shape[0] - loads) // GROUP):
        start = loads + label * GROUP
        own_ref[start : start + GROUP] = jnp.where(own_block == label, traces, 0.0)
    copies[3].wait()
    send_blocks(own_ref[...], place_ref, send_ref)
    copies[4].wait()


def first_kernel(got_ref, own_ref, place_ref, operator_ref, basis_ref, image_ref, send_ref):
    basis = jump_of(own_ref[...], got_ref, place_ref)
    basis_ref[...] = basis
    image = split_dot(basis, operator_ref[0], NT)
    image_ref[...] = image
    send_blocks(image, place_ref, send_ref)


def products_of(left, right):
    both = lax.dot_general(split(left), split(right), NT, preferred_element_type=jnp.float32)
    both = both[: left.shape[0]] + both[left.shape[0] :]
    return both + pltpu.roll(both, right.shape[0], 1)


def with_scalars(top, products, lanes):
    lane = lax.broadcasted_iota(jnp.int32, top.shape, 1)
    for at, product in zip(lanes, products):
        top = jnp.where(lane == at, jnp.sum(product, axis=1, keepdims=True), top)
    return top


def early_kernel(basis_ref, image_ref, terms_ref):
    coarse = terms_ref.shape[1] // 8
    loads = basis_ref.shape[0] - coarse
    basis, image = basis_ref[...], image_ref[...]
    left = jnp.concatenate([basis[:loads], image[:loads], basis[loads:]])
    empty = jnp.zeros((2 * coarse, basis.shape[1]), jnp.float32)
    both = products_of(left, jnp.concatenate([basis[loads:], image[loads:], empty]))
    strip = lax.broadcasted_iota(jnp.int32, (loads, 8 * coarse), 1) // coarse
    top = jnp.where(strip < 2, both[:loads], 0.0)
    top = jnp.where(strip == 4, both[loads : 2 * loads], top)
    residual = basis[:loads]
    terms_ref[:loads] = with_scalars(top, (residual * residual, residual * image[:loads]), SCALAR_LANES[:2])
    strip = lax.broadcasted_iota(jnp.int32, (coarse, 8 * coarse), 1) // coarse
    terms_ref[loads:] = jnp.where(strip < 2, both[2 * loads :], 0.0)


def second_kernel(early_ref, got_ref, basis_ref, image_ref, place_ref, operator_ref, jump_ref, terms_ref):
    coarse = terms_ref.shape[1] // 8
    loads = basis_ref.shape[0] - coarse
    jump = jump_of(image_ref[...], got_ref, place_ref)
    jump_ref[...] = jump
    basis = basis_ref[...]
    second = split_dot(jump, operator_ref[0], NT)
    left = jnp.concatenate([basis[:loads], jump[:loads], second[:loads], basis[loads:], jump[loads:]])
    empty = jnp.zeros((coarse, basis.shape[1]), jnp.float32)
    both = products_of(left, jnp.concatenate([basis[loads:], empty, jump[loads:], second[loads:]]))
    along, jumped, doubled = (both[at * loads : (at + 1) * loads] for at in range(3))
    base, far = both[3 * loads : 3 * loads + coarse], both[3 * loads + coarse :]
    strip = lax.broadcasted_iota(jnp.int32, (loads, 8 * coarse), 1) // coarse
    top = jnp.where(strip == 2, doubled, 0.0)
    top = jnp.where(strip == 3, along, top)
    top = jnp.where(strip == 5, pltpu.roll(doubled, coarse, 1), top)
    top = jnp.where(strip >= 6, jumped, top)
    residual, jump_loads, second_loads = basis[:loads], jump[:loads], second[:loads]
    products = (jump_loads * jump_loads, jump_loads * second_loads, residual * second_loads)
    terms_ref[:loads] = early_ref[:loads] + with_scalars(top, products, SCALAR_LANES[2:])
    strip = lax.broadcasted_iota(jnp.int32, (coarse, 8 * coarse), 1) // coarse
    base = jnp.where((strip == 2) | (strip == 3), base, 0.0)
    height = loads + coarse
    terms_ref[loads:height] = early_ref[loads:] + jnp.where(strip < 4, base, far)
    terms_ref[height:] = jnp.zeros((terms_ref.shape[0] - height, terms_ref.shape[1]), jnp.float32)


def fold_kernel(pieces, got_ref, sum_ref):
    rows = got_ref.shape[0]
    piece = rows // pieces
    tall = max(8, piece)
    total = got_ref[:tall]
    for at in range(1, rows // tall):
        total = total + got_ref[at * tall : (at + 1) * tall]
    shift = piece
    while shift < tall:
        total = total + pltpu.roll(total, shift, 0)
        shift *= 2
    for at in range(rows // tall):
        sum_ref[at * tall : (at + 1) * tall] = total


def inverse_of(gram, coarse):
    row = lax.broadcasted_iota(jnp.int32, (coarse, 2 * coarse), 0)
    lane = lax.broadcasted_iota(jnp.int32, (coarse, 2 * coarse), 1)
    unit = jnp.where(lane - coarse == row, 1.0, 0.0)
    work = jnp.concatenate([gram, unit[:, coarse:]], axis=1)
    work = jnp.where((lane < coarse) & (row % GROUP >= MODES), jnp.where(lane == row, 1.0, 0.0), work)
    work = jnp.where((lane < coarse) & (lane % GROUP >= MODES), jnp.where(lane == row, 1.0, 0.0), work)
    for pivot in range(coarse):
        if pivot % GROUP >= MODES:
            continue
        scaled = work[pivot : pivot + 1] / work[pivot : pivot + 1, pivot : pivot + 1]
        work = jnp.where(row == pivot, scaled, work - work[:, pivot : pivot + 1] * scaled)
    return work[:, coarse:]


def final_kernel(terms_ref, basis_ref, jump_ref, multipliers_ref, amplitudes_ref):
    coarse = terms_ref.shape[1] // 8
    loads = basis_ref.shape[0] - coarse
    groups = coarse // GROUP
    terms = terms_ref[: loads + coarse]

    def scalar(at):
        lane = SCALAR_LANES[at]
        return terms[:loads, lane : lane + 1]

    def total(values):
        return jnp.sum(values, axis=1, keepdims=True)

    used = lax.broadcasted_iota(jnp.int32, (loads, coarse), 1) % GROUP < MODES

    def strip(at):
        return jnp.where(used, terms[:loads, at * coarse : (at + 1) * coarse], 0.0)

    def block(at):
        return terms[loads:, at * coarse : (at + 1) * coarse]

    res_res, res_image, jump_jump, jump_second, res_second = (scalar(at) for at in range(5))
    coarse_res, res_h, second_z, res_dz, image_g, second_g, jump_z, jump_dz = (strip(at) for at in range(8))
    gram, g_h, g_dz, z_z, z_dz = block(0), block(1), block(3), block(6), block(7)
    inverse = inverse_of(gram, coarse)
    amounts = small_dot(coarse_res, inverse)
    inner = res_res - total(amounts * coarse_res)
    products = small_dot(amounts, jnp.concatenate([g_h.T, z_z], axis=1))
    coarse_image = image_g - products[:, :coarse]
    res_along = 2.0 * (res_image - total(amounts * res_h))
    curvature = res_along - 2.0 * total(amounts * coarse_image)
    step = inner / curvature
    along_along = jump_jump - total(amounts * (2.0 * jump_z - products[:, coarse:]))
    norm = res_res - 2.0 * step * res_along + step * step * along_along
    coarse_next = coarse_res - 2.0 * step * coarse_image
    amounts_next = small_dot(coarse_next, inverse)
    renewed = norm - total(amounts_next * coarse_next)
    ratio = renewed / inner
    on_res = 1.0 + ratio
    on_jump = -step
    on_z = step * amounts
    on_g = -(amounts_next + ratio * amounts)
    spread = small_dot(
        jnp.concatenate([on_z, on_g], axis=1),
        jnp.concatenate(
            [
                jnp.concatenate([z_dz.T, g_dz.T], axis=1),
                jnp.concatenate([0.5 * z_z, g_h.T], axis=1),
            ],
            axis=0,
        ),
    )
    at_z = 0.5 * on_res * jump_z + on_jump * second_z + spread[:, :coarse]
    at_g = on_res * image_g + on_jump * second_g + spread[:, coarse:]
    at_res = on_res * res_image + on_jump * res_second + total(on_z * res_dz + on_g * res_h)
    at_jump = 0.5 * on_res * jump_jump + on_jump * jump_second + total(on_z * jump_dz + 0.5 * on_g * jump_z)
    curvature = 2.0 * (on_res * at_res + on_jump * at_jump + total(on_z * at_z + on_g * at_g))
    second_step = renewed / curvature
    amplitudes = small_dot(coarse_next - 2.0 * second_step * at_g, inverse).T
    amplitudes_ref[...] = jnp.concatenate(
        [amplitudes[label * GROUP : label * GROUP + MODES] for label in range(groups)], axis=0
    )
    weights = jnp.concatenate([second_step * on_g - step * amounts, second_step * on_z], axis=1)
    columns = jnp.concatenate([basis_ref[loads:], jump_ref[loads:]], axis=0)
    multipliers_ref[...] = (
        (step + second_step * on_res) * basis_ref[:loads]
        + (second_step * on_jump) * jump_ref[:loads]
        + small_dot(weights, columns)
    )


def call(kernel, shapes, in_specs, name, scratch=()):
    return pl.pallas_call(
        kernel,
        out_shape=[jax.ShapeDtypeStruct(*shape) for shape in shapes],
        in_specs=in_specs,
        out_specs=[VMEM] * len(shapes),
        scratch_shapes=scratch,
        compiler_params=pltpu.CompilerParams(vmem_limit_bytes=24 * 1024 * 1024),
        name=name,
    )


def fused_body(dual_ops, mode_traces, route, mode_block, local_gap):
    peers = lax.axis_size("sub")
    devices = peers * lax.axis_size("rep")
    loads, rows = local_gap.shape
    modes = mode_traces.shape[1]
    subs = mode_block.shape[0]
    groups = subs // AGG_SUBS
    coarse = GROUP * groups
    f32, i32 = jnp.float32, jnp.int32
    height = loads + coarse
    tall = ((height, rows), f32)
    blocks = ((peers, height, rows // peers), f32)
    width = 8 * coarse
    piece = pl.next_power_of_2(pl.cdiv(height, devices))

    def exchange(values):
        return lax.all_to_all(values, "sub", split_axis=0, concat_axis=0, tiled=True)

    def pieces(values):
        values = values.reshape(devices, piece, width)
        values = lax.all_to_all(values, ("sub", "rep"), split_axis=0, concat_axis=0, tiled=True)
        return values.reshape(devices * piece, width)

    place, operator, own, send = call(
        place_kernel,
        [((rows, rows + rows // peers), jnp.bfloat16), (dual_ops.shape, dual_ops.dtype), tall, blocks],
        [HBM] * 5,
        "place",
        [
            pltpu.VMEM((1, rows), i32),
            pltpu.VMEM((1, subs), i32),
            pltpu.VMEM((modes, 1, rows), f32),
            pltpu.SemaphoreType.DMA((5,)),
        ],
    )(route, mode_block.reshape(1, subs), local_gap, mode_traces.transpose(1, 0, 2), dual_ops)
    basis, image, send = call(first_kernel, [tall, tall, blocks], [VMEM] * 4, "first")(
        exchange(send), own, place, operator
    )
    early = call(early_kernel, [((height, width), f32)], [VMEM] * 2, "early")(basis, image)[0]
    jump, terms = call(second_kernel, [tall, ((devices * piece, width), f32)], [VMEM] * 6, "second")(
        early, exchange(send), basis, image, place, operator
    )
    fold = call(functools.partial(fold_kernel, devices), [((devices * piece, width), f32)], [VMEM], "fold")
    terms = pieces(fold(pieces(terms))[0])
    multipliers, amplitudes = call(
        final_kernel, [((loads, rows), f32), ((MODES * groups, loads), f32)], [VMEM] * 3, "final"
    )(terms, basis, jump)
    return multipliers, amplitudes.T


def general_body(dual_ops, mode_traces, route, mode_block, local_gap):
    own_index = lax.axis_index("sub")
    plane_index = lax.axis_index("rep")
    peer_count = lax.axis_size("sub")
    plane_count = lax.axis_size("rep")
    operator = dual_ops[0]
    traces = mode_traces[0]
    slot_rows = route[0]
    rows_here = operator.shape[0]
    load_cases = local_gap.shape[0]
    per_peer = rows_here // peer_count
    blocks = mode_block[:, 0]
    block_count = blocks.shape[0] // AGG_SUBS
    coarse = block_count * MODES
    positions = jnp.arange(rows_here, dtype=jnp.int32)
    inverse = jnp.zeros((rows_here,), jnp.int32).at[slot_rows].set(positions)
    slot_peer = positions // per_peer
    within = positions % per_peer
    flip_index = jnp.where(
        slot_peer == own_index, slot_peer * per_peer + per_peer - 1 - within, positions
    )
    peer_ids = jnp.arange(peer_count, dtype=jnp.int32)
    peer_blocks = blocks[peer_ids * plane_count + plane_index]
    own_block = blocks[own_index * plane_count + plane_index]
    labels = jnp.arange(block_count, dtype=jnp.int32)
    peer_onehot = (peer_blocks[:, None] == labels[None, :]).astype(jnp.float32)
    own_onehot = (labels == own_block).astype(jnp.float32)
    trace_slots = traces[:, slot_rows]
    receive_index = flip_index[inverse]

    def to_peers(values):
        return values[:, slot_rows]

    def from_peers(values):
        return values[:, inverse]

    gap_peers = to_peers(local_gap)
    got_traces = lax.all_to_all(trace_slots, "sub", split_axis=1, concat_axis=1, tiled=True)
    got_gap = lax.all_to_all(gap_peers, "sub", split_axis=1, concat_axis=1, tiled=True)
    partner_traces = got_traces[:, flip_index]
    residual = local_gap - got_gap[:, receive_index]
    own_gram = jnp.dot(traces, traces.T, precision=HIGHEST)
    paired = (trace_slots[:, None, :] * partner_traces[None, :, :]).reshape(
        MODES, MODES, peer_count, per_peer
    )
    cross_terms = jnp.sum(paired, axis=3)
    cross_blocks = jnp.einsum("klq,qb->kbl", cross_terms, peer_onehot, precision=HIGHEST)
    own_blocks = own_gram[:, None, :] * own_onehot[None, :, None]
    row_term = 2.0 * (own_blocks - cross_blocks).reshape(MODES, coarse)
    gram_term = (own_onehot[:, None, None] * row_term[None]).reshape(coarse, coarse)

    def coarse_term(values):
        own_part = 2.0 * jnp.dot(values, traces.T, precision=HIGHEST)
        return (own_part[:, None, :] * own_onehot[None, :, None]).reshape(load_cases, coarse)

    def expand(amounts):
        grouped = amounts.reshape(load_cases, block_count, MODES)
        own_amounts = lax.dynamic_index_in_dim(grouped, own_block, 1, keepdims=False)
        own_part = jnp.dot(own_amounts, traces, precision=HIGHEST)
        peer_amounts = jnp.einsum("qb,rbk->rkq", peer_onehot, grouped, precision=HIGHEST)
        spread = jnp.repeat(peer_amounts, per_peer, axis=2)
        peer_part = jnp.sum(spread * partner_traces[None, :, :], axis=1)
        return own_part - from_peers(peer_part)

    squares = jnp.sum(residual * residual, axis=1)
    gram_matrix, coarse_res, norm_res = lax.psum(
        (gram_term, coarse_term(residual), squares), ("sub", "rep")
    )
    factor = jnp.linalg.cholesky(gram_matrix)

    def solve_coarse(right):
        return jax.scipy.linalg.cho_solve((factor, True), right.T).T

    amplitudes = solve_coarse(coarse_res)
    projected = residual - expand(amplitudes)
    inner_sum = norm_res - jnp.sum(amplitudes * coarse_res, axis=1)
    direction = projected
    multipliers = jnp.zeros_like(residual)
    for iteration in range(ITERS):
        product = lax.dot_general(
            direction.astype(jnp.bfloat16),
            operator,
            (((1,), (1,)), ((), ())),
            preferred_element_type=jnp.float32,
        )
        got_product = lax.all_to_all(
            to_peers(product), "sub", split_axis=1, concat_axis=1, tiled=True
        )
        image_jump = product - got_product[:, receive_index]
        coarse_jump, jump_squares, residual_cross, curvature = lax.psum(
            (
                coarse_term(image_jump),
                jnp.sum(image_jump * image_jump, axis=1),
                jnp.sum(residual * image_jump, axis=1),
                jnp.sum(direction * image_jump, axis=1),
            ),
            ("sub", "rep"),
        )
        step_size = inner_sum / curvature
        multipliers = multipliers + step_size[:, None] * direction
        residual = residual - step_size[:, None] * image_jump
        coarse_res = coarse_res - step_size[:, None] * coarse_jump
        norm_res = (
            norm_res - 2.0 * step_size * residual_cross + step_size * step_size * jump_squares
        )
        amplitudes = solve_coarse(coarse_res)
        if iteration + 1 < ITERS:
            projected = residual - expand(amplitudes)
            renewed = norm_res - jnp.sum(amplitudes * coarse_res, axis=1)
            direction = projected + (renewed / inner_sum)[:, None] * direction
            inner_sum = renewed
    return (multipliers, amplitudes)


def fits(mesh, dual_ops, mode_block, local_gap):
    peers, planes = mesh.shape["sub"], mesh.shape["rep"]
    powers = all(size & (size - 1) == 0 for size in (peers, planes))
    whole = dual_ops.shape[1] % (128 * peers) == 0 and local_gap.shape[0] % 16 == 0
    return powers and whole and 8 * GROUP * (mode_block.shape[0] // AGG_SUBS) == 128


def solution(mesh):
    placed = (
        P(("sub", "rep"), None, None),
        P(("sub", "rep"), None, None),
        P(("sub", "rep"), None),
        P(),
        P(None, ("sub", "rep")),
    )

    def run(dual_ops, mode_traces, route, mode_block, local_gap):
        body = fused_body if fits(mesh, dual_ops, mode_block, local_gap) else general_body
        return jax.shard_map(
            body, mesh=mesh, in_specs=placed, out_specs=(P(None, ("sub", "rep")), P()), check_vma=False
        )(dual_ops, mode_traces, route, mode_block, local_gap)

    return run
```

```python
import jax
import jax.numpy as jnp
from jax import lax
from jax.experimental import pallas as pl
from jax.experimental.pallas import tpu as pltpu
from jax.sharding import PartitionSpec as P

MODES = 6
AGG_SUBS = 16
ITERS = 2
GROUP = 8
SCALAR_LANES = (MODES, MODES + 1, GROUP + MODES, GROUP + MODES + 1, 2 * GROUP + MODES)

HIGHEST = lax.Precision.HIGHEST
VMEM = pl.BlockSpec(memory_space=pltpu.VMEM)
HBM = pl.BlockSpec(memory_space=pltpu.HBM)
NN = (((1,), (0,)), ((), ()))
NT = (((1,), (1,)), ((), ()))


def split(values):
    high = values.astype(jnp.bfloat16).astype(jnp.float32)
    return jnp.concatenate([high, values - high], axis=0).astype(jnp.bfloat16)


def split_dot(values, matrix, dims):
    rows = values.shape[0]
    both = lax.dot_general(split(values), matrix, dims, preferred_element_type=jnp.float32)
    return both[:rows] + both[rows:]


def small_dot(left, right):
    return jnp.dot(left, right, precision=HIGHEST, preferred_element_type=jnp.float32)


def send_blocks(values, place_ref, near_ref, own_ref, *pair_refs):
    height, per_peer = own_ref.shape
    peers = 2 * len(pair_refs) + 2
    slots = split_dot(values, place_ref[:, : peers * per_peer], NN)
    own_ref[...] = slots[:, :per_peer]
    near_ref[...] = slots[:, per_peer : 2 * per_peer]
    for at, ref in enumerate(pair_refs):
        start = (2 * at + 2) * per_peer
        ref[:height] = slots[:, start : start + per_peer]
        ref[height:] = slots[:, start + per_peer : start + 2 * per_peer]


def jump_of(values, place_ref, near_ref, own_ref, *pair_refs):
    height, per_peer = own_ref.shape
    got = []
    for at in range(len(pair_refs) + 1):
        if at:
            got.append(pair_refs[at - 1][:height])
        got.append(near_ref[at * height : (at + 1) * height])
    got = jnp.concatenate([*got, own_ref[...]], axis=1)
    return values - split_dot(got, place_ref[:, per_peer:], NT)


def place_kernel(
    route_hbm, block_hbm, gap_hbm, traces_hbm, operator_hbm,
    place_ref, operator_ref, values_ref, *refs,
):
    *send_refs, route_ref, block_ref, traces_ref, sems = refs
    loads, rows = gap_hbm.shape
    per_peer = send_refs[0].shape[1]
    peers = rows // per_peer
    copies = [
        pltpu.make_async_copy(source, target, sems.at[at])
        for at, (source, target) in enumerate(
            (
                (route_hbm, route_ref),
                (block_hbm, block_ref),
                (traces_hbm, traces_ref),
                (gap_hbm, values_ref.at[pl.ds(0, loads)]),
                (operator_hbm, operator_ref),
            )
        )
    ]
    for copy in copies:
        copy.start()
    own_index = lax.axis_index("sub")
    device = own_index * lax.axis_size("rep") + lax.axis_index("rep")
    row_ids = lax.broadcasted_iota(jnp.int32, (rows, per_peer), 0)
    low = lax.broadcasted_iota(jnp.int32, (per_peer, per_peer), 0)
    high = lax.broadcasted_iota(jnp.int32, (per_peer, per_peer), 1)
    reverse = jnp.where(low + high == per_peer - 1, 1.0, 0.0).astype(jnp.bfloat16)
    copies[0].wait()
    for offset in range(peers):
        start = pl.multiple_of((own_index ^ offset) * per_peer, per_peer)
        hits = row_ids == route_ref[:, pl.ds(start, per_peer)]
        at = (offset if offset else peers) * per_peer
        place_ref[:, at : at + per_peer] = jnp.where(hits, 1.0, 0.0).astype(jnp.bfloat16)
    place_ref[:, :per_peer] = jnp.dot(
        place_ref[:, rows:], reverse, preferred_element_type=jnp.float32
    ).astype(jnp.bfloat16)
    copies[1].wait()
    copies[2].wait()
    blocks = block_ref[...]
    lane = lax.broadcasted_iota(jnp.int32, blocks.shape, 1)
    own_block = jnp.sum(jnp.where(lane == device, blocks, 0), axis=1, keepdims=True)
    modes = traces_ref.shape[0]
    traces = jnp.concatenate(
        [traces_ref[mode] for mode in range(modes)] + [jnp.zeros((GROUP - modes, rows), jnp.float32)], axis=0
    )
    for label in range((values_ref.shape[0] - loads) // GROUP):
        start = loads + label * GROUP
        values_ref[start : start + GROUP] = jnp.where(own_block == label, traces, 0.0)
    copies[3].wait()
    send_blocks(values_ref[...], place_ref, *send_refs)
    copies[4].wait()


def first_kernel(place_ref, operator_ref, values_ref, *refs):
    got_refs, (basis_ref, image_ref, *send_refs) = refs[: len(refs) // 2 - 1], refs[len(refs) // 2 - 1 :]
    basis = jump_of(values_ref[...], place_ref, *got_refs)
    basis_ref[...] = basis
    image = split_dot(basis, operator_ref[0], NT)
    image_ref[...] = image
    send_blocks(image, place_ref, *send_refs)


def products_of(left, right):
    both = lax.dot_general(split(left), split(right), NT, preferred_element_type=jnp.float32)
    both = both[: left.shape[0]] + both[left.shape[0] :]
    return both + pltpu.roll(both, right.shape[0], 1)


def second_kernel(place_ref, operator_ref, basis_ref, image_ref, *refs):
    *got_refs, jump_ref, terms_ref = refs
    coarse = terms_ref.shape[1] // 8
    loads = basis_ref.shape[0] - coarse
    image = image_ref[...]
    jump = jump_of(image, place_ref, *got_refs)
    jump_ref[...] = jump
    basis = basis_ref[...]
    second = split_dot(jump, operator_ref[0], NT)
    left = jnp.concatenate([basis[:loads], jump[:loads], image[:loads], second[:loads], basis[loads:], jump[loads:]])
    both = products_of(left, jnp.concatenate([basis[loads:], image[loads:], jump[loads:], second[loads:]]))
    along, jumped, imaged, doubled = (both[at * loads : (at + 1) * loads] for at in range(4))
    base, far = both[4 * loads : 4 * loads + coarse], both[4 * loads + coarse :]
    lane = lax.broadcasted_iota(jnp.int32, (loads, 8 * coarse), 1)
    strip = lane // coarse
    top = jnp.where(strip == 2, doubled, along)
    top = jnp.where(strip == 4, imaged, top)
    top = jnp.where(strip == 5, pltpu.roll(doubled, coarse, 1), top)
    top = jnp.where(strip >= 6, jumped, top)
    residual, jump_loads = basis[:loads], jump[:loads]
    scalars = (
        residual * residual,
        residual * image[:loads],
        jump_loads * jump_loads,
        jump_loads * second[:loads],
        residual * second[:loads],
    )
    for at, product in zip(SCALAR_LANES, scalars):
        top = jnp.where(lane == at, jnp.sum(product, axis=1, keepdims=True), top)
    lane = lax.broadcasted_iota(jnp.int32, (coarse, 8 * coarse), 1)
    terms_ref[...] = jnp.concatenate([top, jnp.where(lane < 4 * coarse, base, far)], axis=0)


def inverse_of(gram, coarse):
    row = lax.broadcasted_iota(jnp.int32, (coarse, 2 * coarse), 0)
    lane = lax.broadcasted_iota(jnp.int32, (coarse, 2 * coarse), 1)
    unit = jnp.where(lane - coarse == row, 1.0, 0.0)
    work = jnp.concatenate([gram, unit[:, coarse:]], axis=1)
    work = jnp.where((lane < coarse) & (row % GROUP >= MODES), jnp.where(lane == row, 1.0, 0.0), work)
    work = jnp.where((lane < coarse) & (lane % GROUP >= MODES), jnp.where(lane == row, 1.0, 0.0), work)
    for pivot in range(coarse):
        if pivot % GROUP >= MODES:
            continue
        scaled = work[pivot : pivot + 1] / work[pivot : pivot + 1, pivot : pivot + 1]
        work = jnp.where(row == pivot, scaled, work - work[:, pivot : pivot + 1] * scaled)
    return work[:, coarse:]


def final_kernel(terms_ref, basis_ref, jump_ref, multipliers_ref, amplitudes_ref):
    coarse = terms_ref.shape[1] // 8
    loads = basis_ref.shape[0] - coarse
    groups = coarse // GROUP
    terms = terms_ref[: loads + coarse]

    def scalar(at):
        lane = SCALAR_LANES[at]
        return terms[:loads, lane : lane + 1]

    def total(values):
        return jnp.sum(values, axis=1, keepdims=True)

    used = lax.broadcasted_iota(jnp.int32, (loads, coarse), 1) % GROUP < MODES

    def strip(at):
        return jnp.where(used, terms[:loads, at * coarse : (at + 1) * coarse], 0.0)

    def block(at):
        return terms[loads:, at * coarse : (at + 1) * coarse]

    res_res, res_image, jump_jump, jump_second, res_second = (scalar(at) for at in range(5))
    coarse_res, res_h, second_z, res_dz, image_g, second_g, jump_z, jump_dz = (strip(at) for at in range(8))
    gram, g_h, g_dz, z_z, z_dz = block(0), block(1), block(3), block(6), block(7)
    inverse = inverse_of(gram, coarse)
    amounts = small_dot(coarse_res, inverse)
    inner = res_res - total(amounts * coarse_res)
    products = small_dot(amounts, jnp.concatenate([g_h.T, z_z], axis=1))
    coarse_image = image_g - products[:, :coarse]
    res_along = 2.0 * (res_image - total(amounts * res_h))
    curvature = res_along - 2.0 * total(amounts * coarse_image)
    step = inner / curvature
    along_along = jump_jump - total(amounts * (2.0 * jump_z - products[:, coarse:]))
    norm = res_res - 2.0 * step * res_along + step * step * along_along
    coarse_next = coarse_res - 2.0 * step * coarse_image
    amounts_next = small_dot(coarse_next, inverse)
    renewed = norm - total(amounts_next * coarse_next)
    ratio = renewed / inner
    on_res = 1.0 + ratio
    on_jump = -step
    on_z = step * amounts
    on_g = -(amounts_next + ratio * amounts)
    spread = small_dot(
        jnp.concatenate([on_z, on_g], axis=1),
        jnp.concatenate(
            [
                jnp.concatenate([z_dz.T, g_dz.T], axis=1),
                jnp.concatenate([0.5 * z_z, g_h.T], axis=1),
            ],
            axis=0,
        ),
    )
    at_z = 0.5 * on_res * jump_z + on_jump * second_z + spread[:, :coarse]
    at_g = on_res * image_g + on_jump * second_g + spread[:, coarse:]
    at_res = on_res * res_image + on_jump * res_second + total(on_z * res_dz + on_g * res_h)
    at_jump = 0.5 * on_res * jump_jump + on_jump * jump_second + total(on_z * jump_dz + 0.5 * on_g * jump_z)
    curvature = 2.0 * (on_res * at_res + on_jump * at_jump + total(on_z * at_z + on_g * at_g))
    second_step = renewed / curvature
    amplitudes = small_dot(coarse_next - 2.0 * second_step * at_g, inverse).T
    amplitudes_ref[...] = jnp.concatenate(
        [amplitudes[label * GROUP : label * GROUP + MODES] for label in range(groups)], axis=0
    )
    weights = jnp.concatenate([second_step * on_g - step * amounts, second_step * on_z], axis=1)
    columns = jnp.concatenate([basis_ref[loads:], jump_ref[loads:]], axis=0)
    multipliers_ref[...] = (
        (step + second_step * on_res) * basis_ref[:loads]
        + (second_step * on_jump) * jump_ref[:loads]
        + small_dot(weights, columns)
    )


def call(kernel, shapes, in_specs, name, scratch=()):
    return pl.pallas_call(
        kernel,
        out_shape=[jax.ShapeDtypeStruct(*shape) for shape in shapes],
        in_specs=in_specs,
        out_specs=[VMEM] * len(shapes),
        scratch_shapes=scratch,
        compiler_params=pltpu.CompilerParams(vmem_limit_bytes=24 * 1024 * 1024),
        name=name,
    )


def permute(values, axis, offset):
    size = lax.axis_size(axis)
    return lax.ppermute(values, axis, [(at, at ^ offset) for at in range(size)])


def exchange(near, own, *pairs):
    height = own.shape[0]
    pairs = [permute(pair, "sub", 2 * at + 2) for at, pair in enumerate(pairs)]
    near = permute(jnp.concatenate([near, *(pair[height:] for pair in pairs)], axis=0), "sub", 1)
    return near, own, *pairs


def fused_body(dual_ops, mode_traces, route, mode_block, local_gap):
    peers = lax.axis_size("sub")
    loads, rows = local_gap.shape
    modes = mode_traces.shape[1]
    subs = mode_block.shape[0]
    groups = subs // AGG_SUBS
    per_peer = rows // peers
    height = loads + GROUP * groups
    f32, i32 = jnp.float32, jnp.int32
    tall = ((height, rows), f32)
    wide = ((height, 8 * GROUP * groups), f32)
    blocks = [((height, per_peer), f32)] * 2 + [((2 * height, per_peer), f32)] * (peers // 2 - 1)

    inputs = [route, mode_block.reshape(1, subs), local_gap, mode_traces.transpose(1, 0, 2), dual_ops]
    place, operator, values, *send = call(
        place_kernel,
        [((rows, rows + per_peer), jnp.bfloat16), (dual_ops.shape, dual_ops.dtype), tall, *blocks],
        [HBM] * 5,
        "place",
        [
            pltpu.VMEM((1, rows), i32),
            pltpu.VMEM((1, subs), i32),
            pltpu.VMEM((modes, 1, rows), f32),
            pltpu.SemaphoreType.DMA((5,)),
        ],
    )(*(pltpu.with_memory_space_constraint(value, pltpu.HBM) for value in inputs))
    basis, image, *send = call(first_kernel, [tall, tall, *blocks], [VMEM] * (3 + len(blocks)), "first")(
        place, operator, values, *exchange(*send)
    )
    jump, terms = call(second_kernel, [tall, wide], [VMEM] * (4 + len(blocks)), "second")(
        place, operator, basis, image, *exchange(*send)
    )
    for axis in ("sub", "rep"):
        offset = 1
        while offset < lax.axis_size(axis):
            terms = terms + permute(terms, axis, offset)
            offset *= 2
    multipliers, amplitudes = call(
        final_kernel, [((loads, rows), f32), ((MODES * groups, loads), f32)], [VMEM] * 3, "final"
    )(terms, basis, jump)
    return multipliers, amplitudes.T


def general_body(dual_ops, mode_traces, route, mode_block, local_gap):
    own_index = lax.axis_index("sub")
    plane_index = lax.axis_index("rep")
    peer_count = lax.axis_size("sub")
    plane_count = lax.axis_size("rep")
    operator = dual_ops[0]
    traces = mode_traces[0]
    slot_rows = route[0]
    rows_here = operator.shape[0]
    load_cases = local_gap.shape[0]
    per_peer = rows_here // peer_count
    blocks = mode_block[:, 0]
    block_count = blocks.shape[0] // AGG_SUBS
    coarse = block_count * MODES
    positions = jnp.arange(rows_here, dtype=jnp.int32)
    inverse = jnp.zeros((rows_here,), jnp.int32).at[slot_rows].set(positions)
    slot_peer = positions // per_peer
    within = positions % per_peer
    flip_index = jnp.where(
        slot_peer == own_index, slot_peer * per_peer + per_peer - 1 - within, positions
    )
    peer_ids = jnp.arange(peer_count, dtype=jnp.int32)
    peer_blocks = blocks[peer_ids * plane_count + plane_index]
    own_block = blocks[own_index * plane_count + plane_index]
    labels = jnp.arange(block_count, dtype=jnp.int32)
    peer_onehot = (peer_blocks[:, None] == labels[None, :]).astype(jnp.float32)
    own_onehot = (labels == own_block).astype(jnp.float32)
    trace_slots = traces[:, slot_rows]
    receive_index = flip_index[inverse]

    def to_peers(values):
        return values[:, slot_rows]

    def from_peers(values):
        return values[:, inverse]

    gap_peers = to_peers(local_gap)
    got_traces = lax.all_to_all(trace_slots, "sub", split_axis=1, concat_axis=1, tiled=True)
    got_gap = lax.all_to_all(gap_peers, "sub", split_axis=1, concat_axis=1, tiled=True)
    partner_traces = got_traces[:, flip_index]
    residual = local_gap - got_gap[:, receive_index]
    own_gram = jnp.dot(traces, traces.T, precision=HIGHEST)
    paired = (trace_slots[:, None, :] * partner_traces[None, :, :]).reshape(
        MODES, MODES, peer_count, per_peer
    )
    cross_terms = jnp.sum(paired, axis=3)
    cross_blocks = jnp.einsum("klq,qb->kbl", cross_terms, peer_onehot, precision=HIGHEST)
    own_blocks = own_gram[:, None, :] * own_onehot[None, :, None]
    row_term = 2.0 * (own_blocks - cross_blocks).reshape(MODES, coarse)
    gram_term = (own_onehot[:, None, None] * row_term[None]).reshape(coarse, coarse)

    def coarse_term(values):
        own_part = 2.0 * jnp.dot(values, traces.T, precision=HIGHEST)
        return (own_part[:, None, :] * own_onehot[None, :, None]).reshape(load_cases, coarse)

    def expand(amounts):
        grouped = amounts.reshape(load_cases, block_count, MODES)
        own_amounts = lax.dynamic_index_in_dim(grouped, own_block, 1, keepdims=False)
        own_part = jnp.dot(own_amounts, traces, precision=HIGHEST)
        peer_amounts = jnp.einsum("qb,rbk->rkq", peer_onehot, grouped, precision=HIGHEST)
        spread = jnp.repeat(peer_amounts, per_peer, axis=2)
        peer_part = jnp.sum(spread * partner_traces[None, :, :], axis=1)
        return own_part - from_peers(peer_part)

    squares = jnp.sum(residual * residual, axis=1)
    gram_matrix, coarse_res, norm_res = lax.psum(
        (gram_term, coarse_term(residual), squares), ("sub", "rep")
    )
    factor = jnp.linalg.cholesky(gram_matrix)

    def solve_coarse(right):
        return jax.scipy.linalg.cho_solve((factor, True), right.T).T

    amplitudes = solve_coarse(coarse_res)
    projected = residual - expand(amplitudes)
    inner_sum = norm_res - jnp.sum(amplitudes * coarse_res, axis=1)
    direction = projected
    multipliers = jnp.zeros_like(residual)
    for iteration in range(ITERS):
        product = lax.dot_general(
            direction.astype(jnp.bfloat16),
            operator,
            (((1,), (1,)), ((), ())),
            preferred_element_type=jnp.float32,
        )
        got_product = lax.all_to_all(
            to_peers(product), "sub", split_axis=1, concat_axis=1, tiled=True
        )
        image_jump = product - got_product[:, receive_index]
        coarse_jump, jump_squares, residual_cross, curvature = lax.psum(
            (
                coarse_term(image_jump),
                jnp.sum(image_jump * image_jump, axis=1),
                jnp.sum(residual * image_jump, axis=1),
                jnp.sum(direction * image_jump, axis=1),
            ),
            ("sub", "rep"),
        )
        step_size = inner_sum / curvature
        multipliers = multipliers + step_size[:, None] * direction
        residual = residual - step_size[:, None] * image_jump
        coarse_res = coarse_res - step_size[:, None] * coarse_jump
        norm_res = (
            norm_res - 2.0 * step_size * residual_cross + step_size * step_size * jump_squares
        )
        amplitudes = solve_coarse(coarse_res)
        if iteration + 1 < ITERS:
            projected = residual - expand(amplitudes)
            renewed = norm_res - jnp.sum(amplitudes * coarse_res, axis=1)
            direction = projected + (renewed / inner_sum)[:, None] * direction
            inner_sum = renewed
    return (multipliers, amplitudes)


def fits(mesh, dual_ops, mode_block, local_gap):
    peers, planes = mesh.shape["sub"], mesh.shape["rep"]
    powers = all(size & (size - 1) == 0 for size in (peers, planes))
    whole = dual_ops.shape[1] % (128 * peers) == 0 and local_gap.shape[0] % 16 == 0
    return powers and whole and 8 * GROUP * (mode_block.shape[0] // AGG_SUBS) == 128


def solution(mesh):
    placed = (
        P(("sub", "rep"), None, None),
        P(("sub", "rep"), None, None),
        P(("sub", "rep"), None),
        P(),
        P(None, ("sub", "rep")),
    )

    def run(dual_ops, mode_traces, route, mode_block, local_gap):
        body = fused_body if fits(mesh, dual_ops, mode_block, local_gap) else general_body
        return jax.shard_map(
            body, mesh=mesh, in_specs=placed, out_specs=(P(None, ("sub", "rep")), P()), check_vma=False
        )(dual_ops, mode_traces, route, mode_block, local_gap)

    return run
```

```python
import jax
import jax.numpy as jnp
from jax import lax
from jax.experimental import pallas as pl
from jax.experimental.pallas import tpu as pltpu
from jax.sharding import PartitionSpec as P

MODES = 6
AGG_SUBS = 16
ITERS = 2
GROUP = 8
SCALAR_LANES = (MODES, MODES + 1, GROUP + MODES, GROUP + MODES + 1, 2 * GROUP + MODES)

HIGHEST = lax.Precision.HIGHEST
VMEM = pl.BlockSpec(memory_space=pltpu.VMEM)
HBM = pl.BlockSpec(memory_space=pltpu.HBM)
NN = (((1,), (0,)), ((), ()))
NT = (((1,), (1,)), ((), ()))


def split(values):
    high = values.astype(jnp.bfloat16).astype(jnp.float32)
    return jnp.concatenate([high, values - high], axis=0).astype(jnp.bfloat16)


def split_dot(values, matrix, dims):
    rows = values.shape[0]
    both = lax.dot_general(split(values), matrix, dims, preferred_element_type=jnp.float32)
    return both[:rows] + both[rows:]


def small_dot(left, right):
    return jnp.dot(left, right, precision=HIGHEST, preferred_element_type=jnp.float32)


def send_blocks(values, place_ref, near_ref, own_ref, *pair_refs):
    height, per_peer = own_ref.shape
    peers = 2 * len(pair_refs) + 2
    slots = split_dot(values, place_ref[:, : peers * per_peer], NN)
    own_ref[...] = slots[:, :per_peer]
    near_ref[...] = slots[:, per_peer : 2 * per_peer]
    for at, ref in enumerate(pair_refs):
        start = (2 * at + 2) * per_peer
        ref[:height] = slots[:, start : start + per_peer]
        ref[height:] = slots[:, start + per_peer : start + 2 * per_peer]


def jump_of(values, place_ref, near_ref, own_ref, *pair_refs):
    height, per_peer = own_ref.shape
    got = []
    for at in range(len(pair_refs) + 1):
        if at:
            got.append(pair_refs[at - 1][:height])
        got.append(near_ref[at * height : (at + 1) * height])
    got = jnp.concatenate([*got, own_ref[...]], axis=1)
    return values - split_dot(got, place_ref[:, per_peer:], NT)


def place_kernel(
    route_hbm, block_hbm, gap_hbm, traces_hbm, operator_hbm,
    place_ref, operator_ref, values_ref, *refs,
):
    *send_refs, route_ref, block_ref, traces_ref, sems = refs
    loads, rows = gap_hbm.shape
    per_peer = send_refs[0].shape[1]
    peers = rows // per_peer
    copies = [
        pltpu.make_async_copy(source, target, sems.at[at])
        for at, (source, target) in enumerate(
            (
                (route_hbm, route_ref),
                (block_hbm, block_ref),
                (traces_hbm, traces_ref),
                (gap_hbm, values_ref.at[pl.ds(0, loads)]),
                (operator_hbm, operator_ref),
            )
        )
    ]
    for copy in copies:
        copy.start()
    own_index = lax.axis_index("sub")
    device = own_index * lax.axis_size("rep") + lax.axis_index("rep")
    row_ids = lax.broadcasted_iota(jnp.int32, (rows, per_peer), 0)
    low = lax.broadcasted_iota(jnp.int32, (per_peer, per_peer), 0)
    high = lax.broadcasted_iota(jnp.int32, (per_peer, per_peer), 1)
    reverse = jnp.where(low + high == per_peer - 1, 1.0, 0.0).astype(jnp.bfloat16)
    copies[0].wait()
    for offset in range(peers):
        start = pl.multiple_of((own_index ^ offset) * per_peer, per_peer)
        hits = row_ids == route_ref[:, pl.ds(start, per_peer)]
        at = (offset if offset else peers) * per_peer
        place_ref[:, at : at + per_peer] = jnp.where(hits, 1.0, 0.0).astype(jnp.bfloat16)
    place_ref[:, :per_peer] = jnp.dot(
        place_ref[:, rows:], reverse, preferred_element_type=jnp.float32
    ).astype(jnp.bfloat16)
    copies[1].wait()
    copies[2].wait()
    blocks = block_ref[...]
    lane = lax.broadcasted_iota(jnp.int32, blocks.shape, 1)
    own_block = jnp.sum(jnp.where(lane == device, blocks, 0), axis=1, keepdims=True)
    modes = traces_ref.shape[0]
    traces = jnp.concatenate(
        [traces_ref[mode] for mode in range(modes)] + [jnp.zeros((GROUP - modes, rows), jnp.float32)], axis=0
    )
    for label in range((values_ref.shape[0] - loads) // GROUP):
        start = loads + label * GROUP
        values_ref[start : start + GROUP] = jnp.where(own_block == label, traces, 0.0)
    copies[3].wait()
    send_blocks(values_ref[...], place_ref, *send_refs)
    copies[4].wait()


def first_kernel(place_ref, operator_ref, values_ref, *refs):
    got_refs, (basis_ref, image_ref, *send_refs) = refs[: len(refs) // 2 - 1], refs[len(refs) // 2 - 1 :]
    basis = jump_of(values_ref[...], place_ref, *got_refs)
    basis_ref[...] = basis
    image = split_dot(basis, operator_ref[0], NT)
    image_ref[...] = image
    send_blocks(image, place_ref, *send_refs)


def products_of(left, right):
    both = lax.dot_general(split(left), split(right), NT, preferred_element_type=jnp.float32)
    both = both[: left.shape[0]] + both[left.shape[0] :]
    return both + pltpu.roll(both, right.shape[0], 1)


def second_kernel(place_ref, operator_ref, basis_ref, image_ref, *refs):
    *got_refs, jump_ref, terms_ref = refs
    coarse = terms_ref.shape[1] // 8
    loads = basis_ref.shape[0] - coarse
    image = image_ref[...]
    jump = jump_of(image, place_ref, *got_refs)
    jump_ref[...] = jump
    basis = basis_ref[...]
    second = split_dot(jump, operator_ref[0], NT)
    left = jnp.concatenate([basis[:loads], jump[:loads], image[:loads], second[:loads], basis[loads:], jump[loads:]])
    both = products_of(left, jnp.concatenate([basis[loads:], image[loads:], jump[loads:], second[loads:]]))
    along, jumped, imaged, doubled = (both[at * loads : (at + 1) * loads] for at in range(4))
    base, far = both[4 * loads : 4 * loads + coarse], both[4 * loads + coarse :]
    lane = lax.broadcasted_iota(jnp.int32, (loads, 8 * coarse), 1)
    strip = lane // coarse
    top = jnp.where(strip == 2, doubled, along)
    top = jnp.where(strip == 4, imaged, top)
    top = jnp.where(strip == 5, pltpu.roll(doubled, coarse, 1), top)
    top = jnp.where(strip >= 6, jumped, top)
    residual, jump_loads = basis[:loads], jump[:loads]
    scalars = (
        residual * residual,
        residual * image[:loads],
        jump_loads * jump_loads,
        jump_loads * second[:loads],
        residual * second[:loads],
    )
    for at, product in zip(SCALAR_LANES, scalars):
        top = jnp.where(lane == at, jnp.sum(product, axis=1, keepdims=True), top)
    lane = lax.broadcasted_iota(jnp.int32, (coarse, 8 * coarse), 1)
    terms_ref[...] = jnp.concatenate([top, jnp.where(lane < 4 * coarse, base, far)], axis=0)


def inverse_of(gram, coarse):
    row = lax.broadcasted_iota(jnp.int32, (coarse, 2 * coarse), 0)
    lane = lax.broadcasted_iota(jnp.int32, (coarse, 2 * coarse), 1)
    unit = jnp.where(lane - coarse == row, 1.0, 0.0)
    work = jnp.concatenate([gram, unit[:, coarse:]], axis=1)
    work = jnp.where((lane < coarse) & (row % GROUP >= MODES), jnp.where(lane == row, 1.0, 0.0), work)
    work = jnp.where((lane < coarse) & (lane % GROUP >= MODES), jnp.where(lane == row, 1.0, 0.0), work)
    for pivot in range(coarse):
        if pivot % GROUP >= MODES:
            continue
        scaled = work[pivot : pivot + 1] / work[pivot : pivot + 1, pivot : pivot + 1]
        work = jnp.where(row == pivot, scaled, work - work[:, pivot : pivot + 1] * scaled)
    return work[:, coarse:]


def final_kernel(terms_ref, basis_ref, jump_ref, multipliers_ref, amplitudes_ref):
    coarse = terms_ref.shape[1] // 8
    loads = basis_ref.shape[0] - coarse
    groups = coarse // GROUP
    terms = terms_ref[: loads + coarse]

    def scalar(at):
        lane = SCALAR_LANES[at]
        return terms[:loads, lane : lane + 1]

    def total(values):
        return jnp.sum(values, axis=1, keepdims=True)

    used = lax.broadcasted_iota(jnp.int32, (loads, coarse), 1) % GROUP < MODES

    def strip(at):
        return jnp.where(used, terms[:loads, at * coarse : (at + 1) * coarse], 0.0)

    def block(at):
        return terms[loads:, at * coarse : (at + 1) * coarse]

    res_res, res_image, jump_jump, jump_second, res_second = (scalar(at) for at in range(5))
    coarse_res, res_h, second_z, res_dz, image_g, second_g, jump_z, jump_dz = (strip(at) for at in range(8))
    gram, g_h, g_dz, z_z, z_dz = block(0), block(1), block(3), block(6), block(7)
    inverse = inverse_of(gram, coarse)
    amounts = small_dot(coarse_res, inverse)
    inner = res_res - total(amounts * coarse_res)
    products = small_dot(amounts, jnp.concatenate([g_h.T, z_z], axis=1))
    coarse_image = image_g - products[:, :coarse]
    res_along = 2.0 * (res_image - total(amounts * res_h))
    curvature = res_along - 2.0 * total(amounts * coarse_image)
    step = inner / curvature
    along_along = jump_jump - total(amounts * (2.0 * jump_z - products[:, coarse:]))
    norm = res_res - 2.0 * step * res_along + step * step * along_along
    coarse_next = coarse_res - 2.0 * step * coarse_image
    amounts_next = small_dot(coarse_next, inverse)
    renewed = norm - total(amounts_next * coarse_next)
    ratio = renewed / inner
    on_res = 1.0 + ratio
    on_jump = -step
    on_z = step * amounts
    on_g = -(amounts_next + ratio * amounts)
    spread = small_dot(
        jnp.concatenate([on_z, on_g], axis=1),
        jnp.concatenate(
            [
                jnp.concatenate([z_dz.T, g_dz.T], axis=1),
                jnp.concatenate([0.5 * z_z, g_h.T], axis=1),
            ],
            axis=0,
        ),
    )
    at_z = 0.5 * on_res * jump_z + on_jump * second_z + spread[:, :coarse]
    at_g = on_res * image_g + on_jump * second_g + spread[:, coarse:]
    at_res = on_res * res_image + on_jump * res_second + total(on_z * res_dz + on_g * res_h)
    at_jump = 0.5 * on_res * jump_jump + on_jump * jump_second + total(on_z * jump_dz + 0.5 * on_g * jump_z)
    curvature = 2.0 * (on_res * at_res + on_jump * at_jump + total(on_z * at_z + on_g * at_g))
    second_step = renewed / curvature
    amplitudes = small_dot(coarse_next - 2.0 * second_step * at_g, inverse).T
    amplitudes_ref[...] = jnp.concatenate(
        [amplitudes[label * GROUP : label * GROUP + MODES] for label in range(groups)], axis=0
    )
    weights = jnp.concatenate([second_step * on_g - step * amounts, second_step * on_z], axis=1)
    columns = jnp.concatenate([basis_ref[loads:], jump_ref[loads:]], axis=0)
    multipliers_ref[...] = (
        (step + second_step * on_res) * basis_ref[:loads]
        + (second_step * on_jump) * jump_ref[:loads]
        + small_dot(weights, columns)
    )


def call(kernel, shapes, in_specs, name, scratch=()):
    return pl.pallas_call(
        kernel,
        out_shape=[jax.ShapeDtypeStruct(*shape) for shape in shapes],
        in_specs=in_specs,
        out_specs=[VMEM] * len(shapes),
        scratch_shapes=scratch,
        compiler_params=pltpu.CompilerParams(vmem_limit_bytes=24 * 1024 * 1024),
        name=name,
    )


def permute(values, axis, offset):
    size = lax.axis_size(axis)
    return lax.ppermute(values, axis, [(at, at ^ offset) for at in range(size)])


def exchange(near, own, *pairs):
    height = own.shape[0]
    pairs = [permute(pair, "sub", 2 * at + 2) for at, pair in enumerate(pairs)]
    near = permute(jnp.concatenate([near, *(pair[height:] for pair in pairs)], axis=0), "sub", 1)
    return near, own, *pairs


def sum_over(values, axis, offsets):
    parts = [values, *(permute(values, axis, offset) for offset in offsets)]
    while len(parts) > 1:
        parts = [low + high for low, high in zip(parts[::2], parts[1::2])]
    return parts[0]


def fused_body(dual_ops, mode_traces, route, mode_block, local_gap):
    peers = lax.axis_size("sub")
    loads, rows = local_gap.shape
    modes = mode_traces.shape[1]
    subs = mode_block.shape[0]
    groups = subs // AGG_SUBS
    per_peer = rows // peers
    height = loads + GROUP * groups
    f32, i32 = jnp.float32, jnp.int32
    tall = ((height, rows), f32)
    wide = ((height, 8 * GROUP * groups), f32)
    blocks = [((height, per_peer), f32)] * 2 + [((2 * height, per_peer), f32)] * (peers // 2 - 1)

    inputs = [route, mode_block.reshape(1, subs), local_gap, mode_traces.transpose(1, 0, 2), dual_ops]
    place, operator, values, *send = call(
        place_kernel,
        [((rows, rows + per_peer), jnp.bfloat16), (dual_ops.shape, dual_ops.dtype), tall, *blocks],
        [HBM] * 5,
        "place",
        [
            pltpu.VMEM((1, rows), i32),
            pltpu.VMEM((1, subs), i32),
            pltpu.VMEM((modes, 1, rows), f32),
            pltpu.SemaphoreType.DMA((5,)),
        ],
    )(*(pltpu.with_memory_space_constraint(value, pltpu.HBM) for value in inputs))
    basis, image, *send = call(first_kernel, [tall, tall, *blocks], [VMEM] * (3 + len(blocks)), "first")(
        place, operator, values, *exchange(*send)
    )
    jump, terms = call(second_kernel, [tall, wide], [VMEM] * (4 + len(blocks)), "second")(
        place, operator, basis, image, *exchange(*send)
    )
    terms = sum_over(terms, "sub", (1,))
    terms = sum_over(terms, "sub", range(2, peers, 2))
    terms = sum_over(terms, "rep", range(1, lax.axis_size("rep")))
    multipliers, amplitudes = call(
        final_kernel, [((loads, rows), f32), ((MODES * groups, loads), f32)], [VMEM] * 3, "final"
    )(terms, basis, jump)
    return multipliers, amplitudes.T


def general_body(dual_ops, mode_traces, route, mode_block, local_gap):
    own_index = lax.axis_index("sub")
    plane_index = lax.axis_index("rep")
    peer_count = lax.axis_size("sub")
    plane_count = lax.axis_size("rep")
    operator = dual_ops[0]
    traces = mode_traces[0]
    slot_rows = route[0]
    rows_here = operator.shape[0]
    load_cases = local_gap.shape[0]
    per_peer = rows_here // peer_count
    blocks = mode_block[:, 0]
    block_count = blocks.shape[0] // AGG_SUBS
    coarse = block_count * MODES
    positions = jnp.arange(rows_here, dtype=jnp.int32)
    inverse = jnp.zeros((rows_here,), jnp.int32).at[slot_rows].set(positions)
    slot_peer = positions // per_peer
    within = positions % per_peer
    flip_index = jnp.where(
        slot_peer == own_index, slot_peer * per_peer + per_peer - 1 - within, positions
    )
    peer_ids = jnp.arange(peer_count, dtype=jnp.int32)
    peer_blocks = blocks[peer_ids * plane_count + plane_index]
    own_block = blocks[own_index * plane_count + plane_index]
    labels = jnp.arange(block_count, dtype=jnp.int32)
    peer_onehot = (peer_blocks[:, None] == labels[None, :]).astype(jnp.float32)
    own_onehot = (labels == own_block).astype(jnp.float32)
    trace_slots = traces[:, slot_rows]
    receive_index = flip_index[inverse]

    def to_peers(values):
        return values[:, slot_rows]

    def from_peers(values):
        return values[:, inverse]

    gap_peers = to_peers(local_gap)
    got_traces = lax.all_to_all(trace_slots, "sub", split_axis=1, concat_axis=1, tiled=True)
    got_gap = lax.all_to_all(gap_peers, "sub", split_axis=1, concat_axis=1, tiled=True)
    partner_traces = got_traces[:, flip_index]
    residual = local_gap - got_gap[:, receive_index]
    own_gram = jnp.dot(traces, traces.T, precision=HIGHEST)
    paired = (trace_slots[:, None, :] * partner_traces[None, :, :]).reshape(
        MODES, MODES, peer_count, per_peer
    )
    cross_terms = jnp.sum(paired, axis=3)
    cross_blocks = jnp.einsum("klq,qb->kbl", cross_terms, peer_onehot, precision=HIGHEST)
    own_blocks = own_gram[:, None, :] * own_onehot[None, :, None]
    row_term = 2.0 * (own_blocks - cross_blocks).reshape(MODES, coarse)
    gram_term = (own_onehot[:, None, None] * row_term[None]).reshape(coarse, coarse)

    def coarse_term(values):
        own_part = 2.0 * jnp.dot(values, traces.T, precision=HIGHEST)
        return (own_part[:, None, :] * own_onehot[None, :, None]).reshape(load_cases, coarse)

    def expand(amounts):
        grouped = amounts.reshape(load_cases, block_count, MODES)
        own_amounts = lax.dynamic_index_in_dim(grouped, own_block, 1, keepdims=False)
        own_part = jnp.dot(own_amounts, traces, precision=HIGHEST)
        peer_amounts = jnp.einsum("qb,rbk->rkq", peer_onehot, grouped, precision=HIGHEST)
        spread = jnp.repeat(peer_amounts, per_peer, axis=2)
        peer_part = jnp.sum(spread * partner_traces[None, :, :], axis=1)
        return own_part - from_peers(peer_part)

    squares = jnp.sum(residual * residual, axis=1)
    gram_matrix, coarse_res, norm_res = lax.psum(
        (gram_term, coarse_term(residual), squares), ("sub", "rep")
    )
    factor = jnp.linalg.cholesky(gram_matrix)

    def solve_coarse(right):
        return jax.scipy.linalg.cho_solve((factor, True), right.T).T

    amplitudes = solve_coarse(coarse_res)
    projected = residual - expand(amplitudes)
    inner_sum = norm_res - jnp.sum(amplitudes * coarse_res, axis=1)
    direction = projected
    multipliers = jnp.zeros_like(residual)
    for iteration in range(ITERS):
        product = lax.dot_general(
            direction.astype(jnp.bfloat16),
            operator,
            (((1,), (1,)), ((), ())),
            preferred_element_type=jnp.float32,
        )
        got_product = lax.all_to_all(
            to_peers(product), "sub", split_axis=1, concat_axis=1, tiled=True
        )
        image_jump = product - got_product[:, receive_index]
        coarse_jump, jump_squares, residual_cross, curvature = lax.psum(
            (
                coarse_term(image_jump),
                jnp.sum(image_jump * image_jump, axis=1),
                jnp.sum(residual * image_jump, axis=1),
                jnp.sum(direction * image_jump, axis=1),
            ),
            ("sub", "rep"),
        )
        step_size = inner_sum / curvature
        multipliers = multipliers + step_size[:, None] * direction
        residual = residual - step_size[:, None] * image_jump
        coarse_res = coarse_res - step_size[:, None] * coarse_jump
        norm_res = (
            norm_res - 2.0 * step_size * residual_cross + step_size * step_size * jump_squares
        )
        amplitudes = solve_coarse(coarse_res)
        if iteration + 1 < ITERS:
            projected = residual - expand(amplitudes)
            renewed = norm_res - jnp.sum(amplitudes * coarse_res, axis=1)
            direction = projected + (renewed / inner_sum)[:, None] * direction
            inner_sum = renewed
    return (multipliers, amplitudes)


def fits(mesh, dual_ops, mode_block, local_gap):
    peers, planes = mesh.shape["sub"], mesh.shape["rep"]
    powers = all(size & (size - 1) == 0 for size in (peers, planes))
    whole = dual_ops.shape[1] % (128 * peers) == 0 and local_gap.shape[0] % 16 == 0
    return powers and whole and 8 * GROUP * (mode_block.shape[0] // AGG_SUBS) == 128


def solution(mesh):
    placed = (
        P(("sub", "rep"), None, None),
        P(("sub", "rep"), None, None),
        P(("sub", "rep"), None),
        P(),
        P(None, ("sub", "rep")),
    )

    def run(dual_ops, mode_traces, route, mode_block, local_gap):
        body = fused_body if fits(mesh, dual_ops, mode_block, local_gap) else general_body
        return jax.shard_map(
            body, mesh=mesh, in_specs=placed, out_specs=(P(None, ("sub", "rep")), P()), check_vma=False
        )(dual_ops, mode_traces, route, mode_block, local_gap)

    return run
```

```python
import jax
import jax.numpy as jnp
from jax import lax
from jax.experimental import pallas as pl
from jax.experimental.pallas import tpu as pltpu
from jax.sharding import PartitionSpec as P

MODES = 6
AGG_SUBS = 16
ITERS = 2
GROUP = 8
SCALAR_LANES = (MODES, MODES + 1, GROUP + MODES, GROUP + MODES + 1, 2 * GROUP + MODES)

HIGHEST = lax.Precision.HIGHEST
VMEM = pl.BlockSpec(memory_space=pltpu.VMEM)
HBM = pl.BlockSpec(memory_space=pltpu.HBM)
NN = (((1,), (0,)), ((), ()))
NT = (((1,), (1,)), ((), ()))


def split(values):
    high = values.astype(jnp.bfloat16).astype(jnp.float32)
    return jnp.concatenate([high, values - high], axis=0).astype(jnp.bfloat16)


def split_dot(values, matrix, dims):
    rows = values.shape[0]
    both = lax.dot_general(split(values), matrix, dims, preferred_element_type=jnp.float32)
    return both[:rows] + both[rows:]


def small_dot(left, right):
    return jnp.dot(left, right, precision=HIGHEST, preferred_element_type=jnp.float32)


def send_blocks(values, place_ref, near_ref, own_ref, *pair_refs):
    height, per_peer = own_ref.shape
    peers = 2 * len(pair_refs) + 2
    slots = split_dot(values, place_ref[:, : peers * per_peer], NN)
    own_ref[...] = slots[:, :per_peer]
    near_ref[...] = slots[:, per_peer : 2 * per_peer]
    for at, ref in enumerate(pair_refs):
        start = (peers - 2 * at - 2) * per_peer
        ref[:height] = slots[:, start : start + per_peer]
        ref[height:] = slots[:, start + per_peer : start + 2 * per_peer]


def jump_of(values, place_ref, near_ref, own_ref, *pair_refs):
    height, per_peer = own_ref.shape
    got = [near_ref[:height]]
    for at in reversed(range(len(pair_refs))):
        got += [pair_refs[at][:height], near_ref[(at + 1) * height : (at + 2) * height]]
    got = jnp.concatenate([*got, own_ref[...]], axis=1)
    return values - split_dot(got, place_ref[:, per_peer:], NT)


def place_kernel(
    route_hbm, block_hbm, gap_hbm, traces_hbm, operator_hbm,
    place_ref, operator_ref, values_ref, *refs,
):
    *send_refs, route_ref, block_ref, traces_ref, sems = refs
    loads, rows = gap_hbm.shape
    per_peer = send_refs[0].shape[1]
    peers = rows // per_peer
    copies = [
        pltpu.make_async_copy(source, target, sems.at[at])
        for at, (source, target) in enumerate(
            (
                (route_hbm, route_ref),
                (block_hbm, block_ref),
                (traces_hbm, traces_ref),
                (gap_hbm, values_ref.at[pl.ds(0, loads)]),
                (operator_hbm, operator_ref),
            )
        )
    ]
    for copy in copies:
        copy.start()
    own_index = lax.axis_index("sub")
    device = own_index * lax.axis_size("rep") + lax.axis_index("rep")
    row_ids = lax.broadcasted_iota(jnp.int32, (rows, per_peer), 0)
    low = lax.broadcasted_iota(jnp.int32, (per_peer, per_peer), 0)
    high = lax.broadcasted_iota(jnp.int32, (per_peer, per_peer), 1)
    reverse = jnp.where(low + high == per_peer - 1, 1.0, 0.0).astype(jnp.bfloat16)
    copies[0].wait()
    for offset in range(peers):
        start = pl.multiple_of((own_index ^ offset) * per_peer, per_peer)
        hits = row_ids == route_ref[:, pl.ds(start, per_peer)]
        at = (offset if offset else peers) * per_peer
        place_ref[:, at : at + per_peer] = jnp.where(hits, 1.0, 0.0).astype(jnp.bfloat16)
    place_ref[:, :per_peer] = jnp.dot(
        place_ref[:, rows:], reverse, preferred_element_type=jnp.float32
    ).astype(jnp.bfloat16)
    copies[1].wait()
    copies[2].wait()
    blocks = block_ref[...]
    lane = lax.broadcasted_iota(jnp.int32, blocks.shape, 1)
    own_block = jnp.sum(jnp.where(lane == device, blocks, 0), axis=1, keepdims=True)
    modes = traces_ref.shape[0]
    traces = jnp.concatenate(
        [traces_ref[mode] for mode in range(modes)] + [jnp.zeros((GROUP - modes, rows), jnp.float32)], axis=0
    )
    for label in range((values_ref.shape[0] - loads) // GROUP):
        start = loads + label * GROUP
        values_ref[start : start + GROUP] = jnp.where(own_block == label, traces, 0.0)
    copies[3].wait()
    send_blocks(values_ref[...], place_ref, *send_refs)
    copies[4].wait()


def first_kernel(place_ref, operator_ref, values_ref, *refs):
    got_refs, (basis_ref, image_ref, *send_refs) = refs[: len(refs) // 2 - 1], refs[len(refs) // 2 - 1 :]
    basis = jump_of(values_ref[...], place_ref, *got_refs)
    basis_ref[...] = basis
    image = split_dot(basis, operator_ref[0], NT)
    image_ref[...] = image
    send_blocks(image, place_ref, *send_refs)


def products_of(left, right):
    both = lax.dot_general(split(left), split(right), NT, preferred_element_type=jnp.float32)
    both = both[: left.shape[0]] + both[left.shape[0] :]
    return both + pltpu.roll(both, right.shape[0], 1)


def second_kernel(place_ref, operator_ref, basis_ref, image_ref, *refs):
    *got_refs, jump_ref, terms_ref = refs
    coarse = terms_ref.shape[1] // 8
    loads = basis_ref.shape[0] - coarse
    image = image_ref[...]
    jump = jump_of(image, place_ref, *got_refs)
    jump_ref[...] = jump
    basis = basis_ref[...]
    second = split_dot(jump, operator_ref[0], NT)
    left = jnp.concatenate([basis[:loads], jump[:loads], image[:loads], second[:loads], basis[loads:], jump[loads:]])
    both = products_of(left, jnp.concatenate([basis[loads:], image[loads:], jump[loads:], second[loads:]]))
    along, jumped, imaged, doubled = (both[at * loads : (at + 1) * loads] for at in range(4))
    base, far = both[4 * loads : 4 * loads + coarse], both[4 * loads + coarse :]
    lane = lax.broadcasted_iota(jnp.int32, (loads, 8 * coarse), 1)
    strip = lane // coarse
    top = jnp.where(strip == 2, doubled, along)
    top = jnp.where(strip == 4, imaged, top)
    top = jnp.where(strip == 5, pltpu.roll(doubled, coarse, 1), top)
    top = jnp.where(strip >= 6, jumped, top)
    residual, jump_loads = basis[:loads], jump[:loads]
    scalars = (
        residual * residual,
        residual * image[:loads],
        jump_loads * jump_loads,
        jump_loads * second[:loads],
        residual * second[:loads],
    )
    for at, product in zip(SCALAR_LANES, scalars):
        top = jnp.where(lane == at, jnp.sum(product, axis=1, keepdims=True), top)
    lane = lax.broadcasted_iota(jnp.int32, (coarse, 8 * coarse), 1)
    terms_ref[...] = jnp.concatenate([top, jnp.where(lane < 4 * coarse, base, far)], axis=0)


def inverse_of(gram, coarse):
    row = lax.broadcasted_iota(jnp.int32, (coarse, 2 * coarse), 0)
    lane = lax.broadcasted_iota(jnp.int32, (coarse, 2 * coarse), 1)
    unit = jnp.where(lane - coarse == row, 1.0, 0.0)
    work = jnp.concatenate([gram, unit[:, coarse:]], axis=1)
    work = jnp.where((lane < coarse) & (row % GROUP >= MODES), jnp.where(lane == row, 1.0, 0.0), work)
    work = jnp.where((lane < coarse) & (lane % GROUP >= MODES), jnp.where(lane == row, 1.0, 0.0), work)
    for pivot in range(coarse):
        if pivot % GROUP >= MODES:
            continue
        scaled = work[pivot : pivot + 1] / work[pivot : pivot + 1, pivot : pivot + 1]
        work = jnp.where(row == pivot, scaled, work - work[:, pivot : pivot + 1] * scaled)
    return work[:, coarse:]


def final_kernel(terms_ref, basis_ref, jump_ref, multipliers_ref, amplitudes_ref):
    coarse = terms_ref.shape[1] // 8
    loads = basis_ref.shape[0] - coarse
    groups = coarse // GROUP
    terms = terms_ref[: loads + coarse]

    def scalar(at):
        lane = SCALAR_LANES[at]
        return terms[:loads, lane : lane + 1]

    def total(values):
        return jnp.sum(values, axis=1, keepdims=True)

    used = lax.broadcasted_iota(jnp.int32, (loads, coarse), 1) % GROUP < MODES

    def strip(at):
        return jnp.where(used, terms[:loads, at * coarse : (at + 1) * coarse], 0.0)

    def block(at):
        return terms[loads:, at * coarse : (at + 1) * coarse]

    res_res, res_image, jump_jump, jump_second, res_second = (scalar(at) for at in range(5))
    coarse_res, res_h, second_z, res_dz, image_g, second_g, jump_z, jump_dz = (strip(at) for at in range(8))
    gram, g_h, g_dz, z_z, z_dz = block(0), block(1), block(3), block(6), block(7)
    inverse = inverse_of(gram, coarse)
    amounts = small_dot(coarse_res, inverse)
    inner = res_res - total(amounts * coarse_res)
    products = small_dot(amounts, jnp.concatenate([g_h.T, z_z], axis=1))
    coarse_image = image_g - products[:, :coarse]
    res_along = 2.0 * (res_image - total(amounts * res_h))
    curvature = res_along - 2.0 * total(amounts * coarse_image)
    step = inner / curvature
    along_along = jump_jump - total(amounts * (2.0 * jump_z - products[:, coarse:]))
    norm = res_res - 2.0 * step * res_along + step * step * along_along
    coarse_next = coarse_res - 2.0 * step * coarse_image
    amounts_next = small_dot(coarse_next, inverse)
    renewed = norm - total(amounts_next * coarse_next)
    ratio = renewed / inner
    on_res = 1.0 + ratio
    on_jump = -step
    on_z = step * amounts
    on_g = -(amounts_next + ratio * amounts)
    spread = small_dot(
        jnp.concatenate([on_z, on_g], axis=1),
        jnp.concatenate(
            [
                jnp.concatenate([z_dz.T, g_dz.T], axis=1),
                jnp.concatenate([0.5 * z_z, g_h.T], axis=1),
            ],
            axis=0,
        ),
    )
    at_z = 0.5 * on_res * jump_z + on_jump * second_z + spread[:, :coarse]
    at_g = on_res * image_g + on_jump * second_g + spread[:, coarse:]
    at_res = on_res * res_image + on_jump * res_second + total(on_z * res_dz + on_g * res_h)
    at_jump = 0.5 * on_res * jump_jump + on_jump * jump_second + total(on_z * jump_dz + 0.5 * on_g * jump_z)
    curvature = 2.0 * (on_res * at_res + on_jump * at_jump + total(on_z * at_z + on_g * at_g))
    second_step = renewed / curvature
    amplitudes = small_dot(coarse_next - 2.0 * second_step * at_g, inverse).T
    amplitudes_ref[...] = jnp.concatenate(
        [amplitudes[label * GROUP : label * GROUP + MODES] for label in range(groups)], axis=0
    )
    weights = jnp.concatenate([second_step * on_g - step * amounts, second_step * on_z], axis=1)
    columns = jnp.concatenate([basis_ref[loads:], jump_ref[loads:]], axis=0)
    multipliers_ref[...] = (
        (step + second_step * on_res) * basis_ref[:loads]
        + (second_step * on_jump) * jump_ref[:loads]
        + small_dot(weights, columns)
    )


def call(kernel, shapes, in_specs, name, scratch=()):
    return pl.pallas_call(
        kernel,
        out_shape=[jax.ShapeDtypeStruct(*shape) for shape in shapes],
        in_specs=in_specs,
        out_specs=[VMEM] * len(shapes),
        scratch_shapes=scratch,
        compiler_params=pltpu.CompilerParams(vmem_limit_bytes=24 * 1024 * 1024),
        name=name,
    )


def permute(values, axis, offset):
    size = lax.axis_size(axis)
    return lax.ppermute(values, axis, [(at, at ^ offset) for at in range(size)])


def exchange(near, own, *pairs):
    height = own.shape[0]
    pairs = [permute(pair, "sub", 2 * (len(pairs) - at)) for at, pair in enumerate(pairs)]
    near = permute(jnp.concatenate([near, *(pair[height:] for pair in pairs)], axis=0), "sub", 1)
    return near, own, *pairs


def tree_sum(parts):
    while len(parts) > 1:
        parts = [low + high for low, high in zip(parts[::2], parts[1::2])]
    return parts[0]


def sum_over(values, axis, offsets):
    return tree_sum([values, *(permute(values, axis, offset) for offset in offsets)])


def fused_body(dual_ops, mode_traces, route, mode_block, local_gap):
    peers = lax.axis_size("sub")
    loads, rows = local_gap.shape
    modes = mode_traces.shape[1]
    subs = mode_block.shape[0]
    groups = subs // AGG_SUBS
    per_peer = rows // peers
    height = loads + GROUP * groups
    f32, i32 = jnp.float32, jnp.int32
    tall = ((height, rows), f32)
    wide = ((height, 8 * GROUP * groups), f32)
    blocks = [((height, per_peer), f32)] * 2 + [((2 * height, per_peer), f32)] * (peers // 2 - 1)

    inputs = [route, mode_block.reshape(1, subs), local_gap, mode_traces.transpose(1, 0, 2), dual_ops]
    place, operator, values, *send = call(
        place_kernel,
        [((rows, rows + per_peer), jnp.bfloat16), (dual_ops.shape, dual_ops.dtype), tall, *blocks],
        [HBM] * 5,
        "place",
        [
            pltpu.VMEM((1, rows), i32),
            pltpu.VMEM((1, subs), i32),
            pltpu.VMEM((modes, 1, rows), f32),
            pltpu.SemaphoreType.DMA((5,)),
        ],
    )(*(pltpu.with_memory_space_constraint(value, pltpu.HBM) for value in inputs))
    basis, image, *send = call(first_kernel, [tall, tall, *blocks], [VMEM] * (3 + len(blocks)), "first")(
        place, operator, values, *exchange(*send)
    )
    jump, terms = call(second_kernel, [tall, wide], [VMEM] * (4 + len(blocks)), "second")(
        place, operator, basis, image, *exchange(*send)
    )
    terms = sum_over(terms, "sub", (1,))
    terms = sum_over(terms, "sub", range(2, peers, 2))
    planes = lax.axis_size("rep")
    terms = lax.all_to_all(jnp.stack([terms] * planes), "rep", split_axis=0, concat_axis=0, tiled=True)
    terms = tree_sum([terms[plane] for plane in range(planes)])
    multipliers, amplitudes = call(
        final_kernel, [((loads, rows), f32), ((MODES * groups, loads), f32)], [VMEM] * 3, "final"
    )(terms, basis, jump)
    return multipliers, amplitudes.T


def general_body(dual_ops, mode_traces, route, mode_block, local_gap):
    own_index = lax.axis_index("sub")
    plane_index = lax.axis_index("rep")
    peer_count = lax.axis_size("sub")
    plane_count = lax.axis_size("rep")
    operator = dual_ops[0]
    traces = mode_traces[0]
    slot_rows = route[0]
    rows_here = operator.shape[0]
    load_cases = local_gap.shape[0]
    per_peer = rows_here // peer_count
    blocks = mode_block[:, 0]
    block_count = blocks.shape[0] // AGG_SUBS
    coarse = block_count * MODES
    positions = jnp.arange(rows_here, dtype=jnp.int32)
    inverse = jnp.zeros((rows_here,), jnp.int32).at[slot_rows].set(positions)
    slot_peer = positions // per_peer
    within = positions % per_peer
    flip_index = jnp.where(
        slot_peer == own_index, slot_peer * per_peer + per_peer - 1 - within, positions
    )
    peer_ids = jnp.arange(peer_count, dtype=jnp.int32)
    peer_blocks = blocks[peer_ids * plane_count + plane_index]
    own_block = blocks[own_index * plane_count + plane_index]
    labels = jnp.arange(block_count, dtype=jnp.int32)
    peer_onehot = (peer_blocks[:, None] == labels[None, :]).astype(jnp.float32)
    own_onehot = (labels == own_block).astype(jnp.float32)
    trace_slots = traces[:, slot_rows]
    receive_index = flip_index[inverse]

    def to_peers(values):
        return values[:, slot_rows]

    def from_peers(values):
        return values[:, inverse]

    gap_peers = to_peers(local_gap)
    got_traces = lax.all_to_all(trace_slots, "sub", split_axis=1, concat_axis=1, tiled=True)
    got_gap = lax.all_to_all(gap_peers, "sub", split_axis=1, concat_axis=1, tiled=True)
    partner_traces = got_traces[:, flip_index]
    residual = local_gap - got_gap[:, receive_index]
    own_gram = jnp.dot(traces, traces.T, precision=HIGHEST)
    paired = (trace_slots[:, None, :] * partner_traces[None, :, :]).reshape(
        MODES, MODES, peer_count, per_peer
    )
    cross_terms = jnp.sum(paired, axis=3)
    cross_blocks = jnp.einsum("klq,qb->kbl", cross_terms, peer_onehot, precision=HIGHEST)
    own_blocks = own_gram[:, None, :] * own_onehot[None, :, None]
    row_term = 2.0 * (own_blocks - cross_blocks).reshape(MODES, coarse)
    gram_term = (own_onehot[:, None, None] * row_term[None]).reshape(coarse, coarse)

    def coarse_term(values):
        own_part = 2.0 * jnp.dot(values, traces.T, precision=HIGHEST)
        return (own_part[:, None, :] * own_onehot[None, :, None]).reshape(load_cases, coarse)

    def expand(amounts):
        grouped = amounts.reshape(load_cases, block_count, MODES)
        own_amounts = lax.dynamic_index_in_dim(grouped, own_block, 1, keepdims=False)
        own_part = jnp.dot(own_amounts, traces, precision=HIGHEST)
        peer_amounts = jnp.einsum("qb,rbk->rkq", peer_onehot, grouped, precision=HIGHEST)
        spread = jnp.repeat(peer_amounts, per_peer, axis=2)
        peer_part = jnp.sum(spread * partner_traces[None, :, :], axis=1)
        return own_part - from_peers(peer_part)

    squares = jnp.sum(residual * residual, axis=1)
    gram_matrix, coarse_res, norm_res = lax.psum(
        (gram_term, coarse_term(residual), squares), ("sub", "rep")
    )
    factor = jnp.linalg.cholesky(gram_matrix)

    def solve_coarse(right):
        return jax.scipy.linalg.cho_solve((factor, True), right.T).T

    amplitudes = solve_coarse(coarse_res)
    projected = residual - expand(amplitudes)
    inner_sum = norm_res - jnp.sum(amplitudes * coarse_res, axis=1)
    direction = projected
    multipliers = jnp.zeros_like(residual)
    for iteration in range(ITERS):
        product = lax.dot_general(
            direction.astype(jnp.bfloat16),
            operator,
            (((1,), (1,)), ((), ())),
            preferred_element_type=jnp.float32,
        )
        got_product = lax.all_to_all(
            to_peers(product), "sub", split_axis=1, concat_axis=1, tiled=True
        )
        image_jump = product - got_product[:, receive_index]
        coarse_jump, jump_squares, residual_cross, curvature = lax.psum(
            (
                coarse_term(image_jump),
                jnp.sum(image_jump * image_jump, axis=1),
                jnp.sum(residual * image_jump, axis=1),
                jnp.sum(direction * image_jump, axis=1),
            ),
            ("sub", "rep"),
        )
        step_size = inner_sum / curvature
        multipliers = multipliers + step_size[:, None] * direction
        residual = residual - step_size[:, None] * image_jump
        coarse_res = coarse_res - step_size[:, None] * coarse_jump
        norm_res = (
            norm_res - 2.0 * step_size * residual_cross + step_size * step_size * jump_squares
        )
        amplitudes = solve_coarse(coarse_res)
        if iteration + 1 < ITERS:
            projected = residual - expand(amplitudes)
            renewed = norm_res - jnp.sum(amplitudes * coarse_res, axis=1)
            direction = projected + (renewed / inner_sum)[:, None] * direction
            inner_sum = renewed
    return (multipliers, amplitudes)


def fits(mesh, dual_ops, mode_block, local_gap):
    peers, planes = mesh.shape["sub"], mesh.shape["rep"]
    powers = all(size & (size - 1) == 0 for size in (peers, planes))
    whole = dual_ops.shape[1] % (128 * peers) == 0 and local_gap.shape[0] % 16 == 0
    return powers and whole and 8 * GROUP * (mode_block.shape[0] // AGG_SUBS) == 128


def solution(mesh):
    placed = (
        P(("sub", "rep"), None, None),
        P(("sub", "rep"), None, None),
        P(("sub", "rep"), None),
        P(),
        P(None, ("sub", "rep")),
    )

    def run(dual_ops, mode_traces, route, mode_block, local_gap):
        body = fused_body if fits(mesh, dual_ops, mode_block, local_gap) else general_body
        return jax.shard_map(
            body, mesh=mesh, in_specs=placed, out_specs=(P(None, ("sub", "rep")), P()), check_vma=False
        )(dual_ops, mode_traces, route, mode_block, local_gap)

    return run
```

```python
import jax
import jax.numpy as jnp
from jax import lax
from jax.experimental import pallas as pl
from jax.experimental.pallas import tpu as pltpu
from jax.sharding import PartitionSpec as P

MODES = 6
AGG_SUBS = 16
ITERS = 2
GROUP = 8
SCALAR_LANES = (MODES, MODES + 1, GROUP + MODES, GROUP + MODES + 1, 2 * GROUP + MODES)

HIGHEST = lax.Precision.HIGHEST
VMEM = pl.BlockSpec(memory_space=pltpu.VMEM)
HBM = pl.BlockSpec(memory_space=pltpu.HBM)
NN = (((1,), (0,)), ((), ()))
NT = (((1,), (1,)), ((), ()))


def split(values):
    high = values.astype(jnp.bfloat16).astype(jnp.float32)
    return jnp.concatenate([high, values - high], axis=0).astype(jnp.bfloat16)


def split_dot(values, matrix, dims):
    rows = values.shape[0]
    both = lax.dot_general(split(values), matrix, dims, preferred_element_type=jnp.float32)
    return both[:rows] + both[rows:]


def small_dot(left, right):
    return jnp.dot(left, right, precision=HIGHEST, preferred_element_type=jnp.float32)


def send_blocks(values, place_ref, near_ref, own_ref, *pair_refs):
    height, per_peer = own_ref.shape
    peers = 2 * len(pair_refs) + 2
    slots = split_dot(values, place_ref[:, : peers * per_peer], NN)
    own_ref[...] = slots[:, :per_peer]
    near_ref[...] = slots[:, per_peer : 2 * per_peer]
    for at, ref in enumerate(pair_refs):
        start = (peers - 2 * at - 2) * per_peer
        ref[:height] = slots[:, start : start + per_peer]
        ref[height:] = slots[:, start + per_peer : start + 2 * per_peer]


def received(near_ref, own_ref, *pair_refs):
    height = own_ref.shape[0]
    got = [near_ref[:height]]
    for at in reversed(range(len(pair_refs))):
        got += [pair_refs[at][:height], near_ref[(at + 1) * height : (at + 2) * height]]
    return jnp.concatenate([*got, own_ref[...]], axis=1)


def spread(values, loads, groups):
    modes = values[loads:]
    label = modes[MODES : MODES + 1]
    used = lax.broadcasted_iota(jnp.int32, modes.shape, 0) < MODES
    parts = [jnp.where(used & (label == group), modes, 0.0) for group in range(groups)]
    return jnp.concatenate([values[:loads], *parts], axis=0)


def jump_of(values, got, place_ref):
    return values - split_dot(got, place_ref[:, place_ref.shape[1] - values.shape[1] :], NT)


def place_kernel(
    route_hbm, block_hbm, gap_hbm, traces_hbm, operator_hbm,
    place_ref, operator_ref, values_ref, *refs,
):
    *send_refs, route_ref, block_ref, traces_ref, sems = refs
    loads, rows = gap_hbm.shape
    per_peer = send_refs[0].shape[1]
    peers = rows // per_peer
    copies = [
        pltpu.make_async_copy(source, target, sems.at[at])
        for at, (source, target) in enumerate(
            (
                (route_hbm, route_ref),
                (block_hbm, block_ref),
                (traces_hbm, traces_ref),
                (gap_hbm, values_ref.at[pl.ds(0, loads)]),
                (operator_hbm, operator_ref),
            )
        )
    ]
    for copy in copies:
        copy.start()
    own_index = lax.axis_index("sub")
    device = own_index * lax.axis_size("rep") + lax.axis_index("rep")
    row_ids = lax.broadcasted_iota(jnp.int32, (rows, per_peer), 0)
    low = lax.broadcasted_iota(jnp.int32, (per_peer, per_peer), 0)
    high = lax.broadcasted_iota(jnp.int32, (per_peer, per_peer), 1)
    reverse = jnp.where(low + high == per_peer - 1, 1.0, 0.0).astype(jnp.bfloat16)
    copies[0].wait()
    for offset in range(peers):
        start = pl.multiple_of((own_index ^ offset) * per_peer, per_peer)
        hits = row_ids == route_ref[:, pl.ds(start, per_peer)]
        at = (offset if offset else peers) * per_peer
        place_ref[:, at : at + per_peer] = jnp.where(hits, 1.0, 0.0).astype(jnp.bfloat16)
    place_ref[:, :per_peer] = jnp.dot(
        place_ref[:, rows:], reverse, preferred_element_type=jnp.float32
    ).astype(jnp.bfloat16)
    copies[1].wait()
    copies[2].wait()
    blocks = block_ref[...]
    lane = lax.broadcasted_iota(jnp.int32, blocks.shape, 1)
    own_block = jnp.sum(jnp.where(lane == device, blocks, 0), axis=1, keepdims=True)
    modes = traces_ref.shape[0]
    label = jnp.broadcast_to(own_block.astype(jnp.float32), (1, rows))
    for mode in range(modes):
        values_ref[loads + mode : loads + mode + 1] = traces_ref[mode]
    values_ref[loads + modes : loads + modes + 1] = label
    values_ref[loads + modes + 1 :] = jnp.zeros((GROUP - modes - 1, rows), jnp.float32)
    copies[3].wait()
    send_blocks(values_ref[...], place_ref, *send_refs)
    copies[4].wait()


def first_kernel(place_ref, operator_ref, values_ref, *refs):
    half = len(refs) // 2 - 1
    got_refs, (basis_ref, image_ref, *send_refs) = refs[:half], refs[half:]
    loads = values_ref.shape[0] - GROUP
    groups = (basis_ref.shape[0] - loads) // GROUP
    own, got = (spread(values, loads, groups) for values in (values_ref[...], received(*got_refs)))
    basis = jump_of(own, got, place_ref)
    basis_ref[...] = basis
    image = split_dot(basis, operator_ref[0], NT)
    image_ref[...] = image
    send_blocks(image, place_ref, *send_refs)


def products_of(left, right):
    both = lax.dot_general(split(left), split(right), NT, preferred_element_type=jnp.float32)
    both = both[: left.shape[0]] + both[left.shape[0] :]
    return both + pltpu.roll(both, right.shape[0], 1)


def second_kernel(place_ref, operator_ref, basis_ref, image_ref, *refs):
    *got_refs, jump_ref, terms_ref = refs
    coarse = terms_ref.shape[1] // 8
    loads = basis_ref.shape[0] - coarse
    image = image_ref[...]
    jump = jump_of(image, received(*got_refs), place_ref)
    jump_ref[...] = jump
    basis = basis_ref[...]
    second = split_dot(jump, operator_ref[0], NT)
    left = jnp.concatenate([basis[:loads], jump[:loads], image[:loads], second[:loads], basis[loads:], jump[loads:]])
    both = products_of(left, jnp.concatenate([basis[loads:], image[loads:], jump[loads:], second[loads:]]))
    along, jumped, imaged, doubled = (both[at * loads : (at + 1) * loads] for at in range(4))
    base, far = both[4 * loads : 4 * loads + coarse], both[4 * loads + coarse :]
    lane = lax.broadcasted_iota(jnp.int32, (loads, 8 * coarse), 1)
    strip = lane // coarse
    top = jnp.where(strip == 2, doubled, along)
    top = jnp.where(strip == 4, imaged, top)
    top = jnp.where(strip == 5, pltpu.roll(doubled, coarse, 1), top)
    top = jnp.where(strip >= 6, jumped, top)
    residual, jump_loads = basis[:loads], jump[:loads]
    scalars = (
        residual * residual,
        residual * image[:loads],
        jump_loads * jump_loads,
        jump_loads * second[:loads],
        residual * second[:loads],
    )
    for at, product in zip(SCALAR_LANES, scalars):
        top = jnp.where(lane == at, jnp.sum(product, axis=1, keepdims=True), top)
    lane = lax.broadcasted_iota(jnp.int32, (coarse, 8 * coarse), 1)
    terms_ref[...] = jnp.concatenate([top, jnp.where(lane < 4 * coarse, base, far)], axis=0)


def inverse_of(gram, coarse):
    row = lax.broadcasted_iota(jnp.int32, (coarse, 2 * coarse), 0)
    lane = lax.broadcasted_iota(jnp.int32, (coarse, 2 * coarse), 1)
    unit = jnp.where(lane - coarse == row, 1.0, 0.0)
    work = jnp.concatenate([gram, unit[:, coarse:]], axis=1)
    work = jnp.where((lane < coarse) & (row % GROUP >= MODES), jnp.where(lane == row, 1.0, 0.0), work)
    work = jnp.where((lane < coarse) & (lane % GROUP >= MODES), jnp.where(lane == row, 1.0, 0.0), work)
    for pivot in range(coarse):
        if pivot % GROUP >= MODES:
            continue
        scaled = work[pivot : pivot + 1] / work[pivot : pivot + 1, pivot : pivot + 1]
        work = jnp.where(row == pivot, scaled, work - work[:, pivot : pivot + 1] * scaled)
    return work[:, coarse:]


def final_kernel(terms_ref, handed_ref, basis_ref, jump_ref, multipliers_ref, amplitudes_ref):
    coarse = terms_ref.shape[1] // 8
    loads = basis_ref.shape[0] - coarse
    groups = coarse // GROUP
    second_core = lax.axis_index("sub") % 2 == 1
    terms = jnp.where(second_core, terms_ref[...], handed_ref[...])

    def scalar(at):
        lane = SCALAR_LANES[at]
        return terms[:loads, lane : lane + 1]

    def total(values):
        return jnp.sum(values, axis=1, keepdims=True)

    used = lax.broadcasted_iota(jnp.int32, (loads, coarse), 1) % GROUP < MODES

    def strip(at):
        return jnp.where(used, terms[:loads, at * coarse : (at + 1) * coarse], 0.0)

    def block(at):
        return terms[loads:, at * coarse : (at + 1) * coarse]

    res_res, res_image, jump_jump, jump_second, res_second = (scalar(at) for at in range(5))
    coarse_res, res_h, second_z, res_dz, image_g, second_g, jump_z, jump_dz = (strip(at) for at in range(8))
    gram, g_h, g_dz, z_z, z_dz = block(0), block(1), block(3), block(6), block(7)
    inverse = inverse_of(gram, coarse)
    amounts = small_dot(coarse_res, inverse)
    inner = res_res - total(amounts * coarse_res)
    products = small_dot(amounts, jnp.concatenate([g_h.T, z_z], axis=1))
    coarse_image = image_g - products[:, :coarse]
    res_along = 2.0 * (res_image - total(amounts * res_h))
    curvature = res_along - 2.0 * total(amounts * coarse_image)
    step = inner / curvature
    along_along = jump_jump - total(amounts * (2.0 * jump_z - products[:, coarse:]))
    norm = res_res - 2.0 * step * res_along + step * step * along_along
    coarse_next = coarse_res - 2.0 * step * coarse_image
    amounts_next = small_dot(coarse_next, inverse)
    renewed = norm - total(amounts_next * coarse_next)
    ratio = renewed / inner
    on_res = 1.0 + ratio
    on_jump = -step
    on_z = step * amounts
    on_g = -(amounts_next + ratio * amounts)
    spread = small_dot(
        jnp.concatenate([on_z, on_g], axis=1),
        jnp.concatenate(
            [
                jnp.concatenate([z_dz.T, g_dz.T], axis=1),
                jnp.concatenate([0.5 * z_z, g_h.T], axis=1),
            ],
            axis=0,
        ),
    )
    at_z = 0.5 * on_res * jump_z + on_jump * second_z + spread[:, :coarse]
    at_g = on_res * image_g + on_jump * second_g + spread[:, coarse:]
    at_res = on_res * res_image + on_jump * res_second + total(on_z * res_dz + on_g * res_h)
    at_jump = 0.5 * on_res * jump_jump + on_jump * jump_second + total(on_z * jump_dz + 0.5 * on_g * jump_z)
    curvature = 2.0 * (on_res * at_res + on_jump * at_jump + total(on_z * at_z + on_g * at_g))
    second_step = renewed / curvature
    amplitudes = small_dot(coarse_next - 2.0 * second_step * at_g, inverse).T
    amplitudes_ref[...] = jnp.concatenate(
        [amplitudes[label * GROUP : label * GROUP + MODES] for label in range(groups)], axis=0
    )
    weights = jnp.concatenate([second_step * on_g - step * amounts, second_step * on_z], axis=1)
    columns = jnp.concatenate([basis_ref[loads:], jump_ref[loads:]], axis=0)
    multipliers_ref[...] = (
        (step + second_step * on_res) * basis_ref[:loads]
        + (second_step * on_jump) * jump_ref[:loads]
        + small_dot(weights, columns)
    )


def call(kernel, shapes, in_specs, name, scratch=()):
    return pl.pallas_call(
        kernel,
        out_shape=[jax.ShapeDtypeStruct(*shape) for shape in shapes],
        in_specs=in_specs,
        out_specs=[VMEM] * len(shapes),
        scratch_shapes=scratch,
        compiler_params=pltpu.CompilerParams(vmem_limit_bytes=24 * 1024 * 1024),
        name=name,
    )


def permute(values, offset):
    return lax.ppermute(values, "sub", [(at, at ^ offset) for at in range(lax.axis_size("sub"))])


def exchange(near, own, *pairs):
    height = own.shape[0]
    pairs = [permute(pair, 2 * (len(pairs) - at)) for at, pair in enumerate(pairs)]
    near = permute(jnp.concatenate([near, *(pair[height:] for pair in pairs)], axis=0), 1)
    return near, own, *pairs


def reduce_on_seconds(terms):
    axes = ("sub", "rep")
    peers, planes = (lax.axis_size(axis) for axis in axes)
    seconds = [at for at in range(peers * planes) if at // planes % 2]
    terms = terms + lax.ppermute(terms, axes, [(at - planes, at) for at in seconds])
    offsets = [2**power * planes for power in range(1, peers.bit_length() - 1)]
    offsets += [2**power for power in range(planes.bit_length() - 1)]
    for offset in offsets:
        terms = terms + lax.ppermute(terms, axes, [(at, at ^ offset) for at in seconds])
    return terms, lax.ppermute(terms, axes, [(at, at - planes) for at in seconds])


def fused_body(dual_ops, mode_traces, route, mode_block, local_gap):
    peers = lax.axis_size("sub")
    loads, rows = local_gap.shape
    modes = mode_traces.shape[1]
    subs = mode_block.shape[0]
    groups = subs // AGG_SUBS
    per_peer = rows // peers
    height = loads + GROUP * groups
    f32, i32 = jnp.float32, jnp.int32
    tall = ((height, rows), f32)
    wide = ((height, 8 * GROUP * groups), f32)

    def blocks(height):
        return [((height, per_peer), f32)] * 2 + [((2 * height, per_peer), f32)] * (peers // 2 - 1)

    inputs = [route, mode_block.reshape(1, subs), local_gap, mode_traces.transpose(1, 0, 2), dual_ops]
    place, operator, values, *send = call(
        place_kernel,
        [((rows, rows + per_peer), jnp.bfloat16), (dual_ops.shape, dual_ops.dtype),
         ((loads + GROUP, rows), f32), *blocks(loads + GROUP)],
        [HBM] * 5,
        "place",
        [
            pltpu.VMEM((1, rows), i32),
            pltpu.VMEM((1, subs), i32),
            pltpu.VMEM((modes, 1, rows), f32),
            pltpu.SemaphoreType.DMA((5,)),
        ],
    )(*(pltpu.with_memory_space_constraint(value, pltpu.HBM) for value in inputs))
    basis, image, *send = call(first_kernel, [tall, tall, *blocks(height)], [VMEM] * (3 + len(send)), "first")(
        place, operator, values, *exchange(*send)
    )
    jump, terms = call(second_kernel, [tall, wide], [VMEM] * (4 + len(send)), "second")(
        place, operator, basis, image, *exchange(*send)
    )
    multipliers, amplitudes = call(
        final_kernel, [((loads, rows), f32), ((MODES * groups, loads), f32)], [VMEM] * 4, "final"
    )(*reduce_on_seconds(terms), basis, jump)
    return multipliers, amplitudes.T


def general_body(dual_ops, mode_traces, route, mode_block, local_gap):
    own_index = lax.axis_index("sub")
    plane_index = lax.axis_index("rep")
    peer_count = lax.axis_size("sub")
    plane_count = lax.axis_size("rep")
    operator = dual_ops[0]
    traces = mode_traces[0]
    slot_rows = route[0]
    rows_here = operator.shape[0]
    load_cases = local_gap.shape[0]
    per_peer = rows_here // peer_count
    blocks = mode_block[:, 0]
    block_count = blocks.shape[0] // AGG_SUBS
    coarse = block_count * MODES
    positions = jnp.arange(rows_here, dtype=jnp.int32)
    inverse = jnp.zeros((rows_here,), jnp.int32).at[slot_rows].set(positions)
    slot_peer = positions // per_peer
    within = positions % per_peer
    flip_index = jnp.where(
        slot_peer == own_index, slot_peer * per_peer + per_peer - 1 - within, positions
    )
    peer_ids = jnp.arange(peer_count, dtype=jnp.int32)
    peer_blocks = blocks[peer_ids * plane_count + plane_index]
    own_block = blocks[own_index * plane_count + plane_index]
    labels = jnp.arange(block_count, dtype=jnp.int32)
    peer_onehot = (peer_blocks[:, None] == labels[None, :]).astype(jnp.float32)
    own_onehot = (labels == own_block).astype(jnp.float32)
    trace_slots = traces[:, slot_rows]
    receive_index = flip_index[inverse]

    def to_peers(values):
        return values[:, slot_rows]

    def from_peers(values):
        return values[:, inverse]

    gap_peers = to_peers(local_gap)
    got_traces = lax.all_to_all(trace_slots, "sub", split_axis=1, concat_axis=1, tiled=True)
    got_gap = lax.all_to_all(gap_peers, "sub", split_axis=1, concat_axis=1, tiled=True)
    partner_traces = got_traces[:, flip_index]
    residual = local_gap - got_gap[:, receive_index]
    own_gram = jnp.dot(traces, traces.T, precision=HIGHEST)
    paired = (trace_slots[:, None, :] * partner_traces[None, :, :]).reshape(
        MODES, MODES, peer_count, per_peer
    )
    cross_terms = jnp.sum(paired, axis=3)
    cross_blocks = jnp.einsum("klq,qb->kbl", cross_terms, peer_onehot, precision=HIGHEST)
    own_blocks = own_gram[:, None, :] * own_onehot[None, :, None]
    row_term = 2.0 * (own_blocks - cross_blocks).reshape(MODES, coarse)
    gram_term = (own_onehot[:, None, None] * row_term[None]).reshape(coarse, coarse)

    def coarse_term(values):
        own_part = 2.0 * jnp.dot(values, traces.T, precision=HIGHEST)
        return (own_part[:, None, :] * own_onehot[None, :, None]).reshape(load_cases, coarse)

    def expand(amounts):
        grouped = amounts.reshape(load_cases, block_count, MODES)
        own_amounts = lax.dynamic_index_in_dim(grouped, own_block, 1, keepdims=False)
        own_part = jnp.dot(own_amounts, traces, precision=HIGHEST)
        peer_amounts = jnp.einsum("qb,rbk->rkq", peer_onehot, grouped, precision=HIGHEST)
        spread = jnp.repeat(peer_amounts, per_peer, axis=2)
        peer_part = jnp.sum(spread * partner_traces[None, :, :], axis=1)
        return own_part - from_peers(peer_part)

    squares = jnp.sum(residual * residual, axis=1)
    gram_matrix, coarse_res, norm_res = lax.psum(
        (gram_term, coarse_term(residual), squares), ("sub", "rep")
    )
    factor = jnp.linalg.cholesky(gram_matrix)

    def solve_coarse(right):
        return jax.scipy.linalg.cho_solve((factor, True), right.T).T

    amplitudes = solve_coarse(coarse_res)
    projected = residual - expand(amplitudes)
    inner_sum = norm_res - jnp.sum(amplitudes * coarse_res, axis=1)
    direction = projected
    multipliers = jnp.zeros_like(residual)
    for iteration in range(ITERS):
        product = lax.dot_general(
            direction.astype(jnp.bfloat16),
            operator,
            (((1,), (1,)), ((), ())),
            preferred_element_type=jnp.float32,
        )
        got_product = lax.all_to_all(
            to_peers(product), "sub", split_axis=1, concat_axis=1, tiled=True
        )
        image_jump = product - got_product[:, receive_index]
        coarse_jump, jump_squares, residual_cross, curvature = lax.psum(
            (
                coarse_term(image_jump),
                jnp.sum(image_jump * image_jump, axis=1),
                jnp.sum(residual * image_jump, axis=1),
                jnp.sum(direction * image_jump, axis=1),
            ),
            ("sub", "rep"),
        )
        step_size = inner_sum / curvature
        multipliers = multipliers + step_size[:, None] * direction
        residual = residual - step_size[:, None] * image_jump
        coarse_res = coarse_res - step_size[:, None] * coarse_jump
        norm_res = (
            norm_res - 2.0 * step_size * residual_cross + step_size * step_size * jump_squares
        )
        amplitudes = solve_coarse(coarse_res)
        if iteration + 1 < ITERS:
            projected = residual - expand(amplitudes)
            renewed = norm_res - jnp.sum(amplitudes * coarse_res, axis=1)
            direction = projected + (renewed / inner_sum)[:, None] * direction
            inner_sum = renewed
    return (multipliers, amplitudes)


def fits(mesh, dual_ops, mode_block, local_gap):
    peers, planes = mesh.shape["sub"], mesh.shape["rep"]
    powers = all(size & (size - 1) == 0 for size in (peers, planes))
    whole = dual_ops.shape[1] % (128 * peers) == 0 and local_gap.shape[0] % 16 == 0
    return powers and whole and 8 * GROUP * (mode_block.shape[0] // AGG_SUBS) == 128


def solution(mesh):
    placed = (
        P(("sub", "rep"), None, None),
        P(("sub", "rep"), None, None),
        P(("sub", "rep"), None),
        P(),
        P(None, ("sub", "rep")),
    )

    def run(dual_ops, mode_traces, route, mode_block, local_gap):
        body = fused_body if fits(mesh, dual_ops, mode_block, local_gap) else general_body
        return jax.shard_map(
            body, mesh=mesh, in_specs=placed, out_specs=(P(None, ("sub", "rep")), P()), check_vma=False
        )(dual_ops, mode_traces, route, mode_block, local_gap)

    return run
```

```python
import jax
import jax.numpy as jnp
from jax import lax
from jax.experimental import pallas as pl
from jax.experimental.pallas import tpu as pltpu
from jax.sharding import PartitionSpec as P

MODES = 6
AGG_SUBS = 16
ITERS = 2
GROUP = 8
SCALAR_LANES = (MODES, MODES + 1, GROUP + MODES, GROUP + MODES + 1, 2 * GROUP + MODES)

HIGHEST = lax.Precision.HIGHEST
VMEM = pl.BlockSpec(memory_space=pltpu.VMEM)
HBM = pl.BlockSpec(memory_space=pltpu.HBM)
NN = (((1,), (0,)), ((), ()))
NT = (((1,), (1,)), ((), ()))


def split(values):
    high = values.astype(jnp.bfloat16).astype(jnp.float32)
    return jnp.concatenate([high, values - high], axis=0).astype(jnp.bfloat16)


def split_dot(values, matrix, dims):
    rows = values.shape[0]
    both = lax.dot_general(split(values), matrix, dims, preferred_element_type=jnp.float32)
    return both[:rows] + both[rows:]


def small_dot(left, right):
    return jnp.dot(left, right, precision=HIGHEST, preferred_element_type=jnp.float32)


def send_blocks(values, place_ref, near_ref, own_ref, *pair_refs):
    height, per_peer = own_ref.shape
    peers = 2 * len(pair_refs) + 2
    slots = split_dot(values, place_ref[:, : peers * per_peer], NN)
    own_ref[...] = slots[:, :per_peer]
    near_ref[...] = slots[:, per_peer : 2 * per_peer]
    for at, ref in enumerate(pair_refs):
        start = (peers - 2 * at - 2) * per_peer
        ref[:height] = slots[:, start : start + per_peer]
        ref[height:] = slots[:, start + per_peer : start + 2 * per_peer]


def received(near_ref, own_ref, *pair_refs):
    height = own_ref.shape[0]
    got = [near_ref[:height]]
    for at in reversed(range(len(pair_refs))):
        got += [pair_refs[at][:height], near_ref[(at + 1) * height : (at + 2) * height]]
    return jnp.concatenate([*got, own_ref[...]], axis=1)


def spread(values, loads, groups):
    modes = values[loads:]
    label = modes[MODES : MODES + 1]
    used = lax.broadcasted_iota(jnp.int32, modes.shape, 0) < MODES
    parts = [jnp.where(used & (label == group), modes, 0.0) for group in range(groups)]
    return jnp.concatenate([values[:loads], *parts], axis=0)


def jump_of(values, got, place_ref):
    return values - split_dot(got, place_ref[:, place_ref.shape[1] - values.shape[1] :], NT)


def place_kernel(
    route_hbm, block_hbm, gap_hbm, traces_hbm, operator_hbm,
    place_ref, operator_ref, values_ref, *refs,
):
    *send_refs, route_ref, block_ref, traces_ref, sems = refs
    loads, rows = gap_hbm.shape
    per_peer = send_refs[0].shape[1]
    peers = rows // per_peer
    copies = [
        pltpu.make_async_copy(source, target, sems.at[at])
        for at, (source, target) in enumerate(
            (
                (route_hbm, route_ref),
                (block_hbm, block_ref),
                (traces_hbm, traces_ref),
                (gap_hbm, values_ref.at[pl.ds(0, loads)]),
                (operator_hbm, operator_ref),
            )
        )
    ]
    for copy in copies:
        copy.start()
    own_index = lax.axis_index("sub")
    device = own_index * lax.axis_size("rep") + lax.axis_index("rep")
    row_ids = lax.broadcasted_iota(jnp.int32, (rows, per_peer), 0)
    low = lax.broadcasted_iota(jnp.int32, (per_peer, per_peer), 0)
    high = lax.broadcasted_iota(jnp.int32, (per_peer, per_peer), 1)
    reverse = jnp.where(low + high == per_peer - 1, 1.0, 0.0).astype(jnp.bfloat16)
    copies[0].wait()
    for offset in range(peers):
        start = pl.multiple_of((own_index ^ offset) * per_peer, per_peer)
        hits = row_ids == route_ref[:, pl.ds(start, per_peer)]
        at = (offset if offset else peers) * per_peer
        place_ref[:, at : at + per_peer] = jnp.where(hits, 1.0, 0.0).astype(jnp.bfloat16)
    place_ref[:, :per_peer] = jnp.dot(
        place_ref[:, rows:], reverse, preferred_element_type=jnp.float32
    ).astype(jnp.bfloat16)
    copies[1].wait()
    copies[2].wait()
    blocks = block_ref[...]
    lane = lax.broadcasted_iota(jnp.int32, blocks.shape, 1)
    own_block = jnp.sum(jnp.where(lane == device, blocks, 0), axis=1, keepdims=True)
    modes = traces_ref.shape[0]
    label = jnp.broadcast_to(own_block.astype(jnp.float32), (1, rows))
    for mode in range(modes):
        values_ref[loads + mode : loads + mode + 1] = traces_ref[mode]
    values_ref[loads + modes : loads + modes + 1] = label
    values_ref[loads + modes + 1 :] = jnp.zeros((GROUP - modes - 1, rows), jnp.float32)
    copies[3].wait()
    send_blocks(values_ref[...], place_ref, *send_refs)
    copies[4].wait()


def first_kernel(place_ref, operator_ref, values_ref, *refs):
    half = len(refs) // 2 - 1
    got_refs, (basis_ref, image_ref, *send_refs) = refs[:half], refs[half:]
    loads = values_ref.shape[0] - GROUP
    groups = (basis_ref.shape[0] - loads) // GROUP
    own, got = (spread(values, loads, groups) for values in (values_ref[...], received(*got_refs)))
    basis = jump_of(own, got, place_ref)
    basis_ref[...] = basis
    image = split_dot(basis, operator_ref[0], NT)
    image_ref[...] = image
    send_blocks(image, place_ref, *send_refs)


def products_of(left, right):
    both = lax.dot_general(split(left), split(right), NT, preferred_element_type=jnp.float32)
    both = both[: left.shape[0]] + both[left.shape[0] :]
    return both + pltpu.roll(both, right.shape[0], 1)


def second_kernel(place_ref, operator_ref, basis_ref, image_ref, *refs):
    *got_refs, jump_ref, terms_ref = refs
    coarse = terms_ref.shape[1] // 8
    loads = basis_ref.shape[0] - coarse
    image = image_ref[...]
    jump = jump_of(image, received(*got_refs), place_ref)
    jump_ref[...] = jump
    basis = basis_ref[...]
    second = split_dot(jump, operator_ref[0], NT)
    left = jnp.concatenate([basis[:loads], jump[:loads], image[:loads], second[:loads], basis[loads:], jump[loads:]])
    both = products_of(left, jnp.concatenate([basis[loads:], image[loads:], jump[loads:], second[loads:]]))
    along, jumped, imaged, doubled = (both[at * loads : (at + 1) * loads] for at in range(4))
    base, far = both[4 * loads : 4 * loads + coarse], both[4 * loads + coarse :]
    lane = lax.broadcasted_iota(jnp.int32, (loads, 8 * coarse), 1)
    strip = lane // coarse
    top = jnp.where(strip == 2, doubled, along)
    top = jnp.where(strip == 4, imaged, top)
    top = jnp.where(strip == 5, pltpu.roll(doubled, coarse, 1), top)
    top = jnp.where(strip >= 6, jumped, top)
    residual, jump_loads = basis[:loads], jump[:loads]
    scalars = (
        residual * residual,
        residual * image[:loads],
        jump_loads * jump_loads,
        jump_loads * second[:loads],
        residual * second[:loads],
    )
    for at, product in zip(SCALAR_LANES, scalars):
        top = jnp.where(lane == at, jnp.sum(product, axis=1, keepdims=True), top)
    lane = lax.broadcasted_iota(jnp.int32, (coarse, 8 * coarse), 1)
    terms_ref[...] = jnp.concatenate([top, jnp.where(lane < 4 * coarse, base, far)], axis=0)


def inverse_of(gram, coarse):
    row = lax.broadcasted_iota(jnp.int32, (coarse, 2 * coarse), 0)
    lane = lax.broadcasted_iota(jnp.int32, (coarse, 2 * coarse), 1)
    unit = jnp.where(lane - coarse == row, 1.0, 0.0)
    work = jnp.concatenate([gram, unit[:, coarse:]], axis=1)
    work = jnp.where((lane < coarse) & (row % GROUP >= MODES), jnp.where(lane == row, 1.0, 0.0), work)
    work = jnp.where((lane < coarse) & (lane % GROUP >= MODES), jnp.where(lane == row, 1.0, 0.0), work)
    for pivot in range(coarse):
        if pivot % GROUP >= MODES:
            continue
        scaled = work[pivot : pivot + 1] / work[pivot : pivot + 1, pivot : pivot + 1]
        work = jnp.where(row == pivot, scaled, work - work[:, pivot : pivot + 1] * scaled)
    return work[:, coarse:]


def final_kernel(terms_ref, handed_ref, basis_ref, jump_ref, multipliers_ref, amplitudes_ref):
    coarse = terms_ref.shape[1] // 8
    loads = basis_ref.shape[0] - coarse
    groups = coarse // GROUP
    second_core = lax.axis_index("sub") % 2 == 1
    terms = jnp.where(second_core, terms_ref[...], handed_ref[...])

    def scalar(at):
        lane = SCALAR_LANES[at]
        return terms[:loads, lane : lane + 1]

    def total(values):
        return jnp.sum(values, axis=1, keepdims=True)

    used = lax.broadcasted_iota(jnp.int32, (loads, coarse), 1) % GROUP < MODES

    def strip(at):
        return jnp.where(used, terms[:loads, at * coarse : (at + 1) * coarse], 0.0)

    def block(at):
        return terms[loads:, at * coarse : (at + 1) * coarse]

    res_res, res_image, jump_jump, jump_second, res_second = (scalar(at) for at in range(5))
    coarse_res, res_h, second_z, res_dz, image_g, second_g, jump_z, jump_dz = (strip(at) for at in range(8))
    gram, g_h, g_dz, z_z, z_dz = block(0), block(1), block(3), block(6), block(7)
    inverse = inverse_of(gram, coarse)
    amounts = small_dot(coarse_res, inverse)
    inner = res_res - total(amounts * coarse_res)
    products = small_dot(amounts, jnp.concatenate([g_h.T, z_z], axis=1))
    coarse_image = image_g - products[:, :coarse]
    res_along = 2.0 * (res_image - total(amounts * res_h))
    curvature = res_along - 2.0 * total(amounts * coarse_image)
    step = inner / curvature
    along_along = jump_jump - total(amounts * (2.0 * jump_z - products[:, coarse:]))
    norm = res_res - 2.0 * step * res_along + step * step * along_along
    coarse_next = coarse_res - 2.0 * step * coarse_image
    amounts_next = small_dot(coarse_next, inverse)
    renewed = norm - total(amounts_next * coarse_next)
    ratio = renewed / inner
    on_res = 1.0 + ratio
    on_jump = -step
    on_z = step * amounts
    on_g = -(amounts_next + ratio * amounts)
    spread = small_dot(
        jnp.concatenate([on_z, on_g], axis=1),
        jnp.concatenate(
            [
                jnp.concatenate([z_dz.T, g_dz.T], axis=1),
                jnp.concatenate([0.5 * z_z, g_h.T], axis=1),
            ],
            axis=0,
        ),
    )
    at_z = 0.5 * on_res * jump_z + on_jump * second_z + spread[:, :coarse]
    at_g = on_res * image_g + on_jump * second_g + spread[:, coarse:]
    at_res = on_res * res_image + on_jump * res_second + total(on_z * res_dz + on_g * res_h)
    at_jump = 0.5 * on_res * jump_jump + on_jump * jump_second + total(on_z * jump_dz + 0.5 * on_g * jump_z)
    curvature = 2.0 * (on_res * at_res + on_jump * at_jump + total(on_z * at_z + on_g * at_g))
    second_step = renewed / curvature
    amplitudes = small_dot(coarse_next - 2.0 * second_step * at_g, inverse).T
    amplitudes_ref[...] = jnp.concatenate(
        [amplitudes[label * GROUP : label * GROUP + MODES] for label in range(groups)], axis=0
    )
    weights = jnp.concatenate([second_step * on_g - step * amounts, second_step * on_z], axis=1)
    columns = jnp.concatenate([basis_ref[loads:], jump_ref[loads:]], axis=0)
    multipliers_ref[...] = (
        (step + second_step * on_res) * basis_ref[:loads]
        + (second_step * on_jump) * jump_ref[:loads]
        + small_dot(weights, columns)
    )


def call(kernel, shapes, in_specs, name, scratch=()):
    return pl.pallas_call(
        kernel,
        out_shape=[jax.ShapeDtypeStruct(*shape) for shape in shapes],
        in_specs=in_specs,
        out_specs=[VMEM] * len(shapes),
        scratch_shapes=scratch,
        compiler_params=pltpu.CompilerParams(vmem_limit_bytes=24 * 1024 * 1024),
        name=name,
    )


def permute(values, offset):
    return lax.ppermute(values, "sub", [(at, at ^ offset) for at in range(lax.axis_size("sub"))])


def exchange(near, own, *pairs):
    height = own.shape[0]
    pairs = [permute(pair, 2 * (len(pairs) - at)) for at, pair in enumerate(pairs)]
    near = permute(jnp.concatenate([near, *(pair[height:] for pair in pairs)], axis=0), 1)
    return near, own, *pairs


def reduce_on_seconds(terms):
    axes = ("sub", "rep")
    peers, planes = (lax.axis_size(axis) for axis in axes)
    devices = range(peers * planes)

    def permute_by(values, offsets):
        return lax.ppermute(values, axes, [(at, at ^ offsets[at // planes % 2]) for at in devices])

    terms = terms + permute_by(terms, (planes, planes))
    offsets = [2**power * planes for power in range(1, peers.bit_length() - 1)]
    offsets += [2**power for power in range(planes.bit_length() - 1)]
    for offset in offsets:
        terms = terms + permute_by(terms, (0, offset))
    return terms, permute_by(terms, (planes, planes))


def fused_body(dual_ops, mode_traces, route, mode_block, local_gap):
    peers = lax.axis_size("sub")
    loads, rows = local_gap.shape
    modes = mode_traces.shape[1]
    subs = mode_block.shape[0]
    groups = subs // AGG_SUBS
    per_peer = rows // peers
    height = loads + GROUP * groups
    f32, i32 = jnp.float32, jnp.int32
    tall = ((height, rows), f32)
    wide = ((height, 8 * GROUP * groups), f32)

    def blocks(height):
        return [((height, per_peer), f32)] * 2 + [((2 * height, per_peer), f32)] * (peers // 2 - 1)

    inputs = [route, mode_block.reshape(1, subs), local_gap, mode_traces.transpose(1, 0, 2), dual_ops]
    place, operator, values, *send = call(
        place_kernel,
        [((rows, rows + per_peer), jnp.bfloat16), (dual_ops.shape, dual_ops.dtype),
         ((loads + GROUP, rows), f32), *blocks(loads + GROUP)],
        [HBM] * 5,
        "place",
        [
            pltpu.VMEM((1, rows), i32),
            pltpu.VMEM((1, subs), i32),
            pltpu.VMEM((modes, 1, rows), f32),
            pltpu.SemaphoreType.DMA((5,)),
        ],
    )(*(pltpu.with_memory_space_constraint(value, pltpu.HBM) for value in inputs))
    basis, image, *send = call(first_kernel, [tall, tall, *blocks(height)], [VMEM] * (3 + len(send)), "first")(
        place, operator, values, *exchange(*send)
    )
    jump, terms = call(second_kernel, [tall, wide], [VMEM] * (4 + len(send)), "second")(
        place, operator, basis, image, *exchange(*send)
    )
    multipliers, amplitudes = call(
        final_kernel, [((loads, rows), f32), ((MODES * groups, loads), f32)], [VMEM] * 4, "final"
    )(*reduce_on_seconds(terms), basis, jump)
    return multipliers, amplitudes.T


def general_body(dual_ops, mode_traces, route, mode_block, local_gap):
    own_index = lax.axis_index("sub")
    plane_index = lax.axis_index("rep")
    peer_count = lax.axis_size("sub")
    plane_count = lax.axis_size("rep")
    operator = dual_ops[0]
    traces = mode_traces[0]
    slot_rows = route[0]
    rows_here = operator.shape[0]
    load_cases = local_gap.shape[0]
    per_peer = rows_here // peer_count
    blocks = mode_block[:, 0]
    block_count = blocks.shape[0] // AGG_SUBS
    coarse = block_count * MODES
    positions = jnp.arange(rows_here, dtype=jnp.int32)
    inverse = jnp.zeros((rows_here,), jnp.int32).at[slot_rows].set(positions)
    slot_peer = positions // per_peer
    within = positions % per_peer
    flip_index = jnp.where(
        slot_peer == own_index, slot_peer * per_peer + per_peer - 1 - within, positions
    )
    peer_ids = jnp.arange(peer_count, dtype=jnp.int32)
    peer_blocks = blocks[peer_ids * plane_count + plane_index]
    own_block = blocks[own_index * plane_count + plane_index]
    labels = jnp.arange(block_count, dtype=jnp.int32)
    peer_onehot = (peer_blocks[:, None] == labels[None, :]).astype(jnp.float32)
    own_onehot = (labels == own_block).astype(jnp.float32)
    trace_slots = traces[:, slot_rows]
    receive_index = flip_index[inverse]

    def to_peers(values):
        return values[:, slot_rows]

    def from_peers(values):
        return values[:, inverse]

    gap_peers = to_peers(local_gap)
    got_traces = lax.all_to_all(trace_slots, "sub", split_axis=1, concat_axis=1, tiled=True)
    got_gap = lax.all_to_all(gap_peers, "sub", split_axis=1, concat_axis=1, tiled=True)
    partner_traces = got_traces[:, flip_index]
    residual = local_gap - got_gap[:, receive_index]
    own_gram = jnp.dot(traces, traces.T, precision=HIGHEST)
    paired = (trace_slots[:, None, :] * partner_traces[None, :, :]).reshape(
        MODES, MODES, peer_count, per_peer
    )
    cross_terms = jnp.sum(paired, axis=3)
    cross_blocks = jnp.einsum("klq,qb->kbl", cross_terms, peer_onehot, precision=HIGHEST)
    own_blocks = own_gram[:, None, :] * own_onehot[None, :, None]
    row_term = 2.0 * (own_blocks - cross_blocks).reshape(MODES, coarse)
    gram_term = (own_onehot[:, None, None] * row_term[None]).reshape(coarse, coarse)

    def coarse_term(values):
        own_part = 2.0 * jnp.dot(values, traces.T, precision=HIGHEST)
        return (own_part[:, None, :] * own_onehot[None, :, None]).reshape(load_cases, coarse)

    def expand(amounts):
        grouped = amounts.reshape(load_cases, block_count, MODES)
        own_amounts = lax.dynamic_index_in_dim(grouped, own_block, 1, keepdims=False)
        own_part = jnp.dot(own_amounts, traces, precision=HIGHEST)
        peer_amounts = jnp.einsum("qb,rbk->rkq", peer_onehot, grouped, precision=HIGHEST)
        spread = jnp.repeat(peer_amounts, per_peer, axis=2)
        peer_part = jnp.sum(spread * partner_traces[None, :, :], axis=1)
        return own_part - from_peers(peer_part)

    squares = jnp.sum(residual * residual, axis=1)
    gram_matrix, coarse_res, norm_res = lax.psum(
        (gram_term, coarse_term(residual), squares), ("sub", "rep")
    )
    factor = jnp.linalg.cholesky(gram_matrix)

    def solve_coarse(right):
        return jax.scipy.linalg.cho_solve((factor, True), right.T).T

    amplitudes = solve_coarse(coarse_res)
    projected = residual - expand(amplitudes)
    inner_sum = norm_res - jnp.sum(amplitudes * coarse_res, axis=1)
    direction = projected
    multipliers = jnp.zeros_like(residual)
    for iteration in range(ITERS):
        product = lax.dot_general(
            direction.astype(jnp.bfloat16),
            operator,
            (((1,), (1,)), ((), ())),
            preferred_element_type=jnp.float32,
        )
        got_product = lax.all_to_all(
            to_peers(product), "sub", split_axis=1, concat_axis=1, tiled=True
        )
        image_jump = product - got_product[:, receive_index]
        coarse_jump, jump_squares, residual_cross, curvature = lax.psum(
            (
                coarse_term(image_jump),
                jnp.sum(image_jump * image_jump, axis=1),
                jnp.sum(residual * image_jump, axis=1),
                jnp.sum(direction * image_jump, axis=1),
            ),
            ("sub", "rep"),
        )
        step_size = inner_sum / curvature
        multipliers = multipliers + step_size[:, None] * direction
        residual = residual - step_size[:, None] * image_jump
        coarse_res = coarse_res - step_size[:, None] * coarse_jump
        norm_res = (
            norm_res - 2.0 * step_size * residual_cross + step_size * step_size * jump_squares
        )
        amplitudes = solve_coarse(coarse_res)
        if iteration + 1 < ITERS:
            projected = residual - expand(amplitudes)
            renewed = norm_res - jnp.sum(amplitudes * coarse_res, axis=1)
            direction = projected + (renewed / inner_sum)[:, None] * direction
            inner_sum = renewed
    return (multipliers, amplitudes)


def fits(mesh, dual_ops, mode_block, local_gap):
    peers, planes = mesh.shape["sub"], mesh.shape["rep"]
    powers = all(size & (size - 1) == 0 for size in (peers, planes))
    whole = dual_ops.shape[1] % (128 * peers) == 0 and local_gap.shape[0] % 16 == 0
    return powers and whole and 8 * GROUP * (mode_block.shape[0] // AGG_SUBS) == 128


def solution(mesh):
    placed = (
        P(("sub", "rep"), None, None),
        P(("sub", "rep"), None, None),
        P(("sub", "rep"), None),
        P(),
        P(None, ("sub", "rep")),
    )

    def run(dual_ops, mode_traces, route, mode_block, local_gap):
        body = fused_body if fits(mesh, dual_ops, mode_block, local_gap) else general_body
        return jax.shard_map(
            body, mesh=mesh, in_specs=placed, out_specs=(P(None, ("sub", "rep")), P()), check_vma=False
        )(dual_ops, mode_traces, route, mode_block, local_gap)

    return run
```

```python
import jax
import jax.numpy as jnp
from jax import lax
from jax.experimental import pallas as pl
from jax.experimental.pallas import tpu as pltpu
from jax.sharding import PartitionSpec as P

MODES = 6
AGG_SUBS = 16
ITERS = 2
GROUP = 8
SCALAR_LANES = (MODES, MODES + 1, GROUP + MODES, GROUP + MODES + 1, 2 * GROUP + MODES)

HIGHEST = lax.Precision.HIGHEST
VMEM = pl.BlockSpec(memory_space=pltpu.VMEM)
HBM = pl.BlockSpec(memory_space=pltpu.HBM)
NN = (((1,), (0,)), ((), ()))
NT = (((1,), (1,)), ((), ()))


def split(values):
    high = values.astype(jnp.bfloat16).astype(jnp.float32)
    return jnp.concatenate([high, values - high], axis=0).astype(jnp.bfloat16)


def split_dot(values, matrix, dims):
    rows = values.shape[0]
    both = lax.dot_general(split(values), matrix, dims, preferred_element_type=jnp.float32)
    return both[:rows] + both[rows:]


def small_dot(left, right):
    return jnp.dot(left, right, precision=HIGHEST, preferred_element_type=jnp.float32)


def send_blocks(values, place_ref, near_ref, own_ref, *pair_refs):
    height, per_peer = own_ref.shape
    peers = 2 * len(pair_refs) + 2
    slots = split_dot(values, place_ref[:, : peers * per_peer], NN)
    own_ref[...] = slots[:, :per_peer]
    near_ref[...] = slots[:, per_peer : 2 * per_peer]
    for at, ref in enumerate(pair_refs):
        start = (peers - 2 * at - 2) * per_peer
        ref[:height] = slots[:, start + per_peer : start + 2 * per_peer]
        ref[height:] = slots[:, start : start + per_peer]


def received(near_ref, own_ref, *pair_refs):
    height = own_ref.shape[0]
    got = [near_ref[:height]]
    for at in reversed(range(len(pair_refs))):
        got += [near_ref[(at + 1) * height : (at + 2) * height], pair_refs[at][:height]]
    return jnp.concatenate([*got, own_ref[...]], axis=1)


def spread(values, loads, groups):
    modes = values[loads:]
    label = modes[MODES : MODES + 1]
    used = lax.broadcasted_iota(jnp.int32, modes.shape, 0) < MODES
    parts = [jnp.where(used & (label == group), modes, 0.0) for group in range(groups)]
    return jnp.concatenate([values[:loads], *parts], axis=0)


def jump_of(values, got, place_ref):
    return values - split_dot(got, place_ref[:, place_ref.shape[1] - values.shape[1] :], NT)


def place_kernel(
    route_hbm, block_hbm, gap_hbm, traces_hbm, operator_hbm,
    place_ref, operator_ref, values_ref, *refs,
):
    *send_refs, route_ref, block_ref, traces_ref, sems = refs
    loads, rows = gap_hbm.shape
    per_peer = send_refs[0].shape[1]
    peers = rows // per_peer
    copies = [
        pltpu.make_async_copy(source, target, sems.at[at])
        for at, (source, target) in enumerate(
            (
                (route_hbm, route_ref),
                (block_hbm, block_ref),
                (traces_hbm, traces_ref),
                (gap_hbm, values_ref.at[pl.ds(0, loads)]),
                (operator_hbm, operator_ref),
            )
        )
    ]
    for copy in copies:
        copy.start()
    own_index = lax.axis_index("sub")
    device = own_index * lax.axis_size("rep") + lax.axis_index("rep")
    row_ids = lax.broadcasted_iota(jnp.int32, (rows, per_peer), 0)
    low = lax.broadcasted_iota(jnp.int32, (per_peer, per_peer), 0)
    high = lax.broadcasted_iota(jnp.int32, (per_peer, per_peer), 1)
    reverse = jnp.where(low + high == per_peer - 1, 1.0, 0.0).astype(jnp.bfloat16)
    copies[0].wait()
    for offset in range(peers):
        start = pl.multiple_of((own_index ^ offset) * per_peer, per_peer)
        hits = row_ids == route_ref[:, pl.ds(start, per_peer)]
        at = (offset if offset else peers) * per_peer
        place_ref[:, at : at + per_peer] = jnp.where(hits, 1.0, 0.0).astype(jnp.bfloat16)
    place_ref[:, :per_peer] = jnp.dot(
        place_ref[:, rows:], reverse, preferred_element_type=jnp.float32
    ).astype(jnp.bfloat16)
    copies[1].wait()
    copies[2].wait()
    blocks = block_ref[...]
    lane = lax.broadcasted_iota(jnp.int32, blocks.shape, 1)
    own_block = jnp.sum(jnp.where(lane == device, blocks, 0), axis=1, keepdims=True)
    modes = traces_ref.shape[0]
    label = jnp.broadcast_to(own_block.astype(jnp.float32), (1, rows))
    for mode in range(modes):
        values_ref[loads + mode : loads + mode + 1] = traces_ref[mode]
    values_ref[loads + modes : loads + modes + 1] = label
    values_ref[loads + modes + 1 :] = jnp.zeros((GROUP - modes - 1, rows), jnp.float32)
    copies[3].wait()
    send_blocks(values_ref[...], place_ref, *send_refs)
    copies[4].wait()


def first_kernel(place_ref, operator_ref, values_ref, *refs):
    half = len(refs) // 2 - 1
    got_refs, (basis_ref, image_ref, *send_refs) = refs[:half], refs[half:]
    loads = values_ref.shape[0] - GROUP
    groups = (basis_ref.shape[0] - loads) // GROUP
    own, got = (spread(values, loads, groups) for values in (values_ref[...], received(*got_refs)))
    basis = jump_of(own, got, place_ref)
    basis_ref[...] = basis
    image = split_dot(basis, operator_ref[0], NT)
    image_ref[...] = image
    send_blocks(image, place_ref, *send_refs)


def products_of(left, right):
    both = lax.dot_general(split(left), split(right), NT, preferred_element_type=jnp.float32)
    both = both[: left.shape[0]] + both[left.shape[0] :]
    return both + pltpu.roll(both, right.shape[0], 1)


def second_kernel(place_ref, operator_ref, basis_ref, image_ref, *refs):
    *got_refs, jump_ref, terms_ref = refs
    coarse = terms_ref.shape[1] // 8
    loads = basis_ref.shape[0] - coarse
    image = image_ref[...]
    jump = jump_of(image, received(*got_refs), place_ref)
    jump_ref[...] = jump
    basis = basis_ref[...]
    second = split_dot(jump, operator_ref[0], NT)
    left = jnp.concatenate([basis[:loads], jump[:loads], image[:loads], second[:loads], basis[loads:], jump[loads:]])
    both = products_of(left, jnp.concatenate([basis[loads:], image[loads:], jump[loads:], second[loads:]]))
    along, jumped, imaged, doubled = (both[at * loads : (at + 1) * loads] for at in range(4))
    base, far = both[4 * loads : 4 * loads + coarse], both[4 * loads + coarse :]
    lane = lax.broadcasted_iota(jnp.int32, (loads, 8 * coarse), 1)
    strip = lane // coarse
    top = jnp.where(strip == 2, doubled, along)
    top = jnp.where(strip == 4, imaged, top)
    top = jnp.where(strip == 5, pltpu.roll(doubled, coarse, 1), top)
    top = jnp.where(strip >= 6, jumped, top)
    residual, jump_loads = basis[:loads], jump[:loads]
    scalars = (
        residual * residual,
        residual * image[:loads],
        jump_loads * jump_loads,
        jump_loads * second[:loads],
        residual * second[:loads],
    )
    for at, product in zip(SCALAR_LANES, scalars):
        top = jnp.where(lane == at, jnp.sum(product, axis=1, keepdims=True), top)
    lane = lax.broadcasted_iota(jnp.int32, (coarse, 8 * coarse), 1)
    terms_ref[...] = jnp.concatenate([top, jnp.where(lane < 4 * coarse, base, far)], axis=0)


def inverse_of(gram, coarse):
    row = lax.broadcasted_iota(jnp.int32, (coarse, 2 * coarse), 0)
    lane = lax.broadcasted_iota(jnp.int32, (coarse, 2 * coarse), 1)
    unit = jnp.where(lane - coarse == row, 1.0, 0.0)
    work = jnp.concatenate([gram, unit[:, coarse:]], axis=1)
    work = jnp.where((lane < coarse) & (row % GROUP >= MODES), jnp.where(lane == row, 1.0, 0.0), work)
    work = jnp.where((lane < coarse) & (lane % GROUP >= MODES), jnp.where(lane == row, 1.0, 0.0), work)
    for pivot in range(coarse):
        if pivot % GROUP >= MODES:
            continue
        scaled = work[pivot : pivot + 1] / work[pivot : pivot + 1, pivot : pivot + 1]
        work = jnp.where(row == pivot, scaled, work - work[:, pivot : pivot + 1] * scaled)
    return work[:, coarse:]


def final_kernel(terms_ref, basis_ref, jump_ref, multipliers_ref, amplitudes_ref):
    coarse = terms_ref.shape[1] // 8
    loads = basis_ref.shape[0] - coarse
    groups = coarse // GROUP
    terms = terms_ref[...]

    def scalar(at):
        lane = SCALAR_LANES[at]
        return terms[:loads, lane : lane + 1]

    def total(values):
        return jnp.sum(values, axis=1, keepdims=True)

    used = lax.broadcasted_iota(jnp.int32, (loads, coarse), 1) % GROUP < MODES

    def strip(at):
        return jnp.where(used, terms[:loads, at * coarse : (at + 1) * coarse], 0.0)

    def block(at):
        return terms[loads:, at * coarse : (at + 1) * coarse]

    res_res, res_image, jump_jump, jump_second, res_second = (scalar(at) for at in range(5))
    coarse_res, res_h, second_z, res_dz, image_g, second_g, jump_z, jump_dz = (strip(at) for at in range(8))
    gram, g_h, g_dz, z_z, z_dz = block(0), block(1), block(3), block(6), block(7)
    inverse = inverse_of(gram, coarse)
    amounts = small_dot(coarse_res, inverse)
    inner = res_res - total(amounts * coarse_res)
    products = small_dot(amounts, jnp.concatenate([g_h.T, z_z], axis=1))
    coarse_image = image_g - products[:, :coarse]
    res_along = 2.0 * (res_image - total(amounts * res_h))
    curvature = res_along - 2.0 * total(amounts * coarse_image)
    step = inner / curvature
    along_along = jump_jump - total(amounts * (2.0 * jump_z - products[:, coarse:]))
    norm = res_res - 2.0 * step * res_along + step * step * along_along
    coarse_next = coarse_res - 2.0 * step * coarse_image
    amounts_next = small_dot(coarse_next, inverse)
    renewed = norm - total(amounts_next * coarse_next)
    ratio = renewed / inner
    on_res = 1.0 + ratio
    on_jump = -step
    on_z = step * amounts
    on_g = -(amounts_next + ratio * amounts)
    spread = small_dot(
        jnp.concatenate([on_z, on_g], axis=1),
        jnp.concatenate(
            [
                jnp.concatenate([z_dz.T, g_dz.T], axis=1),
                jnp.concatenate([0.5 * z_z, g_h.T], axis=1),
            ],
            axis=0,
        ),
    )
    at_z = 0.5 * on_res * jump_z + on_jump * second_z + spread[:, :coarse]
    at_g = on_res * image_g + on_jump * second_g + spread[:, coarse:]
    at_res = on_res * res_image + on_jump * res_second + total(on_z * res_dz + on_g * res_h)
    at_jump = 0.5 * on_res * jump_jump + on_jump * jump_second + total(on_z * jump_dz + 0.5 * on_g * jump_z)
    curvature = 2.0 * (on_res * at_res + on_jump * at_jump + total(on_z * at_z + on_g * at_g))
    second_step = renewed / curvature
    amplitudes = small_dot(coarse_next - 2.0 * second_step * at_g, inverse).T
    amplitudes_ref[...] = jnp.concatenate(
        [amplitudes[label * GROUP : label * GROUP + MODES] for label in range(groups)], axis=0
    )
    weights = jnp.concatenate([second_step * on_g - step * amounts, second_step * on_z], axis=1)
    columns = jnp.concatenate([basis_ref[loads:], jump_ref[loads:]], axis=0)
    multipliers_ref[...] = (
        (step + second_step * on_res) * basis_ref[:loads]
        + (second_step * on_jump) * jump_ref[:loads]
        + small_dot(weights, columns)
    )


def call(kernel, shapes, in_specs, name, scratch=()):
    return pl.pallas_call(
        kernel,
        out_shape=[jax.ShapeDtypeStruct(*shape) for shape in shapes],
        in_specs=in_specs,
        out_specs=[VMEM] * len(shapes),
        scratch_shapes=scratch,
        compiler_params=pltpu.CompilerParams(vmem_limit_bytes=24 * 1024 * 1024),
        name=name,
    )


def permute(values, offset, plane_offset=0):
    peers, planes = lax.axis_size("sub"), lax.axis_size("rep")
    offset = offset * planes + plane_offset
    return lax.ppermute(values, ("sub", "rep"), [(at, at ^ offset) for at in range(peers * planes)])


def exchange(near, own, *pairs):
    height = own.shape[0]
    pairs = [permute(pair, 2 * (len(pairs) - at) + 1) for at, pair in enumerate(pairs)]
    near = permute(jnp.concatenate([near, *(pair[height:] for pair in pairs)], axis=0), 1)
    return near, own, *pairs


def total(terms):
    chips = [(offset + 1, 0) for offset in range(2, lax.axis_size("sub"), 2)]
    planes = [(1, offset) for offset in range(1, lax.axis_size("rep"))]
    for offsets in ([(1, 0)], chips, planes):
        parts = [terms, *(permute(terms, *offset) for offset in offsets)]
        while len(parts) > 1:
            parts = [low + high for low, high in zip(parts[::2], parts[1::2])]
        terms = parts[0]
    return terms


def fused_body(dual_ops, mode_traces, route, mode_block, local_gap):
    peers = lax.axis_size("sub")
    loads, rows = local_gap.shape
    modes = mode_traces.shape[1]
    subs = mode_block.shape[0]
    groups = subs // AGG_SUBS
    per_peer = rows // peers
    height = loads + GROUP * groups
    f32, i32 = jnp.float32, jnp.int32
    tall = ((height, rows), f32)
    wide = ((height, 8 * GROUP * groups), f32)

    def blocks(height):
        return [((height, per_peer), f32)] * 2 + [((2 * height, per_peer), f32)] * (peers // 2 - 1)

    inputs = [route, mode_block.reshape(1, subs), local_gap, mode_traces.transpose(1, 0, 2), dual_ops]
    place, operator, values, *send = call(
        place_kernel,
        [((rows, rows + per_peer), jnp.bfloat16), (dual_ops.shape, dual_ops.dtype),
         ((loads + GROUP, rows), f32), *blocks(loads + GROUP)],
        [HBM] * 5,
        "place",
        [
            pltpu.VMEM((1, rows), i32),
            pltpu.VMEM((1, subs), i32),
            pltpu.VMEM((modes, 1, rows), f32),
            pltpu.SemaphoreType.DMA((5,)),
        ],
    )(*(pltpu.with_memory_space_constraint(value, pltpu.HBM) for value in inputs))
    basis, image, *send = call(first_kernel, [tall, tall, *blocks(height)], [VMEM] * (3 + len(send)), "first")(
        place, operator, values, *exchange(*send)
    )
    jump, terms = call(second_kernel, [tall, wide], [VMEM] * (4 + len(send)), "second")(
        place, operator, basis, image, *exchange(*send)
    )
    multipliers, amplitudes = call(
        final_kernel, [((loads, rows), f32), ((MODES * groups, loads), f32)], [VMEM] * 3, "final"
    )(total(terms), basis, jump)
    return multipliers, amplitudes.T


def general_body(dual_ops, mode_traces, route, mode_block, local_gap):
    own_index = lax.axis_index("sub")
    plane_index = lax.axis_index("rep")
    peer_count = lax.axis_size("sub")
    plane_count = lax.axis_size("rep")
    operator = dual_ops[0]
    traces = mode_traces[0]
    slot_rows = route[0]
    rows_here = operator.shape[0]
    load_cases = local_gap.shape[0]
    per_peer = rows_here // peer_count
    blocks = mode_block[:, 0]
    block_count = blocks.shape[0] // AGG_SUBS
    coarse = block_count * MODES
    positions = jnp.arange(rows_here, dtype=jnp.int32)
    inverse = jnp.zeros((rows_here,), jnp.int32).at[slot_rows].set(positions)
    slot_peer = positions // per_peer
    within = positions % per_peer
    flip_index = jnp.where(
        slot_peer == own_index, slot_peer * per_peer + per_peer - 1 - within, positions
    )
    peer_ids = jnp.arange(peer_count, dtype=jnp.int32)
    peer_blocks = blocks[peer_ids * plane_count + plane_index]
    own_block = blocks[own_index * plane_count + plane_index]
    labels = jnp.arange(block_count, dtype=jnp.int32)
    peer_onehot = (peer_blocks[:, None] == labels[None, :]).astype(jnp.float32)
    own_onehot = (labels == own_block).astype(jnp.float32)
    trace_slots = traces[:, slot_rows]
    receive_index = flip_index[inverse]

    def to_peers(values):
        return values[:, slot_rows]

    def from_peers(values):
        return values[:, inverse]

    gap_peers = to_peers(local_gap)
    got_traces = lax.all_to_all(trace_slots, "sub", split_axis=1, concat_axis=1, tiled=True)
    got_gap = lax.all_to_all(gap_peers, "sub", split_axis=1, concat_axis=1, tiled=True)
    partner_traces = got_traces[:, flip_index]
    residual = local_gap - got_gap[:, receive_index]
    own_gram = jnp.dot(traces, traces.T, precision=HIGHEST)
    paired = (trace_slots[:, None, :] * partner_traces[None, :, :]).reshape(
        MODES, MODES, peer_count, per_peer
    )
    cross_terms = jnp.sum(paired, axis=3)
    cross_blocks = jnp.einsum("klq,qb->kbl", cross_terms, peer_onehot, precision=HIGHEST)
    own_blocks = own_gram[:, None, :] * own_onehot[None, :, None]
    row_term = 2.0 * (own_blocks - cross_blocks).reshape(MODES, coarse)
    gram_term = (own_onehot[:, None, None] * row_term[None]).reshape(coarse, coarse)

    def coarse_term(values):
        own_part = 2.0 * jnp.dot(values, traces.T, precision=HIGHEST)
        return (own_part[:, None, :] * own_onehot[None, :, None]).reshape(load_cases, coarse)

    def expand(amounts):
        grouped = amounts.reshape(load_cases, block_count, MODES)
        own_amounts = lax.dynamic_index_in_dim(grouped, own_block, 1, keepdims=False)
        own_part = jnp.dot(own_amounts, traces, precision=HIGHEST)
        peer_amounts = jnp.einsum("qb,rbk->rkq", peer_onehot, grouped, precision=HIGHEST)
        spread = jnp.repeat(peer_amounts, per_peer, axis=2)
        peer_part = jnp.sum(spread * partner_traces[None, :, :], axis=1)
        return own_part - from_peers(peer_part)

    squares = jnp.sum(residual * residual, axis=1)
    gram_matrix, coarse_res, norm_res = lax.psum(
        (gram_term, coarse_term(residual), squares), ("sub", "rep")
    )
    factor = jnp.linalg.cholesky(gram_matrix)

    def solve_coarse(right):
        return jax.scipy.linalg.cho_solve((factor, True), right.T).T

    amplitudes = solve_coarse(coarse_res)
    projected = residual - expand(amplitudes)
    inner_sum = norm_res - jnp.sum(amplitudes * coarse_res, axis=1)
    direction = projected
    multipliers = jnp.zeros_like(residual)
    for iteration in range(ITERS):
        product = lax.dot_general(
            direction.astype(jnp.bfloat16),
            operator,
            (((1,), (1,)), ((), ())),
            preferred_element_type=jnp.float32,
        )
        got_product = lax.all_to_all(
            to_peers(product), "sub", split_axis=1, concat_axis=1, tiled=True
        )
        image_jump = product - got_product[:, receive_index]
        coarse_jump, jump_squares, residual_cross, curvature = lax.psum(
            (
                coarse_term(image_jump),
                jnp.sum(image_jump * image_jump, axis=1),
                jnp.sum(residual * image_jump, axis=1),
                jnp.sum(direction * image_jump, axis=1),
            ),
            ("sub", "rep"),
        )
        step_size = inner_sum / curvature
        multipliers = multipliers + step_size[:, None] * direction
        residual = residual - step_size[:, None] * image_jump
        coarse_res = coarse_res - step_size[:, None] * coarse_jump
        norm_res = (
            norm_res - 2.0 * step_size * residual_cross + step_size * step_size * jump_squares
        )
        amplitudes = solve_coarse(coarse_res)
        if iteration + 1 < ITERS:
            projected = residual - expand(amplitudes)
            renewed = norm_res - jnp.sum(amplitudes * coarse_res, axis=1)
            direction = projected + (renewed / inner_sum)[:, None] * direction
            inner_sum = renewed
    return (multipliers, amplitudes)


def fits(mesh, dual_ops, mode_block, local_gap):
    peers, planes = mesh.shape["sub"], mesh.shape["rep"]
    powers = all(size & (size - 1) == 0 for size in (peers, planes))
    whole = dual_ops.shape[1] % (128 * peers) == 0 and local_gap.shape[0] % 16 == 0
    return powers and whole and 8 * GROUP * (mode_block.shape[0] // AGG_SUBS) == 128


def solution(mesh):
    placed = (
        P(("sub", "rep"), None, None),
        P(("sub", "rep"), None, None),
        P(("sub", "rep"), None),
        P(),
        P(None, ("sub", "rep")),
    )

    def run(dual_ops, mode_traces, route, mode_block, local_gap):
        body = fused_body if fits(mesh, dual_ops, mode_block, local_gap) else general_body
        return jax.shard_map(
            body, mesh=mesh, in_specs=placed, out_specs=(P(None, ("sub", "rep")), P()), check_vma=False
        )(dual_ops, mode_traces, route, mode_block, local_gap)

    return run
```

```python
import jax
import jax.numpy as jnp
from jax import lax
from jax.experimental import pallas as pl
from jax.experimental.pallas import tpu as pltpu
from jax.sharding import PartitionSpec as P

MODES = 6
AGG_SUBS = 16
ITERS = 2
GROUP = 8
SCALAR_LANES = (MODES, MODES + 1, GROUP + MODES, GROUP + MODES + 1, 2 * GROUP + MODES)

HIGHEST = lax.Precision.HIGHEST
VMEM = pl.BlockSpec(memory_space=pltpu.VMEM)
HBM = pl.BlockSpec(memory_space=pltpu.HBM)
NN = (((1,), (0,)), ((), ()))
NT = (((1,), (1,)), ((), ()))


def split(values):
    high = values.astype(jnp.bfloat16).astype(jnp.float32)
    return jnp.concatenate([high, values - high], axis=0).astype(jnp.bfloat16)


def split_dot(values, matrix, dims):
    rows = values.shape[0]
    both = lax.dot_general(split(values), matrix, dims, preferred_element_type=jnp.float32)
    return both[:rows] + both[rows:]


def small_dot(left, right):
    return jnp.dot(left, right, precision=HIGHEST, preferred_element_type=jnp.float32)


def send_blocks(values, place_ref, near_ref, own_ref, *pair_refs):
    height, per_peer = own_ref.shape
    peers = 2 * len(pair_refs) + 2
    slots = split_dot(values, place_ref[:, : peers * per_peer], NN)
    own_ref[...] = slots[:, :per_peer]
    near_ref[...] = slots[:, per_peer : 2 * per_peer]
    for at, ref in enumerate(pair_refs):
        start = (peers - 2 * at - 2) * per_peer
        ref[:height] = slots[:, start + per_peer : start + 2 * per_peer]
        ref[height:] = slots[:, start : start + per_peer]


def received(near_ref, own_ref, *pair_refs):
    height = own_ref.shape[0]
    got = [near_ref[:height]]
    for at in reversed(range(len(pair_refs))):
        got += [near_ref[(at + 1) * height : (at + 2) * height], pair_refs[at][:height]]
    return jnp.concatenate([*got, own_ref[...]], axis=1)


def spread(values, loads, groups):
    modes = values[loads:]
    label = modes[MODES : MODES + 1]
    used = lax.broadcasted_iota(jnp.int32, modes.shape, 0) < MODES
    parts = [jnp.where(used & (label == group), modes, 0.0) for group in range(groups)]
    return jnp.concatenate([values[:loads], *parts], axis=0)


def jump_of(values, got, place_ref):
    return values - split_dot(got, place_ref[:, place_ref.shape[1] - values.shape[1] :], NT)


def place_kernel(
    route_hbm, block_hbm, gap_hbm, traces_hbm, operator_hbm,
    place_ref, operator_ref, values_ref, *refs,
):
    *send_refs, route_ref, block_ref, traces_ref, sems = refs
    loads, rows = gap_hbm.shape
    per_peer = send_refs[0].shape[1]
    peers = rows // per_peer
    copies = [
        pltpu.make_async_copy(source, target, sems.at[at])
        for at, (source, target) in enumerate(
            (
                (route_hbm, route_ref),
                (block_hbm, block_ref),
                (traces_hbm, traces_ref),
                (gap_hbm, values_ref.at[pl.ds(0, loads)]),
                (operator_hbm, operator_ref),
            )
        )
    ]
    for copy in copies:
        copy.start()
    own_index = lax.axis_index("sub")
    device = own_index * lax.axis_size("rep") + lax.axis_index("rep")
    row_ids = lax.broadcasted_iota(jnp.int32, (rows, per_peer), 0)
    low = lax.broadcasted_iota(jnp.int32, (per_peer, per_peer), 0)
    high = lax.broadcasted_iota(jnp.int32, (per_peer, per_peer), 1)
    reverse = jnp.where(low + high == per_peer - 1, 1.0, 0.0).astype(jnp.bfloat16)
    copies[0].wait()
    for offset in range(peers):
        start = pl.multiple_of((own_index ^ offset) * per_peer, per_peer)
        hits = row_ids == route_ref[:, pl.ds(start, per_peer)]
        at = (offset if offset else peers) * per_peer
        place_ref[:, at : at + per_peer] = jnp.where(hits, 1.0, 0.0).astype(jnp.bfloat16)
    place_ref[:, :per_peer] = jnp.dot(
        place_ref[:, rows:], reverse, preferred_element_type=jnp.float32
    ).astype(jnp.bfloat16)
    copies[1].wait()
    copies[2].wait()
    blocks = block_ref[...]
    lane = lax.broadcasted_iota(jnp.int32, blocks.shape, 1)
    own_block = jnp.sum(jnp.where(lane == device, blocks, 0), axis=1, keepdims=True)
    modes = traces_ref.shape[0]
    label = jnp.broadcast_to(own_block.astype(jnp.float32), (1, rows))
    for mode in range(modes):
        values_ref[loads + mode : loads + mode + 1] = traces_ref[mode]
    values_ref[loads + modes : loads + modes + 1] = label
    values_ref[loads + modes + 1 :] = jnp.zeros((GROUP - modes - 1, rows), jnp.float32)
    copies[3].wait()
    send_blocks(values_ref[...], place_ref, *send_refs)
    copies[4].wait()


def first_kernel(place_ref, operator_ref, values_ref, *refs):
    half = len(refs) // 2 - 1
    got_refs, (basis_ref, image_ref, *send_refs) = refs[:half], refs[half:]
    loads = values_ref.shape[0] - GROUP
    groups = (basis_ref.shape[0] - loads) // GROUP
    own, got = (spread(values, loads, groups) for values in (values_ref[...], received(*got_refs)))
    basis = jump_of(own, got, place_ref)
    basis_ref[...] = basis
    image = split_dot(basis, operator_ref[0], NT)
    image_ref[...] = image
    send_blocks(image, place_ref, *send_refs)


def products_of(left, right):
    both = lax.dot_general(split(left), split(right), NT, preferred_element_type=jnp.float32)
    both = both[: left.shape[0]] + both[left.shape[0] :]
    return both + pltpu.roll(both, right.shape[0], 1)


def second_kernel(place_ref, operator_ref, basis_ref, image_ref, *refs):
    *got_refs, jump_ref, terms_ref = refs
    coarse = terms_ref.shape[1] // 8
    loads = basis_ref.shape[0] - coarse
    image = image_ref[...]
    jump = jump_of(image, received(*got_refs), place_ref)
    jump_ref[...] = jump
    basis = basis_ref[...]
    second = split_dot(jump, operator_ref[0], NT)
    left = jnp.concatenate([basis[:loads], jump[:loads], image[:loads], second[:loads], basis[loads:], jump[loads:]])
    both = products_of(left, jnp.concatenate([basis[loads:], image[loads:], jump[loads:], second[loads:]]))
    along, jumped, imaged, doubled = (both[at * loads : (at + 1) * loads] for at in range(4))
    base, far = both[4 * loads : 4 * loads + coarse], both[4 * loads + coarse :]
    lane = lax.broadcasted_iota(jnp.int32, (loads, 8 * coarse), 1)
    strip = lane // coarse
    top = jnp.where(strip == 2, doubled, along)
    top = jnp.where(strip == 4, imaged, top)
    top = jnp.where(strip == 5, pltpu.roll(doubled, coarse, 1), top)
    top = jnp.where(strip >= 6, jumped, top)
    residual, jump_loads = basis[:loads], jump[:loads]
    scalars = (
        residual * residual,
        residual * image[:loads],
        jump_loads * jump_loads,
        jump_loads * second[:loads],
        residual * second[:loads],
    )
    for at, product in zip(SCALAR_LANES, scalars):
        top = jnp.where(lane == at, jnp.sum(product, axis=1, keepdims=True), top)
    lane = lax.broadcasted_iota(jnp.int32, (coarse, 8 * coarse), 1)
    terms_ref[...] = jnp.concatenate([top, jnp.where(lane < 4 * coarse, base, far)], axis=0)


def eliminate(work, coarse):
    row = lax.broadcasted_iota(jnp.int32, work.shape, 0)
    for first in range(coarse):
        if first % 2 or first % GROUP >= MODES:
            continue
        second = first + 1
        left = jnp.broadcast_to(work[:, first : first + 1], work.shape)
        right = jnp.broadcast_to(work[:, second : second + 1], work.shape)
        upper, lower = work[first : first + 1], work[second : second + 1]
        pivot = 1.0 / left[first : first + 1]
        ratio = left[second : second + 1] * pivot
        corner = 1.0 / (right[second : second + 1] - ratio * right[first : first + 1])
        lower = (lower - ratio * upper) * corner
        upper = (upper - right[first : first + 1] * lower) * pivot
        work = work - left * upper - right * lower
        work = jnp.where(row == first, upper, jnp.where(row == second, lower, work))
    return work


def thin_dot(left, right):
    high, right_high = (value.astype(jnp.bfloat16).astype(jnp.float32) for value in (left, right))
    return jnp.dot(
        jnp.concatenate([high, left - high, high], axis=1).astype(jnp.bfloat16),
        jnp.concatenate([right_high, right_high, right - right_high], axis=0).astype(jnp.bfloat16),
        preferred_element_type=jnp.float32,
    )


def final_kernel(terms_ref, basis_ref, jump_ref, multipliers_ref, amplitudes_ref):
    coarse = terms_ref.shape[1] // 8
    loads = basis_ref.shape[0] - coarse
    groups = coarse // GROUP
    by_load = terms_ref[:loads].T
    used = lax.broadcasted_iota(jnp.int32, (coarse, loads), 0) % GROUP < MODES

    def strip(at):
        return by_load[at * coarse : (at + 1) * coarse]

    def block(at):
        return terms_ref[loads:, at * coarse : (at + 1) * coarse]

    def total(values):
        return jnp.sum(values, axis=0, keepdims=True)

    res_res, res_image, jump_jump, jump_second, res_second = (by_load[at : at + 1] for at in SCALAR_LANES)
    coarse_res, res_h = (jnp.where(used, strip(at), 0.0) for at in (0, 1))
    second_z, res_dz, image_g, second_g, jump_z, jump_dz = (strip(at) for at in range(2, 8))
    g_h, g_dz, z_z, z_dz = block(1), block(3), block(6), block(7)
    row = lax.broadcasted_iota(jnp.int32, (coarse, coarse), 0)
    unit = jnp.where(row == lax.broadcasted_iota(jnp.int32, (coarse, coarse), 1), 1.0, 0.0)
    empty = jnp.zeros((coarse, 5 * coarse - 2 * loads), jnp.float32)
    solved = eliminate(
        jnp.concatenate([terms_ref[loads:, : 2 * coarse], coarse_res, image_g, unit, empty], axis=1), coarse
    )
    inverse_h = solved[:, coarse : 2 * coarse]
    amounts = solved[:, 2 * coarse : 2 * coarse + loads]
    inverse_image = solved[:, 2 * coarse + loads : 2 * coarse + 2 * loads]
    inverse = solved[:, 2 * coarse + 2 * loads : 3 * coarse + 2 * loads]
    products = small_dot(jnp.concatenate([inverse_h, g_h, z_z, g_dz, z_dz], axis=0), amounts)
    inverse_h_amounts, h_amounts, z_amounts, g_dz_amounts, z_dz_amounts = (
        products[at * coarse : (at + 1) * coarse] for at in range(5)
    )
    shares = 2.0 * (inverse_image - inverse_h_amounts)
    both = jnp.concatenate([amounts, shares], axis=0).T
    basis_g, jump_z_rows = basis_ref[loads:], jump_ref[loads:]
    d = basis_ref[:loads] - thin_dot(both[:, :coarse], basis_g)
    u = jump_ref[:loads] - thin_dot(both, jnp.concatenate([jump_z_rows, basis_g], axis=0))
    products = small_dot(jnp.concatenate([g_h, z_z], axis=0), shares)
    image_d = image_g - h_amounts
    inner = res_res - total(amounts * coarse_res)
    curvature = 2.0 * (res_image - total(amounts * (res_h + image_d)))
    u_u = jump_jump - total(amounts * (2.0 * jump_z - z_amounts) + 2.0 * image_d * shares)
    second_u = second_g - g_dz_amounts - products[:coarse]
    jump_u = second_z - z_dz_amounts - 0.5 * products[coarse:]
    d_second = res_second - total(amounts * (res_dz + second_u) + shares * res_h)
    u_second = jump_second - total(amounts * (jump_dz + jump_u) + shares * (0.5 * jump_z + second_u))
    step = inner / curvature
    renewed = step * step * u_u - inner
    grown = 1.0 + renewed / inner
    curvature = grown * grown * curvature - grown * step * (2.0 * d_second + u_u) + 2.0 * step * step * u_second
    second_step = renewed / curvature
    on_d, on_u = step + second_step * grown, second_step * step
    amplitudes = amounts - on_d * shares + 2.0 * on_u * small_dot(inverse, second_u)
    amplitudes_ref[...] = jnp.concatenate(
        [amplitudes[label * GROUP : label * GROUP + MODES] for label in range(groups)], axis=0
    )
    weights = jnp.concatenate([on_d, on_u, jnp.zeros((6, loads), jnp.float32)], axis=0).T
    multipliers_ref[...] = weights[:, 0:1] * d - weights[:, 1:2] * u


def call(kernel, shapes, in_specs, name, scratch=()):
    return pl.pallas_call(
        kernel,
        out_shape=[jax.ShapeDtypeStruct(*shape) for shape in shapes],
        in_specs=in_specs,
        out_specs=[VMEM] * len(shapes),
        scratch_shapes=scratch,
        compiler_params=pltpu.CompilerParams(vmem_limit_bytes=24 * 1024 * 1024),
        name=name,
    )


def permute(values, offset, plane_offset=0):
    peers, planes = lax.axis_size("sub"), lax.axis_size("rep")
    offset = offset * planes + plane_offset
    return lax.ppermute(values, ("sub", "rep"), [(at, at ^ offset) for at in range(peers * planes)])


def exchange(near, own, *pairs):
    height = own.shape[0]
    pairs = [permute(pair, 2 * (len(pairs) - at) + 1) for at, pair in enumerate(pairs)]
    near = permute(jnp.concatenate([near, *(pair[height:] for pair in pairs)], axis=0), 1)
    return near, own, *pairs


def total(terms):
    chips = [(offset + 1, 0) for offset in range(2, lax.axis_size("sub"), 2)]
    planes = [(1, offset) for offset in range(1, lax.axis_size("rep"))]
    for offsets in ([(1, 0)], chips, planes):
        parts = [terms, *(permute(terms, *offset) for offset in offsets)]
        while len(parts) > 1:
            parts = [low + high for low, high in zip(parts[::2], parts[1::2])]
        terms = parts[0]
    return terms


def fused_body(dual_ops, mode_traces, route, mode_block, local_gap):
    peers = lax.axis_size("sub")
    loads, rows = local_gap.shape
    modes = mode_traces.shape[1]
    subs = mode_block.shape[0]
    groups = subs // AGG_SUBS
    per_peer = rows // peers
    height = loads + GROUP * groups
    f32, i32 = jnp.float32, jnp.int32
    tall = ((height, rows), f32)
    wide = ((height, 8 * GROUP * groups), f32)

    def blocks(height):
        return [((height, per_peer), f32)] * 2 + [((2 * height, per_peer), f32)] * (peers // 2 - 1)

    inputs = [route, mode_block.reshape(1, subs), local_gap, mode_traces.transpose(1, 0, 2), dual_ops]
    place, operator, values, *send = call(
        place_kernel,
        [((rows, rows + per_peer), jnp.bfloat16), (dual_ops.shape, dual_ops.dtype),
         ((loads + GROUP, rows), f32), *blocks(loads + GROUP)],
        [HBM] * 5,
        "place",
        [
            pltpu.VMEM((1, rows), i32),
            pltpu.VMEM((1, subs), i32),
            pltpu.VMEM((modes, 1, rows), f32),
            pltpu.SemaphoreType.DMA((5,)),
        ],
    )(*(pltpu.with_memory_space_constraint(value, pltpu.HBM) for value in inputs))
    basis, image, *send = call(first_kernel, [tall, tall, *blocks(height)], [VMEM] * (3 + len(send)), "first")(
        place, operator, values, *exchange(*send)
    )
    jump, terms = call(second_kernel, [tall, wide], [VMEM] * (4 + len(send)), "second")(
        place, operator, basis, image, *exchange(*send)
    )
    multipliers, amplitudes = call(
        final_kernel, [((loads, rows), f32), ((MODES * groups, loads), f32)], [VMEM] * 3, "final"
    )(total(terms), basis, jump)
    return multipliers, amplitudes.T


def general_body(dual_ops, mode_traces, route, mode_block, local_gap):
    own_index = lax.axis_index("sub")
    plane_index = lax.axis_index("rep")
    peer_count = lax.axis_size("sub")
    plane_count = lax.axis_size("rep")
    operator = dual_ops[0]
    traces = mode_traces[0]
    slot_rows = route[0]
    rows_here = operator.shape[0]
    load_cases = local_gap.shape[0]
    per_peer = rows_here // peer_count
    blocks = mode_block[:, 0]
    block_count = blocks.shape[0] // AGG_SUBS
    coarse = block_count * MODES
    positions = jnp.arange(rows_here, dtype=jnp.int32)
    inverse = jnp.zeros((rows_here,), jnp.int32).at[slot_rows].set(positions)
    slot_peer = positions // per_peer
    within = positions % per_peer
    flip_index = jnp.where(
        slot_peer == own_index, slot_peer * per_peer + per_peer - 1 - within, positions
    )
    peer_ids = jnp.arange(peer_count, dtype=jnp.int32)
    peer_blocks = blocks[peer_ids * plane_count + plane_index]
    own_block = blocks[own_index * plane_count + plane_index]
    labels = jnp.arange(block_count, dtype=jnp.int32)
    peer_onehot = (peer_blocks[:, None] == labels[None, :]).astype(jnp.float32)
    own_onehot = (labels == own_block).astype(jnp.float32)
    trace_slots = traces[:, slot_rows]
    receive_index = flip_index[inverse]

    def to_peers(values):
        return values[:, slot_rows]

    def from_peers(values):
        return values[:, inverse]

    gap_peers = to_peers(local_gap)
    got_traces = lax.all_to_all(trace_slots, "sub", split_axis=1, concat_axis=1, tiled=True)
    got_gap = lax.all_to_all(gap_peers, "sub", split_axis=1, concat_axis=1, tiled=True)
    partner_traces = got_traces[:, flip_index]
    residual = local_gap - got_gap[:, receive_index]
    own_gram = jnp.dot(traces, traces.T, precision=HIGHEST)
    paired = (trace_slots[:, None, :] * partner_traces[None, :, :]).reshape(
        MODES, MODES, peer_count, per_peer
    )
    cross_terms = jnp.sum(paired, axis=3)
    cross_blocks = jnp.einsum("klq,qb->kbl", cross_terms, peer_onehot, precision=HIGHEST)
    own_blocks = own_gram[:, None, :] * own_onehot[None, :, None]
    row_term = 2.0 * (own_blocks - cross_blocks).reshape(MODES, coarse)
    gram_term = (own_onehot[:, None, None] * row_term[None]).reshape(coarse, coarse)

    def coarse_term(values):
        own_part = 2.0 * jnp.dot(values, traces.T, precision=HIGHEST)
        return (own_part[:, None, :] * own_onehot[None, :, None]).reshape(load_cases, coarse)

    def expand(amounts):
        grouped = amounts.reshape(load_cases, block_count, MODES)
        own_amounts = lax.dynamic_index_in_dim(grouped, own_block, 1, keepdims=False)
        own_part = jnp.dot(own_amounts, traces, precision=HIGHEST)
        peer_amounts = jnp.einsum("qb,rbk->rkq", peer_onehot, grouped, precision=HIGHEST)
        spread = jnp.repeat(peer_amounts, per_peer, axis=2)
        peer_part = jnp.sum(spread * partner_traces[None, :, :], axis=1)
        return own_part - from_peers(peer_part)

    squares = jnp.sum(residual * residual, axis=1)
    gram_matrix, coarse_res, norm_res = lax.psum(
        (gram_term, coarse_term(residual), squares), ("sub", "rep")
    )
    factor = jnp.linalg.cholesky(gram_matrix)

    def solve_coarse(right):
        return jax.scipy.linalg.cho_solve((factor, True), right.T).T

    amplitudes = solve_coarse(coarse_res)
    projected = residual - expand(amplitudes)
    inner_sum = norm_res - jnp.sum(amplitudes * coarse_res, axis=1)
    direction = projected
    multipliers = jnp.zeros_like(residual)
    for iteration in range(ITERS):
        product = lax.dot_general(
            direction.astype(jnp.bfloat16),
            operator,
            (((1,), (1,)), ((), ())),
            preferred_element_type=jnp.float32,
        )
        got_product = lax.all_to_all(
            to_peers(product), "sub", split_axis=1, concat_axis=1, tiled=True
        )
        image_jump = product - got_product[:, receive_index]
        coarse_jump, jump_squares, residual_cross, curvature = lax.psum(
            (
                coarse_term(image_jump),
                jnp.sum(image_jump * image_jump, axis=1),
                jnp.sum(residual * image_jump, axis=1),
                jnp.sum(direction * image_jump, axis=1),
            ),
            ("sub", "rep"),
        )
        step_size = inner_sum / curvature
        multipliers = multipliers + step_size[:, None] * direction
        residual = residual - step_size[:, None] * image_jump
        coarse_res = coarse_res - step_size[:, None] * coarse_jump
        norm_res = (
            norm_res - 2.0 * step_size * residual_cross + step_size * step_size * jump_squares
        )
        amplitudes = solve_coarse(coarse_res)
        if iteration + 1 < ITERS:
            projected = residual - expand(amplitudes)
            renewed = norm_res - jnp.sum(amplitudes * coarse_res, axis=1)
            direction = projected + (renewed / inner_sum)[:, None] * direction
            inner_sum = renewed
    return (multipliers, amplitudes)


def fits(mesh, dual_ops, mode_block, local_gap):
    peers, planes = mesh.shape["sub"], mesh.shape["rep"]
    powers = all(size & (size - 1) == 0 for size in (peers, planes))
    whole = dual_ops.shape[1] % (128 * peers) == 0 and local_gap.shape[0] % 16 == 0
    return powers and whole and 8 * GROUP * (mode_block.shape[0] // AGG_SUBS) == 128


def solution(mesh):
    placed = (
        P(("sub", "rep"), None, None),
        P(("sub", "rep"), None, None),
        P(("sub", "rep"), None),
        P(),
        P(None, ("sub", "rep")),
    )

    def run(dual_ops, mode_traces, route, mode_block, local_gap):
        body = fused_body if fits(mesh, dual_ops, mode_block, local_gap) else general_body
        return jax.shard_map(
            body, mesh=mesh, in_specs=placed, out_specs=(P(None, ("sub", "rep")), P()), check_vma=False
        )(dual_ops, mode_traces, route, mode_block, local_gap)

    return run
```

```python
import jax
import jax.numpy as jnp
from jax import lax
from jax.experimental import pallas as pl
from jax.experimental.pallas import tpu as pltpu
from jax.sharding import PartitionSpec as P

MODES = 6
AGG_SUBS = 16
ITERS = 2
GROUP = 8
SCALAR_LANES = (MODES, MODES + 1, GROUP + MODES, GROUP + MODES + 1, 2 * GROUP + MODES)

HIGHEST = lax.Precision.HIGHEST
VMEM = pl.BlockSpec(memory_space=pltpu.VMEM)
HBM = pl.BlockSpec(memory_space=pltpu.HBM)
NN = (((1,), (0,)), ((), ()))
NT = (((1,), (1,)), ((), ()))


def split(values):
    high = values.astype(jnp.bfloat16).astype(jnp.float32)
    return jnp.concatenate([high, values - high], axis=0).astype(jnp.bfloat16)


def split_dot(values, matrix, dims):
    rows = values.shape[0]
    both = lax.dot_general(split(values), matrix, dims, preferred_element_type=jnp.float32)
    return both[:rows] + both[rows:]


def small_dot(left, right):
    return jnp.dot(left, right, precision=HIGHEST, preferred_element_type=jnp.float32)


def send_blocks(values, place_ref, near_ref, own_ref, *pair_refs):
    height, per_peer = own_ref.shape
    peers = 2 * len(pair_refs) + 2
    slots = split_dot(values, place_ref[:, : peers * per_peer], NN)
    own_ref[...] = slots[:, :per_peer]
    near_ref[...] = slots[:, per_peer : 2 * per_peer]
    for at, ref in enumerate(pair_refs):
        start = (peers - 2 * at - 2) * per_peer
        ref[:height] = slots[:, start + per_peer : start + 2 * per_peer]
        ref[height:] = slots[:, start : start + per_peer]


def received(near_ref, own_ref, *pair_refs):
    height = own_ref.shape[0]
    got = [near_ref[:height]]
    for at in reversed(range(len(pair_refs))):
        got += [near_ref[(at + 1) * height : (at + 2) * height], pair_refs[at][:height]]
    return jnp.concatenate([*got, own_ref[...]], axis=1)


def spread(values, loads, groups):
    modes = values[loads:]
    label = modes[MODES : MODES + 1]
    used = lax.broadcasted_iota(jnp.int32, modes.shape, 0) < MODES
    parts = [jnp.where(used & (label == group), modes, 0.0) for group in range(groups)]
    return jnp.concatenate([values[:loads], *parts], axis=0)


def by_slot(place_ref):
    rows = place_ref.shape[0]
    return place_ref[:, place_ref.shape[1] - rows :]


def place_kernel(
    route_hbm, block_hbm, gap_hbm, traces_hbm,
    place_ref, values_ref, *refs,
):
    *send_refs, route_ref, block_ref, traces_ref, sems = refs
    loads, rows = gap_hbm.shape
    per_peer = send_refs[0].shape[1]
    peers = rows // per_peer
    copies = [
        pltpu.make_async_copy(source, target, sems.at[at])
        for at, (source, target) in enumerate(
            (
                (route_hbm, route_ref),
                (block_hbm, block_ref),
                (traces_hbm, traces_ref),
                (gap_hbm, values_ref.at[pl.ds(0, loads)]),
            )
        )
    ]
    for copy in copies:
        copy.start()
    own_index = lax.axis_index("sub")
    device = own_index * lax.axis_size("rep") + lax.axis_index("rep")
    row_ids = lax.broadcasted_iota(jnp.int32, (rows, per_peer), 0)
    low = lax.broadcasted_iota(jnp.int32, (per_peer, per_peer), 0)
    high = lax.broadcasted_iota(jnp.int32, (per_peer, per_peer), 1)
    reverse = jnp.where(low + high == per_peer - 1, 1.0, 0.0).astype(jnp.bfloat16)
    copies[0].wait()
    for offset in range(peers):
        start = pl.multiple_of((own_index ^ offset) * per_peer, per_peer)
        hits = row_ids == route_ref[:, pl.ds(start, per_peer)]
        at = (offset if offset else peers) * per_peer
        place_ref[:, at : at + per_peer] = jnp.where(hits, 1.0, 0.0).astype(jnp.bfloat16)
    place_ref[:, :per_peer] = jnp.dot(
        place_ref[:, rows:], reverse, preferred_element_type=jnp.float32
    ).astype(jnp.bfloat16)
    copies[1].wait()
    copies[2].wait()
    blocks = block_ref[...]
    lane = lax.broadcasted_iota(jnp.int32, blocks.shape, 1)
    own_block = jnp.sum(jnp.where(lane == device, blocks, 0), axis=1, keepdims=True)
    modes = traces_ref.shape[0]
    label = jnp.broadcast_to(own_block.astype(jnp.float32), (1, rows))
    for mode in range(modes):
        values_ref[loads + mode : loads + mode + 1] = traces_ref[mode]
    values_ref[loads + modes : loads + modes + 1] = label
    values_ref[loads + modes + 1 :] = jnp.zeros((GROUP - modes - 1, rows), jnp.float32)
    copies[3].wait()
    send_blocks(values_ref[...], place_ref, *send_refs)


def ready_kernel(operator_hbm, place_ref, values_ref, operator_ref, placed_ref, own_ref, image_ref, sem):
    copy = pltpu.make_async_copy(operator_hbm, operator_ref, sem)
    copy.start()
    values = values_ref[...]
    loads = values.shape[0] - GROUP
    own = spread(values, loads, (own_ref.shape[0] - loads) // GROUP)
    own_ref[...] = own
    copy.wait()
    operator = operator_ref[0]
    image_ref[...] = split_dot(own, operator, NT)
    placed_ref[...] = jnp.dot(
        operator, by_slot(place_ref), preferred_element_type=jnp.float32
    ).astype(operator.dtype)


def first_kernel(place_ref, placed_ref, own_image_ref, *refs):
    half = len(refs) // 2
    got_refs, (image_ref, *send_refs) = refs[:half], refs[half:]
    height = got_refs[1].shape[0]
    got = spread(received(*got_refs), height - GROUP, (image_ref.shape[0] - height) // GROUP + 1)
    image = own_image_ref[...] - split_dot(got, placed_ref[...], NT)
    image_ref[...] = image
    send_blocks(image, place_ref, *send_refs)


def products_of(left, right):
    both = lax.dot_general(split(left), split(right), NT, preferred_element_type=jnp.float32)
    both = both[: left.shape[0]] + both[left.shape[0] :]
    return both + pltpu.roll(both, right.shape[0], 1)


def with_scalars(top, products, lanes):
    lane = lax.broadcasted_iota(jnp.int32, top.shape, 1)
    for at, product in zip(lanes, products):
        top = jnp.where(lane == at, jnp.sum(product, axis=1, keepdims=True), top)
    return top


def middle_kernel(place_ref, operator_ref, own_ref, image_ref, *refs):
    *got_refs, basis_ref, twice_ref, terms_ref = refs
    coarse = terms_ref.shape[1] // 8
    loads = own_ref.shape[0] - coarse
    got = spread(received(*got_refs), loads, coarse // GROUP)
    basis = own_ref[...] - split_dot(got, by_slot(place_ref), NT)
    basis_ref[...] = basis
    image = image_ref[...]
    twice_ref[...] = split_dot(image, operator_ref[0], NT)
    left = jnp.concatenate([basis[:loads], image[:loads], basis[loads:]])
    empty = jnp.zeros((2 * coarse, basis.shape[1]), jnp.float32)
    both = products_of(left, jnp.concatenate([basis[loads:], image[loads:], empty]))
    strip = lax.broadcasted_iota(jnp.int32, (loads, 8 * coarse), 1) // coarse
    top = jnp.where(strip < 2, both[:loads], 0.0)
    top = jnp.where(strip == 4, both[loads : 2 * loads], top)
    residual = basis[:loads]
    terms_ref[:loads] = with_scalars(top, (residual * residual, residual * image[:loads]), SCALAR_LANES[:2])
    strip = lax.broadcasted_iota(jnp.int32, (coarse, 8 * coarse), 1) // coarse
    terms_ref[loads:] = jnp.where(strip < 2, both[2 * loads :], 0.0)


def second_kernel(place_ref, placed_ref, basis_ref, image_ref, twice_ref, early_ref, *refs):
    *got_refs, jump_ref, terms_ref = refs
    coarse = terms_ref.shape[1] // 8
    loads = basis_ref.shape[0] - coarse
    got = received(*got_refs)
    jump = image_ref[...] - split_dot(got, by_slot(place_ref), NT)
    second = twice_ref[...] - split_dot(got, placed_ref[...], NT)
    jump_ref[...] = jump
    basis = basis_ref[...]
    left = jnp.concatenate([basis[:loads], jump[:loads], second[:loads], basis[loads:], jump[loads:]])
    empty = jnp.zeros((coarse, basis.shape[1]), jnp.float32)
    both = products_of(left, jnp.concatenate([basis[loads:], empty, jump[loads:], second[loads:]]))
    along, jumped, doubled = (both[at * loads : (at + 1) * loads] for at in range(3))
    base, far = both[3 * loads : 3 * loads + coarse], both[3 * loads + coarse :]
    strip = lax.broadcasted_iota(jnp.int32, (loads, 8 * coarse), 1) // coarse
    top = jnp.where(strip == 2, doubled, 0.0)
    top = jnp.where(strip == 3, along, top)
    top = jnp.where(strip == 5, pltpu.roll(doubled, coarse, 1), top)
    top = jnp.where(strip >= 6, jumped, top)
    residual, jump_loads, second_loads = basis[:loads], jump[:loads], second[:loads]
    products = (jump_loads * jump_loads, jump_loads * second_loads, residual * second_loads)
    terms_ref[:loads] = early_ref[:loads] + with_scalars(top, products, SCALAR_LANES[2:])
    strip = lax.broadcasted_iota(jnp.int32, (coarse, 8 * coarse), 1) // coarse
    base = jnp.where((strip == 2) | (strip == 3), base, 0.0)
    terms_ref[loads:] = early_ref[loads:] + jnp.where(strip < 4, base, far)


def eliminate(work, coarse):
    row = lax.broadcasted_iota(jnp.int32, work.shape, 0)
    for first in range(coarse):
        if first % 2 or first % GROUP >= MODES:
            continue
        second = first + 1
        left = jnp.broadcast_to(work[:, first : first + 1], work.shape)
        right = jnp.broadcast_to(work[:, second : second + 1], work.shape)
        upper, lower = work[first : first + 1], work[second : second + 1]
        pivot = 1.0 / left[first : first + 1]
        ratio = left[second : second + 1] * pivot
        corner = 1.0 / (right[second : second + 1] - ratio * right[first : first + 1])
        lower = (lower - ratio * upper) * corner
        upper = (upper - right[first : first + 1] * lower) * pivot
        work = work - left * upper - right * lower
        work = jnp.where(row == first, upper, jnp.where(row == second, lower, work))
    return work


def thin_dot(left, right):
    high, right_high = (value.astype(jnp.bfloat16).astype(jnp.float32) for value in (left, right))
    return jnp.dot(
        jnp.concatenate([high, left - high, high], axis=1).astype(jnp.bfloat16),
        jnp.concatenate([right_high, right_high, right - right_high], axis=0).astype(jnp.bfloat16),
        preferred_element_type=jnp.float32,
    )


def final_kernel(terms_ref, basis_ref, jump_ref, multipliers_ref, amplitudes_ref):
    coarse = terms_ref.shape[1] // 8
    loads = basis_ref.shape[0] - coarse
    groups = coarse // GROUP
    by_load = terms_ref[:loads].T
    used = lax.broadcasted_iota(jnp.int32, (coarse, loads), 0) % GROUP < MODES

    def strip(at):
        return by_load[at * coarse : (at + 1) * coarse]

    def block(at):
        return terms_ref[loads:, at * coarse : (at + 1) * coarse]

    def total(values):
        return jnp.sum(values, axis=0, keepdims=True)

    res_res, res_image, jump_jump, jump_second, res_second = (by_load[at : at + 1] for at in SCALAR_LANES)
    coarse_res, res_h = (jnp.where(used, strip(at), 0.0) for at in (0, 1))
    second_z, res_dz, image_g, second_g, jump_z, jump_dz = (strip(at) for at in range(2, 8))
    g_h, g_dz, z_z, z_dz = block(1), block(3), block(6), block(7)
    row = lax.broadcasted_iota(jnp.int32, (coarse, coarse), 0)
    unit = jnp.where(row == lax.broadcasted_iota(jnp.int32, (coarse, coarse), 1), 1.0, 0.0)
    empty = jnp.zeros((coarse, 5 * coarse - 2 * loads), jnp.float32)
    solved = eliminate(
        jnp.concatenate([terms_ref[loads:, : 2 * coarse], coarse_res, image_g, unit, empty], axis=1), coarse
    )
    inverse_h = solved[:, coarse : 2 * coarse]
    amounts = solved[:, 2 * coarse : 2 * coarse + loads]
    inverse_image = solved[:, 2 * coarse + loads : 2 * coarse + 2 * loads]
    inverse = solved[:, 2 * coarse + 2 * loads : 3 * coarse + 2 * loads]
    products = small_dot(jnp.concatenate([inverse_h, g_h, z_z, g_dz, z_dz], axis=0), amounts)
    inverse_h_amounts, h_amounts, z_amounts, g_dz_amounts, z_dz_amounts = (
        products[at * coarse : (at + 1) * coarse] for at in range(5)
    )
    shares = 2.0 * (inverse_image - inverse_h_amounts)
    both = jnp.concatenate([amounts, shares], axis=0).T
    basis_g, jump_z_rows = basis_ref[loads:], jump_ref[loads:]
    d = basis_ref[:loads] - thin_dot(both[:, :coarse], basis_g)
    u = jump_ref[:loads] - thin_dot(both, jnp.concatenate([jump_z_rows, basis_g], axis=0))
    products = small_dot(jnp.concatenate([g_h, z_z], axis=0), shares)
    image_d = image_g - h_amounts
    inner = res_res - total(amounts * coarse_res)
    curvature = 2.0 * (res_image - total(amounts * (res_h + image_d)))
    u_u = jump_jump - total(amounts * (2.0 * jump_z - z_amounts) + 2.0 * image_d * shares)
    second_u = second_g - g_dz_amounts - products[:coarse]
    jump_u = second_z - z_dz_amounts - 0.5 * products[coarse:]
    d_second = res_second - total(amounts * (res_dz + second_u) + shares * res_h)
    u_second = jump_second - total(amounts * (jump_dz + jump_u) + shares * (0.5 * jump_z + second_u))
    step = inner / curvature
    renewed = step * step * u_u - inner
    grown = 1.0 + renewed / inner
    curvature = grown * grown * curvature - grown * step * (2.0 * d_second + u_u) + 2.0 * step * step * u_second
    second_step = renewed / curvature
    on_d, on_u = step + second_step * grown, second_step * step
    amplitudes = amounts - on_d * shares + 2.0 * on_u * small_dot(inverse, second_u)
    amplitudes_ref[...] = jnp.concatenate(
        [amplitudes[label * GROUP : label * GROUP + MODES] for label in range(groups)], axis=0
    )
    weights = jnp.concatenate([on_d, on_u, jnp.zeros((6, loads), jnp.float32)], axis=0).T
    multipliers_ref[...] = weights[:, 0:1] * d - weights[:, 1:2] * u


def call(kernel, shapes, in_specs, name, scratch=(), flops=0):
    return pl.pallas_call(
        kernel,
        out_shape=[jax.ShapeDtypeStruct(*shape) for shape in shapes],
        in_specs=in_specs,
        out_specs=[VMEM] * len(shapes),
        scratch_shapes=scratch,
        compiler_params=pltpu.CompilerParams(vmem_limit_bytes=24 * 1024 * 1024),
        cost_estimate=pl.CostEstimate(flops=flops, bytes_accessed=2**20, transcendentals=0),
        name=name,
    )


def permute(values, offset, plane_offset=0):
    peers, planes = lax.axis_size("sub"), lax.axis_size("rep")
    offset = offset * planes + plane_offset
    return lax.ppermute(values, ("sub", "rep"), [(at, at ^ offset) for at in range(peers * planes)])


def exchange(near, own, *pairs):
    height = own.shape[0]
    pairs = [permute(pair, 2 * (len(pairs) - at) + 1) for at, pair in enumerate(pairs)]
    near = permute(jnp.concatenate([near, *(pair[height:] for pair in pairs)], axis=0), 1)
    return near, own, *pairs


def total(terms):
    chips = [(offset + 1, 0) for offset in range(2, lax.axis_size("sub"), 2)]
    planes = [(1, offset) for offset in range(1, lax.axis_size("rep"))]
    for offsets in ([(1, 0)], chips, planes):
        parts = [terms, *(permute(terms, *offset) for offset in offsets)]
        while len(parts) > 1:
            parts = [low + high for low, high in zip(parts[::2], parts[1::2])]
        terms = parts[0]
    return terms


def fused_body(dual_ops, mode_traces, route, mode_block, local_gap):
    peers = lax.axis_size("sub")
    loads, rows = local_gap.shape
    modes = mode_traces.shape[1]
    subs = mode_block.shape[0]
    groups = subs // AGG_SUBS
    per_peer = rows // peers
    height = loads + GROUP * groups
    f32, i32 = jnp.float32, jnp.int32
    tall = ((height, rows), f32)
    wide = ((height, 8 * GROUP * groups), f32)

    def blocks(height):
        return [((height, per_peer), f32)] * 2 + [((2 * height, per_peer), f32)] * (peers // 2 - 1)

    def held(value):
        return pltpu.with_memory_space_constraint(value, pltpu.HBM)

    matrix = ((rows, rows), dual_ops.dtype)
    inputs = [route, mode_block.reshape(1, subs), local_gap, mode_traces.transpose(1, 0, 2)]
    place, values, *send = call(
        place_kernel,
        [((rows, rows + per_peer), jnp.bfloat16), ((loads + GROUP, rows), f32), *blocks(loads + GROUP)],
        [HBM] * 4,
        "place",
        [
            pltpu.VMEM((1, rows), i32),
            pltpu.VMEM((1, subs), i32),
            pltpu.VMEM((modes, 1, rows), f32),
            pltpu.SemaphoreType.DMA((4,)),
        ],
    )(*(held(value) for value in inputs))
    got = exchange(*send)
    operator, placed, own, own_image = call(
        ready_kernel,
        [(dual_ops.shape, dual_ops.dtype), matrix, tall, tall],
        [HBM, VMEM, VMEM],
        "ready",
        [pltpu.SemaphoreType.DMA],
        2 * rows * rows * (rows + 2 * height),
    )(held(dual_ops), place, values)
    image, *send = call(first_kernel, [tall, *blocks(height)], [VMEM] * (3 + len(got)), "first")(
        place, placed, own_image, *got
    )
    got_image = exchange(*send)
    basis, twice, terms = call(
        middle_kernel,
        [tall, tall, wide],
        [VMEM] * (4 + len(got)),
        "middle",
        flops=8 * rows * rows * height,
    )(place, operator, own, image, *got)
    jump, terms = call(second_kernel, [tall, wide], [VMEM] * (6 + len(got)), "second")(
        place, placed, basis, image, twice, terms, *got_image
    )
    multipliers, amplitudes = call(
        final_kernel, [((loads, rows), f32), ((MODES * groups, loads), f32)], [VMEM] * 3, "final"
    )(total(terms), basis, jump)
    return multipliers, amplitudes.T


def general_body(dual_ops, mode_traces, route, mode_block, local_gap):
    own_index = lax.axis_index("sub")
    plane_index = lax.axis_index("rep")
    peer_count = lax.axis_size("sub")
    plane_count = lax.axis_size("rep")
    operator = dual_ops[0]
    traces = mode_traces[0]
    slot_rows = route[0]
    rows_here = operator.shape[0]
    load_cases = local_gap.shape[0]
    per_peer = rows_here // peer_count
    blocks = mode_block[:, 0]
    block_count = blocks.shape[0] // AGG_SUBS
    coarse = block_count * MODES
    positions = jnp.arange(rows_here, dtype=jnp.int32)
    inverse = jnp.zeros((rows_here,), jnp.int32).at[slot_rows].set(positions)
    slot_peer = positions // per_peer
    within = positions % per_peer
    flip_index = jnp.where(
        slot_peer == own_index, slot_peer * per_peer + per_peer - 1 - within, positions
    )
    peer_ids = jnp.arange(peer_count, dtype=jnp.int32)
    peer_blocks = blocks[peer_ids * plane_count + plane_index]
    own_block = blocks[own_index * plane_count + plane_index]
    labels = jnp.arange(block_count, dtype=jnp.int32)
    peer_onehot = (peer_blocks[:, None] == labels[None, :]).astype(jnp.float32)
    own_onehot = (labels == own_block).astype(jnp.float32)
    trace_slots = traces[:, slot_rows]
    receive_index = flip_index[inverse]

    def to_peers(values):
        return values[:, slot_rows]

    def from_peers(values):
        return values[:, inverse]

    gap_peers = to_peers(local_gap)
    got_traces = lax.all_to_all(trace_slots, "sub", split_axis=1, concat_axis=1, tiled=True)
    got_gap = lax.all_to_all(gap_peers, "sub", split_axis=1, concat_axis=1, tiled=True)
    partner_traces = got_traces[:, flip_index]
    residual = local_gap - got_gap[:, receive_index]
    own_gram = jnp.dot(traces, traces.T, precision=HIGHEST)
    paired = (trace_slots[:, None, :] * partner_traces[None, :, :]).reshape(
        MODES, MODES, peer_count, per_peer
    )
    cross_terms = jnp.sum(paired, axis=3)
    cross_blocks = jnp.einsum("klq,qb->kbl", cross_terms, peer_onehot, precision=HIGHEST)
    own_blocks = own_gram[:, None, :] * own_onehot[None, :, None]
    row_term = 2.0 * (own_blocks - cross_blocks).reshape(MODES, coarse)
    gram_term = (own_onehot[:, None, None] * row_term[None]).reshape(coarse, coarse)

    def coarse_term(values):
        own_part = 2.0 * jnp.dot(values, traces.T, precision=HIGHEST)
        return (own_part[:, None, :] * own_onehot[None, :, None]).reshape(load_cases, coarse)

    def expand(amounts):
        grouped = amounts.reshape(load_cases, block_count, MODES)
        own_amounts = lax.dynamic_index_in_dim(grouped, own_block, 1, keepdims=False)
        own_part = jnp.dot(own_amounts, traces, precision=HIGHEST)
        peer_amounts = jnp.einsum("qb,rbk->rkq", peer_onehot, grouped, precision=HIGHEST)
        spread = jnp.repeat(peer_amounts, per_peer, axis=2)
        peer_part = jnp.sum(spread * partner_traces[None, :, :], axis=1)
        return own_part - from_peers(peer_part)

    squares = jnp.sum(residual * residual, axis=1)
    gram_matrix, coarse_res, norm_res = lax.psum(
        (gram_term, coarse_term(residual), squares), ("sub", "rep")
    )
    factor = jnp.linalg.cholesky(gram_matrix)

    def solve_coarse(right):
        return jax.scipy.linalg.cho_solve((factor, True), right.T).T

    amplitudes = solve_coarse(coarse_res)
    projected = residual - expand(amplitudes)
    inner_sum = norm_res - jnp.sum(amplitudes * coarse_res, axis=1)
    direction = projected
    multipliers = jnp.zeros_like(residual)
    for iteration in range(ITERS):
        product = lax.dot_general(
            direction.astype(jnp.bfloat16),
            operator,
            (((1,), (1,)), ((), ())),
            preferred_element_type=jnp.float32,
        )
        got_product = lax.all_to_all(
            to_peers(product), "sub", split_axis=1, concat_axis=1, tiled=True
        )
        image_jump = product - got_product[:, receive_index]
        coarse_jump, jump_squares, residual_cross, curvature = lax.psum(
            (
                coarse_term(image_jump),
                jnp.sum(image_jump * image_jump, axis=1),
                jnp.sum(residual * image_jump, axis=1),
                jnp.sum(direction * image_jump, axis=1),
            ),
            ("sub", "rep"),
        )
        step_size = inner_sum / curvature
        multipliers = multipliers + step_size[:, None] * direction
        residual = residual - step_size[:, None] * image_jump
        coarse_res = coarse_res - step_size[:, None] * coarse_jump
        norm_res = (
            norm_res - 2.0 * step_size * residual_cross + step_size * step_size * jump_squares
        )
        amplitudes = solve_coarse(coarse_res)
        if iteration + 1 < ITERS:
            projected = residual - expand(amplitudes)
            renewed = norm_res - jnp.sum(amplitudes * coarse_res, axis=1)
            direction = projected + (renewed / inner_sum)[:, None] * direction
            inner_sum = renewed
    return (multipliers, amplitudes)


def fits(mesh, dual_ops, mode_block, local_gap):
    peers, planes = mesh.shape["sub"], mesh.shape["rep"]
    powers = all(size & (size - 1) == 0 for size in (peers, planes))
    whole = dual_ops.shape[1] % (128 * peers) == 0 and local_gap.shape[0] % 16 == 0
    return powers and whole and 8 * GROUP * (mode_block.shape[0] // AGG_SUBS) == 128


def solution(mesh):
    placed = (
        P(("sub", "rep"), None, None),
        P(("sub", "rep"), None, None),
        P(("sub", "rep"), None),
        P(),
        P(None, ("sub", "rep")),
    )

    def run(dual_ops, mode_traces, route, mode_block, local_gap):
        body = fused_body if fits(mesh, dual_ops, mode_block, local_gap) else general_body
        return jax.shard_map(
            body, mesh=mesh, in_specs=placed, out_specs=(P(None, ("sub", "rep")), P()), check_vma=False
        )(dual_ops, mode_traces, route, mode_block, local_gap)

    return run
```

```python
import jax
import jax.numpy as jnp
from jax import lax
from jax.experimental import pallas as pl
from jax.experimental.pallas import tpu as pltpu
from jax.sharding import PartitionSpec as P

MODES = 6
AGG_SUBS = 16
ITERS = 2
GROUP = 8
SCALAR_LANES = (MODES, MODES + 1, GROUP + MODES, GROUP + MODES + 1, 2 * GROUP + MODES)

HIGHEST = lax.Precision.HIGHEST
VMEM = pl.BlockSpec(memory_space=pltpu.VMEM)
HBM = pl.BlockSpec(memory_space=pltpu.HBM)
NN = (((1,), (0,)), ((), ()))
NT = (((1,), (1,)), ((), ()))


def split(values):
    high = values.astype(jnp.bfloat16).astype(jnp.float32)
    return jnp.concatenate([high, values - high], axis=0).astype(jnp.bfloat16)


def split_dot(values, matrix, dims):
    rows = values.shape[0]
    both = lax.dot_general(split(values), matrix, dims, preferred_element_type=jnp.float32)
    return both[:rows] + both[rows:]


def small_dot(left, right):
    return jnp.dot(left, right, precision=HIGHEST, preferred_element_type=jnp.float32)


def send_far(values, far_ref, *pair_refs):
    height = values.shape[0]
    per_peer = pair_refs[0].shape[1]
    slots = split_dot(values, far_ref[...], NN)
    for at, ref in enumerate(reversed(pair_refs)):
        start = 2 * at * per_peer
        ref[:height] = slots[:, start + per_peer : start + 2 * per_peer]
        ref[height:] = slots[:, start : start + per_peer]


def send_near(values, place_ref, near_ref, own_ref):
    per_peer = own_ref.shape[1]
    slots = split_dot(values, place_ref[:, : 2 * per_peer], NN)
    own_ref[...] = slots[:, :per_peer]
    near_ref[...] = slots[:, per_peer:]


def received(near_ref, own_ref, *pair_refs):
    height = own_ref.shape[0]
    got = [near_ref[:height]]
    for at in reversed(range(len(pair_refs))):
        got += [near_ref[(at + 1) * height : (at + 2) * height], pair_refs[at][:height]]
    return jnp.concatenate([*got, own_ref[...]], axis=1)


def spread(values, loads, groups):
    modes = values[loads:]
    label = modes[MODES : MODES + 1]
    used = lax.broadcasted_iota(jnp.int32, modes.shape, 0) < MODES
    parts = [jnp.where(used & (label == group), modes, 0.0) for group in range(groups)]
    return jnp.concatenate([values[:loads], *parts], axis=0)


def by_slot(place_ref):
    rows = place_ref.shape[0]
    return place_ref[:, place_ref.shape[1] - rows :]


def one_hot(route_ref, peer, per_peer):
    start = pl.multiple_of(peer * per_peer, per_peer)
    row_ids = lax.broadcasted_iota(jnp.int32, (route_ref.shape[1], per_peer), 0)
    return jnp.where(row_ids == route_ref[:, pl.ds(start, per_peer)], 1.0, 0.0).astype(jnp.bfloat16)


def place_kernel(
    route_hbm, block_hbm, gap_hbm, traces_hbm, operator_hbm,
    far_ref, values_ref, operator_ref, route_ref, *refs,
):
    *pair_refs, block_ref, traces_ref, sems = refs
    loads, rows = gap_hbm.shape
    per_peer = pair_refs[0].shape[1]
    peers = rows // per_peer
    copies = [
        pltpu.make_async_copy(source, target, sems.at[at])
        for at, (source, target) in enumerate(
            (
                (route_hbm, route_ref),
                (block_hbm, block_ref),
                (traces_hbm, traces_ref),
                (gap_hbm, values_ref.at[pl.ds(0, loads)]),
                (operator_hbm, operator_ref),
            )
        )
    ]
    for copy in copies:
        copy.start()
    own_index = lax.axis_index("sub")
    device = own_index * lax.axis_size("rep") + lax.axis_index("rep")
    copies[0].wait()
    for offset in range(2, peers):
        at = (offset - 2) * per_peer
        far_ref[:, at : at + per_peer] = one_hot(route_ref, own_index ^ offset, per_peer)
    copies[1].wait()
    copies[2].wait()
    blocks = block_ref[...]
    lane = lax.broadcasted_iota(jnp.int32, blocks.shape, 1)
    own_block = jnp.sum(jnp.where(lane == device, blocks, 0), axis=1, keepdims=True)
    modes = traces_ref.shape[0]
    label = jnp.broadcast_to(own_block.astype(jnp.float32), (1, rows))
    for mode in range(modes):
        values_ref[loads + mode : loads + mode + 1] = traces_ref[mode]
    values_ref[loads + modes : loads + modes + 1] = label
    values_ref[loads + modes + 1 :] = jnp.zeros((GROUP - modes - 1, rows), jnp.float32)
    copies[3].wait()
    send_far(values_ref[...], far_ref, *pair_refs)
    copies[4].wait()


def ready_kernel(
    route_ref, far_ref, values_ref, operator_ref,
    place_ref, placed_ref, own_ref, image_ref, near_ref, back_ref,
):
    rows = place_ref.shape[0]
    per_peer = back_ref.shape[1]
    own_index = lax.axis_index("sub")
    low = lax.broadcasted_iota(jnp.int32, (per_peer, per_peer), 0)
    high = lax.broadcasted_iota(jnp.int32, (per_peer, per_peer), 1)
    reverse = jnp.where(low + high == per_peer - 1, 1.0, 0.0).astype(jnp.bfloat16)
    own_columns = one_hot(route_ref, own_index, per_peer)
    place_ref[:, rows:] = own_columns
    place_ref[:, per_peer : 2 * per_peer] = one_hot(route_ref, own_index ^ 1, per_peer)
    place_ref[:, 2 * per_peer : rows] = far_ref[...]
    place_ref[:, :per_peer] = jnp.dot(own_columns, reverse, preferred_element_type=jnp.float32).astype(jnp.bfloat16)
    values = values_ref[...]
    send_near(values, place_ref, near_ref, back_ref)
    loads = values.shape[0] - GROUP
    own = spread(values, loads, (own_ref.shape[0] - loads) // GROUP)
    own_ref[...] = own
    operator = operator_ref[0]
    image_ref[...] = split_dot(own, operator, NT)
    placed_ref[...] = jnp.dot(
        operator, by_slot(place_ref), preferred_element_type=jnp.float32
    ).astype(operator.dtype)


def first_kernel(far_ref, placed_ref, own_image_ref, *refs):
    half = (len(refs) + 1) // 2
    got_refs, (image_ref, *pair_refs) = refs[:half], refs[half:]
    height = got_refs[1].shape[0]
    got = spread(received(*got_refs), height - GROUP, (image_ref.shape[0] - height) // GROUP + 1)
    image = own_image_ref[...] - split_dot(got, placed_ref[...], NT)
    image_ref[...] = image
    send_far(image, far_ref, *pair_refs)


def products_of(left, right):
    both = lax.dot_general(split(left), split(right), NT, preferred_element_type=jnp.float32)
    both = both[: left.shape[0]] + both[left.shape[0] :]
    return both + pltpu.roll(both, right.shape[0], 1)


def with_scalars(top, products, lanes):
    lane = lax.broadcasted_iota(jnp.int32, top.shape, 1)
    for at, product in zip(lanes, products):
        top = jnp.where(lane == at, jnp.sum(product, axis=1, keepdims=True), top)
    return top


def middle_kernel(place_ref, operator_ref, own_ref, image_ref, *refs):
    *got_refs, basis_ref, twice_ref, terms_ref, near_ref, back_ref = refs
    send_near(image_ref[...], place_ref, near_ref, back_ref)
    coarse = terms_ref.shape[1] // 8
    loads = own_ref.shape[0] - coarse
    got = spread(received(*got_refs), loads, coarse // GROUP)
    basis = own_ref[...] - split_dot(got, by_slot(place_ref), NT)
    basis_ref[...] = basis
    image = image_ref[...]
    twice_ref[...] = split_dot(image, operator_ref[0], NT)
    left = jnp.concatenate([basis[:loads], image[:loads], basis[loads:]])
    empty = jnp.zeros((2 * coarse, basis.shape[1]), jnp.float32)
    both = products_of(left, jnp.concatenate([basis[loads:], image[loads:], empty]))
    strip = lax.broadcasted_iota(jnp.int32, (loads, 8 * coarse), 1) // coarse
    top = jnp.where(strip < 2, both[:loads], 0.0)
    top = jnp.where(strip == 4, both[loads : 2 * loads], top)
    residual = basis[:loads]
    terms_ref[:loads] = with_scalars(top, (residual * residual, residual * image[:loads]), SCALAR_LANES[:2])
    strip = lax.broadcasted_iota(jnp.int32, (coarse, 8 * coarse), 1) // coarse
    terms_ref[loads:] = jnp.where(strip < 2, both[2 * loads :], 0.0)


def second_kernel(place_ref, placed_ref, basis_ref, image_ref, twice_ref, early_ref, *refs):
    *got_refs, jump_ref, terms_ref = refs
    coarse = terms_ref.shape[1] // 8
    loads = basis_ref.shape[0] - coarse
    got = received(*got_refs)
    jump = image_ref[...] - split_dot(got, by_slot(place_ref), NT)
    second = twice_ref[...] - split_dot(got, placed_ref[...], NT)
    jump_ref[...] = jump
    basis = basis_ref[...]
    left = jnp.concatenate([basis[:loads], jump[:loads], second[:loads], basis[loads:], jump[loads:]])
    empty = jnp.zeros((coarse, basis.shape[1]), jnp.float32)
    both = products_of(left, jnp.concatenate([basis[loads:], empty, jump[loads:], second[loads:]]))
    along, jumped, doubled = (both[at * loads : (at + 1) * loads] for at in range(3))
    base, far = both[3 * loads : 3 * loads + coarse], both[3 * loads + coarse :]
    strip = lax.broadcasted_iota(jnp.int32, (loads, 8 * coarse), 1) // coarse
    top = jnp.where(strip == 2, doubled, 0.0)
    top = jnp.where(strip == 3, along, top)
    top = jnp.where(strip == 5, pltpu.roll(doubled, coarse, 1), top)
    top = jnp.where(strip >= 6, jumped, top)
    residual, jump_loads, second_loads = basis[:loads], jump[:loads], second[:loads]
    products = (jump_loads * jump_loads, jump_loads * second_loads, residual * second_loads)
    terms_ref[:loads] = early_ref[:loads] + with_scalars(top, products, SCALAR_LANES[2:])
    strip = lax.broadcasted_iota(jnp.int32, (coarse, 8 * coarse), 1) // coarse
    base = jnp.where((strip == 2) | (strip == 3), base, 0.0)
    terms_ref[loads:] = early_ref[loads:] + jnp.where(strip < 4, base, far)


def eliminate(work, coarse):
    row = lax.broadcasted_iota(jnp.int32, work.shape, 0)
    for first in range(coarse):
        if first % 2 or first % GROUP >= MODES:
            continue
        second = first + 1
        left = jnp.broadcast_to(work[:, first : first + 1], work.shape)
        right = jnp.broadcast_to(work[:, second : second + 1], work.shape)
        upper, lower = work[first : first + 1], work[second : second + 1]
        pivot = 1.0 / left[first : first + 1]
        ratio = left[second : second + 1] * pivot
        corner = 1.0 / (right[second : second + 1] - ratio * right[first : first + 1])
        lower = (lower - ratio * upper) * corner
        upper = (upper - right[first : first + 1] * lower) * pivot
        work = work - left * upper - right * lower
        work = jnp.where(row == first, upper, jnp.where(row == second, lower, work))
    return work


def thin_dot(left, right):
    high, right_high = (value.astype(jnp.bfloat16).astype(jnp.float32) for value in (left, right))
    return jnp.dot(
        jnp.concatenate([high, left - high, high], axis=1).astype(jnp.bfloat16),
        jnp.concatenate([right_high, right_high, right - right_high], axis=0).astype(jnp.bfloat16),
        preferred_element_type=jnp.float32,
    )


def final_kernel(terms_ref, basis_ref, jump_ref, multipliers_ref, amplitudes_ref):
    coarse = terms_ref.shape[1] // 8
    loads = basis_ref.shape[0] - coarse
    groups = coarse // GROUP
    by_load = terms_ref[:loads].T
    used = lax.broadcasted_iota(jnp.int32, (coarse, loads), 0) % GROUP < MODES

    def strip(at):
        return by_load[at * coarse : (at + 1) * coarse]

    def block(at):
        return terms_ref[loads:, at * coarse : (at + 1) * coarse]

    def total(values):
        return jnp.sum(values, axis=0, keepdims=True)

    res_res, res_image, jump_jump, jump_second, res_second = (by_load[at : at + 1] for at in SCALAR_LANES)
    coarse_res, res_h = (jnp.where(used, strip(at), 0.0) for at in (0, 1))
    second_z, res_dz, image_g, second_g, jump_z, jump_dz = (strip(at) for at in range(2, 8))
    g_h, g_dz, z_z, z_dz = block(1), block(3), block(6), block(7)
    row = lax.broadcasted_iota(jnp.int32, (coarse, coarse), 0)
    unit = jnp.where(row == lax.broadcasted_iota(jnp.int32, (coarse, coarse), 1), 1.0, 0.0)
    empty = jnp.zeros((coarse, 5 * coarse - 2 * loads), jnp.float32)
    solved = eliminate(
        jnp.concatenate([terms_ref[loads:, : 2 * coarse], coarse_res, image_g, unit, empty], axis=1), coarse
    )
    inverse_h = solved[:, coarse : 2 * coarse]
    amounts = solved[:, 2 * coarse : 2 * coarse + loads]
    inverse_image = solved[:, 2 * coarse + loads : 2 * coarse + 2 * loads]
    inverse = solved[:, 2 * coarse + 2 * loads : 3 * coarse + 2 * loads]
    products = small_dot(jnp.concatenate([inverse_h, g_h, z_z, g_dz, z_dz], axis=0), amounts)
    inverse_h_amounts, h_amounts, z_amounts, g_dz_amounts, z_dz_amounts = (
        products[at * coarse : (at + 1) * coarse] for at in range(5)
    )
    shares = 2.0 * (inverse_image - inverse_h_amounts)
    both = jnp.concatenate([amounts, shares], axis=0).T
    basis_g, jump_z_rows = basis_ref[loads:], jump_ref[loads:]
    d = basis_ref[:loads] - thin_dot(both[:, :coarse], basis_g)
    u = jump_ref[:loads] - thin_dot(both, jnp.concatenate([jump_z_rows, basis_g], axis=0))
    products = small_dot(jnp.concatenate([g_h, z_z], axis=0), shares)
    image_d = image_g - h_amounts
    inner = res_res - total(amounts * coarse_res)
    curvature = 2.0 * (res_image - total(amounts * (res_h + image_d)))
    u_u = jump_jump - total(amounts * (2.0 * jump_z - z_amounts) + 2.0 * image_d * shares)
    second_u = second_g - g_dz_amounts - products[:coarse]
    jump_u = second_z - z_dz_amounts - 0.5 * products[coarse:]
    d_second = res_second - total(amounts * (res_dz + second_u) + shares * res_h)
    u_second = jump_second - total(amounts * (jump_dz + jump_u) + shares * (0.5 * jump_z + second_u))
    step = inner / curvature
    renewed = step * step * u_u - inner
    grown = 1.0 + renewed / inner
    curvature = grown * grown * curvature - grown * step * (2.0 * d_second + u_u) + 2.0 * step * step * u_second
    second_step = renewed / curvature
    on_d, on_u = step + second_step * grown, second_step * step
    amplitudes = amounts - on_d * shares + 2.0 * on_u * small_dot(inverse, second_u)
    amplitudes_ref[...] = jnp.concatenate(
        [amplitudes[label * GROUP : label * GROUP + MODES] for label in range(groups)], axis=0
    )
    weights = jnp.concatenate([on_d, on_u, jnp.zeros((6, loads), jnp.float32)], axis=0).T
    multipliers_ref[...] = weights[:, 0:1] * d - weights[:, 1:2] * u


def call(kernel, shapes, in_specs, name, scratch=(), flops=0):
    return pl.pallas_call(
        kernel,
        out_shape=[jax.ShapeDtypeStruct(*shape) for shape in shapes],
        in_specs=in_specs,
        out_specs=[VMEM] * len(shapes),
        scratch_shapes=scratch,
        compiler_params=pltpu.CompilerParams(vmem_limit_bytes=24 * 1024 * 1024),
        cost_estimate=pl.CostEstimate(flops=flops, bytes_accessed=2**20, transcendentals=0),
        name=name,
    )


def permute(values, offset, plane_offset=0):
    peers, planes = lax.axis_size("sub"), lax.axis_size("rep")
    offset = offset * planes + plane_offset
    return lax.ppermute(values, ("sub", "rep"), [(at, at ^ offset) for at in range(peers * planes)])


def to_chips(*pairs):
    return [permute(pair, 2 * (len(pairs) - at) + 1) for at, pair in enumerate(pairs)]


def to_core(near, own, *pairs):
    height = own.shape[0]
    return permute(jnp.concatenate([near, *(pair[height:] for pair in pairs)], axis=0), 1), own, *pairs


def total(terms):
    chips = [(offset + 1, 0) for offset in range(2, lax.axis_size("sub"), 2)]
    planes = [(1, offset) for offset in range(1, lax.axis_size("rep"))]
    for offsets in ([(1, 0)], chips, planes):
        parts = [terms, *(permute(terms, *offset) for offset in offsets)]
        while len(parts) > 1:
            parts = [low + high for low, high in zip(parts[::2], parts[1::2])]
        terms = parts[0]
    return terms


def fused_body(dual_ops, mode_traces, route, mode_block, local_gap):
    peers = lax.axis_size("sub")
    loads, rows = local_gap.shape
    modes = mode_traces.shape[1]
    subs = mode_block.shape[0]
    groups = subs // AGG_SUBS
    per_peer = rows // peers
    height = loads + GROUP * groups
    f32, i32 = jnp.float32, jnp.int32
    tall = ((height, rows), f32)
    wide = ((height, 8 * GROUP * groups), f32)

    def pairs(height):
        return [((2 * height, per_peer), f32)] * (peers // 2 - 1)

    def singles(height):
        return [((height, per_peer), f32)] * 2

    def held(value):
        return pltpu.with_memory_space_constraint(value, pltpu.HBM)

    matrix = ((rows, rows), dual_ops.dtype)
    inputs = [route, mode_block.reshape(1, subs), local_gap, mode_traces.transpose(1, 0, 2), dual_ops]
    short = loads + GROUP
    far, values, operator, route, *send = call(
        place_kernel,
        [
            ((rows, rows - 2 * per_peer), jnp.bfloat16),
            ((short, rows), f32),
            (dual_ops.shape, dual_ops.dtype),
            (route.shape, i32),
            *pairs(short),
        ],
        [HBM] * 5,
        "place",
        [pltpu.VMEM((1, subs), i32), pltpu.VMEM((modes, 1, rows), f32), pltpu.SemaphoreType.DMA((5,))],
    )(*(held(value) for value in inputs))
    got = to_chips(*send)
    place, placed, own, own_image, *stay = call(
        ready_kernel,
        [((rows, rows + per_peer), jnp.bfloat16), matrix, tall, tall, *singles(short)],
        [VMEM] * 4,
        "ready",
        flops=2 * rows * rows * (rows + 2 * height),
    )(route, far, values, operator)
    got = to_core(*stay, *got)
    image, *send = call(first_kernel, [tall, *pairs(height)], [VMEM] * (3 + len(got)), "first")(
        far, placed, own_image, *got
    )
    got_image = to_chips(*send)
    basis, twice, terms, *stay = call(
        middle_kernel,
        [tall, tall, wide, *singles(height)],
        [VMEM] * (4 + len(got)),
        "middle",
        flops=8 * rows * rows * height,
    )(place, operator, own, image, *got)
    got_image = to_core(*stay, *got_image)
    jump, terms = call(second_kernel, [tall, wide], [VMEM] * (6 + len(got)), "second")(
        place, placed, basis, image, twice, terms, *got_image
    )
    multipliers, amplitudes = call(
        final_kernel, [((loads, rows), f32), ((MODES * groups, loads), f32)], [VMEM] * 3, "final"
    )(total(terms), basis, jump)
    return multipliers, amplitudes.T


def general_body(dual_ops, mode_traces, route, mode_block, local_gap):
    own_index = lax.axis_index("sub")
    plane_index = lax.axis_index("rep")
    peer_count = lax.axis_size("sub")
    plane_count = lax.axis_size("rep")
    operator = dual_ops[0]
    traces = mode_traces[0]
    slot_rows = route[0]
    rows_here = operator.shape[0]
    load_cases = local_gap.shape[0]
    per_peer = rows_here // peer_count
    blocks = mode_block[:, 0]
    block_count = blocks.shape[0] // AGG_SUBS
    coarse = block_count * MODES
    positions = jnp.arange(rows_here, dtype=jnp.int32)
    inverse = jnp.zeros((rows_here,), jnp.int32).at[slot_rows].set(positions)
    slot_peer = positions // per_peer
    within = positions % per_peer
    flip_index = jnp.where(
        slot_peer == own_index, slot_peer * per_peer + per_peer - 1 - within, positions
    )
    peer_ids = jnp.arange(peer_count, dtype=jnp.int32)
    peer_blocks = blocks[peer_ids * plane_count + plane_index]
    own_block = blocks[own_index * plane_count + plane_index]
    labels = jnp.arange(block_count, dtype=jnp.int32)
    peer_onehot = (peer_blocks[:, None] == labels[None, :]).astype(jnp.float32)
    own_onehot = (labels == own_block).astype(jnp.float32)
    trace_slots = traces[:, slot_rows]
    receive_index = flip_index[inverse]

    def to_peers(values):
        return values[:, slot_rows]

    def from_peers(values):
        return values[:, inverse]

    gap_peers = to_peers(local_gap)
    got_traces = lax.all_to_all(trace_slots, "sub", split_axis=1, concat_axis=1, tiled=True)
    got_gap = lax.all_to_all(gap_peers, "sub", split_axis=1, concat_axis=1, tiled=True)
    partner_traces = got_traces[:, flip_index]
    residual = local_gap - got_gap[:, receive_index]
    own_gram = jnp.dot(traces, traces.T, precision=HIGHEST)
    paired = (trace_slots[:, None, :] * partner_traces[None, :, :]).reshape(
        MODES, MODES, peer_count, per_peer
    )
    cross_terms = jnp.sum(paired, axis=3)
    cross_blocks = jnp.einsum("klq,qb->kbl", cross_terms, peer_onehot, precision=HIGHEST)
    own_blocks = own_gram[:, None, :] * own_onehot[None, :, None]
    row_term = 2.0 * (own_blocks - cross_blocks).reshape(MODES, coarse)
    gram_term = (own_onehot[:, None, None] * row_term[None]).reshape(coarse, coarse)

    def coarse_term(values):
        own_part = 2.0 * jnp.dot(values, traces.T, precision=HIGHEST)
        return (own_part[:, None, :] * own_onehot[None, :, None]).reshape(load_cases, coarse)

    def expand(amounts):
        grouped = amounts.reshape(load_cases, block_count, MODES)
        own_amounts = lax.dynamic_index_in_dim(grouped, own_block, 1, keepdims=False)
        own_part = jnp.dot(own_amounts, traces, precision=HIGHEST)
        peer_amounts = jnp.einsum("qb,rbk->rkq", peer_onehot, grouped, precision=HIGHEST)
        spread = jnp.repeat(peer_amounts, per_peer, axis=2)
        peer_part = jnp.sum(spread * partner_traces[None, :, :], axis=1)
        return own_part - from_peers(peer_part)

    squares = jnp.sum(residual * residual, axis=1)
    gram_matrix, coarse_res, norm_res = lax.psum(
        (gram_term, coarse_term(residual), squares), ("sub", "rep")
    )
    factor = jnp.linalg.cholesky(gram_matrix)

    def solve_coarse(right):
        return jax.scipy.linalg.cho_solve((factor, True), right.T).T

    amplitudes = solve_coarse(coarse_res)
    projected = residual - expand(amplitudes)
    inner_sum = norm_res - jnp.sum(amplitudes * coarse_res, axis=1)
    direction = projected
    multipliers = jnp.zeros_like(residual)
    for iteration in range(ITERS):
        product = lax.dot_general(
            direction.astype(jnp.bfloat16),
            operator,
            (((1,), (1,)), ((), ())),
            preferred_element_type=jnp.float32,
        )
        got_product = lax.all_to_all(
            to_peers(product), "sub", split_axis=1, concat_axis=1, tiled=True
        )
        image_jump = product - got_product[:, receive_index]
        coarse_jump, jump_squares, residual_cross, curvature = lax.psum(
            (
                coarse_term(image_jump),
                jnp.sum(image_jump * image_jump, axis=1),
                jnp.sum(residual * image_jump, axis=1),
                jnp.sum(direction * image_jump, axis=1),
            ),
            ("sub", "rep"),
        )
        step_size = inner_sum / curvature
        multipliers = multipliers + step_size[:, None] * direction
        residual = residual - step_size[:, None] * image_jump
        coarse_res = coarse_res - step_size[:, None] * coarse_jump
        norm_res = (
            norm_res - 2.0 * step_size * residual_cross + step_size * step_size * jump_squares
        )
        amplitudes = solve_coarse(coarse_res)
        if iteration + 1 < ITERS:
            projected = residual - expand(amplitudes)
            renewed = norm_res - jnp.sum(amplitudes * coarse_res, axis=1)
            direction = projected + (renewed / inner_sum)[:, None] * direction
            inner_sum = renewed
    return (multipliers, amplitudes)


def fits(mesh, dual_ops, mode_block, local_gap):
    peers, planes = mesh.shape["sub"], mesh.shape["rep"]
    powers = all(size & (size - 1) == 0 for size in (peers, planes))
    whole = dual_ops.shape[1] % (128 * peers) == 0 and local_gap.shape[0] % 16 == 0
    return powers and whole and 8 * GROUP * (mode_block.shape[0] // AGG_SUBS) == 128


def solution(mesh):
    placed = (
        P(("sub", "rep"), None, None),
        P(("sub", "rep"), None, None),
        P(("sub", "rep"), None),
        P(),
        P(None, ("sub", "rep")),
    )

    def run(dual_ops, mode_traces, route, mode_block, local_gap):
        body = fused_body if fits(mesh, dual_ops, mode_block, local_gap) else general_body
        return jax.shard_map(
            body, mesh=mesh, in_specs=placed, out_specs=(P(None, ("sub", "rep")), P()), check_vma=False
        )(dual_ops, mode_traces, route, mode_block, local_gap)

    return run
```

```python
import jax
import jax.numpy as jnp
from jax import lax
from jax.experimental import pallas as pl
from jax.experimental.pallas import tpu as pltpu
from jax.sharding import PartitionSpec as P

MODES = 6
AGG_SUBS = 16
ITERS = 2
GROUP = 8
SCALAR_LANES = (MODES, MODES + 1, GROUP + MODES, GROUP + MODES + 1, 2 * GROUP + MODES)

HIGHEST = lax.Precision.HIGHEST
VMEM = pl.BlockSpec(memory_space=pltpu.VMEM)
HBM = pl.BlockSpec(memory_space=pltpu.HBM)
NN = (((1,), (0,)), ((), ()))
NT = (((1,), (1,)), ((), ()))


def split(values):
    high = values.astype(jnp.bfloat16).astype(jnp.float32)
    return jnp.concatenate([high, values - high], axis=0).astype(jnp.bfloat16)


def split_dot(values, matrix, dims):
    rows = values.shape[0]
    both = lax.dot_general(split(values), matrix, dims, preferred_element_type=jnp.float32)
    return both[:rows] + both[rows:]


def small_dot(left, right):
    return jnp.dot(left, right, precision=HIGHEST, preferred_element_type=jnp.float32)


def send_far(values, far_ref, *pair_refs):
    height = values.shape[0]
    per_peer = pair_refs[0].shape[1]
    slots = split_dot(values, far_ref[...], NN)
    for at, ref in enumerate(reversed(pair_refs)):
        start = 2 * at * per_peer
        ref[:height] = slots[:, start + per_peer : start + 2 * per_peer]
        ref[height:] = slots[:, start : start + per_peer]


def send_near(values, edge_ref, near_ref, back_ref):
    per_peer = back_ref.shape[1]
    slots = split_dot(values, edge_ref[...], NN)
    near_ref[...] = slots[:, :per_peer]
    back_ref[...] = slots[:, per_peer:]


def straight(back_ref, *pair_refs):
    height = back_ref.shape[0]
    return jnp.concatenate([*(ref[:height] for ref in pair_refs), back_ref[...]], axis=1)


def handed(near_ref, height):
    return jnp.concatenate([near_ref[at : at + height] for at in range(0, near_ref.shape[0], height)], axis=1)


def spread(values, loads, groups):
    modes = values[loads:]
    label = modes[MODES : MODES + 1]
    used = lax.broadcasted_iota(jnp.int32, modes.shape, 0) < MODES
    parts = [jnp.where(used & (label == group), modes, 0.0) for group in range(groups)]
    return jnp.concatenate([values[:loads], *parts], axis=0)


def one_hot(route_ref, peer, per_peer):
    start = pl.multiple_of(peer * per_peer, per_peer)
    row_ids = lax.broadcasted_iota(jnp.int32, (route_ref.shape[1], per_peer), 0)
    return jnp.where(row_ids == route_ref[:, pl.ds(start, per_peer)], 1.0, 0.0).astype(jnp.bfloat16)


def place_kernel(
    route_hbm, block_hbm, gap_hbm, traces_hbm, operator_hbm,
    far_ref, values_ref, operator_ref, route_ref, *refs,
):
    *pair_refs, block_ref, traces_ref, sems = refs
    loads, rows = gap_hbm.shape
    per_peer = pair_refs[0].shape[1]
    peers = rows // per_peer
    copies = [
        pltpu.make_async_copy(source, target, sems.at[at])
        for at, (source, target) in enumerate(
            (
                (route_hbm, route_ref),
                (block_hbm, block_ref),
                (traces_hbm, traces_ref),
                (gap_hbm, values_ref.at[pl.ds(0, loads)]),
                (operator_hbm, operator_ref),
            )
        )
    ]
    for copy in copies:
        copy.start()
    own_index = lax.axis_index("sub")
    device = own_index * lax.axis_size("rep") + lax.axis_index("rep")
    copies[0].wait()
    for offset in range(2, peers):
        at = (offset - 2) * per_peer
        far_ref[:, at : at + per_peer] = one_hot(route_ref, own_index ^ offset, per_peer)
    copies[1].wait()
    copies[2].wait()
    blocks = block_ref[...]
    lane = lax.broadcasted_iota(jnp.int32, blocks.shape, 1)
    own_block = jnp.sum(jnp.where(lane == device, blocks, 0), axis=1, keepdims=True)
    modes = traces_ref.shape[0]
    label = jnp.broadcast_to(own_block.astype(jnp.float32), (1, rows))
    for mode in range(modes):
        values_ref[loads + mode : loads + mode + 1] = traces_ref[mode]
    values_ref[loads + modes : loads + modes + 1] = label
    values_ref[loads + modes + 1 :] = jnp.zeros((GROUP - modes - 1, rows), jnp.float32)
    copies[3].wait()
    send_far(values_ref[...], far_ref, *pair_refs)
    copies[4].wait()


def ready_kernel(
    route_ref, far_ref, values_ref, operator_ref,
    edge_ref, slots_ref, placed_ref, own_ref, image_ref, near_ref, back_ref,
):
    per_peer = back_ref.shape[1]
    peers = far_ref.shape[1] // per_peer + 2
    own_index = lax.axis_index("sub")
    low = lax.broadcasted_iota(jnp.int32, (per_peer, per_peer), 0)
    high = lax.broadcasted_iota(jnp.int32, (per_peer, per_peer), 1)
    reverse = jnp.where(low + high == per_peer - 1, 1.0, 0.0).astype(jnp.bfloat16)
    own_columns = one_hot(route_ref, own_index, per_peer)
    near_columns = one_hot(route_ref, own_index ^ 1, per_peer)
    edge_ref[:, :per_peer] = near_columns
    edge_ref[:, per_peer:] = jnp.dot(own_columns, reverse, preferred_element_type=jnp.float32).astype(jnp.bfloat16)
    for at in range(peers // 2 - 1):
        start = (peers - 4 - 2 * at) * per_peer
        slots_ref[0, :, at * per_peer : (at + 1) * per_peer] = far_ref[:, start + per_peer : start + 2 * per_peer]
        slots_ref[1, :, (at + 1) * per_peer : (at + 2) * per_peer] = far_ref[:, start : start + per_peer]
    slots_ref[0, :, (peers // 2 - 1) * per_peer :] = own_columns
    slots_ref[1, :, :per_peer] = near_columns
    values = values_ref[...]
    send_near(values, edge_ref, near_ref, back_ref)
    loads = values.shape[0] - GROUP
    own = spread(values, loads, (own_ref.shape[0] - loads) // GROUP)
    own_ref[...] = own
    operator = operator_ref[0]
    image_ref[...] = split_dot(own, operator, NT)
    for half in range(2):
        placed_ref[half] = jnp.dot(
            operator, slots_ref[half], preferred_element_type=jnp.float32
        ).astype(operator.dtype)


def first_half_kernel(placed_ref, own_image_ref, back_ref, *refs):
    *pair_refs, image_ref = refs
    height = back_ref.shape[0]
    got = spread(straight(back_ref, *pair_refs), height - GROUP, (image_ref.shape[0] - height) // GROUP + 1)
    image_ref[...] = own_image_ref[...] - split_dot(got, placed_ref[0], NT)


def first_kernel(far_ref, placed_ref, half_ref, near_ref, image_ref, *pair_refs):
    height = near_ref.shape[0] * near_ref.shape[1] * 2 // image_ref.shape[1]
    got = spread(handed(near_ref, height), height - GROUP, (image_ref.shape[0] - height) // GROUP + 1)
    image = half_ref[...] - split_dot(got, placed_ref[1], NT)
    image_ref[...] = image
    send_far(image, far_ref, *pair_refs)


def products_of(left, right):
    both = lax.dot_general(split(left), split(right), NT, preferred_element_type=jnp.float32)
    both = both[: left.shape[0]] + both[left.shape[0] :]
    return both + pltpu.roll(both, right.shape[0], 1)


def with_scalars(top, products, lanes):
    lane = lax.broadcasted_iota(jnp.int32, top.shape, 1)
    for at, product in zip(lanes, products):
        top = jnp.where(lane == at, jnp.sum(product, axis=1, keepdims=True), top)
    return top


def middle_kernel(edge_ref, slots_ref, operator_ref, own_ref, image_ref, got_near_ref, got_back_ref, *refs):
    *pair_refs, basis_ref, twice_ref, terms_ref, near_ref, back_ref = refs
    send_near(image_ref[...], edge_ref, near_ref, back_ref)
    coarse = terms_ref.shape[1] // 8
    loads = own_ref.shape[0] - coarse
    basis = own_ref[...]
    for half, got in enumerate((straight(got_back_ref, *pair_refs), handed(got_near_ref, got_back_ref.shape[0]))):
        basis = basis - split_dot(spread(got, loads, coarse // GROUP), slots_ref[half], NT)
    basis_ref[...] = basis
    image = image_ref[...]
    twice_ref[...] = split_dot(image, operator_ref[0], NT)
    left = jnp.concatenate([basis[:loads], image[:loads], basis[loads:]])
    empty = jnp.zeros((2 * coarse, basis.shape[1]), jnp.float32)
    both = products_of(left, jnp.concatenate([basis[loads:], image[loads:], empty]))
    strip = lax.broadcasted_iota(jnp.int32, (loads, 8 * coarse), 1) // coarse
    top = jnp.where(strip < 2, both[:loads], 0.0)
    top = jnp.where(strip == 4, both[loads : 2 * loads], top)
    residual = basis[:loads]
    terms_ref[:loads] = with_scalars(top, (residual * residual, residual * image[:loads]), SCALAR_LANES[:2])
    strip = lax.broadcasted_iota(jnp.int32, (coarse, 8 * coarse), 1) // coarse
    terms_ref[loads:] = jnp.where(strip < 2, both[2 * loads :], 0.0)


def second_half_kernel(slots_ref, placed_ref, image_ref, twice_ref, back_ref, *refs):
    *pair_refs, jump_ref, second_ref = refs
    got = straight(back_ref, *pair_refs)
    jump_ref[...] = image_ref[...] - split_dot(got, slots_ref[0], NT)
    second_ref[...] = twice_ref[...] - split_dot(got, placed_ref[0], NT)


def second_kernel(
    slots_ref, placed_ref, basis_ref, half_jump_ref, half_second_ref, early_ref, near_ref, jump_ref, terms_ref
):
    coarse = terms_ref.shape[1] // 8
    loads = basis_ref.shape[0] - coarse
    got = handed(near_ref, loads + coarse)
    jump = half_jump_ref[...] - split_dot(got, slots_ref[1], NT)
    second = half_second_ref[...] - split_dot(got, placed_ref[1], NT)
    jump_ref[...] = jump
    basis = basis_ref[...]
    left = jnp.concatenate([basis[:loads], jump[:loads], second[:loads], basis[loads:], jump[loads:]])
    empty = jnp.zeros((coarse, basis.shape[1]), jnp.float32)
    both = products_of(left, jnp.concatenate([basis[loads:], empty, jump[loads:], second[loads:]]))
    along, jumped, doubled = (both[at * loads : (at + 1) * loads] for at in range(3))
    base, far = both[3 * loads : 3 * loads + coarse], both[3 * loads + coarse :]
    strip = lax.broadcasted_iota(jnp.int32, (loads, 8 * coarse), 1) // coarse
    top = jnp.where(strip == 2, doubled, 0.0)
    top = jnp.where(strip == 3, along, top)
    top = jnp.where(strip == 5, pltpu.roll(doubled, coarse, 1), top)
    top = jnp.where(strip >= 6, jumped, top)
    residual, jump_loads, second_loads = basis[:loads], jump[:loads], second[:loads]
    products = (jump_loads * jump_loads, jump_loads * second_loads, residual * second_loads)
    terms_ref[:loads] = early_ref[:loads] + with_scalars(top, products, SCALAR_LANES[2:])
    strip = lax.broadcasted_iota(jnp.int32, (coarse, 8 * coarse), 1) // coarse
    base = jnp.where((strip == 2) | (strip == 3), base, 0.0)
    terms_ref[loads:] = early_ref[loads:] + jnp.where(strip < 4, base, far)


def eliminate(work, coarse):
    row = lax.broadcasted_iota(jnp.int32, work.shape, 0)
    for first in range(coarse):
        if first % 2 or first % GROUP >= MODES:
            continue
        second = first + 1
        left = jnp.broadcast_to(work[:, first : first + 1], work.shape)
        right = jnp.broadcast_to(work[:, second : second + 1], work.shape)
        upper, lower = work[first : first + 1], work[second : second + 1]
        pivot = 1.0 / left[first : first + 1]
        ratio = left[second : second + 1] * pivot
        corner = 1.0 / (right[second : second + 1] - ratio * right[first : first + 1])
        lower = (lower - ratio * upper) * corner
        upper = (upper - right[first : first + 1] * lower) * pivot
        work = work - left * upper - right * lower
        work = jnp.where(row == first, upper, jnp.where(row == second, lower, work))
    return work


def thin_dot(left, right):
    high, right_high = (value.astype(jnp.bfloat16).astype(jnp.float32) for value in (left, right))
    return jnp.dot(
        jnp.concatenate([high, left - high, high], axis=1).astype(jnp.bfloat16),
        jnp.concatenate([right_high, right_high, right - right_high], axis=0).astype(jnp.bfloat16),
        preferred_element_type=jnp.float32,
    )


def final_kernel(terms_ref, basis_ref, jump_ref, multipliers_ref, amplitudes_ref):
    coarse = terms_ref.shape[1] // 8
    loads = basis_ref.shape[0] - coarse
    groups = coarse // GROUP
    by_load = terms_ref[:loads].T
    used = lax.broadcasted_iota(jnp.int32, (coarse, loads), 0) % GROUP < MODES

    def strip(at):
        return by_load[at * coarse : (at + 1) * coarse]

    def block(at):
        return terms_ref[loads:, at * coarse : (at + 1) * coarse]

    def total(values):
        return jnp.sum(values, axis=0, keepdims=True)

    res_res, res_image, jump_jump, jump_second, res_second = (by_load[at : at + 1] for at in SCALAR_LANES)
    coarse_res, res_h = (jnp.where(used, strip(at), 0.0) for at in (0, 1))
    second_z, res_dz, image_g, second_g, jump_z, jump_dz = (strip(at) for at in range(2, 8))
    g_h, g_dz, z_z, z_dz = block(1), block(3), block(6), block(7)
    row = lax.broadcasted_iota(jnp.int32, (coarse, coarse), 0)
    unit = jnp.where(row == lax.broadcasted_iota(jnp.int32, (coarse, coarse), 1), 1.0, 0.0)
    empty = jnp.zeros((coarse, 5 * coarse - 2 * loads), jnp.float32)
    solved = eliminate(
        jnp.concatenate([terms_ref[loads:, : 2 * coarse], coarse_res, image_g, unit, empty], axis=1), coarse
    )
    inverse_h = solved[:, coarse : 2 * coarse]
    amounts = solved[:, 2 * coarse : 2 * coarse + loads]
    inverse_image = solved[:, 2 * coarse + loads : 2 * coarse + 2 * loads]
    inverse = solved[:, 2 * coarse + 2 * loads : 3 * coarse + 2 * loads]
    products = small_dot(jnp.concatenate([inverse_h, g_h, z_z, g_dz, z_dz], axis=0), amounts)
    inverse_h_amounts, h_amounts, z_amounts, g_dz_amounts, z_dz_amounts = (
        products[at * coarse : (at + 1) * coarse] for at in range(5)
    )
    shares = 2.0 * (inverse_image - inverse_h_amounts)
    both = jnp.concatenate([amounts, shares], axis=0).T
    basis_g, jump_z_rows = basis_ref[loads:], jump_ref[loads:]
    d = basis_ref[:loads] - thin_dot(both[:, :coarse], basis_g)
    u = jump_ref[:loads] - thin_dot(both, jnp.concatenate([jump_z_rows, basis_g], axis=0))
    products = small_dot(jnp.concatenate([g_h, z_z], axis=0), shares)
    image_d = image_g - h_amounts
    inner = res_res - total(amounts * coarse_res)
    curvature = 2.0 * (res_image - total(amounts * (res_h + image_d)))
    u_u = jump_jump - total(amounts * (2.0 * jump_z - z_amounts) + 2.0 * image_d * shares)
    second_u = second_g - g_dz_amounts - products[:coarse]
    jump_u = second_z - z_dz_amounts - 0.5 * products[coarse:]
    d_second = res_second - total(amounts * (res_dz + second_u) + shares * res_h)
    u_second = jump_second - total(amounts * (jump_dz + jump_u) + shares * (0.5 * jump_z + second_u))
    step = inner / curvature
    renewed = step * step * u_u - inner
    grown = 1.0 + renewed / inner
    curvature = grown * grown * curvature - grown * step * (2.0 * d_second + u_u) + 2.0 * step * step * u_second
    second_step = renewed / curvature
    on_d, on_u = step + second_step * grown, second_step * step
    amplitudes = amounts - on_d * shares + 2.0 * on_u * small_dot(inverse, second_u)
    amplitudes_ref[...] = jnp.concatenate(
        [amplitudes[label * GROUP : label * GROUP + MODES] for label in range(groups)], axis=0
    )
    weights = jnp.concatenate([on_d, on_u, jnp.zeros((6, loads), jnp.float32)], axis=0).T
    multipliers_ref[...] = weights[:, 0:1] * d - weights[:, 1:2] * u


def call(kernel, shapes, in_specs, name, scratch=(), flops=0):
    return pl.pallas_call(
        kernel,
        out_shape=[jax.ShapeDtypeStruct(*shape) for shape in shapes],
        in_specs=in_specs,
        out_specs=[VMEM] * len(shapes),
        scratch_shapes=scratch,
        compiler_params=pltpu.CompilerParams(vmem_limit_bytes=24 * 1024 * 1024),
        cost_estimate=pl.CostEstimate(flops=flops, bytes_accessed=2**20, transcendentals=0),
        name=name,
    )


def permute(values, offset, plane_offset=0):
    peers, planes = lax.axis_size("sub"), lax.axis_size("rep")
    offset = offset * planes + plane_offset
    return lax.ppermute(values, ("sub", "rep"), [(at, at ^ offset) for at in range(peers * planes)])


def to_chips(*pairs):
    return [permute(pair, 2 * (len(pairs) - at) + 1) for at, pair in enumerate(pairs)]


def to_core(near, *pairs):
    return permute(jnp.concatenate([near, *(pair[near.shape[0] :] for pair in pairs)], axis=0), 1)


def total(terms):
    chips = [(offset + 1, 0) for offset in range(2, lax.axis_size("sub"), 2)]
    planes = [(1, offset) for offset in range(1, lax.axis_size("rep"))]
    for offsets in ([(1, 0)], chips, planes):
        parts = [terms, *(permute(terms, *offset) for offset in offsets)]
        while len(parts) > 1:
            parts = [low + high for low, high in zip(parts[::2], parts[1::2])]
        terms = parts[0]
    return terms


def fused_body(dual_ops, mode_traces, route, mode_block, local_gap):
    peers = lax.axis_size("sub")
    loads, rows = local_gap.shape
    modes = mode_traces.shape[1]
    subs = mode_block.shape[0]
    groups = subs // AGG_SUBS
    per_peer = rows // peers
    height = loads + GROUP * groups
    f32, i32 = jnp.float32, jnp.int32
    tall = ((height, rows), f32)
    wide = ((height, 8 * GROUP * groups), f32)

    def pairs(height):
        return [((2 * height, per_peer), f32)] * (peers // 2 - 1)

    def singles(height):
        return [((height, per_peer), f32)] * 2

    def held(value):
        return pltpu.with_memory_space_constraint(value, pltpu.HBM)

    inputs = [route, mode_block.reshape(1, subs), local_gap, mode_traces.transpose(1, 0, 2), dual_ops]
    short = loads + GROUP
    far, values, operator, route, *send = call(
        place_kernel,
        [
            ((rows, rows - 2 * per_peer), jnp.bfloat16),
            ((short, rows), f32),
            (dual_ops.shape, dual_ops.dtype),
            (route.shape, i32),
            *pairs(short),
        ],
        [HBM] * 5,
        "place",
        [pltpu.VMEM((1, subs), i32), pltpu.VMEM((modes, 1, rows), f32), pltpu.SemaphoreType.DMA((5,))],
    )(*(held(value) for value in inputs))
    got = to_chips(*send)
    halves = ((2, rows, rows // 2), dual_ops.dtype)
    edge, slots, placed, own, own_image, near, back = call(
        ready_kernel,
        [((rows, 2 * per_peer), jnp.bfloat16), halves, halves, tall, tall, *singles(short)],
        [VMEM] * 4,
        "ready",
        flops=2 * rows * rows * (rows + 2 * height),
    )(route, far, values, operator)
    got_near = to_core(near, *got)
    half = call(first_half_kernel, [tall], [VMEM] * (3 + len(got)), "first_half", flops=2 * rows * rows * height)(
        placed, own_image, back, *got
    )[0]
    image, *send = call(first_kernel, [tall, *pairs(height)], [VMEM] * 4, "first")(far, placed, half, got_near)
    got_image = to_chips(*send)
    basis, twice, terms, image_near, image_back = call(
        middle_kernel,
        [tall, tall, wide, *singles(height)],
        [VMEM] * (7 + len(got)),
        "middle",
        flops=8 * rows * rows * height,
    )(edge, slots, operator, own, image, got_near, back, *got)
    image_near = to_core(image_near, *got_image)
    half_jump, half_second = call(
        second_half_kernel, [tall, tall], [VMEM] * (5 + len(got)), "second_half", flops=4 * rows * rows * height
    )(slots, placed, image, twice, image_back, *got_image)
    jump, terms = call(second_kernel, [tall, wide], [VMEM] * 7, "second")(
        slots, placed, basis, half_jump, half_second, terms, image_near
    )
    multipliers, amplitudes = call(
        final_kernel, [((loads, rows), f32), ((MODES * groups, loads), f32)], [VMEM] * 3, "final"
    )(total(terms), basis, jump)
    return multipliers, amplitudes.T


def general_body(dual_ops, mode_traces, route, mode_block, local_gap):
    own_index = lax.axis_index("sub")
    plane_index = lax.axis_index("rep")
    peer_count = lax.axis_size("sub")
    plane_count = lax.axis_size("rep")
    operator = dual_ops[0]
    traces = mode_traces[0]
    slot_rows = route[0]
    rows_here = operator.shape[0]
    load_cases = local_gap.shape[0]
    per_peer = rows_here // peer_count
    blocks = mode_block[:, 0]
    block_count = blocks.shape[0] // AGG_SUBS
    coarse = block_count * MODES
    positions = jnp.arange(rows_here, dtype=jnp.int32)
    inverse = jnp.zeros((rows_here,), jnp.int32).at[slot_rows].set(positions)
    slot_peer = positions // per_peer
    within = positions % per_peer
    flip_index = jnp.where(
        slot_peer == own_index, slot_peer * per_peer + per_peer - 1 - within, positions
    )
    peer_ids = jnp.arange(peer_count, dtype=jnp.int32)
    peer_blocks = blocks[peer_ids * plane_count + plane_index]
    own_block = blocks[own_index * plane_count + plane_index]
    labels = jnp.arange(block_count, dtype=jnp.int32)
    peer_onehot = (peer_blocks[:, None] == labels[None, :]).astype(jnp.float32)
    own_onehot = (labels == own_block).astype(jnp.float32)
    trace_slots = traces[:, slot_rows]
    receive_index = flip_index[inverse]

    def to_peers(values):
        return values[:, slot_rows]

    def from_peers(values):
        return values[:, inverse]

    gap_peers = to_peers(local_gap)
    got_traces = lax.all_to_all(trace_slots, "sub", split_axis=1, concat_axis=1, tiled=True)
    got_gap = lax.all_to_all(gap_peers, "sub", split_axis=1, concat_axis=1, tiled=True)
    partner_traces = got_traces[:, flip_index]
    residual = local_gap - got_gap[:, receive_index]
    own_gram = jnp.dot(traces, traces.T, precision=HIGHEST)
    paired = (trace_slots[:, None, :] * partner_traces[None, :, :]).reshape(
        MODES, MODES, peer_count, per_peer
    )
    cross_terms = jnp.sum(paired, axis=3)
    cross_blocks = jnp.einsum("klq,qb->kbl", cross_terms, peer_onehot, precision=HIGHEST)
    own_blocks = own_gram[:, None, :] * own_onehot[None, :, None]
    row_term = 2.0 * (own_blocks - cross_blocks).reshape(MODES, coarse)
    gram_term = (own_onehot[:, None, None] * row_term[None]).reshape(coarse, coarse)

    def coarse_term(values):
        own_part = 2.0 * jnp.dot(values, traces.T, precision=HIGHEST)
        return (own_part[:, None, :] * own_onehot[None, :, None]).reshape(load_cases, coarse)

    def expand(amounts):
        grouped = amounts.reshape(load_cases, block_count, MODES)
        own_amounts = lax.dynamic_index_in_dim(grouped, own_block, 1, keepdims=False)
        own_part = jnp.dot(own_amounts, traces, precision=HIGHEST)
        peer_amounts = jnp.einsum("qb,rbk->rkq", peer_onehot, grouped, precision=HIGHEST)
        spread = jnp.repeat(peer_amounts, per_peer, axis=2)
        peer_part = jnp.sum(spread * partner_traces[None, :, :], axis=1)
        return own_part - from_peers(peer_part)

    squares = jnp.sum(residual * residual, axis=1)
    gram_matrix, coarse_res, norm_res = lax.psum(
        (gram_term, coarse_term(residual), squares), ("sub", "rep")
    )
    factor = jnp.linalg.cholesky(gram_matrix)

    def solve_coarse(right):
        return jax.scipy.linalg.cho_solve((factor, True), right.T).T

    amplitudes = solve_coarse(coarse_res)
    projected = residual - expand(amplitudes)
    inner_sum = norm_res - jnp.sum(amplitudes * coarse_res, axis=1)
    direction = projected
    multipliers = jnp.zeros_like(residual)
    for iteration in range(ITERS):
        product = lax.dot_general(
            direction.astype(jnp.bfloat16),
            operator,
            (((1,), (1,)), ((), ())),
            preferred_element_type=jnp.float32,
        )
        got_product = lax.all_to_all(
            to_peers(product), "sub", split_axis=1, concat_axis=1, tiled=True
        )
        image_jump = product - got_product[:, receive_index]
        coarse_jump, jump_squares, residual_cross, curvature = lax.psum(
            (
                coarse_term(image_jump),
                jnp.sum(image_jump * image_jump, axis=1),
                jnp.sum(residual * image_jump, axis=1),
                jnp.sum(direction * image_jump, axis=1),
            ),
            ("sub", "rep"),
        )
        step_size = inner_sum / curvature
        multipliers = multipliers + step_size[:, None] * direction
        residual = residual - step_size[:, None] * image_jump
        coarse_res = coarse_res - step_size[:, None] * coarse_jump
        norm_res = (
            norm_res - 2.0 * step_size * residual_cross + step_size * step_size * jump_squares
        )
        amplitudes = solve_coarse(coarse_res)
        if iteration + 1 < ITERS:
            projected = residual - expand(amplitudes)
            renewed = norm_res - jnp.sum(amplitudes * coarse_res, axis=1)
            direction = projected + (renewed / inner_sum)[:, None] * direction
            inner_sum = renewed
    return (multipliers, amplitudes)


def fits(mesh, dual_ops, mode_block, local_gap):
    peers, planes = mesh.shape["sub"], mesh.shape["rep"]
    powers = all(size & (size - 1) == 0 for size in (peers, planes))
    whole = dual_ops.shape[1] % (128 * peers) == 0 and local_gap.shape[0] % 16 == 0
    return powers and whole and 8 * GROUP * (mode_block.shape[0] // AGG_SUBS) == 128


def solution(mesh):
    placed = (
        P(("sub", "rep"), None, None),
        P(("sub", "rep"), None, None),
        P(("sub", "rep"), None),
        P(),
        P(None, ("sub", "rep")),
    )

    def run(dual_ops, mode_traces, route, mode_block, local_gap):
        body = fused_body if fits(mesh, dual_ops, mode_block, local_gap) else general_body
        return jax.shard_map(
            body, mesh=mesh, in_specs=placed, out_specs=(P(None, ("sub", "rep")), P()), check_vma=False
        )(dual_ops, mode_traces, route, mode_block, local_gap)

    return run
```

```python
import jax
import jax.numpy as jnp
from jax import lax
from jax.experimental import pallas as pl
from jax.experimental.pallas import tpu as pltpu
from jax.sharding import PartitionSpec as P

MODES = 6
AGG_SUBS = 16
ITERS = 2
GROUP = 8
SCALAR_LANES = (MODES, MODES + 1, GROUP + MODES, GROUP + MODES + 1, 2 * GROUP + MODES)

HIGHEST = lax.Precision.HIGHEST
VMEM = pl.BlockSpec(memory_space=pltpu.VMEM)
HBM = pl.BlockSpec(memory_space=pltpu.HBM)
NN = (((1,), (0,)), ((), ()))
NT = (((1,), (1,)), ((), ()))


def split(values):
    high = values.astype(jnp.bfloat16).astype(jnp.float32)
    return jnp.concatenate([high, values - high], axis=0).astype(jnp.bfloat16)


def split_dot(values, matrix, dims):
    rows = values.shape[0]
    both = lax.dot_general(split(values), matrix, dims, preferred_element_type=jnp.float32)
    return both[:rows] + both[rows:]


def small_dot(left, right):
    return jnp.dot(left, right, precision=HIGHEST, preferred_element_type=jnp.float32)


def send_far(values, far_ref, *pair_refs):
    height = values.shape[0]
    per_peer = pair_refs[0].shape[1]
    slots = split_dot(values, far_ref[...], NN)
    for at, ref in enumerate(reversed(pair_refs)):
        start = 2 * at * per_peer
        ref[:height] = slots[:, start + per_peer : start + 2 * per_peer]
        ref[height:] = slots[:, start : start + per_peer]


def send_near(values, edge_ref, near_ref, back_ref, stay_ref):
    per_peer = back_ref.shape[1]
    slots = split_dot(values, edge_ref[...], NN)
    for at, ref in enumerate((near_ref, back_ref, stay_ref)):
        ref[...] = slots[:, at * per_peer : (at + 1) * per_peer]


def straight(last_ref, pair_refs):
    height = last_ref.shape[0]
    return jnp.concatenate([*(ref[:height] for ref in pair_refs), last_ref[...]], axis=1)


def for_other(near_ref, pair_refs):
    height = near_ref.shape[0]
    return jnp.concatenate([near_ref[...], *(ref[height:] for ref in pair_refs)], axis=1)


def handed(got_ref, height):
    return jnp.concatenate([got_ref[at : at + height] for at in range(0, got_ref.shape[0], height)], axis=1)


def spread(values, loads, groups):
    modes = values[loads:]
    label = modes[MODES : MODES + 1]
    used = lax.broadcasted_iota(jnp.int32, modes.shape, 0) < MODES
    parts = [jnp.where(used & (label == group), modes, 0.0) for group in range(groups)]
    return jnp.concatenate([values[:loads], *parts], axis=0)


def one_hot(route_ref, peer, per_peer):
    start = pl.multiple_of(peer * per_peer, per_peer)
    row_ids = lax.broadcasted_iota(jnp.int32, (route_ref.shape[1], per_peer), 0)
    return jnp.where(row_ids == route_ref[:, pl.ds(start, per_peer)], 1.0, 0.0).astype(jnp.bfloat16)


def place_kernel(
    route_hbm, block_hbm, gap_hbm, traces_hbm, operator_hbm,
    far_ref, values_ref, operator_ref, route_ref, *refs,
):
    *pair_refs, block_ref, traces_ref, sems = refs
    loads, rows = gap_hbm.shape
    per_peer = pair_refs[0].shape[1]
    peers = rows // per_peer
    copies = [
        pltpu.make_async_copy(source, target, sems.at[at])
        for at, (source, target) in enumerate(
            (
                (route_hbm, route_ref),
                (block_hbm, block_ref),
                (traces_hbm, traces_ref),
                (gap_hbm, values_ref.at[pl.ds(0, loads)]),
                (operator_hbm, operator_ref),
            )
        )
    ]
    for copy in copies:
        copy.start()
    own_index = lax.axis_index("sub")
    device = own_index * lax.axis_size("rep") + lax.axis_index("rep")
    copies[0].wait()
    for offset in range(2, peers):
        at = (offset - 2) * per_peer
        far_ref[:, at : at + per_peer] = one_hot(route_ref, own_index ^ offset, per_peer)
    copies[1].wait()
    copies[2].wait()
    blocks = block_ref[...]
    lane = lax.broadcasted_iota(jnp.int32, blocks.shape, 1)
    own_block = jnp.sum(jnp.where(lane == device, blocks, 0), axis=1, keepdims=True)
    modes = traces_ref.shape[0]
    label = jnp.broadcast_to(own_block.astype(jnp.float32), (1, rows))
    for mode in range(modes):
        values_ref[loads + mode : loads + mode + 1] = traces_ref[mode]
    values_ref[loads + modes : loads + modes + 1] = label
    values_ref[loads + modes + 1 :] = jnp.zeros((GROUP - modes - 1, rows), jnp.float32)
    copies[3].wait()
    send_far(values_ref[...], far_ref, *pair_refs)
    copies[4].wait()


def ready_kernel(
    route_ref, far_ref, values_ref, operator_ref,
    edge_ref, slots_ref, placed_ref, near_ref, back_ref, stay_ref,
):
    per_peer = back_ref.shape[1]
    peers = far_ref.shape[1] // per_peer + 2
    own_index = lax.axis_index("sub")
    low = lax.broadcasted_iota(jnp.int32, (per_peer, per_peer), 0)
    high = lax.broadcasted_iota(jnp.int32, (per_peer, per_peer), 1)
    reverse = jnp.where(low + high == per_peer - 1, 1.0, 0.0).astype(jnp.bfloat16)
    own_columns = one_hot(route_ref, own_index, per_peer)
    near_columns = one_hot(route_ref, own_index ^ 1, per_peer)
    reversed_columns = jnp.dot(own_columns, reverse, preferred_element_type=jnp.float32).astype(jnp.bfloat16)
    edge_ref[...] = jnp.concatenate([near_columns, reversed_columns, own_columns], axis=1)
    for at in range(peers // 2 - 1):
        start = (peers - 4 - 2 * at) * per_peer
        slots_ref[0, :, at * per_peer : (at + 1) * per_peer] = far_ref[:, start + per_peer : start + 2 * per_peer]
        slots_ref[1, :, (at + 1) * per_peer : (at + 2) * per_peer] = far_ref[:, start : start + per_peer]
    slots_ref[0, :, (peers // 2 - 1) * per_peer :] = own_columns
    slots_ref[1, :, :per_peer] = near_columns
    send_near(values_ref[...], edge_ref, near_ref, back_ref, stay_ref)
    operator = operator_ref[0]
    for half in range(2):
        placed_ref[half] = jnp.dot(
            operator, slots_ref[half], preferred_element_type=jnp.float32
        ).astype(operator.dtype)


def first_half_kernel(placed_ref, stay_ref, back_ref, *refs):
    *pair_refs, jump_ref, image_ref = refs
    sent_refs, got_refs = pair_refs[: len(pair_refs) // 2], pair_refs[len(pair_refs) // 2 :]
    loads = stay_ref.shape[0] - GROUP
    groups = (jump_ref.shape[0] - loads) // GROUP
    own, got = (spread(straight(*refs), loads, groups) for refs in ((stay_ref, sent_refs), (back_ref, got_refs)))
    jump_ref[...] = own - got
    image_ref[...] = split_dot(own - got, placed_ref[0], NT)


def first_kernel(far_ref, placed_ref, half_ref, got_ref, near_ref, *refs):
    sent_refs, (jump_ref, image_ref, *pair_refs) = refs[: len(refs) // 2 - 1], refs[len(refs) // 2 - 1 :]
    height = near_ref.shape[0]
    loads = height - GROUP
    groups = (image_ref.shape[0] - loads) // GROUP
    own, got = (spread(value, loads, groups) for value in (for_other(near_ref, sent_refs), handed(got_ref, height)))
    jump_ref[...] = own - got
    image = half_ref[...] + split_dot(own - got, placed_ref[1], NT)
    image_ref[...] = image
    send_far(image, far_ref, *pair_refs)


def products_of(left, right):
    both = lax.dot_general(split(left), split(right), NT, preferred_element_type=jnp.float32)
    both = both[: left.shape[0]] + both[left.shape[0] :]
    return both + pltpu.roll(both, right.shape[0], 1)


def with_scalars(top, products, lanes):
    lane = lax.broadcasted_iota(jnp.int32, top.shape, 1)
    for at, product in zip(lanes, products):
        top = jnp.where(lane == at, jnp.sum(product, axis=1, keepdims=True), top)
    return top


def middle_kernel(
    edge_ref, slots_ref, straight_ref, handed_ref, image_ref, basis_ref, terms_ref, near_ref, back_ref, stay_ref
):
    image = image_ref[...]
    send_near(image, edge_ref, near_ref, back_ref, stay_ref)
    coarse = terms_ref.shape[1] // 8
    loads = image.shape[0] - coarse
    basis = split_dot(straight_ref[...], slots_ref[0], NT) + split_dot(handed_ref[...], slots_ref[1], NT)
    basis_ref[...] = basis
    left = jnp.concatenate([basis[:loads], image[:loads], basis[loads:]])
    empty = jnp.zeros((2 * coarse, basis.shape[1]), jnp.float32)
    both = products_of(left, jnp.concatenate([basis[loads:], image[loads:], empty]))
    strip = lax.broadcasted_iota(jnp.int32, (loads, 8 * coarse), 1) // coarse
    top = jnp.where(strip < 2, both[:loads], 0.0)
    top = jnp.where(strip == 4, both[loads : 2 * loads], top)
    residual = basis[:loads]
    terms_ref[:loads] = with_scalars(top, (residual * residual, residual * image[:loads]), SCALAR_LANES[:2])
    strip = lax.broadcasted_iota(jnp.int32, (coarse, 8 * coarse), 1) // coarse
    terms_ref[loads:] = jnp.where(strip < 2, both[2 * loads :], 0.0)


def second_half_kernel(slots_ref, placed_ref, stay_ref, back_ref, *refs):
    *pair_refs, jump_ref, second_ref = refs
    sent_refs, got_refs = pair_refs[: len(pair_refs) // 2], pair_refs[len(pair_refs) // 2 :]
    jump = straight(stay_ref, sent_refs) - straight(back_ref, got_refs)
    jump_ref[...] = split_dot(jump, slots_ref[0], NT)
    second_ref[...] = split_dot(jump, placed_ref[0], NT)


def second_kernel(slots_ref, placed_ref, basis_ref, half_jump_ref, half_second_ref, early_ref, got_ref, near_ref, *refs):
    *sent_refs, jump_ref, terms_ref = refs
    coarse = terms_ref.shape[1] // 8
    loads = basis_ref.shape[0] - coarse
    jump = for_other(near_ref, sent_refs) - handed(got_ref, loads + coarse)
    second = half_second_ref[...] + split_dot(jump, placed_ref[1], NT)
    jump = half_jump_ref[...] + split_dot(jump, slots_ref[1], NT)
    jump_ref[...] = jump
    basis = basis_ref[...]
    left = jnp.concatenate([basis[:loads], jump[:loads], second[:loads], basis[loads:], jump[loads:]])
    empty = jnp.zeros((coarse, basis.shape[1]), jnp.float32)
    both = products_of(left, jnp.concatenate([basis[loads:], empty, jump[loads:], second[loads:]]))
    along, jumped, doubled = (both[at * loads : (at + 1) * loads] for at in range(3))
    base, far = both[3 * loads : 3 * loads + coarse], both[3 * loads + coarse :]
    strip = lax.broadcasted_iota(jnp.int32, (loads, 8 * coarse), 1) // coarse
    top = jnp.where(strip == 2, doubled, 0.0)
    top = jnp.where(strip == 3, along, top)
    top = jnp.where(strip == 5, pltpu.roll(doubled, coarse, 1), top)
    top = jnp.where(strip >= 6, jumped, top)
    residual, jump_loads, second_loads = basis[:loads], jump[:loads], second[:loads]
    products = (jump_loads * jump_loads, jump_loads * second_loads, residual * second_loads)
    terms_ref[:loads] = early_ref[:loads] + with_scalars(top, products, SCALAR_LANES[2:])
    strip = lax.broadcasted_iota(jnp.int32, (coarse, 8 * coarse), 1) // coarse
    base = jnp.where((strip == 2) | (strip == 3), base, 0.0)
    terms_ref[loads:] = early_ref[loads:] + jnp.where(strip < 4, base, far)


def eliminate(work, coarse):
    row = lax.broadcasted_iota(jnp.int32, work.shape, 0)
    for first in range(coarse):
        if first % 2 or first % GROUP >= MODES:
            continue
        second = first + 1
        left = jnp.broadcast_to(work[:, first : first + 1], work.shape)
        right = jnp.broadcast_to(work[:, second : second + 1], work.shape)
        upper, lower = work[first : first + 1], work[second : second + 1]
        pivot = 1.0 / left[first : first + 1]
        ratio = left[second : second + 1] * pivot
        corner = 1.0 / (right[second : second + 1] - ratio * right[first : first + 1])
        lower = (lower - ratio * upper) * corner
        upper = (upper - right[first : first + 1] * lower) * pivot
        work = work - left * upper - right * lower
        work = jnp.where(row == first, upper, jnp.where(row == second, lower, work))
    return work


def thin_dot(left, right):
    high, right_high = (value.astype(jnp.bfloat16).astype(jnp.float32) for value in (left, right))
    return jnp.dot(
        jnp.concatenate([high, left - high, high], axis=1).astype(jnp.bfloat16),
        jnp.concatenate([right_high, right_high, right - right_high], axis=0).astype(jnp.bfloat16),
        preferred_element_type=jnp.float32,
    )


def final_kernel(terms_ref, basis_ref, jump_ref, multipliers_ref, amplitudes_ref):
    coarse = terms_ref.shape[1] // 8
    loads = basis_ref.shape[0] - coarse
    groups = coarse // GROUP
    by_load = terms_ref[:loads].T
    used = lax.broadcasted_iota(jnp.int32, (coarse, loads), 0) % GROUP < MODES

    def strip(at):
        return by_load[at * coarse : (at + 1) * coarse]

    def block(at):
        return terms_ref[loads:, at * coarse : (at + 1) * coarse]

    def total(values):
        return jnp.sum(values, axis=0, keepdims=True)

    res_res, res_image, jump_jump, jump_second, res_second = (by_load[at : at + 1] for at in SCALAR_LANES)
    coarse_res, res_h = (jnp.where(used, strip(at), 0.0) for at in (0, 1))
    second_z, res_dz, image_g, second_g, jump_z, jump_dz = (strip(at) for at in range(2, 8))
    g_h, g_dz, z_z, z_dz = block(1), block(3), block(6), block(7)
    row = lax.broadcasted_iota(jnp.int32, (coarse, coarse), 0)
    unit = jnp.where(row == lax.broadcasted_iota(jnp.int32, (coarse, coarse), 1), 1.0, 0.0)
    empty = jnp.zeros((coarse, 5 * coarse - 2 * loads), jnp.float32)
    solved = eliminate(
        jnp.concatenate([terms_ref[loads:, : 2 * coarse], coarse_res, image_g, unit, empty], axis=1), coarse
    )
    inverse_h = solved[:, coarse : 2 * coarse]
    amounts = solved[:, 2 * coarse : 2 * coarse + loads]
    inverse_image = solved[:, 2 * coarse + loads : 2 * coarse + 2 * loads]
    inverse = solved[:, 2 * coarse + 2 * loads : 3 * coarse + 2 * loads]
    products = small_dot(jnp.concatenate([inverse_h, g_h, z_z, g_dz, z_dz], axis=0), amounts)
    inverse_h_amounts, h_amounts, z_amounts, g_dz_amounts, z_dz_amounts = (
        products[at * coarse : (at + 1) * coarse] for at in range(5)
    )
    shares = 2.0 * (inverse_image - inverse_h_amounts)
    both = jnp.concatenate([amounts, shares], axis=0).T
    basis_g, jump_z_rows = basis_ref[loads:], jump_ref[loads:]
    d = basis_ref[:loads] - thin_dot(both[:, :coarse], basis_g)
    u = jump_ref[:loads] - thin_dot(both, jnp.concatenate([jump_z_rows, basis_g], axis=0))
    products = small_dot(jnp.concatenate([g_h, z_z], axis=0), shares)
    image_d = image_g - h_amounts
    inner = res_res - total(amounts * coarse_res)
    curvature = 2.0 * (res_image - total(amounts * (res_h + image_d)))
    u_u = jump_jump - total(amounts * (2.0 * jump_z - z_amounts) + 2.0 * image_d * shares)
    second_u = second_g - g_dz_amounts - products[:coarse]
    jump_u = second_z - z_dz_amounts - 0.5 * products[coarse:]
    d_second = res_second - total(amounts * (res_dz + second_u) + shares * res_h)
    u_second = jump_second - total(amounts * (jump_dz + jump_u) + shares * (0.5 * jump_z + second_u))
    step = inner / curvature
    renewed = step * step * u_u - inner
    grown = 1.0 + renewed / inner
    curvature = grown * grown * curvature - grown * step * (2.0 * d_second + u_u) + 2.0 * step * step * u_second
    second_step = renewed / curvature
    on_d, on_u = step + second_step * grown, second_step * step
    amplitudes = amounts - on_d * shares + 2.0 * on_u * small_dot(inverse, second_u)
    amplitudes_ref[...] = jnp.concatenate(
        [amplitudes[label * GROUP : label * GROUP + MODES] for label in range(groups)], axis=0
    )
    weights = jnp.concatenate([on_d, on_u, jnp.zeros((6, loads), jnp.float32)], axis=0).T
    multipliers_ref[...] = weights[:, 0:1] * d - weights[:, 1:2] * u


def call(kernel, shapes, in_specs, name, scratch=(), flops=0):
    return pl.pallas_call(
        kernel,
        out_shape=[jax.ShapeDtypeStruct(*shape) for shape in shapes],
        in_specs=in_specs,
        out_specs=[VMEM] * len(shapes),
        scratch_shapes=scratch,
        compiler_params=pltpu.CompilerParams(vmem_limit_bytes=24 * 1024 * 1024),
        cost_estimate=pl.CostEstimate(flops=flops, bytes_accessed=2**20, transcendentals=0),
        name=name,
    )


def permute(values, offset, plane_offset=0):
    peers, planes = lax.axis_size("sub"), lax.axis_size("rep")
    offset = offset * planes + plane_offset
    return lax.ppermute(values, ("sub", "rep"), [(at, at ^ offset) for at in range(peers * planes)])


def to_chips(*pairs):
    return [permute(pair, 2 * (len(pairs) - at) + 1) for at, pair in enumerate(pairs)]


def to_core(near, *pairs):
    return permute(jnp.concatenate([near, *(pair[near.shape[0] :] for pair in pairs)], axis=0), 1)


def total(terms):
    chips = [(offset + 1, 0) for offset in range(2, lax.axis_size("sub"), 2)]
    planes = [(1, offset) for offset in range(1, lax.axis_size("rep"))]
    for offsets in ([(1, 0)], chips, planes):
        parts = [terms, *(permute(terms, *offset) for offset in offsets)]
        while len(parts) > 1:
            parts = [low + high for low, high in zip(parts[::2], parts[1::2])]
        terms = parts[0]
    return terms


def fused_body(dual_ops, mode_traces, route, mode_block, local_gap):
    peers = lax.axis_size("sub")
    loads, rows = local_gap.shape
    modes = mode_traces.shape[1]
    subs = mode_block.shape[0]
    groups = subs // AGG_SUBS
    per_peer = rows // peers
    height = loads + GROUP * groups
    f32, i32 = jnp.float32, jnp.int32
    tall = ((height, rows), f32)
    wide = ((height, 8 * GROUP * groups), f32)

    def pairs(height):
        return [((2 * height, per_peer), f32)] * (peers // 2 - 1)

    def singles(height):
        return [((height, per_peer), f32)] * 3

    def held(value):
        return pltpu.with_memory_space_constraint(value, pltpu.HBM)

    inputs = [route, mode_block.reshape(1, subs), local_gap, mode_traces.transpose(1, 0, 2), dual_ops]
    short = loads + GROUP
    far, values, operator, route, *send = call(
        place_kernel,
        [
            ((rows, rows - 2 * per_peer), jnp.bfloat16),
            ((short, rows), f32),
            (dual_ops.shape, dual_ops.dtype),
            (route.shape, i32),
            *pairs(short),
        ],
        [HBM] * 5,
        "place",
        [pltpu.VMEM((1, subs), i32), pltpu.VMEM((modes, 1, rows), f32), pltpu.SemaphoreType.DMA((5,))],
    )(*(held(value) for value in inputs))
    got = to_chips(*send)
    halves = ((2, rows, rows // 2), dual_ops.dtype)
    edge, slots, placed, near, back, stay = call(
        ready_kernel,
        [((rows, 3 * per_peer), jnp.bfloat16), halves, halves, *singles(short)],
        [VMEM] * 4,
        "ready",
        flops=2 * rows * rows * rows,
    )(route, far, values, operator)
    got_near = to_core(near, *got)
    half = ((height, rows // 2), f32)
    straight_jump, half_image = call(
        first_half_kernel, [half, tall], [VMEM] * (3 + 2 * len(got)), "first_half", flops=2 * rows * rows * height
    )(placed, stay, back, *send, *got)
    handed_jump, image, *image_send = call(
        first_kernel, [half, tall, *pairs(height)], [VMEM] * (5 + len(send)), "first"
    )(far, placed, half_image, got_near, near, *send)
    got = to_chips(*image_send)
    basis, terms, near, back, stay = call(
        middle_kernel, [tall, wide, *singles(height)], [VMEM] * 5, "middle", flops=4 * rows * rows * height
    )(edge, slots, straight_jump, handed_jump, image)
    got_near = to_core(near, *got)
    half_jump, half_second = call(
        second_half_kernel, [tall, tall], [VMEM] * (4 + 2 * len(got)), "second_half", flops=4 * rows * rows * height
    )(slots, placed, stay, back, *image_send, *got)
    jump, terms = call(second_kernel, [tall, wide], [VMEM] * (8 + len(got)), "second")(
        slots, placed, basis, half_jump, half_second, terms, got_near, near, *image_send
    )
    multipliers, amplitudes = call(
        final_kernel, [((loads, rows), f32), ((MODES * groups, loads), f32)], [VMEM] * 3, "final"
    )(total(terms), basis, jump)
    return multipliers, amplitudes.T


def general_body(dual_ops, mode_traces, route, mode_block, local_gap):
    own_index = lax.axis_index("sub")
    plane_index = lax.axis_index("rep")
    peer_count = lax.axis_size("sub")
    plane_count = lax.axis_size("rep")
    operator = dual_ops[0]
    traces = mode_traces[0]
    slot_rows = route[0]
    rows_here = operator.shape[0]
    load_cases = local_gap.shape[0]
    per_peer = rows_here // peer_count
    blocks = mode_block[:, 0]
    block_count = blocks.shape[0] // AGG_SUBS
    coarse = block_count * MODES
    positions = jnp.arange(rows_here, dtype=jnp.int32)
    inverse = jnp.zeros((rows_here,), jnp.int32).at[slot_rows].set(positions)
    slot_peer = positions // per_peer
    within = positions % per_peer
    flip_index = jnp.where(
        slot_peer == own_index, slot_peer * per_peer + per_peer - 1 - within, positions
    )
    peer_ids = jnp.arange(peer_count, dtype=jnp.int32)
    peer_blocks = blocks[peer_ids * plane_count + plane_index]
    own_block = blocks[own_index * plane_count + plane_index]
    labels = jnp.arange(block_count, dtype=jnp.int32)
    peer_onehot = (peer_blocks[:, None] == labels[None, :]).astype(jnp.float32)
    own_onehot = (labels == own_block).astype(jnp.float32)
    trace_slots = traces[:, slot_rows]
    receive_index = flip_index[inverse]

    def to_peers(values):
        return values[:, slot_rows]

    def from_peers(values):
        return values[:, inverse]

    gap_peers = to_peers(local_gap)
    got_traces = lax.all_to_all(trace_slots, "sub", split_axis=1, concat_axis=1, tiled=True)
    got_gap = lax.all_to_all(gap_peers, "sub", split_axis=1, concat_axis=1, tiled=True)
    partner_traces = got_traces[:, flip_index]
    residual = local_gap - got_gap[:, receive_index]
    own_gram = jnp.dot(traces, traces.T, precision=HIGHEST)
    paired = (trace_slots[:, None, :] * partner_traces[None, :, :]).reshape(
        MODES, MODES, peer_count, per_peer
    )
    cross_terms = jnp.sum(paired, axis=3)
    cross_blocks = jnp.einsum("klq,qb->kbl", cross_terms, peer_onehot, precision=HIGHEST)
    own_blocks = own_gram[:, None, :] * own_onehot[None, :, None]
    row_term = 2.0 * (own_blocks - cross_blocks).reshape(MODES, coarse)
    gram_term = (own_onehot[:, None, None] * row_term[None]).reshape(coarse, coarse)

    def coarse_term(values):
        own_part = 2.0 * jnp.dot(values, traces.T, precision=HIGHEST)
        return (own_part[:, None, :] * own_onehot[None, :, None]).reshape(load_cases, coarse)

    def expand(amounts):
        grouped = amounts.reshape(load_cases, block_count, MODES)
        own_amounts = lax.dynamic_index_in_dim(grouped, own_block, 1, keepdims=False)
        own_part = jnp.dot(own_amounts, traces, precision=HIGHEST)
        peer_amounts = jnp.einsum("qb,rbk->rkq", peer_onehot, grouped, precision=HIGHEST)
        spread = jnp.repeat(peer_amounts, per_peer, axis=2)
        peer_part = jnp.sum(spread * partner_traces[None, :, :], axis=1)
        return own_part - from_peers(peer_part)

    squares = jnp.sum(residual * residual, axis=1)
    gram_matrix, coarse_res, norm_res = lax.psum(
        (gram_term, coarse_term(residual), squares), ("sub", "rep")
    )
    factor = jnp.linalg.cholesky(gram_matrix)

    def solve_coarse(right):
        return jax.scipy.linalg.cho_solve((factor, True), right.T).T

    amplitudes = solve_coarse(coarse_res)
    projected = residual - expand(amplitudes)
    inner_sum = norm_res - jnp.sum(amplitudes * coarse_res, axis=1)
    direction = projected
    multipliers = jnp.zeros_like(residual)
    for iteration in range(ITERS):
        product = lax.dot_general(
            direction.astype(jnp.bfloat16),
            operator,
            (((1,), (1,)), ((), ())),
            preferred_element_type=jnp.float32,
        )
        got_product = lax.all_to_all(
            to_peers(product), "sub", split_axis=1, concat_axis=1, tiled=True
        )
        image_jump = product - got_product[:, receive_index]
        coarse_jump, jump_squares, residual_cross, curvature = lax.psum(
            (
                coarse_term(image_jump),
                jnp.sum(image_jump * image_jump, axis=1),
                jnp.sum(residual * image_jump, axis=1),
                jnp.sum(direction * image_jump, axis=1),
            ),
            ("sub", "rep"),
        )
        step_size = inner_sum / curvature
        multipliers = multipliers + step_size[:, None] * direction
        residual = residual - step_size[:, None] * image_jump
        coarse_res = coarse_res - step_size[:, None] * coarse_jump
        norm_res = (
            norm_res - 2.0 * step_size * residual_cross + step_size * step_size * jump_squares
        )
        amplitudes = solve_coarse(coarse_res)
        if iteration + 1 < ITERS:
            projected = residual - expand(amplitudes)
            renewed = norm_res - jnp.sum(amplitudes * coarse_res, axis=1)
            direction = projected + (renewed / inner_sum)[:, None] * direction
            inner_sum = renewed
    return (multipliers, amplitudes)


def fits(mesh, dual_ops, mode_block, local_gap):
    peers, planes = mesh.shape["sub"], mesh.shape["rep"]
    powers = all(size & (size - 1) == 0 for size in (peers, planes))
    whole = dual_ops.shape[1] % (128 * peers) == 0 and local_gap.shape[0] % 16 == 0
    return powers and whole and 8 * GROUP * (mode_block.shape[0] // AGG_SUBS) == 128


def solution(mesh):
    placed = (
        P(("sub", "rep"), None, None),
        P(("sub", "rep"), None, None),
        P(("sub", "rep"), None),
        P(),
        P(None, ("sub", "rep")),
    )

    def run(dual_ops, mode_traces, route, mode_block, local_gap):
        body = fused_body if fits(mesh, dual_ops, mode_block, local_gap) else general_body
        return jax.shard_map(
            body, mesh=mesh, in_specs=placed, out_specs=(P(None, ("sub", "rep")), P()), check_vma=False
        )(dual_ops, mode_traces, route, mode_block, local_gap)

    return run
```

```python
import functools

import jax
import jax.numpy as jnp
from jax import lax
from jax.experimental import pallas as pl
from jax.experimental.pallas import tpu as pltpu
from jax.sharding import PartitionSpec as P

MODES = 6
AGG_SUBS = 16
ITERS = 2
GROUP = 8
SCALAR_LANES = (MODES, MODES + 1, GROUP + MODES, GROUP + MODES + 1, 2 * GROUP + MODES)

HIGHEST = lax.Precision.HIGHEST
VMEM = pl.BlockSpec(memory_space=pltpu.VMEM)
HBM = pl.BlockSpec(memory_space=pltpu.HBM)
NN = (((1,), (0,)), ((), ()))
NT = (((1,), (1,)), ((), ()))


def split(values):
    high = values.astype(jnp.bfloat16).astype(jnp.float32)
    return jnp.concatenate([high, values - high], axis=0).astype(jnp.bfloat16)


def split_dot(values, matrix, dims):
    rows = values.shape[0]
    both = lax.dot_general(split(values), matrix, dims, preferred_element_type=jnp.float32)
    return both[:rows] + both[rows:]


def small_dot(left, right):
    return jnp.dot(left, right, precision=HIGHEST, preferred_element_type=jnp.float32)


def send_far(values, far_ref, *pair_refs):
    height = values.shape[0]
    per_peer = pair_refs[0].shape[1]
    slots = split_dot(values, far_ref[...], NN)
    for at, ref in enumerate(reversed(pair_refs)):
        start = 2 * at * per_peer
        ref[:height] = slots[:, start + per_peer : start + 2 * per_peer]
        ref[height:] = slots[:, start : start + per_peer]


def send_near(values, edge_ref, near_ref, back_ref, stay_ref):
    per_peer = back_ref.shape[1]
    slots = split_dot(values, edge_ref[...], NN)
    for at, ref in enumerate((near_ref, back_ref, stay_ref)):
        ref[...] = slots[:, at * per_peer : (at + 1) * per_peer]


def straight(last_ref, pair_refs):
    height = last_ref.shape[0]
    return jnp.concatenate([*(ref[:height] for ref in pair_refs), last_ref[...]], axis=1)


def for_other(near_ref, pair_refs):
    height = near_ref.shape[0]
    return jnp.concatenate([near_ref[...], *(ref[height:] for ref in pair_refs)], axis=1)


def handed(got_ref, height):
    return jnp.concatenate([got_ref[at : at + height] for at in range(0, got_ref.shape[0], height)], axis=1)


def spread(values, loads, groups):
    modes = values[loads:]
    label = modes[MODES : MODES + 1]
    used = lax.broadcasted_iota(jnp.int32, modes.shape, 0) < MODES
    parts = [jnp.where(used & (label == group), modes, 0.0) for group in range(groups)]
    return jnp.concatenate([values[:loads], *parts], axis=0)


def one_hot(route_ref, peer, per_peer):
    start = pl.multiple_of(peer * per_peer, per_peer)
    row_ids = lax.broadcasted_iota(jnp.int32, (route_ref.shape[1], per_peer), 0)
    return jnp.where(row_ids == route_ref[:, pl.ds(start, per_peer)], 1.0, 0.0).astype(jnp.bfloat16)


def place_kernel(
    route_hbm, block_hbm, gap_hbm, traces_hbm, operator_hbm,
    far_ref, values_ref, operator_ref, route_ref, *refs,
):
    *pair_refs, block_ref, traces_ref, sems = refs
    loads, rows = gap_hbm.shape
    per_peer = pair_refs[0].shape[1]
    peers = rows // per_peer
    copies = [
        pltpu.make_async_copy(source, target, sems.at[at])
        for at, (source, target) in enumerate(
            (
                (route_hbm, route_ref),
                (block_hbm, block_ref),
                (traces_hbm, traces_ref),
                (gap_hbm, values_ref.at[pl.ds(0, loads)]),
                (operator_hbm, operator_ref),
            )
        )
    ]
    for copy in copies:
        copy.start()
    own_index = lax.axis_index("sub")
    device = own_index * lax.axis_size("rep") + lax.axis_index("rep")
    copies[0].wait()
    for offset in range(2, peers):
        at = (offset - 2) * per_peer
        far_ref[:, at : at + per_peer] = one_hot(route_ref, own_index ^ offset, per_peer)
    copies[1].wait()
    copies[2].wait()
    blocks = block_ref[...]
    lane = lax.broadcasted_iota(jnp.int32, blocks.shape, 1)
    own_block = jnp.sum(jnp.where(lane == device, blocks, 0), axis=1, keepdims=True)
    modes = traces_ref.shape[0]
    label = jnp.broadcast_to(own_block.astype(jnp.float32), (1, rows))
    for mode in range(modes):
        values_ref[loads + mode : loads + mode + 1] = traces_ref[mode]
    values_ref[loads + modes : loads + modes + 1] = label
    values_ref[loads + modes + 1 :] = jnp.zeros((GROUP - modes - 1, rows), jnp.float32)
    copies[3].wait()
    send_far(values_ref[...], far_ref, *pair_refs)
    copies[4].wait()


def ready_kernel(
    route_ref, far_ref, values_ref, operator_ref,
    edge_ref, slots_ref, placed_ref, near_ref, back_ref, stay_ref,
):
    per_peer = back_ref.shape[1]
    peers = far_ref.shape[1] // per_peer + 2
    own_index = lax.axis_index("sub")
    low = lax.broadcasted_iota(jnp.int32, (per_peer, per_peer), 0)
    high = lax.broadcasted_iota(jnp.int32, (per_peer, per_peer), 1)
    reverse = jnp.where(low + high == per_peer - 1, 1.0, 0.0).astype(jnp.bfloat16)
    own_columns = one_hot(route_ref, own_index, per_peer)
    near_columns = one_hot(route_ref, own_index ^ 1, per_peer)
    reversed_columns = jnp.dot(own_columns, reverse, preferred_element_type=jnp.float32).astype(jnp.bfloat16)
    edge_ref[...] = jnp.concatenate([near_columns, reversed_columns, own_columns], axis=1)
    for at in range(peers // 2 - 1):
        start = (peers - 4 - 2 * at) * per_peer
        slots_ref[0, :, at * per_peer : (at + 1) * per_peer] = far_ref[:, start + per_peer : start + 2 * per_peer]
        slots_ref[1, :, (at + 1) * per_peer : (at + 2) * per_peer] = far_ref[:, start : start + per_peer]
    slots_ref[0, :, (peers // 2 - 1) * per_peer :] = own_columns
    slots_ref[1, :, :per_peer] = near_columns
    send_near(values_ref[...], edge_ref, near_ref, back_ref, stay_ref)
    operator = operator_ref[0]
    for half in range(2):
        placed_ref[half] = jnp.dot(
            operator, slots_ref[half], preferred_element_type=jnp.float32
        ).astype(operator.dtype)


def first_half_kernel(placed_ref, stay_ref, back_ref, *refs):
    *pair_refs, jump_ref, image_ref = refs
    sent_refs, got_refs = pair_refs[: len(pair_refs) // 2], pair_refs[len(pair_refs) // 2 :]
    loads = stay_ref.shape[0] - GROUP
    groups = (jump_ref.shape[0] - loads) // GROUP
    own, got = (spread(straight(*refs), loads, groups) for refs in ((stay_ref, sent_refs), (back_ref, got_refs)))
    jump_ref[...] = own - got
    image_ref[...] = split_dot(own - got, placed_ref[0], NT)


def first_kernel(far_ref, placed_ref, half_ref, got_ref, near_ref, *refs):
    sent_refs, (jump_ref, image_ref, *pair_refs) = refs[: len(refs) // 2 - 1], refs[len(refs) // 2 - 1 :]
    height = near_ref.shape[0]
    loads = height - GROUP
    groups = (image_ref.shape[0] - loads) // GROUP
    own, got = (spread(value, loads, groups) for value in (for_other(near_ref, sent_refs), handed(got_ref, height)))
    jump_ref[...] = own - got
    image = half_ref[...] + split_dot(own - got, placed_ref[1], NT)
    image_ref[...] = image
    send_far(image, far_ref, *pair_refs)


def products_of(left, right):
    both = lax.dot_general(split(left), split(right), NT, preferred_element_type=jnp.float32)
    both = both[: left.shape[0]] + both[left.shape[0] :]
    return both + pltpu.roll(both, right.shape[0], 1)


def with_scalars(top, products, lanes):
    lane = lax.broadcasted_iota(jnp.int32, top.shape, 1)
    for at, product in zip(lanes, products):
        top = jnp.where(lane == at, jnp.sum(product, axis=1, keepdims=True), top)
    return top


def middle_kernel(
    edge_ref, slots_ref, straight_ref, handed_ref, image_ref, basis_ref, terms_ref, near_ref, back_ref, stay_ref
):
    image = image_ref[...]
    send_near(image, edge_ref, near_ref, back_ref, stay_ref)
    coarse = terms_ref.shape[1] // 8
    loads = image.shape[0] - coarse
    basis = split_dot(straight_ref[...], slots_ref[0], NT) + split_dot(handed_ref[...], slots_ref[1], NT)
    basis_ref[...] = basis
    left = jnp.concatenate([basis[:loads], image[:loads], basis[loads:]])
    empty = jnp.zeros((2 * coarse, basis.shape[1]), jnp.float32)
    both = products_of(left, jnp.concatenate([basis[loads:], image[loads:], empty]))
    strip = lax.broadcasted_iota(jnp.int32, (loads, 8 * coarse), 1) // coarse
    top = jnp.where(strip < 2, both[:loads], 0.0)
    top = jnp.where(strip == 4, both[loads : 2 * loads], top)
    residual = basis[:loads]
    terms_ref[:loads] = with_scalars(top, (residual * residual, residual * image[:loads]), SCALAR_LANES[:2])
    strip = lax.broadcasted_iota(jnp.int32, (coarse, 8 * coarse), 1) // coarse
    terms_ref[loads:] = jnp.where(strip < 2, both[2 * loads :], 0.0)


def second_half_kernel(slots_ref, placed_ref, stay_ref, back_ref, *refs):
    *pair_refs, jump_ref, second_ref = refs
    sent_refs, got_refs = pair_refs[: len(pair_refs) // 2], pair_refs[len(pair_refs) // 2 :]
    jump = straight(stay_ref, sent_refs) - straight(back_ref, got_refs)
    jump_ref[...] = split_dot(jump, slots_ref[0], NT)
    second_ref[...] = split_dot(jump, placed_ref[0], NT)


def second_kernel(slots_ref, placed_ref, basis_ref, half_jump_ref, half_second_ref, early_ref, got_ref, near_ref, *refs):
    *sent_refs, jump_ref, terms_ref = refs
    coarse = terms_ref.shape[1] // 8
    loads = basis_ref.shape[0] - coarse
    jump = for_other(near_ref, sent_refs) - handed(got_ref, loads + coarse)
    second = half_second_ref[...] + split_dot(jump, placed_ref[1], NT)
    jump = half_jump_ref[...] + split_dot(jump, slots_ref[1], NT)
    jump_ref[...] = jump
    basis = basis_ref[...]
    left = jnp.concatenate([basis[:loads], jump[:loads], second[:loads], basis[loads:], jump[loads:]])
    empty = jnp.zeros((coarse, basis.shape[1]), jnp.float32)
    both = products_of(left, jnp.concatenate([basis[loads:], empty, jump[loads:], second[loads:]]))
    along, jumped, doubled = (both[at * loads : (at + 1) * loads] for at in range(3))
    base, far = both[3 * loads : 3 * loads + coarse], both[3 * loads + coarse :]
    strip = lax.broadcasted_iota(jnp.int32, (loads, 8 * coarse), 1) // coarse
    top = jnp.where(strip == 2, doubled, 0.0)
    top = jnp.where(strip == 3, along, top)
    top = jnp.where(strip == 5, pltpu.roll(doubled, coarse, 1), top)
    top = jnp.where(strip >= 6, jumped, top)
    residual, jump_loads, second_loads = basis[:loads], jump[:loads], second[:loads]
    products = (jump_loads * jump_loads, jump_loads * second_loads, residual * second_loads)
    terms_ref[:loads] = early_ref[:loads] + with_scalars(top, products, SCALAR_LANES[2:])
    strip = lax.broadcasted_iota(jnp.int32, (coarse, 8 * coarse), 1) // coarse
    base = jnp.where((strip == 2) | (strip == 3), base, 0.0)
    terms_ref[loads:] = early_ref[loads:] + jnp.where(strip < 4, base, far)


def sum_kernel(count, *refs):
    parts = [ref[...] for ref in refs[:count]]
    while len(parts) > 1:
        parts = [low + high for low, high in zip(parts[::2], parts[1::2])]
    for ref in refs[count:]:
        ref[...] = parts[0]


def eliminate(work, coarse):
    row = lax.broadcasted_iota(jnp.int32, work.shape, 0)
    for first in range(coarse):
        if first % 2 or first % GROUP >= MODES:
            continue
        second = first + 1
        left = jnp.broadcast_to(work[:, first : first + 1], work.shape)
        right = jnp.broadcast_to(work[:, second : second + 1], work.shape)
        upper, lower = work[first : first + 1], work[second : second + 1]
        pivot = 1.0 / left[first : first + 1]
        ratio = left[second : second + 1] * pivot
        corner = 1.0 / (right[second : second + 1] - ratio * right[first : first + 1])
        lower = (lower - ratio * upper) * corner
        upper = (upper - right[first : first + 1] * lower) * pivot
        work = work - left * upper - right * lower
        work = jnp.where(row == first, upper, jnp.where(row == second, lower, work))
    return work


def thin_dot(left, right):
    high, right_high = (value.astype(jnp.bfloat16).astype(jnp.float32) for value in (left, right))
    return jnp.dot(
        jnp.concatenate([high, left - high, high], axis=1).astype(jnp.bfloat16),
        jnp.concatenate([right_high, right_high, right - right_high], axis=0).astype(jnp.bfloat16),
        preferred_element_type=jnp.float32,
    )


def final_kernel(terms_ref, basis_ref, jump_ref, multipliers_ref, amplitudes_ref):
    coarse = terms_ref.shape[1] // 8
    loads = basis_ref.shape[0] - coarse
    groups = coarse // GROUP
    by_load = terms_ref[:loads].T
    used = lax.broadcasted_iota(jnp.int32, (coarse, loads), 0) % GROUP < MODES

    def strip(at):
        return by_load[at * coarse : (at + 1) * coarse]

    def block(at):
        return terms_ref[loads:, at * coarse : (at + 1) * coarse]

    def total(values):
        return jnp.sum(values, axis=0, keepdims=True)

    res_res, res_image, jump_jump, jump_second, res_second = (by_load[at : at + 1] for at in SCALAR_LANES)
    coarse_res, res_h = (jnp.where(used, strip(at), 0.0) for at in (0, 1))
    second_z, res_dz, image_g, second_g, jump_z, jump_dz = (strip(at) for at in range(2, 8))
    g_h, g_dz, z_z, z_dz = block(1), block(3), block(6), block(7)
    row = lax.broadcasted_iota(jnp.int32, (coarse, coarse), 0)
    unit = jnp.where(row == lax.broadcasted_iota(jnp.int32, (coarse, coarse), 1), 1.0, 0.0)
    empty = jnp.zeros((coarse, 5 * coarse - 2 * loads), jnp.float32)
    solved = eliminate(
        jnp.concatenate([terms_ref[loads:, : 2 * coarse], coarse_res, image_g, unit, empty], axis=1), coarse
    )
    inverse_h = solved[:, coarse : 2 * coarse]
    amounts = solved[:, 2 * coarse : 2 * coarse + loads]
    inverse_image = solved[:, 2 * coarse + loads : 2 * coarse + 2 * loads]
    inverse = solved[:, 2 * coarse + 2 * loads : 3 * coarse + 2 * loads]
    products = small_dot(jnp.concatenate([inverse_h, g_h, z_z, g_dz, z_dz], axis=0), amounts)
    inverse_h_amounts, h_amounts, z_amounts, g_dz_amounts, z_dz_amounts = (
        products[at * coarse : (at + 1) * coarse] for at in range(5)
    )
    shares = 2.0 * (inverse_image - inverse_h_amounts)
    both = jnp.concatenate([amounts, shares], axis=0).T
    basis_g, jump_z_rows = basis_ref[loads:], jump_ref[loads:]
    d = basis_ref[:loads] - thin_dot(both[:, :coarse], basis_g)
    u = jump_ref[:loads] - thin_dot(both, jnp.concatenate([jump_z_rows, basis_g], axis=0))
    products = small_dot(jnp.concatenate([g_h, z_z], axis=0), shares)
    image_d = image_g - h_amounts
    inner = res_res - total(amounts * coarse_res)
    curvature = 2.0 * (res_image - total(amounts * (res_h + image_d)))
    u_u = jump_jump - total(amounts * (2.0 * jump_z - z_amounts) + 2.0 * image_d * shares)
    second_u = second_g - g_dz_amounts - products[:coarse]
    jump_u = second_z - z_dz_amounts - 0.5 * products[coarse:]
    d_second = res_second - total(amounts * (res_dz + second_u) + shares * res_h)
    u_second = jump_second - total(amounts * (jump_dz + jump_u) + shares * (0.5 * jump_z + second_u))
    step = inner / curvature
    renewed = step * step * u_u - inner
    grown = 1.0 + renewed / inner
    curvature = grown * grown * curvature - grown * step * (2.0 * d_second + u_u) + 2.0 * step * step * u_second
    second_step = renewed / curvature
    on_d, on_u = step + second_step * grown, second_step * step
    amplitudes = amounts - on_d * shares + 2.0 * on_u * small_dot(inverse, second_u)
    amplitudes_ref[...] = jnp.concatenate(
        [amplitudes[label * GROUP : label * GROUP + MODES] for label in range(groups)], axis=0
    )
    weights = jnp.concatenate([on_d, on_u, jnp.zeros((6, loads), jnp.float32)], axis=0).T
    multipliers_ref[...] = weights[:, 0:1] * d - weights[:, 1:2] * u


def call(kernel, shapes, in_specs, name, scratch=(), flops=0):
    return pl.pallas_call(
        kernel,
        out_shape=[jax.ShapeDtypeStruct(*shape) for shape in shapes],
        in_specs=in_specs,
        out_specs=[VMEM] * len(shapes),
        scratch_shapes=scratch,
        compiler_params=pltpu.CompilerParams(vmem_limit_bytes=24 * 1024 * 1024),
        cost_estimate=pl.CostEstimate(flops=flops, bytes_accessed=2**20, transcendentals=0),
        name=name,
    )


def permute(values, offset, plane_offset=0):
    peers, planes = lax.axis_size("sub"), lax.axis_size("rep")
    offset = offset * planes + plane_offset
    return lax.ppermute(values, ("sub", "rep"), [(at, at ^ offset) for at in range(peers * planes)])


def to_chips(*pairs):
    return [permute(pair, 2 * (len(pairs) - at) + 1) for at, pair in enumerate(pairs)]


def to_core(near, *pairs):
    return permute(jnp.concatenate([near, *(pair[near.shape[0] :] for pair in pairs)], axis=0), 1)


def total(terms):
    chips = [(offset + 1, 0) for offset in reversed(range(2, lax.axis_size("sub"), 2))]
    planes = [(1, offset) for offset in reversed(range(1, lax.axis_size("rep")))]
    copies = [terms]
    for offsets, following in (([(1, 0)], len(chips)), (chips, len(planes)), (planes, 1)):
        parts = [permute(copy, *offset) for copy, offset in zip(copies, offsets)]
        kernel = functools.partial(sum_kernel, len(parts) + 1)
        copies = call(kernel, [(terms.shape, terms.dtype)] * following, [VMEM] * (len(parts) + 1), "sum")(
            copies[0], *reversed(parts)
        )
    return copies[0]


def fused_body(dual_ops, mode_traces, route, mode_block, local_gap):
    peers = lax.axis_size("sub")
    loads, rows = local_gap.shape
    modes = mode_traces.shape[1]
    subs = mode_block.shape[0]
    groups = subs // AGG_SUBS
    per_peer = rows // peers
    height = loads + GROUP * groups
    f32, i32 = jnp.float32, jnp.int32
    tall = ((height, rows), f32)
    wide = ((height, 8 * GROUP * groups), f32)

    def pairs(height):
        return [((2 * height, per_peer), f32)] * (peers // 2 - 1)

    def singles(height):
        return [((height, per_peer), f32)] * 3

    def held(value):
        return pltpu.with_memory_space_constraint(value, pltpu.HBM)

    inputs = [route, mode_block.reshape(1, subs), local_gap, mode_traces.transpose(1, 0, 2), dual_ops]
    short = loads + GROUP
    far, values, operator, route, *send = call(
        place_kernel,
        [
            ((rows, rows - 2 * per_peer), jnp.bfloat16),
            ((short, rows), f32),
            (dual_ops.shape, dual_ops.dtype),
            (route.shape, i32),
            *pairs(short),
        ],
        [HBM] * 5,
        "place",
        [pltpu.VMEM((1, subs), i32), pltpu.VMEM((modes, 1, rows), f32), pltpu.SemaphoreType.DMA((5,))],
    )(*(held(value) for value in inputs))
    got = to_chips(*send)
    halves = ((2, rows, rows // 2), dual_ops.dtype)
    edge, slots, placed, near, back, stay = call(
        ready_kernel,
        [((rows, 3 * per_peer), jnp.bfloat16), halves, halves, *singles(short)],
        [VMEM] * 4,
        "ready",
        flops=2 * rows * rows * rows,
    )(route, far, values, operator)
    got_near = to_core(near, *got)
    half = ((height, rows // 2), f32)
    straight_jump, half_image = call(
        first_half_kernel, [half, tall], [VMEM] * (3 + 2 * len(got)), "first_half", flops=2 * rows * rows * height
    )(placed, stay, back, *send, *got)
    handed_jump, image, *image_send = call(
        first_kernel, [half, tall, *pairs(height)], [VMEM] * (5 + len(send)), "first"
    )(far, placed, half_image, got_near, near, *send)
    got = to_chips(*image_send)
    basis, terms, near, back, stay = call(
        middle_kernel, [tall, wide, *singles(height)], [VMEM] * 5, "middle", flops=4 * rows * rows * height
    )(edge, slots, straight_jump, handed_jump, image)
    got_near = to_core(near, *got)
    half_jump, half_second = call(
        second_half_kernel, [tall, tall], [VMEM] * (4 + 2 * len(got)), "second_half", flops=4 * rows * rows * height
    )(slots, placed, stay, back, *image_send, *got)
    jump, terms = call(second_kernel, [tall, wide], [VMEM] * (8 + len(got)), "second")(
        slots, placed, basis, half_jump, half_second, terms, got_near, near, *image_send
    )
    multipliers, amplitudes = call(
        final_kernel, [((loads, rows), f32), ((MODES * groups, loads), f32)], [VMEM] * 3, "final"
    )(total(terms), basis, jump)
    return multipliers, amplitudes.T


def general_body(dual_ops, mode_traces, route, mode_block, local_gap):
    own_index = lax.axis_index("sub")
    plane_index = lax.axis_index("rep")
    peer_count = lax.axis_size("sub")
    plane_count = lax.axis_size("rep")
    operator = dual_ops[0]
    traces = mode_traces[0]
    slot_rows = route[0]
    rows_here = operator.shape[0]
    load_cases = local_gap.shape[0]
    per_peer = rows_here // peer_count
    blocks = mode_block[:, 0]
    block_count = blocks.shape[0] // AGG_SUBS
    coarse = block_count * MODES
    positions = jnp.arange(rows_here, dtype=jnp.int32)
    inverse = jnp.zeros((rows_here,), jnp.int32).at[slot_rows].set(positions)
    slot_peer = positions // per_peer
    within = positions % per_peer
    flip_index = jnp.where(
        slot_peer == own_index, slot_peer * per_peer + per_peer - 1 - within, positions
    )
    peer_ids = jnp.arange(peer_count, dtype=jnp.int32)
    peer_blocks = blocks[peer_ids * plane_count + plane_index]
    own_block = blocks[own_index * plane_count + plane_index]
    labels = jnp.arange(block_count, dtype=jnp.int32)
    peer_onehot = (peer_blocks[:, None] == labels[None, :]).astype(jnp.float32)
    own_onehot = (labels == own_block).astype(jnp.float32)
    trace_slots = traces[:, slot_rows]
    receive_index = flip_index[inverse]

    def to_peers(values):
        return values[:, slot_rows]

    def from_peers(values):
        return values[:, inverse]

    gap_peers = to_peers(local_gap)
    got_traces = lax.all_to_all(trace_slots, "sub", split_axis=1, concat_axis=1, tiled=True)
    got_gap = lax.all_to_all(gap_peers, "sub", split_axis=1, concat_axis=1, tiled=True)
    partner_traces = got_traces[:, flip_index]
    residual = local_gap - got_gap[:, receive_index]
    own_gram = jnp.dot(traces, traces.T, precision=HIGHEST)
    paired = (trace_slots[:, None, :] * partner_traces[None, :, :]).reshape(
        MODES, MODES, peer_count, per_peer
    )
    cross_terms = jnp.sum(paired, axis=3)
    cross_blocks = jnp.einsum("klq,qb->kbl", cross_terms, peer_onehot, precision=HIGHEST)
    own_blocks = own_gram[:, None, :] * own_onehot[None, :, None]
    row_term = 2.0 * (own_blocks - cross_blocks).reshape(MODES, coarse)
    gram_term = (own_onehot[:, None, None] * row_term[None]).reshape(coarse, coarse)

    def coarse_term(values):
        own_part = 2.0 * jnp.dot(values, traces.T, precision=HIGHEST)
        return (own_part[:, None, :] * own_onehot[None, :, None]).reshape(load_cases, coarse)

    def expand(amounts):
        grouped = amounts.reshape(load_cases, block_count, MODES)
        own_amounts = lax.dynamic_index_in_dim(grouped, own_block, 1, keepdims=False)
        own_part = jnp.dot(own_amounts, traces, precision=HIGHEST)
        peer_amounts = jnp.einsum("qb,rbk->rkq", peer_onehot, grouped, precision=HIGHEST)
        spread = jnp.repeat(peer_amounts, per_peer, axis=2)
        peer_part = jnp.sum(spread * partner_traces[None, :, :], axis=1)
        return own_part - from_peers(peer_part)

    squares = jnp.sum(residual * residual, axis=1)
    gram_matrix, coarse_res, norm_res = lax.psum(
        (gram_term, coarse_term(residual), squares), ("sub", "rep")
    )
    factor = jnp.linalg.cholesky(gram_matrix)

    def solve_coarse(right):
        return jax.scipy.linalg.cho_solve((factor, True), right.T).T

    amplitudes = solve_coarse(coarse_res)
    projected = residual - expand(amplitudes)
    inner_sum = norm_res - jnp.sum(amplitudes * coarse_res, axis=1)
    direction = projected
    multipliers = jnp.zeros_like(residual)
    for iteration in range(ITERS):
        product = lax.dot_general(
            direction.astype(jnp.bfloat16),
            operator,
            (((1,), (1,)), ((), ())),
            preferred_element_type=jnp.float32,
        )
        got_product = lax.all_to_all(
            to_peers(product), "sub", split_axis=1, concat_axis=1, tiled=True
        )
        image_jump = product - got_product[:, receive_index]
        coarse_jump, jump_squares, residual_cross, curvature = lax.psum(
            (
                coarse_term(image_jump),
                jnp.sum(image_jump * image_jump, axis=1),
                jnp.sum(residual * image_jump, axis=1),
                jnp.sum(direction * image_jump, axis=1),
            ),
            ("sub", "rep"),
        )
        step_size = inner_sum / curvature
        multipliers = multipliers + step_size[:, None] * direction
        residual = residual - step_size[:, None] * image_jump
        coarse_res = coarse_res - step_size[:, None] * coarse_jump
        norm_res = (
            norm_res - 2.0 * step_size * residual_cross + step_size * step_size * jump_squares
        )
        amplitudes = solve_coarse(coarse_res)
        if iteration + 1 < ITERS:
            projected = residual - expand(amplitudes)
            renewed = norm_res - jnp.sum(amplitudes * coarse_res, axis=1)
            direction = projected + (renewed / inner_sum)[:, None] * direction
            inner_sum = renewed
    return (multipliers, amplitudes)


def fits(mesh, dual_ops, mode_block, local_gap):
    peers, planes = mesh.shape["sub"], mesh.shape["rep"]
    powers = all(size & (size - 1) == 0 for size in (peers, planes))
    whole = dual_ops.shape[1] % (128 * peers) == 0 and local_gap.shape[0] % 16 == 0
    return powers and whole and 8 * GROUP * (mode_block.shape[0] // AGG_SUBS) == 128


def solution(mesh):
    placed = (
        P(("sub", "rep"), None, None),
        P(("sub", "rep"), None, None),
        P(("sub", "rep"), None),
        P(),
        P(None, ("sub", "rep")),
    )

    def run(dual_ops, mode_traces, route, mode_block, local_gap):
        body = fused_body if fits(mesh, dual_ops, mode_block, local_gap) else general_body
        return jax.shard_map(
            body, mesh=mesh, in_specs=placed, out_specs=(P(None, ("sub", "rep")), P()), check_vma=False
        )(dual_ops, mode_traces, route, mode_block, local_gap)

    return run
```

```python
import functools

import jax
import jax.numpy as jnp
from jax import lax
from jax.experimental import pallas as pl
from jax.experimental.pallas import tpu as pltpu
from jax.sharding import PartitionSpec as P

MODES = 6
AGG_SUBS = 16
ITERS = 2
GROUP = 8
SCALAR_LANES = (MODES, MODES + 1, GROUP + MODES, GROUP + MODES + 1, 2 * GROUP + MODES)

HIGHEST = lax.Precision.HIGHEST
VMEM = pl.BlockSpec(memory_space=pltpu.VMEM)
HBM = pl.BlockSpec(memory_space=pltpu.HBM)
NN = (((1,), (0,)), ((), ()))
NT = (((1,), (1,)), ((), ()))


def split(values):
    high = values.astype(jnp.bfloat16).astype(jnp.float32)
    return jnp.concatenate([high, values - high], axis=0).astype(jnp.bfloat16)


def split_dot(values, matrix, dims):
    rows = values.shape[0]
    both = lax.dot_general(split(values), matrix, dims, preferred_element_type=jnp.float32)
    return both[:rows] + both[rows:]


def small_dot(left, right):
    return jnp.dot(left, right, precision=HIGHEST, preferred_element_type=jnp.float32)


def send_far(values, far_ref, *pair_refs):
    height = values.shape[0]
    per_peer = pair_refs[0].shape[1]
    slots = split_dot(values, far_ref[...], NN)
    for at, ref in enumerate(reversed(pair_refs)):
        start = 2 * at * per_peer
        ref[:height] = slots[:, start + per_peer : start + 2 * per_peer]
        ref[height:] = slots[:, start : start + per_peer]


def send_near(values, edge_ref, near_ref, back_ref, stay_ref):
    per_peer = back_ref.shape[1]
    slots = split_dot(values, edge_ref[...], NN)
    for at, ref in enumerate((near_ref, back_ref, stay_ref)):
        ref[...] = slots[:, at * per_peer : (at + 1) * per_peer]


def straight(last_ref, pair_refs):
    height = last_ref.shape[0]
    return jnp.concatenate([*(ref[:height] for ref in pair_refs), last_ref[...]], axis=1)


def for_other(near_ref, pair_refs):
    height = near_ref.shape[0]
    return jnp.concatenate([near_ref[...], *(ref[height:] for ref in pair_refs)], axis=1)


def handed(got_ref, height):
    return jnp.concatenate([got_ref[at : at + height] for at in range(0, got_ref.shape[0], height)], axis=1)


def spread(values, loads, groups):
    modes = values[loads:]
    label = modes[MODES : MODES + 1]
    used = lax.broadcasted_iota(jnp.int32, modes.shape, 0) < MODES
    parts = [jnp.where(used & (label == group), modes, 0.0) for group in range(groups)]
    return jnp.concatenate([values[:loads], *parts], axis=0)


def one_hot(route_ref, peer, per_peer):
    start = pl.multiple_of(peer * per_peer, per_peer)
    row_ids = lax.broadcasted_iota(jnp.int32, (route_ref.shape[1], per_peer), 0)
    return jnp.where(row_ids == route_ref[:, pl.ds(start, per_peer)], 1.0, 0.0).astype(jnp.bfloat16)


def place_kernel(
    route_hbm, block_hbm, gap_hbm, traces_hbm, operator_hbm,
    far_ref, values_ref, operator_ref, route_ref, *refs,
):
    *pair_refs, block_ref, traces_ref, sems = refs
    loads, rows = gap_hbm.shape
    per_peer = pair_refs[0].shape[1]
    peers = rows // per_peer
    copies = [
        pltpu.make_async_copy(source, target, sems.at[at])
        for at, (source, target) in enumerate(
            (
                (route_hbm, route_ref),
                (block_hbm, block_ref),
                (traces_hbm, traces_ref),
                (gap_hbm, values_ref.at[pl.ds(0, loads)]),
                (operator_hbm, operator_ref),
            )
        )
    ]
    for copy in copies:
        copy.start()
    own_index = lax.axis_index("sub")
    device = own_index * lax.axis_size("rep") + lax.axis_index("rep")
    copies[0].wait()
    for offset in range(2, peers):
        at = (offset - 2) * per_peer
        far_ref[:, at : at + per_peer] = one_hot(route_ref, own_index ^ offset, per_peer)
    copies[1].wait()
    copies[2].wait()
    blocks = block_ref[...]
    lane = lax.broadcasted_iota(jnp.int32, blocks.shape, 1)
    own_block = jnp.sum(jnp.where(lane == device, blocks, 0), axis=1, keepdims=True)
    modes = traces_ref.shape[0]
    label = jnp.broadcast_to(own_block.astype(jnp.float32), (1, rows))
    for mode in range(modes):
        values_ref[loads + mode : loads + mode + 1] = traces_ref[mode]
    values_ref[loads + modes : loads + modes + 1] = label
    values_ref[loads + modes + 1 :] = jnp.zeros((GROUP - modes - 1, rows), jnp.float32)
    copies[3].wait()
    send_far(values_ref[...], far_ref, *pair_refs)
    copies[4].wait()


def ready_kernel(
    route_ref, far_ref, values_ref, operator_ref,
    edge_ref, slots_ref, placed_ref, near_ref, back_ref, stay_ref,
):
    per_peer = back_ref.shape[1]
    peers = far_ref.shape[1] // per_peer + 2
    own_index = lax.axis_index("sub")
    low = lax.broadcasted_iota(jnp.int32, (per_peer, per_peer), 0)
    high = lax.broadcasted_iota(jnp.int32, (per_peer, per_peer), 1)
    reverse = jnp.where(low + high == per_peer - 1, 1.0, 0.0).astype(jnp.bfloat16)
    own_columns = one_hot(route_ref, own_index, per_peer)
    near_columns = one_hot(route_ref, own_index ^ 1, per_peer)
    reversed_columns = jnp.dot(own_columns, reverse, preferred_element_type=jnp.float32).astype(jnp.bfloat16)
    edge_ref[...] = jnp.concatenate([near_columns, reversed_columns, own_columns], axis=1)
    for at in range(peers // 2 - 1):
        start = (peers - 4 - 2 * at) * per_peer
        slots_ref[0, :, at * per_peer : (at + 1) * per_peer] = far_ref[:, start + per_peer : start + 2 * per_peer]
        slots_ref[1, :, (at + 1) * per_peer : (at + 2) * per_peer] = far_ref[:, start : start + per_peer]
    slots_ref[0, :, (peers // 2 - 1) * per_peer :] = own_columns
    slots_ref[1, :, :per_peer] = near_columns
    send_near(values_ref[...], edge_ref, near_ref, back_ref, stay_ref)
    operator = operator_ref[0]
    for half in range(2):
        placed_ref[half] = jnp.dot(
            operator, slots_ref[half], preferred_element_type=jnp.float32
        ).astype(operator.dtype)


def first_half_kernel(placed_ref, stay_ref, back_ref, *refs):
    *pair_refs, jump_ref, image_ref = refs
    sent_refs, got_refs = pair_refs[: len(pair_refs) // 2], pair_refs[len(pair_refs) // 2 :]
    loads = stay_ref.shape[0] - GROUP
    groups = (jump_ref.shape[0] - loads) // GROUP
    own, got = (spread(straight(*refs), loads, groups) for refs in ((stay_ref, sent_refs), (back_ref, got_refs)))
    jump_ref[...] = own - got
    image_ref[...] = split_dot(own - got, placed_ref[0], NT)


def first_kernel(far_ref, placed_ref, half_ref, got_ref, near_ref, *refs):
    sent_refs, (jump_ref, image_ref, *pair_refs) = refs[: len(refs) // 2 - 1], refs[len(refs) // 2 - 1 :]
    height = near_ref.shape[0]
    loads = height - GROUP
    groups = (image_ref.shape[0] - loads) // GROUP
    own, got = (spread(value, loads, groups) for value in (for_other(near_ref, sent_refs), handed(got_ref, height)))
    jump_ref[...] = own - got
    image = half_ref[...] + split_dot(own - got, placed_ref[1], NT)
    image_ref[...] = image
    send_far(image, far_ref, *pair_refs)


def products_of(left, right):
    both = lax.dot_general(split(left), split(right), NT, preferred_element_type=jnp.float32)
    both = both[: left.shape[0]] + both[left.shape[0] :]
    return both + pltpu.roll(both, right.shape[0], 1)


def with_scalars(top, products, lanes):
    lane = lax.broadcasted_iota(jnp.int32, top.shape, 1)
    for at, product in zip(lanes, products):
        top = jnp.where(lane == at, jnp.sum(product, axis=1, keepdims=True), top)
    return top


def middle_kernel(
    edge_ref, slots_ref, straight_ref, handed_ref, image_ref, basis_ref, terms_ref, near_ref, back_ref, stay_ref
):
    image = image_ref[...]
    send_near(image, edge_ref, near_ref, back_ref, stay_ref)
    coarse = terms_ref.shape[1] // 8
    loads = image.shape[0] - coarse
    basis = split_dot(straight_ref[...], slots_ref[0], NT) + split_dot(handed_ref[...], slots_ref[1], NT)
    basis_ref[...] = basis
    left = jnp.concatenate([basis[:loads], image[:loads], basis[loads:]])
    empty = jnp.zeros((2 * coarse, basis.shape[1]), jnp.float32)
    both = products_of(left, jnp.concatenate([basis[loads:], image[loads:], empty]))
    strip = lax.broadcasted_iota(jnp.int32, (loads, 8 * coarse), 1) // coarse
    top = jnp.where(strip < 2, both[:loads], 0.0)
    top = jnp.where(strip == 4, both[loads : 2 * loads], top)
    residual = basis[:loads]
    terms_ref[:loads] = with_scalars(top, (residual * residual, residual * image[:loads]), SCALAR_LANES[:2])
    strip = lax.broadcasted_iota(jnp.int32, (coarse, 8 * coarse), 1) // coarse
    terms_ref[loads:] = jnp.where(strip < 2, both[2 * loads :], 0.0)


def second_half_kernel(slots_ref, placed_ref, stay_ref, back_ref, *refs):
    *pair_refs, jump_ref, second_ref = refs
    sent_refs, got_refs = pair_refs[: len(pair_refs) // 2], pair_refs[len(pair_refs) // 2 :]
    jump = straight(stay_ref, sent_refs) - straight(back_ref, got_refs)
    jump_ref[...] = split_dot(jump, slots_ref[0], NT)
    second_ref[...] = split_dot(jump, placed_ref[0], NT)


def second_kernel(slots_ref, placed_ref, basis_ref, half_jump_ref, half_second_ref, early_ref, got_ref, near_ref, *refs):
    *sent_refs, jump_ref, terms_ref = refs
    coarse = terms_ref.shape[1] // 8
    loads = basis_ref.shape[0] - coarse
    jump = for_other(near_ref, sent_refs) - handed(got_ref, loads + coarse)
    second = half_second_ref[...] + split_dot(jump, placed_ref[1], NT)
    jump = half_jump_ref[...] + split_dot(jump, slots_ref[1], NT)
    jump_ref[...] = jump
    basis = basis_ref[...]
    left = jnp.concatenate([basis[:loads], jump[:loads], second[:loads], basis[loads:], jump[loads:]])
    empty = jnp.zeros((coarse, basis.shape[1]), jnp.float32)
    both = products_of(left, jnp.concatenate([basis[loads:], empty, jump[loads:], second[loads:]]))
    along, jumped, doubled = (both[at * loads : (at + 1) * loads] for at in range(3))
    base, far = both[3 * loads : 3 * loads + coarse], both[3 * loads + coarse :]
    strip = lax.broadcasted_iota(jnp.int32, (loads, 8 * coarse), 1) // coarse
    top = jnp.where(strip == 2, doubled, 0.0)
    top = jnp.where(strip == 3, along, top)
    top = jnp.where(strip == 5, pltpu.roll(doubled, coarse, 1), top)
    top = jnp.where(strip >= 6, jumped, top)
    residual, jump_loads, second_loads = basis[:loads], jump[:loads], second[:loads]
    products = (jump_loads * jump_loads, jump_loads * second_loads, residual * second_loads)
    terms_ref[:loads] = early_ref[:loads] + with_scalars(top, products, SCALAR_LANES[2:])
    strip = lax.broadcasted_iota(jnp.int32, (coarse, 8 * coarse), 1) // coarse
    base = jnp.where((strip == 2) | (strip == 3), base, 0.0)
    terms_ref[loads:] = early_ref[loads:] + jnp.where(strip < 4, base, far)


def sum_kernel(count, *refs):
    parts = [ref[...] for ref in reversed(refs[:count])]
    while len(parts) > 1:
        parts = [low + high for low, high in zip(parts[::2], parts[1::2])]
    for ref in refs[count:]:
        ref[...] = parts[0]


def eliminate(work, coarse):
    row = lax.broadcasted_iota(jnp.int32, work.shape, 0)
    for first in range(coarse):
        if first % 2 or first % GROUP >= MODES:
            continue
        second = first + 1
        left = jnp.broadcast_to(work[:, first : first + 1], work.shape)
        right = jnp.broadcast_to(work[:, second : second + 1], work.shape)
        upper, lower = work[first : first + 1], work[second : second + 1]
        pivot = 1.0 / left[first : first + 1]
        ratio = left[second : second + 1] * pivot
        corner = 1.0 / (right[second : second + 1] - ratio * right[first : first + 1])
        lower = (lower - ratio * upper) * corner
        upper = (upper - right[first : first + 1] * lower) * pivot
        work = work - left * upper - right * lower
        work = jnp.where(row == first, upper, jnp.where(row == second, lower, work))
    return work


def thin_dot(left, right):
    high, right_high = (value.astype(jnp.bfloat16).astype(jnp.float32) for value in (left, right))
    return jnp.dot(
        jnp.concatenate([high, left - high, high], axis=1).astype(jnp.bfloat16),
        jnp.concatenate([right_high, right_high, right - right_high], axis=0).astype(jnp.bfloat16),
        preferred_element_type=jnp.float32,
    )


def final_kernel(terms_ref, basis_ref, jump_ref, multipliers_ref, amplitudes_ref):
    coarse = terms_ref.shape[1] // 8
    loads = basis_ref.shape[0] - coarse
    groups = coarse // GROUP
    by_load = terms_ref[:loads].T
    used = lax.broadcasted_iota(jnp.int32, (coarse, loads), 0) % GROUP < MODES

    def strip(at):
        return by_load[at * coarse : (at + 1) * coarse]

    def block(at):
        return terms_ref[loads:, at * coarse : (at + 1) * coarse]

    def total(values):
        return jnp.sum(values, axis=0, keepdims=True)

    res_res, res_image, jump_jump, jump_second, res_second = (by_load[at : at + 1] for at in SCALAR_LANES)
    coarse_res, res_h = (jnp.where(used, strip(at), 0.0) for at in (0, 1))
    second_z, res_dz, image_g, second_g, jump_z, jump_dz = (strip(at) for at in range(2, 8))
    g_h, g_dz, z_z, z_dz = block(1), block(3), block(6), block(7)
    row = lax.broadcasted_iota(jnp.int32, (coarse, coarse), 0)
    unit = jnp.where(row == lax.broadcasted_iota(jnp.int32, (coarse, coarse), 1), 1.0, 0.0)
    empty = jnp.zeros((coarse, 5 * coarse - 2 * loads), jnp.float32)
    solved = eliminate(
        jnp.concatenate([terms_ref[loads:, : 2 * coarse], coarse_res, image_g, unit, empty], axis=1), coarse
    )
    inverse_h = solved[:, coarse : 2 * coarse]
    amounts = solved[:, 2 * coarse : 2 * coarse + loads]
    inverse_image = solved[:, 2 * coarse + loads : 2 * coarse + 2 * loads]
    inverse = solved[:, 2 * coarse + 2 * loads : 3 * coarse + 2 * loads]
    products = small_dot(jnp.concatenate([inverse_h, g_h, z_z, g_dz, z_dz], axis=0), amounts)
    inverse_h_amounts, h_amounts, z_amounts, g_dz_amounts, z_dz_amounts = (
        products[at * coarse : (at + 1) * coarse] for at in range(5)
    )
    shares = 2.0 * (inverse_image - inverse_h_amounts)
    both = jnp.concatenate([amounts, shares], axis=0).T
    basis_g, jump_z_rows = basis_ref[loads:], jump_ref[loads:]
    d = basis_ref[:loads] - thin_dot(both[:, :coarse], basis_g)
    u = jump_ref[:loads] - thin_dot(both, jnp.concatenate([jump_z_rows, basis_g], axis=0))
    products = small_dot(jnp.concatenate([g_h, z_z], axis=0), shares)
    image_d = image_g - h_amounts
    inner = res_res - total(amounts * coarse_res)
    curvature = 2.0 * (res_image - total(amounts * (res_h + image_d)))
    u_u = jump_jump - total(amounts * (2.0 * jump_z - z_amounts) + 2.0 * image_d * shares)
    second_u = second_g - g_dz_amounts - products[:coarse]
    jump_u = second_z - z_dz_amounts - 0.5 * products[coarse:]
    d_second = res_second - total(amounts * (res_dz + second_u) + shares * res_h)
    u_second = jump_second - total(amounts * (jump_dz + jump_u) + shares * (0.5 * jump_z + second_u))
    step = inner / curvature
    renewed = step * step * u_u - inner
    grown = 1.0 + renewed / inner
    curvature = grown * grown * curvature - grown * step * (2.0 * d_second + u_u) + 2.0 * step * step * u_second
    second_step = renewed / curvature
    on_d, on_u = step + second_step * grown, second_step * step
    amplitudes = amounts - on_d * shares + 2.0 * on_u * small_dot(inverse, second_u)
    amplitudes_ref[...] = jnp.concatenate(
        [amplitudes[label * GROUP : label * GROUP + MODES] for label in range(groups)], axis=0
    )
    weights = jnp.concatenate([on_d, on_u, jnp.zeros((6, loads), jnp.float32)], axis=0).T
    multipliers_ref[...] = weights[:, 0:1] * d - weights[:, 1:2] * u


def call(kernel, shapes, in_specs, name, scratch=(), flops=0):
    return pl.pallas_call(
        kernel,
        out_shape=[jax.ShapeDtypeStruct(*shape) for shape in shapes],
        in_specs=in_specs,
        out_specs=[VMEM] * len(shapes),
        scratch_shapes=scratch,
        compiler_params=pltpu.CompilerParams(vmem_limit_bytes=24 * 1024 * 1024),
        cost_estimate=pl.CostEstimate(flops=flops, bytes_accessed=2**20, transcendentals=0),
        name=name,
    )


def permute(values, offset, plane_offset=0):
    peers, planes = lax.axis_size("sub"), lax.axis_size("rep")
    offset = offset * planes + plane_offset
    return lax.ppermute(values, ("sub", "rep"), [(at, at ^ offset) for at in range(peers * planes)])


def to_chips(*pairs):
    return [permute(pair, 2 * (len(pairs) - at) + 1) for at, pair in enumerate(pairs)]


def to_core(near, *pairs):
    return permute(jnp.concatenate([near, *(pair[near.shape[0] :] for pair in pairs)], axis=0), 1)


def total(terms):
    chips = [(offset + 1, 0) for offset in reversed(range(2, lax.axis_size("sub"), 2))]
    chips = chips[-1:] + chips[:-1]
    planes = [(1, offset) for offset in reversed(range(1, lax.axis_size("rep")))]
    copies = [terms]
    for offsets, following in (([(1, 0)], len(chips)), (chips, len(planes)), (planes, 1)):
        parts = [permute(copy, *offset) for copy, offset in zip(copies, offsets)]
        kernel = functools.partial(sum_kernel, len(parts) + 1)
        copies = call(kernel, [(terms.shape, terms.dtype)] * following, [VMEM] * (len(parts) + 1), "sum")(
            *parts, copies[0]
        )
    return copies[0]


def fused_body(dual_ops, mode_traces, route, mode_block, local_gap):
    peers = lax.axis_size("sub")
    loads, rows = local_gap.shape
    modes = mode_traces.shape[1]
    subs = mode_block.shape[0]
    groups = subs // AGG_SUBS
    per_peer = rows // peers
    height = loads + GROUP * groups
    f32, i32 = jnp.float32, jnp.int32
    tall = ((height, rows), f32)
    wide = ((height, 8 * GROUP * groups), f32)

    def pairs(height):
        return [((2 * height, per_peer), f32)] * (peers // 2 - 1)

    def singles(height):
        return [((height, per_peer), f32)] * 3

    def held(value):
        return pltpu.with_memory_space_constraint(value, pltpu.HBM)

    inputs = [route, mode_block.reshape(1, subs), local_gap, mode_traces.transpose(1, 0, 2), dual_ops]
    short = loads + GROUP
    far, values, operator, route, *send = call(
        place_kernel,
        [
            ((rows, rows - 2 * per_peer), jnp.bfloat16),
            ((short, rows), f32),
            (dual_ops.shape, dual_ops.dtype),
            (route.shape, i32),
            *pairs(short),
        ],
        [HBM] * 5,
        "place",
        [pltpu.VMEM((1, subs), i32), pltpu.VMEM((modes, 1, rows), f32), pltpu.SemaphoreType.DMA((5,))],
    )(*(held(value) for value in inputs))
    got = to_chips(*send)
    halves = ((2, rows, rows // 2), dual_ops.dtype)
    edge, slots, placed, near, back, stay = call(
        ready_kernel,
        [((rows, 3 * per_peer), jnp.bfloat16), halves, halves, *singles(short)],
        [VMEM] * 4,
        "ready",
        flops=2 * rows * rows * rows,
    )(route, far, values, operator)
    got_near = to_core(near, *got)
    half = ((height, rows // 2), f32)
    straight_jump, half_image = call(
        first_half_kernel, [half, tall], [VMEM] * (3 + 2 * len(got)), "first_half", flops=2 * rows * rows * height
    )(placed, stay, back, *send, *got)
    handed_jump, image, *image_send = call(
        first_kernel, [half, tall, *pairs(height)], [VMEM] * (5 + len(send)), "first"
    )(far, placed, half_image, got_near, near, *send)
    got = to_chips(*image_send)
    basis, terms, near, back, stay = call(
        middle_kernel, [tall, wide, *singles(height)], [VMEM] * 5, "middle", flops=4 * rows * rows * height
    )(edge, slots, straight_jump, handed_jump, image)
    got_near = to_core(near, *got)
    half_jump, half_second = call(
        second_half_kernel, [tall, tall], [VMEM] * (4 + 2 * len(got)), "second_half", flops=4 * rows * rows * height
    )(slots, placed, stay, back, *image_send, *got)
    jump, terms = call(second_kernel, [tall, wide], [VMEM] * (8 + len(got)), "second")(
        slots, placed, basis, half_jump, half_second, terms, got_near, near, *image_send
    )
    multipliers, amplitudes = call(
        final_kernel, [((loads, rows), f32), ((MODES * groups, loads), f32)], [VMEM] * 3, "final"
    )(total(terms), basis, jump)
    return multipliers, amplitudes.T


def general_body(dual_ops, mode_traces, route, mode_block, local_gap):
    own_index = lax.axis_index("sub")
    plane_index = lax.axis_index("rep")
    peer_count = lax.axis_size("sub")
    plane_count = lax.axis_size("rep")
    operator = dual_ops[0]
    traces = mode_traces[0]
    slot_rows = route[0]
    rows_here = operator.shape[0]
    load_cases = local_gap.shape[0]
    per_peer = rows_here // peer_count
    blocks = mode_block[:, 0]
    block_count = blocks.shape[0] // AGG_SUBS
    coarse = block_count * MODES
    positions = jnp.arange(rows_here, dtype=jnp.int32)
    inverse = jnp.zeros((rows_here,), jnp.int32).at[slot_rows].set(positions)
    slot_peer = positions // per_peer
    within = positions % per_peer
    flip_index = jnp.where(
        slot_peer == own_index, slot_peer * per_peer + per_peer - 1 - within, positions
    )
    peer_ids = jnp.arange(peer_count, dtype=jnp.int32)
    peer_blocks = blocks[peer_ids * plane_count + plane_index]
    own_block = blocks[own_index * plane_count + plane_index]
    labels = jnp.arange(block_count, dtype=jnp.int32)
    peer_onehot = (peer_blocks[:, None] == labels[None, :]).astype(jnp.float32)
    own_onehot = (labels == own_block).astype(jnp.float32)
    trace_slots = traces[:, slot_rows]
    receive_index = flip_index[inverse]

    def to_peers(values):
        return values[:, slot_rows]

    def from_peers(values):
        return values[:, inverse]

    gap_peers = to_peers(local_gap)
    got_traces = lax.all_to_all(trace_slots, "sub", split_axis=1, concat_axis=1, tiled=True)
    got_gap = lax.all_to_all(gap_peers, "sub", split_axis=1, concat_axis=1, tiled=True)
    partner_traces = got_traces[:, flip_index]
    residual = local_gap - got_gap[:, receive_index]
    own_gram = jnp.dot(traces, traces.T, precision=HIGHEST)
    paired = (trace_slots[:, None, :] * partner_traces[None, :, :]).reshape(
        MODES, MODES, peer_count, per_peer
    )
    cross_terms = jnp.sum(paired, axis=3)
    cross_blocks = jnp.einsum("klq,qb->kbl", cross_terms, peer_onehot, precision=HIGHEST)
    own_blocks = own_gram[:, None, :] * own_onehot[None, :, None]
    row_term = 2.0 * (own_blocks - cross_blocks).reshape(MODES, coarse)
    gram_term = (own_onehot[:, None, None] * row_term[None]).reshape(coarse, coarse)

    def coarse_term(values):
        own_part = 2.0 * jnp.dot(values, traces.T, precision=HIGHEST)
        return (own_part[:, None, :] * own_onehot[None, :, None]).reshape(load_cases, coarse)

    def expand(amounts):
        grouped = amounts.reshape(load_cases, block_count, MODES)
        own_amounts = lax.dynamic_index_in_dim(grouped, own_block, 1, keepdims=False)
        own_part = jnp.dot(own_amounts, traces, precision=HIGHEST)
        peer_amounts = jnp.einsum("qb,rbk->rkq", peer_onehot, grouped, precision=HIGHEST)
        spread = jnp.repeat(peer_amounts, per_peer, axis=2)
        peer_part = jnp.sum(spread * partner_traces[None, :, :], axis=1)
        return own_part - from_peers(peer_part)

    squares = jnp.sum(residual * residual, axis=1)
    gram_matrix, coarse_res, norm_res = lax.psum(
        (gram_term, coarse_term(residual), squares), ("sub", "rep")
    )
    factor = jnp.linalg.cholesky(gram_matrix)

    def solve_coarse(right):
        return jax.scipy.linalg.cho_solve((factor, True), right.T).T

    amplitudes = solve_coarse(coarse_res)
    projected = residual - expand(amplitudes)
    inner_sum = norm_res - jnp.sum(amplitudes * coarse_res, axis=1)
    direction = projected
    multipliers = jnp.zeros_like(residual)
    for iteration in range(ITERS):
        product = lax.dot_general(
            direction.astype(jnp.bfloat16),
            operator,
            (((1,), (1,)), ((), ())),
            preferred_element_type=jnp.float32,
        )
        got_product = lax.all_to_all(
            to_peers(product), "sub", split_axis=1, concat_axis=1, tiled=True
        )
        image_jump = product - got_product[:, receive_index]
        coarse_jump, jump_squares, residual_cross, curvature = lax.psum(
            (
                coarse_term(image_jump),
                jnp.sum(image_jump * image_jump, axis=1),
                jnp.sum(residual * image_jump, axis=1),
                jnp.sum(direction * image_jump, axis=1),
            ),
            ("sub", "rep"),
        )
        step_size = inner_sum / curvature
        multipliers = multipliers + step_size[:, None] * direction
        residual = residual - step_size[:, None] * image_jump
        coarse_res = coarse_res - step_size[:, None] * coarse_jump
        norm_res = (
            norm_res - 2.0 * step_size * residual_cross + step_size * step_size * jump_squares
        )
        amplitudes = solve_coarse(coarse_res)
        if iteration + 1 < ITERS:
            projected = residual - expand(amplitudes)
            renewed = norm_res - jnp.sum(amplitudes * coarse_res, axis=1)
            direction = projected + (renewed / inner_sum)[:, None] * direction
            inner_sum = renewed
    return (multipliers, amplitudes)


def fits(mesh, dual_ops, mode_block, local_gap):
    peers, planes = mesh.shape["sub"], mesh.shape["rep"]
    powers = all(size & (size - 1) == 0 for size in (peers, planes))
    whole = dual_ops.shape[1] % (128 * peers) == 0 and local_gap.shape[0] % 16 == 0
    return powers and whole and 8 * GROUP * (mode_block.shape[0] // AGG_SUBS) == 128


def solution(mesh):
    placed = (
        P(("sub", "rep"), None, None),
        P(("sub", "rep"), None, None),
        P(("sub", "rep"), None),
        P(),
        P(None, ("sub", "rep")),
    )

    def run(dual_ops, mode_traces, route, mode_block, local_gap):
        body = fused_body if fits(mesh, dual_ops, mode_block, local_gap) else general_body
        return jax.shard_map(
            body, mesh=mesh, in_specs=placed, out_specs=(P(None, ("sub", "rep")), P()), check_vma=False
        )(dual_ops, mode_traces, route, mode_block, local_gap)

    return run
```

```python
import functools

import jax
import jax.numpy as jnp
from jax import lax
from jax.experimental import pallas as pl
from jax.experimental.pallas import tpu as pltpu
from jax.sharding import PartitionSpec as P

MODES = 6
AGG_SUBS = 16
ITERS = 2
GROUP = 8
SCALAR_LANES = (MODES, MODES + 1, GROUP + MODES, GROUP + MODES + 1, 2 * GROUP + MODES)

HIGHEST = lax.Precision.HIGHEST
VMEM = pl.BlockSpec(memory_space=pltpu.VMEM)
HBM = pl.BlockSpec(memory_space=pltpu.HBM)
NN = (((1,), (0,)), ((), ()))
NT = (((1,), (1,)), ((), ()))


def split(values):
    high = values.astype(jnp.bfloat16).astype(jnp.float32)
    return jnp.concatenate([high, values - high], axis=0).astype(jnp.bfloat16)


def split_dot(values, matrix, dims):
    rows = values.shape[0]
    both = lax.dot_general(split(values), matrix, dims, preferred_element_type=jnp.float32)
    return both[:rows] + both[rows:]


def small_dot(left, right):
    return jnp.dot(left, right, precision=HIGHEST, preferred_element_type=jnp.float32)


def send_far(values, far_ref, *pair_refs):
    height = values.shape[0]
    per_peer = pair_refs[0].shape[1]
    values = split(values)
    for at, ref in enumerate(pair_refs):
        columns = far_ref[:, 2 * at * per_peer : (2 * at + 2) * per_peer]
        slots = jnp.dot(values, columns, preferred_element_type=jnp.float32)
        slots = slots[:height] + slots[height:]
        ref[:height] = slots[:, :per_peer]
        ref[height:] = slots[:, per_peer:]


def send_near(values, edge_ref, near_ref, back_ref, stay_ref):
    per_peer = back_ref.shape[1]
    slots = split_dot(values, edge_ref[...], NN)
    for at, ref in enumerate((near_ref, back_ref, stay_ref)):
        ref[...] = slots[:, at * per_peer : (at + 1) * per_peer]


def straight(last_ref, pair_refs):
    height = last_ref.shape[0]
    return jnp.concatenate([*(ref[:height] for ref in pair_refs), last_ref[...]], axis=1)


def for_other(near_ref, pair_refs):
    height = near_ref.shape[0]
    return jnp.concatenate([near_ref[...], *(ref[height:] for ref in pair_refs)], axis=1)


def handed(got_ref, height):
    return jnp.concatenate([got_ref[at : at + height] for at in range(0, got_ref.shape[0], height)], axis=1)


def spread(values, loads, groups):
    modes = values[loads:]
    label = modes[MODES : MODES + 1]
    used = lax.broadcasted_iota(jnp.int32, modes.shape, 0) < MODES
    parts = [jnp.where(used & (label == group), modes, 0.0) for group in range(groups)]
    return jnp.concatenate([values[:loads], *parts], axis=0)


def one_hot(route_ref, peer, per_peer):
    start = pl.multiple_of(peer * per_peer, per_peer)
    row_ids = lax.broadcasted_iota(jnp.int32, (route_ref.shape[1], per_peer), 0)
    return jnp.where(row_ids == route_ref[:, pl.ds(start, per_peer)], 1.0, 0.0).astype(jnp.bfloat16)


def place_kernel(
    route_hbm, block_hbm, gap_hbm, traces_hbm, operator_hbm,
    far_ref, values_ref, operator_ref, route_ref, *refs,
):
    *pair_refs, block_ref, traces_ref, sems = refs
    loads, rows = gap_hbm.shape
    per_peer = pair_refs[0].shape[1]
    peers = rows // per_peer
    copies = [
        pltpu.make_async_copy(source, target, sems.at[at])
        for at, (source, target) in enumerate(
            (
                (route_hbm, route_ref),
                (block_hbm, block_ref),
                (traces_hbm, traces_ref),
                (gap_hbm, values_ref.at[pl.ds(0, loads)]),
                (operator_hbm, operator_ref),
            )
        )
    ]

    def build(at):
        peer = own_index ^ (peers - 1 - at)
        far_ref[:, at * per_peer : (at + 1) * per_peer] = one_hot(route_ref, peer, per_peer)

    for copy in copies:
        copy.start()
    own_index = lax.axis_index("sub")
    device = own_index * lax.axis_size("rep") + lax.axis_index("rep")
    copies[0].wait()
    for at in range(peers - 4):
        build(at)
    copies[1].wait()
    copies[2].wait()
    blocks = block_ref[...]
    lane = lax.broadcasted_iota(jnp.int32, blocks.shape, 1)
    own_block = jnp.sum(jnp.where(lane == device, blocks, 0), axis=1, keepdims=True)
    modes = traces_ref.shape[0]
    label = jnp.broadcast_to(own_block.astype(jnp.float32), (1, rows))
    for mode in range(modes):
        values_ref[loads + mode : loads + mode + 1] = traces_ref[mode]
    values_ref[loads + modes : loads + modes + 1] = label
    values_ref[loads + modes + 1 :] = jnp.zeros((GROUP - modes - 1, rows), jnp.float32)
    copies[3].wait()
    for at in range(peers - 4, peers - 2):
        build(at)
    send_far(values_ref[...], far_ref, *pair_refs)
    copies[4].wait()


def ready_kernel(
    route_ref, far_ref, values_ref, operator_ref,
    edge_ref, slots_ref, placed_ref, near_ref, back_ref, stay_ref,
):
    per_peer = back_ref.shape[1]
    peers = far_ref.shape[1] // per_peer + 2
    own_index = lax.axis_index("sub")
    low = lax.broadcasted_iota(jnp.int32, (per_peer, per_peer), 0)
    high = lax.broadcasted_iota(jnp.int32, (per_peer, per_peer), 1)
    reverse = jnp.where(low + high == per_peer - 1, 1.0, 0.0).astype(jnp.bfloat16)
    own_columns = one_hot(route_ref, own_index, per_peer)
    near_columns = one_hot(route_ref, own_index ^ 1, per_peer)
    reversed_columns = jnp.dot(own_columns, reverse, preferred_element_type=jnp.float32).astype(jnp.bfloat16)
    edge_ref[...] = jnp.concatenate([near_columns, reversed_columns, own_columns], axis=1)
    for at in range(peers // 2 - 1):
        start = 2 * at * per_peer
        slots_ref[0, :, at * per_peer : (at + 1) * per_peer] = far_ref[:, start : start + per_peer]
        slots_ref[1, :, (at + 1) * per_peer : (at + 2) * per_peer] = far_ref[:, start + per_peer : start + 2 * per_peer]
    slots_ref[0, :, (peers // 2 - 1) * per_peer :] = own_columns
    slots_ref[1, :, :per_peer] = near_columns
    send_near(values_ref[...], edge_ref, near_ref, back_ref, stay_ref)
    operator = operator_ref[0]
    for half in range(2):
        placed_ref[half] = jnp.dot(
            operator, slots_ref[half], preferred_element_type=jnp.float32
        ).astype(operator.dtype)


def first_half_kernel(placed_ref, stay_ref, back_ref, *refs):
    *pair_refs, jump_ref, image_ref = refs
    sent_refs, got_refs = pair_refs[: len(pair_refs) // 2], pair_refs[len(pair_refs) // 2 :]
    loads = stay_ref.shape[0] - GROUP
    groups = (jump_ref.shape[0] - loads) // GROUP
    own, got = (spread(straight(*refs), loads, groups) for refs in ((stay_ref, sent_refs), (back_ref, got_refs)))
    jump_ref[...] = own - got
    image_ref[...] = split_dot(own - got, placed_ref[0], NT)


def first_kernel(far_ref, placed_ref, half_ref, got_ref, near_ref, *refs):
    sent_refs, (jump_ref, image_ref, *pair_refs) = refs[: len(refs) // 2 - 1], refs[len(refs) // 2 - 1 :]
    height = near_ref.shape[0]
    loads = height - GROUP
    groups = (image_ref.shape[0] - loads) // GROUP
    own, got = (spread(value, loads, groups) for value in (for_other(near_ref, sent_refs), handed(got_ref, height)))
    jump_ref[...] = own - got
    image = half_ref[...] + split_dot(own - got, placed_ref[1], NT)
    image_ref[...] = image
    send_far(image, far_ref, *pair_refs)


def products_of(left, right):
    both = lax.dot_general(split(left), split(right), NT, preferred_element_type=jnp.float32)
    both = both[: left.shape[0]] + both[left.shape[0] :]
    return both + pltpu.roll(both, right.shape[0], 1)


def with_scalars(top, products, lanes):
    lane = lax.broadcasted_iota(jnp.int32, top.shape, 1)
    for at, product in zip(lanes, products):
        top = jnp.where(lane == at, jnp.sum(product, axis=1, keepdims=True), top)
    return top


def middle_kernel(
    edge_ref, slots_ref, straight_ref, handed_ref, image_ref, basis_ref, terms_ref, near_ref, back_ref, stay_ref
):
    image = image_ref[...]
    send_near(image, edge_ref, near_ref, back_ref, stay_ref)
    coarse = terms_ref.shape[1] // 8
    loads = image.shape[0] - coarse
    basis = split_dot(straight_ref[...], slots_ref[0], NT) + split_dot(handed_ref[...], slots_ref[1], NT)
    basis_ref[...] = basis
    left = jnp.concatenate([basis[:loads], image[:loads], basis[loads:]])
    empty = jnp.zeros((2 * coarse, basis.shape[1]), jnp.float32)
    both = products_of(left, jnp.concatenate([basis[loads:], image[loads:], empty]))
    strip = lax.broadcasted_iota(jnp.int32, (loads, 8 * coarse), 1) // coarse
    top = jnp.where(strip < 2, both[:loads], 0.0)
    top = jnp.where(strip == 4, both[loads : 2 * loads], top)
    residual = basis[:loads]
    terms_ref[:loads] = with_scalars(top, (residual * residual, residual * image[:loads]), SCALAR_LANES[:2])
    strip = lax.broadcasted_iota(jnp.int32, (coarse, 8 * coarse), 1) // coarse
    terms_ref[loads:] = jnp.where(strip < 2, both[2 * loads :], 0.0)


def second_half_kernel(slots_ref, placed_ref, stay_ref, back_ref, *refs):
    *pair_refs, jump_ref, second_ref = refs
    sent_refs, got_refs = pair_refs[: len(pair_refs) // 2], pair_refs[len(pair_refs) // 2 :]
    jump = straight(stay_ref, sent_refs) - straight(back_ref, got_refs)
    jump_ref[...] = split_dot(jump, slots_ref[0], NT)
    second_ref[...] = split_dot(jump, placed_ref[0], NT)


def second_kernel(slots_ref, placed_ref, basis_ref, half_jump_ref, half_second_ref, early_ref, got_ref, near_ref, *refs):
    *sent_refs, jump_ref, terms_ref = refs
    coarse = terms_ref.shape[1] // 8
    loads = basis_ref.shape[0] - coarse
    jump = for_other(near_ref, sent_refs) - handed(got_ref, loads + coarse)
    second = half_second_ref[...] + split_dot(jump, placed_ref[1], NT)
    jump = half_jump_ref[...] + split_dot(jump, slots_ref[1], NT)
    jump_ref[...] = jump
    basis = basis_ref[...]
    left = jnp.concatenate([basis[:loads], jump[:loads], second[:loads], basis[loads:], jump[loads:]])
    empty = jnp.zeros((coarse, basis.shape[1]), jnp.float32)
    both = products_of(left, jnp.concatenate([basis[loads:], empty, jump[loads:], second[loads:]]))
    along, jumped, doubled = (both[at * loads : (at + 1) * loads] for at in range(3))
    base, far = both[3 * loads : 3 * loads + coarse], both[3 * loads + coarse :]
    strip = lax.broadcasted_iota(jnp.int32, (loads, 8 * coarse), 1) // coarse
    top = jnp.where(strip == 2, doubled, 0.0)
    top = jnp.where(strip == 3, along, top)
    top = jnp.where(strip == 5, pltpu.roll(doubled, coarse, 1), top)
    top = jnp.where(strip >= 6, jumped, top)
    residual, jump_loads, second_loads = basis[:loads], jump[:loads], second[:loads]
    products = (jump_loads * jump_loads, jump_loads * second_loads, residual * second_loads)
    terms_ref[:loads] = early_ref[:loads] + with_scalars(top, products, SCALAR_LANES[2:])
    strip = lax.broadcasted_iota(jnp.int32, (coarse, 8 * coarse), 1) // coarse
    base = jnp.where((strip == 2) | (strip == 3), base, 0.0)
    terms_ref[loads:] = early_ref[loads:] + jnp.where(strip < 4, base, far)


def sum_kernel(count, *refs):
    parts = [ref[...] for ref in reversed(refs[:count])]
    while len(parts) > 1:
        parts = [low + high for low, high in zip(parts[::2], parts[1::2])]
    for ref in refs[count:]:
        ref[...] = parts[0]


def eliminate(work, coarse):
    row = lax.broadcasted_iota(jnp.int32, work.shape, 0)
    for start in range(0, coarse, GROUP):
        pivots = range(start, start + MODES)
        columns = [jnp.broadcast_to(work[:, pivot : pivot + 1], work.shape) for pivot in pivots]
        square = [[column[pivot : pivot + 1] for column in columns] for pivot in pivots]
        rows = [work[pivot : pivot + 1] for pivot in pivots]
        for at in range(MODES):
            scale = 1.0 / square[at][at]
            rows[at] = rows[at] * scale
            square[at] = [value * scale for value in square[at]]
            for other in range(MODES):
                if other != at:
                    factor = square[other][at]
                    rows[other] = rows[other] - factor * rows[at]
                    square[other] = [
                        value if to <= at else value - factor * square[at][to]
                        for to, value in enumerate(square[other])
                    ]
        for column, solved in zip(columns, rows):
            work = work - column * solved
        for pivot, solved in zip(pivots, rows):
            work = jnp.where(row == pivot, solved, work)
    return work


def thin_dot(left, right):
    high, right_high = (value.astype(jnp.bfloat16).astype(jnp.float32) for value in (left, right))
    return jnp.dot(
        jnp.concatenate([high, left - high, high], axis=1).astype(jnp.bfloat16),
        jnp.concatenate([right_high, right_high, right - right_high], axis=0).astype(jnp.bfloat16),
        preferred_element_type=jnp.float32,
    )


def final_kernel(terms_ref, basis_ref, jump_ref, multipliers_ref, amplitudes_ref):
    coarse = terms_ref.shape[1] // 8
    loads = basis_ref.shape[0] - coarse
    groups = coarse // GROUP
    by_load = terms_ref[:loads].T
    used = lax.broadcasted_iota(jnp.int32, (coarse, loads), 0) % GROUP < MODES

    def strip(at):
        return by_load[at * coarse : (at + 1) * coarse]

    def block(at):
        return terms_ref[loads:, at * coarse : (at + 1) * coarse]

    def total(values):
        return jnp.sum(values, axis=0, keepdims=True)

    res_res, res_image, jump_jump, jump_second, res_second = (by_load[at : at + 1] for at in SCALAR_LANES)
    coarse_res, res_h = (jnp.where(used, strip(at), 0.0) for at in (0, 1))
    second_z, res_dz, image_g, second_g, jump_z, jump_dz = (strip(at) for at in range(2, 8))
    g_h, g_dz, z_z, z_dz = block(1), block(3), block(6), block(7)
    row = lax.broadcasted_iota(jnp.int32, (coarse, coarse), 0)
    unit = jnp.where(row == lax.broadcasted_iota(jnp.int32, (coarse, coarse), 1), 1.0, 0.0)
    empty = jnp.zeros((coarse, 5 * coarse - 2 * loads), jnp.float32)
    solved = eliminate(
        jnp.concatenate([terms_ref[loads:, : 2 * coarse], coarse_res, image_g, unit, empty], axis=1), coarse
    )
    inverse_h = solved[:, coarse : 2 * coarse]
    amounts = solved[:, 2 * coarse : 2 * coarse + loads]
    inverse_image = solved[:, 2 * coarse + loads : 2 * coarse + 2 * loads]
    inverse = solved[:, 2 * coarse + 2 * loads : 3 * coarse + 2 * loads]
    products = small_dot(jnp.concatenate([inverse_h, g_h, z_z, g_dz, z_dz], axis=0), amounts)
    inverse_h_amounts, h_amounts, z_amounts, g_dz_amounts, z_dz_amounts = (
        products[at * coarse : (at + 1) * coarse] for at in range(5)
    )
    shares = 2.0 * (inverse_image - inverse_h_amounts)
    both = jnp.concatenate([amounts, shares], axis=0).T
    basis_g, jump_z_rows = basis_ref[loads:], jump_ref[loads:]
    d = basis_ref[:loads] - thin_dot(both[:, :coarse], basis_g)
    u = jump_ref[:loads] - thin_dot(both, jnp.concatenate([jump_z_rows, basis_g], axis=0))
    products = small_dot(jnp.concatenate([g_h, z_z], axis=0), shares)
    image_d = image_g - h_amounts
    inner = res_res - total(amounts * coarse_res)
    curvature = 2.0 * (res_image - total(amounts * (res_h + image_d)))
    u_u = jump_jump - total(amounts * (2.0 * jump_z - z_amounts) + 2.0 * image_d * shares)
    second_u = second_g - g_dz_amounts - products[:coarse]
    jump_u = second_z - z_dz_amounts - 0.5 * products[coarse:]
    d_second = res_second - total(amounts * (res_dz + second_u) + shares * res_h)
    u_second = jump_second - total(amounts * (jump_dz + jump_u) + shares * (0.5 * jump_z + second_u))
    step = inner / curvature
    renewed = step * step * u_u - inner
    grown = 1.0 + renewed / inner
    curvature = grown * grown * curvature - grown * step * (2.0 * d_second + u_u) + 2.0 * step * step * u_second
    second_step = renewed / curvature
    on_d, on_u = step + second_step * grown, second_step * step
    amplitudes = amounts - on_d * shares + 2.0 * on_u * small_dot(inverse, second_u)
    amplitudes_ref[...] = jnp.concatenate(
        [amplitudes[label * GROUP : label * GROUP + MODES] for label in range(groups)], axis=0
    )
    weights = jnp.concatenate([on_d, on_u, jnp.zeros((6, loads), jnp.float32)], axis=0).T
    multipliers_ref[...] = weights[:, 0:1] * d - weights[:, 1:2] * u


def call(kernel, shapes, in_specs, name, scratch=(), flops=0):
    return pl.pallas_call(
        kernel,
        out_shape=[jax.ShapeDtypeStruct(*shape) for shape in shapes],
        in_specs=in_specs,
        out_specs=[VMEM] * len(shapes),
        scratch_shapes=scratch,
        compiler_params=pltpu.CompilerParams(vmem_limit_bytes=24 * 1024 * 1024),
        cost_estimate=pl.CostEstimate(flops=flops, bytes_accessed=2**20, transcendentals=0),
        name=name,
    )


def permute(values, offset, plane_offset=0):
    peers, planes = lax.axis_size("sub"), lax.axis_size("rep")
    offset = offset * planes + plane_offset
    return lax.ppermute(values, ("sub", "rep"), [(at, at ^ offset) for at in range(peers * planes)])


def to_chips(*pairs):
    return [permute(pair, 2 * (len(pairs) - at) + 1) for at, pair in enumerate(pairs)]


def to_core(near, *pairs):
    return permute(jnp.concatenate([near, *(pair[near.shape[0] :] for pair in pairs)], axis=0), 1)


def total(terms):
    chips = [(offset + 1, 0) for offset in reversed(range(2, lax.axis_size("sub"), 2))]
    chips = chips[-1:] + chips[:-1]
    planes = [(1, offset) for offset in reversed(range(1, lax.axis_size("rep")))]
    copies = [terms]
    for offsets, following in (([(1, 0)], len(chips)), (chips, len(planes)), (planes, 1)):
        parts = [permute(copy, *offset) for copy, offset in zip(copies, offsets)]
        kernel = functools.partial(sum_kernel, len(parts) + 1)
        copies = call(kernel, [(terms.shape, terms.dtype)] * following, [VMEM] * (len(parts) + 1), "sum")(
            *parts, copies[0]
        )
    return copies[0]


def fused_body(dual_ops, mode_traces, route, mode_block, local_gap):
    peers = lax.axis_size("sub")
    loads, rows = local_gap.shape
    modes = mode_traces.shape[1]
    subs = mode_block.shape[0]
    groups = subs // AGG_SUBS
    per_peer = rows // peers
    height = loads + GROUP * groups
    f32, i32 = jnp.float32, jnp.int32
    tall = ((height, rows), f32)
    wide = ((height, 8 * GROUP * groups), f32)

    def pairs(height):
        return [((2 * height, per_peer), f32)] * (peers // 2 - 1)

    def singles(height):
        return [((height, per_peer), f32)] * 3

    def held(value):
        return pltpu.with_memory_space_constraint(value, pltpu.HBM)

    inputs = [route, mode_block.reshape(1, subs), local_gap, mode_traces.transpose(1, 0, 2), dual_ops]
    short = loads + GROUP
    far, values, operator, route, *send = call(
        place_kernel,
        [
            ((rows, rows - 2 * per_peer), jnp.bfloat16),
            ((short, rows), f32),
            (dual_ops.shape, dual_ops.dtype),
            (route.shape, i32),
            *pairs(short),
        ],
        [HBM] * 5,
        "place",
        [pltpu.VMEM((1, subs), i32), pltpu.VMEM((modes, 1, rows), f32), pltpu.SemaphoreType.DMA((5,))],
    )(*(held(value) for value in inputs))
    got = to_chips(*send)
    halves = ((2, rows, rows // 2), dual_ops.dtype)
    edge, slots, placed, near, back, stay = call(
        ready_kernel,
        [((rows, 3 * per_peer), jnp.bfloat16), halves, halves, *singles(short)],
        [VMEM] * 4,
        "ready",
        flops=2 * rows * rows * rows,
    )(route, far, values, operator)
    got_near = to_core(near, *got)
    half = ((height, rows // 2), f32)
    straight_jump, half_image = call(
        first_half_kernel, [half, tall], [VMEM] * (3 + 2 * len(got)), "first_half", flops=2 * rows * rows * height
    )(placed, stay, back, *send, *got)
    handed_jump, image, *image_send = call(
        first_kernel, [half, tall, *pairs(height)], [VMEM] * (5 + len(send)), "first"
    )(far, placed, half_image, got_near, near, *send)
    got = to_chips(*image_send)
    basis, terms, near, back, stay = call(
        middle_kernel, [tall, wide, *singles(height)], [VMEM] * 5, "middle", flops=4 * rows * rows * height
    )(edge, slots, straight_jump, handed_jump, image)
    got_near = to_core(near, *got)
    half_jump, half_second = call(
        second_half_kernel, [tall, tall], [VMEM] * (4 + 2 * len(got)), "second_half", flops=4 * rows * rows * height
    )(slots, placed, stay, back, *image_send, *got)
    jump, terms = call(second_kernel, [tall, wide], [VMEM] * (8 + len(got)), "second")(
        slots, placed, basis, half_jump, half_second, terms, got_near, near, *image_send
    )
    multipliers, amplitudes = call(
        final_kernel, [((loads, rows), f32), ((MODES * groups, loads), f32)], [VMEM] * 3, "final"
    )(total(terms), basis, jump)
    return multipliers, amplitudes.T


def general_body(dual_ops, mode_traces, route, mode_block, local_gap):
    own_index = lax.axis_index("sub")
    plane_index = lax.axis_index("rep")
    peer_count = lax.axis_size("sub")
    plane_count = lax.axis_size("rep")
    operator = dual_ops[0]
    traces = mode_traces[0]
    slot_rows = route[0]
    rows_here = operator.shape[0]
    load_cases = local_gap.shape[0]
    per_peer = rows_here // peer_count
    blocks = mode_block[:, 0]
    block_count = blocks.shape[0] // AGG_SUBS
    coarse = block_count * MODES
    positions = jnp.arange(rows_here, dtype=jnp.int32)
    inverse = jnp.zeros((rows_here,), jnp.int32).at[slot_rows].set(positions)
    slot_peer = positions // per_peer
    within = positions % per_peer
    flip_index = jnp.where(
        slot_peer == own_index, slot_peer * per_peer + per_peer - 1 - within, positions
    )
    peer_ids = jnp.arange(peer_count, dtype=jnp.int32)
    peer_blocks = blocks[peer_ids * plane_count + plane_index]
    own_block = blocks[own_index * plane_count + plane_index]
    labels = jnp.arange(block_count, dtype=jnp.int32)
    peer_onehot = (peer_blocks[:, None] == labels[None, :]).astype(jnp.float32)
    own_onehot = (labels == own_block).astype(jnp.float32)
    trace_slots = traces[:, slot_rows]
    receive_index = flip_index[inverse]

    def to_peers(values):
        return values[:, slot_rows]

    def from_peers(values):
        return values[:, inverse]

    gap_peers = to_peers(local_gap)
    got_traces = lax.all_to_all(trace_slots, "sub", split_axis=1, concat_axis=1, tiled=True)
    got_gap = lax.all_to_all(gap_peers, "sub", split_axis=1, concat_axis=1, tiled=True)
    partner_traces = got_traces[:, flip_index]
    residual = local_gap - got_gap[:, receive_index]
    own_gram = jnp.dot(traces, traces.T, precision=HIGHEST)
    paired = (trace_slots[:, None, :] * partner_traces[None, :, :]).reshape(
        MODES, MODES, peer_count, per_peer
    )
    cross_terms = jnp.sum(paired, axis=3)
    cross_blocks = jnp.einsum("klq,qb->kbl", cross_terms, peer_onehot, precision=HIGHEST)
    own_blocks = own_gram[:, None, :] * own_onehot[None, :, None]
    row_term = 2.0 * (own_blocks - cross_blocks).reshape(MODES, coarse)
    gram_term = (own_onehot[:, None, None] * row_term[None]).reshape(coarse, coarse)

    def coarse_term(values):
        own_part = 2.0 * jnp.dot(values, traces.T, precision=HIGHEST)
        return (own_part[:, None, :] * own_onehot[None, :, None]).reshape(load_cases, coarse)

    def expand(amounts):
        grouped = amounts.reshape(load_cases, block_count, MODES)
        own_amounts = lax.dynamic_index_in_dim(grouped, own_block, 1, keepdims=False)
        own_part = jnp.dot(own_amounts, traces, precision=HIGHEST)
        peer_amounts = jnp.einsum("qb,rbk->rkq", peer_onehot, grouped, precision=HIGHEST)
        spread = jnp.repeat(peer_amounts, per_peer, axis=2)
        peer_part = jnp.sum(spread * partner_traces[None, :, :], axis=1)
        return own_part - from_peers(peer_part)

    squares = jnp.sum(residual * residual, axis=1)
    gram_matrix, coarse_res, norm_res = lax.psum(
        (gram_term, coarse_term(residual), squares), ("sub", "rep")
    )
    factor = jnp.linalg.cholesky(gram_matrix)

    def solve_coarse(right):
        return jax.scipy.linalg.cho_solve((factor, True), right.T).T

    amplitudes = solve_coarse(coarse_res)
    projected = residual - expand(amplitudes)
    inner_sum = norm_res - jnp.sum(amplitudes * coarse_res, axis=1)
    direction = projected
    multipliers = jnp.zeros_like(residual)
    for iteration in range(ITERS):
        product = lax.dot_general(
            direction.astype(jnp.bfloat16),
            operator,
            (((1,), (1,)), ((), ())),
            preferred_element_type=jnp.float32,
        )
        got_product = lax.all_to_all(
            to_peers(product), "sub", split_axis=1, concat_axis=1, tiled=True
        )
        image_jump = product - got_product[:, receive_index]
        coarse_jump, jump_squares, residual_cross, curvature = lax.psum(
            (
                coarse_term(image_jump),
                jnp.sum(image_jump * image_jump, axis=1),
                jnp.sum(residual * image_jump, axis=1),
                jnp.sum(direction * image_jump, axis=1),
            ),
            ("sub", "rep"),
        )
        step_size = inner_sum / curvature
        multipliers = multipliers + step_size[:, None] * direction
        residual = residual - step_size[:, None] * image_jump
        coarse_res = coarse_res - step_size[:, None] * coarse_jump
        norm_res = (
            norm_res - 2.0 * step_size * residual_cross + step_size * step_size * jump_squares
        )
        amplitudes = solve_coarse(coarse_res)
        if iteration + 1 < ITERS:
            projected = residual - expand(amplitudes)
            renewed = norm_res - jnp.sum(amplitudes * coarse_res, axis=1)
            direction = projected + (renewed / inner_sum)[:, None] * direction
            inner_sum = renewed
    return (multipliers, amplitudes)


def fits(mesh, dual_ops, mode_block, local_gap):
    peers, planes = mesh.shape["sub"], mesh.shape["rep"]
    powers = all(size & (size - 1) == 0 for size in (peers, planes))
    whole = dual_ops.shape[1] % (128 * peers) == 0 and local_gap.shape[0] % 16 == 0
    return powers and whole and 8 * GROUP * (mode_block.shape[0] // AGG_SUBS) == 128


def solution(mesh):
    placed = (
        P(("sub", "rep"), None, None),
        P(("sub", "rep"), None, None),
        P(("sub", "rep"), None),
        P(),
        P(None, ("sub", "rep")),
    )

    def run(dual_ops, mode_traces, route, mode_block, local_gap):
        body = fused_body if fits(mesh, dual_ops, mode_block, local_gap) else general_body
        return jax.shard_map(
            body, mesh=mesh, in_specs=placed, out_specs=(P(None, ("sub", "rep")), P()), check_vma=False
        )(dual_ops, mode_traces, route, mode_block, local_gap)

    return run
```

```python
import functools

import jax
import jax.numpy as jnp
from jax import lax
from jax.experimental import pallas as pl
from jax.experimental.pallas import tpu as pltpu
from jax.sharding import PartitionSpec as P

MODES = 6
AGG_SUBS = 16
ITERS = 2
GROUP = 8
SCALAR_LANES = (MODES, MODES + 1, GROUP + MODES, GROUP + MODES + 1, 2 * GROUP + MODES)
OPERATOR_PARTS = 8

HIGHEST = lax.Precision.HIGHEST
VMEM = pl.BlockSpec(memory_space=pltpu.VMEM)
HBM = pl.BlockSpec(memory_space=pltpu.HBM)
NN = (((1,), (0,)), ((), ()))
NT = (((1,), (1,)), ((), ()))


def split(values):
    high = values.astype(jnp.bfloat16).astype(jnp.float32)
    return jnp.concatenate([high, values - high], axis=0).astype(jnp.bfloat16)


def split_dot(values, matrix, dims):
    rows = values.shape[0]
    both = lax.dot_general(split(values), matrix, dims, preferred_element_type=jnp.float32)
    return both[:rows] + both[rows:]


def send_far(values, far_ref, *pair_refs):
    height = values.shape[0]
    per_peer = pair_refs[0].shape[1]
    values = split(values)
    for at, ref in enumerate(pair_refs):
        columns = far_ref[:, 2 * at * per_peer : (2 * at + 2) * per_peer]
        slots = jnp.dot(values, columns, preferred_element_type=jnp.float32)
        slots = slots[:height] + slots[height:]
        ref[:height] = slots[:, :per_peer]
        ref[height:] = slots[:, per_peer:]


def send_near(values, edge_ref, near_ref, back_ref, stay_ref):
    per_peer = back_ref.shape[1]
    slots = split_dot(values, edge_ref[...], NN)
    for at, ref in enumerate((near_ref, back_ref, stay_ref)):
        ref[...] = slots[:, at * per_peer : (at + 1) * per_peer]


def straight(last_ref, pair_refs):
    height = last_ref.shape[0]
    return jnp.concatenate([*(ref[:height] for ref in pair_refs), last_ref[...]], axis=1)


def for_other(near_ref, pair_refs):
    height = near_ref.shape[0]
    return jnp.concatenate([near_ref[...], *(ref[height:] for ref in pair_refs)], axis=1)


def handed(got_ref, height):
    return jnp.concatenate([got_ref[at : at + height] for at in range(0, got_ref.shape[0], height)], axis=1)


def spread(values, loads, groups):
    modes = values[loads:]
    label = modes[MODES : MODES + 1]
    used = lax.broadcasted_iota(jnp.int32, modes.shape, 0) < MODES
    parts = [jnp.where(used & (label == group), modes, 0.0) for group in range(groups)]
    return jnp.concatenate([values[:loads], *parts], axis=0)


def one_hot(route_ref, peer, per_peer):
    start = pl.multiple_of(peer * per_peer, per_peer)
    row_ids = lax.broadcasted_iota(jnp.int32, (route_ref.shape[1], per_peer), 0)
    return jnp.where(row_ids == route_ref[:, pl.ds(start, per_peer)], 1.0, 0.0).astype(jnp.bfloat16)


def place_kernel(
    route_hbm, block_hbm, gap_hbm, traces_hbm, operator_hbm,
    far_ref, values_ref, operator_ref, route_ref, *refs,
):
    *pair_refs, block_ref, traces_ref, sems = refs
    loads, rows = gap_hbm.shape
    per_peer = pair_refs[0].shape[1]
    peers = rows // per_peer
    height = rows // OPERATOR_PARTS
    parts = [pl.ds(start, height) for start in range(0, rows, height)]
    copies = [
        pltpu.make_async_copy(source, target, sems.at[at])
        for at, (source, target) in enumerate(
            (
                (route_hbm, route_ref),
                (block_hbm, block_ref),
                (traces_hbm, traces_ref),
                (gap_hbm, values_ref.at[pl.ds(0, loads)]),
                *((operator_hbm.at[:, part], operator_ref.at[:, part]) for part in parts),
            )
        )
    ]

    def build(at):
        peer = own_index ^ (peers - 1 - at)
        far_ref[:, at * per_peer : (at + 1) * per_peer] = one_hot(route_ref, peer, per_peer)

    for copy in copies:
        copy.start()
    own_index = lax.axis_index("sub")
    device = own_index * lax.axis_size("rep") + lax.axis_index("rep")
    copies[0].wait()
    for at in range(peers - 4):
        build(at)
    copies[1].wait()
    copies[2].wait()
    blocks = block_ref[...]
    lane = lax.broadcasted_iota(jnp.int32, blocks.shape, 1)
    own_block = jnp.sum(jnp.where(lane == device, blocks, 0), axis=1, keepdims=True)
    modes = traces_ref.shape[0]
    label = jnp.broadcast_to(own_block.astype(jnp.float32), (1, rows))
    for mode in range(modes):
        values_ref[loads + mode : loads + mode + 1] = traces_ref[mode]
    values_ref[loads + modes : loads + modes + 1] = label
    values_ref[loads + modes + 1 :] = jnp.zeros((GROUP - modes - 1, rows), jnp.float32)
    copies[3].wait()
    for at in range(peers - 4, peers - 2):
        build(at)
    send_far(values_ref[...], far_ref, *pair_refs)
    for copy in copies[4:]:
        copy.wait()


def ready_kernel(
    route_ref, far_ref, values_ref, operator_ref,
    edge_ref, slots_ref, placed_ref, near_ref, back_ref, stay_ref,
):
    per_peer = back_ref.shape[1]
    peers = far_ref.shape[1] // per_peer + 2
    own_index = lax.axis_index("sub")
    low = lax.broadcasted_iota(jnp.int32, (per_peer, per_peer), 0)
    high = lax.broadcasted_iota(jnp.int32, (per_peer, per_peer), 1)
    reverse = jnp.where(low + high == per_peer - 1, 1.0, 0.0).astype(jnp.bfloat16)
    own_columns = one_hot(route_ref, own_index, per_peer)
    near_columns = one_hot(route_ref, own_index ^ 1, per_peer)
    reversed_columns = jnp.dot(own_columns, reverse, preferred_element_type=jnp.float32).astype(jnp.bfloat16)
    edge_ref[...] = jnp.concatenate([near_columns, reversed_columns, own_columns], axis=1)
    for at in range(peers // 2 - 1):
        start = 2 * at * per_peer
        slots_ref[0, :, at * per_peer : (at + 1) * per_peer] = far_ref[:, start : start + per_peer]
        slots_ref[1, :, (at + 1) * per_peer : (at + 2) * per_peer] = far_ref[:, start + per_peer : start + 2 * per_peer]
    slots_ref[0, :, (peers // 2 - 1) * per_peer :] = own_columns
    slots_ref[1, :, :per_peer] = near_columns
    send_near(values_ref[...], edge_ref, near_ref, back_ref, stay_ref)
    operator = operator_ref[0]
    for half in range(2):
        placed_ref[half] = jnp.dot(
            operator, slots_ref[half], preferred_element_type=jnp.float32
        ).astype(operator.dtype)


def first_half_kernel(placed_ref, stay_ref, back_ref, *refs):
    *pair_refs, jump_ref, image_ref = refs
    sent_refs, got_refs = pair_refs[: len(pair_refs) // 2], pair_refs[len(pair_refs) // 2 :]
    loads = stay_ref.shape[0] - GROUP
    groups = (jump_ref.shape[0] - loads) // GROUP
    own, got = (spread(straight(*refs), loads, groups) for refs in ((stay_ref, sent_refs), (back_ref, got_refs)))
    jump_ref[...] = own - got
    image_ref[...] = split_dot(own - got, placed_ref[0], NT)


def first_kernel(far_ref, placed_ref, half_ref, got_ref, near_ref, *refs):
    sent_refs, (jump_ref, image_ref, *pair_refs) = refs[: len(refs) // 2 - 1], refs[len(refs) // 2 - 1 :]
    height = near_ref.shape[0]
    loads = height - GROUP
    groups = (image_ref.shape[0] - loads) // GROUP
    own, got = (spread(value, loads, groups) for value in (for_other(near_ref, sent_refs), handed(got_ref, height)))
    jump_ref[...] = own - got
    image = half_ref[...] + split_dot(own - got, placed_ref[1], NT)
    image_ref[...] = image
    send_far(image, far_ref, *pair_refs)


def products_of(left, right):
    both = lax.dot_general(split(left), split(right), NT, preferred_element_type=jnp.float32)
    both = both[: left.shape[0]] + both[left.shape[0] :]
    return both + pltpu.roll(both, right.shape[0], 1)


def with_scalars(top, products, lanes):
    lane = lax.broadcasted_iota(jnp.int32, top.shape, 1)
    for at, product in zip(lanes, products):
        top = jnp.where(lane == at, jnp.sum(product, axis=1, keepdims=True), top)
    return top


def middle_kernel(
    edge_ref, slots_ref, straight_ref, handed_ref, image_ref, basis_ref, terms_ref, near_ref, back_ref, stay_ref
):
    image = image_ref[...]
    send_near(image, edge_ref, near_ref, back_ref, stay_ref)
    coarse = terms_ref.shape[1] // 8
    loads = image.shape[0] - coarse
    basis = split_dot(straight_ref[...], slots_ref[0], NT) + split_dot(handed_ref[...], slots_ref[1], NT)
    basis_ref[...] = basis
    left = jnp.concatenate([basis[:loads], image[:loads], basis[loads:]])
    empty = jnp.zeros((2 * coarse, basis.shape[1]), jnp.float32)
    both = products_of(left, jnp.concatenate([basis[loads:], image[loads:], empty]))
    strip = lax.broadcasted_iota(jnp.int32, (loads, 8 * coarse), 1) // coarse
    top = jnp.where(strip < 2, both[:loads], 0.0)
    top = jnp.where(strip == 4, both[loads : 2 * loads], top)
    residual = basis[:loads]
    terms_ref[:loads] = with_scalars(top, (residual * residual, residual * image[:loads]), SCALAR_LANES[:2])
    strip = lax.broadcasted_iota(jnp.int32, (coarse, 8 * coarse), 1) // coarse
    terms_ref[loads:] = jnp.where(strip < 2, both[2 * loads :], 0.0)


def second_half_kernel(slots_ref, placed_ref, stay_ref, back_ref, *refs):
    *pair_refs, jump_ref, second_ref = refs
    sent_refs, got_refs = pair_refs[: len(pair_refs) // 2], pair_refs[len(pair_refs) // 2 :]
    jump = straight(stay_ref, sent_refs) - straight(back_ref, got_refs)
    jump_ref[...] = split_dot(jump, slots_ref[0], NT)
    second_ref[...] = split_dot(jump, placed_ref[0], NT)


def second_kernel(slots_ref, placed_ref, basis_ref, half_jump_ref, half_second_ref, early_ref, got_ref, near_ref, *refs):
    *sent_refs, jump_ref, terms_ref = refs
    coarse = terms_ref.shape[1] // 8
    loads = basis_ref.shape[0] - coarse
    jump = for_other(near_ref, sent_refs) - handed(got_ref, loads + coarse)
    second = half_second_ref[...] + split_dot(jump, placed_ref[1], NT)
    jump = half_jump_ref[...] + split_dot(jump, slots_ref[1], NT)
    jump_ref[...] = jump
    basis = basis_ref[...]
    left = jnp.concatenate([basis[:loads], jump[:loads], second[:loads], basis[loads:], jump[loads:]])
    empty = jnp.zeros((coarse, basis.shape[1]), jnp.float32)
    both = products_of(left, jnp.concatenate([basis[loads:], empty, jump[loads:], second[loads:]]))
    along, jumped, doubled = (both[at * loads : (at + 1) * loads] for at in range(3))
    base, far = both[3 * loads : 3 * loads + coarse], both[3 * loads + coarse :]
    strip = lax.broadcasted_iota(jnp.int32, (loads, 8 * coarse), 1) // coarse
    top = jnp.where(strip == 2, doubled, 0.0)
    top = jnp.where(strip == 3, along, top)
    top = jnp.where(strip == 5, pltpu.roll(doubled, coarse, 1), top)
    top = jnp.where(strip >= 6, jumped, top)
    residual, jump_loads, second_loads = basis[:loads], jump[:loads], second[:loads]
    products = (jump_loads * jump_loads, jump_loads * second_loads, residual * second_loads)
    terms_ref[:loads] = early_ref[:loads] + with_scalars(top, products, SCALAR_LANES[2:])
    strip = lax.broadcasted_iota(jnp.int32, (coarse, 8 * coarse), 1) // coarse
    base = jnp.where((strip == 2) | (strip == 3), base, 0.0)
    terms_ref[loads:] = early_ref[loads:] + jnp.where(strip < 4, base, far)


def sum_kernel(count, *refs):
    parts = [ref[...] for ref in reversed(refs[:count])]
    while len(parts) > 1:
        parts = [low + high for low, high in zip(parts[::2], parts[1::2])]
    for ref in refs[count:]:
        ref[...] = parts[0]


def eliminate(work, coarse):
    row = lax.broadcasted_iota(jnp.int32, work.shape, 0)
    for start in range(0, coarse, GROUP):
        pivots = range(start, start + MODES)
        columns = [jnp.broadcast_to(work[:, pivot : pivot + 1], work.shape) for pivot in pivots]
        square = [[column[pivot : pivot + 1] for column in columns] for pivot in pivots]
        rows = [work[pivot : pivot + 1] for pivot in pivots]
        for at in range(MODES):
            scale = 1.0 / square[at][at]
            rows[at] = rows[at] * scale
            square[at] = [value * scale for value in square[at]]
            for other in range(MODES):
                if other != at:
                    factor = square[other][at]
                    rows[other] = rows[other] - factor * rows[at]
                    square[other] = [
                        value if to <= at else value - factor * square[at][to]
                        for to, value in enumerate(square[other])
                    ]
        for column, solved in zip(columns, rows):
            work = work - column * solved
        for pivot, solved in zip(pivots, rows):
            work = jnp.where(row == pivot, solved, work)
    return work


def thin_dot(left, right):
    high, right_high = (value.astype(jnp.bfloat16).astype(jnp.float32) for value in (left, right))
    return jnp.dot(
        jnp.concatenate([high, left - high, high], axis=1).astype(jnp.bfloat16),
        jnp.concatenate([right_high, right_high, right - right_high], axis=0).astype(jnp.bfloat16),
        preferred_element_type=jnp.float32,
    )


def final_kernel(terms_ref, basis_ref, jump_ref, multipliers_ref, amplitudes_ref):
    coarse = terms_ref.shape[1] // 8
    loads = basis_ref.shape[0] - coarse
    groups = coarse // GROUP
    by_load = terms_ref[:loads].T
    used = lax.broadcasted_iota(jnp.int32, (coarse, loads), 0) % GROUP < MODES

    def strip(at):
        return by_load[at * coarse : (at + 1) * coarse]

    def block(at):
        return terms_ref[loads:, at * coarse : (at + 1) * coarse]

    def total(values):
        return jnp.sum(values, axis=0, keepdims=True)

    res_res, res_image, jump_jump, jump_second, res_second = (by_load[at : at + 1] for at in SCALAR_LANES)
    coarse_res, res_h = (jnp.where(used, strip(at), 0.0) for at in (0, 1))
    second_z, res_dz, image_g, second_g, jump_z, jump_dz = (strip(at) for at in range(2, 8))
    g_h, g_dz, z_z, z_dz = block(1), block(3), block(6), block(7)
    row = lax.broadcasted_iota(jnp.int32, (coarse, coarse), 0)
    unit = jnp.where(row == lax.broadcasted_iota(jnp.int32, (coarse, coarse), 1), 1.0, 0.0)
    empty = jnp.zeros((coarse, 5 * coarse - 2 * loads), jnp.float32)
    solved = eliminate(
        jnp.concatenate([terms_ref[loads:, : 2 * coarse], coarse_res, image_g, unit, empty], axis=1), coarse
    )
    inverse_h = solved[:, coarse : 2 * coarse]
    amounts = solved[:, 2 * coarse : 2 * coarse + loads]
    inverse_image = solved[:, 2 * coarse + loads : 2 * coarse + 2 * loads]
    inverse = solved[:, 2 * coarse + 2 * loads : 3 * coarse + 2 * loads]
    products = thin_dot(jnp.concatenate([inverse_h, g_h, z_z, g_dz, z_dz], axis=0), amounts)
    inverse_h_amounts, h_amounts, z_amounts, g_dz_amounts, z_dz_amounts = (
        products[at * coarse : (at + 1) * coarse] for at in range(5)
    )
    shares = 2.0 * (inverse_image - inverse_h_amounts)
    both = jnp.concatenate([amounts, shares], axis=0).T
    basis_g, jump_z_rows = basis_ref[loads:], jump_ref[loads:]
    d = basis_ref[:loads] - thin_dot(both[:, :coarse], basis_g)
    u = jump_ref[:loads] - thin_dot(both, jnp.concatenate([jump_z_rows, basis_g], axis=0))
    products = thin_dot(jnp.concatenate([g_h, z_z], axis=0), shares)
    image_d = image_g - h_amounts
    inner = res_res - total(amounts * coarse_res)
    curvature = 2.0 * (res_image - total(amounts * (res_h + image_d)))
    u_u = jump_jump - total(amounts * (2.0 * jump_z - z_amounts) + 2.0 * image_d * shares)
    second_u = second_g - g_dz_amounts - products[:coarse]
    jump_u = second_z - z_dz_amounts - 0.5 * products[coarse:]
    d_second = res_second - total(amounts * (res_dz + second_u) + shares * res_h)
    u_second = jump_second - total(amounts * (jump_dz + jump_u) + shares * (0.5 * jump_z + second_u))
    step = inner / curvature
    renewed = step * step * u_u - inner
    grown = 1.0 + renewed / inner
    curvature = grown * grown * curvature - grown * step * (2.0 * d_second + u_u) + 2.0 * step * step * u_second
    second_step = renewed / curvature
    on_d, on_u = step + second_step * grown, second_step * step
    amplitudes = amounts - on_d * shares + 2.0 * on_u * thin_dot(inverse, second_u)
    amplitudes_ref[...] = jnp.concatenate(
        [amplitudes[label * GROUP : label * GROUP + MODES] for label in range(groups)], axis=0
    )
    weights = jnp.concatenate([on_d, on_u, jnp.zeros((6, loads), jnp.float32)], axis=0).T
    multipliers_ref[...] = weights[:, 0:1] * d - weights[:, 1:2] * u


def call(kernel, shapes, in_specs, name, scratch=(), flops=0):
    return pl.pallas_call(
        kernel,
        out_shape=[jax.ShapeDtypeStruct(*shape) for shape in shapes],
        in_specs=in_specs,
        out_specs=[VMEM] * len(shapes),
        scratch_shapes=scratch,
        compiler_params=pltpu.CompilerParams(vmem_limit_bytes=24 * 1024 * 1024),
        cost_estimate=pl.CostEstimate(flops=flops, bytes_accessed=2**20, transcendentals=0),
        name=name,
    )


def permute(values, offset, plane_offset=0):
    peers, planes = lax.axis_size("sub"), lax.axis_size("rep")
    offset = offset * planes + plane_offset
    return lax.ppermute(values, ("sub", "rep"), [(at, at ^ offset) for at in range(peers * planes)])


def to_chips(*pairs):
    return [permute(pair, 2 * (len(pairs) - at) + 1) for at, pair in enumerate(pairs)]


def to_core(near, *pairs):
    return permute(jnp.concatenate([near, *(pair[near.shape[0] :] for pair in pairs)], axis=0), 1)


def total(terms):
    chips = [(offset + 1, 0) for offset in reversed(range(2, lax.axis_size("sub"), 2))]
    chips = chips[-1:] + chips[:-1]
    planes = [(1, offset) for offset in reversed(range(1, lax.axis_size("rep")))]
    copies = [terms]
    for offsets, following in (([(1, 0)], len(chips)), (chips, len(planes)), (planes, 1)):
        parts = [permute(copy, *offset) for copy, offset in zip(copies, offsets)]
        kernel = functools.partial(sum_kernel, len(parts) + 1)
        copies = call(kernel, [(terms.shape, terms.dtype)] * following, [VMEM] * (len(parts) + 1), "sum")(
            *parts, copies[0]
        )
    return copies[0]


def fused_body(dual_ops, mode_traces, route, mode_block, local_gap):
    peers = lax.axis_size("sub")
    loads, rows = local_gap.shape
    modes = mode_traces.shape[1]
    subs = mode_block.shape[0]
    groups = subs // AGG_SUBS
    per_peer = rows // peers
    height = loads + GROUP * groups
    f32, i32 = jnp.float32, jnp.int32
    tall = ((height, rows), f32)
    wide = ((height, 8 * GROUP * groups), f32)

    def pairs(height):
        return [((2 * height, per_peer), f32)] * (peers // 2 - 1)

    def singles(height):
        return [((height, per_peer), f32)] * 3

    def held(value):
        return pltpu.with_memory_space_constraint(value, pltpu.HBM)

    inputs = [route, mode_block.reshape(1, subs), local_gap, mode_traces.transpose(1, 0, 2), dual_ops]
    short = loads + GROUP
    far, values, operator, route, *send = call(
        place_kernel,
        [
            ((rows, rows - 2 * per_peer), jnp.bfloat16),
            ((short, rows), f32),
            (dual_ops.shape, dual_ops.dtype),
            (route.shape, i32),
            *pairs(short),
        ],
        [HBM] * 5,
        "place",
        [pltpu.VMEM((1, subs), i32), pltpu.VMEM((modes, 1, rows), f32), pltpu.SemaphoreType.DMA((4 + OPERATOR_PARTS,))],
    )(*(held(value) for value in inputs))
    got = to_chips(*send)
    halves = ((2, rows, rows // 2), dual_ops.dtype)
    edge, slots, placed, near, back, stay = call(
        ready_kernel,
        [((rows, 3 * per_peer), jnp.bfloat16), halves, halves, *singles(short)],
        [VMEM] * 4,
        "ready",
        flops=2 * rows * rows * rows,
    )(route, far, values, operator)
    got_near = to_core(near, *got)
    half = ((height, rows // 2), f32)
    straight_jump, half_image = call(
        first_half_kernel, [half, tall], [VMEM] * (3 + 2 * len(got)), "first_half", flops=2 * rows * rows * height
    )(placed, stay, back, *send, *got)
    handed_jump, image, *image_send = call(
        first_kernel, [half, tall, *pairs(height)], [VMEM] * (5 + len(send)), "first"
    )(far, placed, half_image, got_near, near, *send)
    got = to_chips(*image_send)
    basis, terms, near, back, stay = call(
        middle_kernel, [tall, wide, *singles(height)], [VMEM] * 5, "middle", flops=4 * rows * rows * height
    )(edge, slots, straight_jump, handed_jump, image)
    got_near = to_core(near, *got)
    half_jump, half_second = call(
        second_half_kernel, [tall, tall], [VMEM] * (4 + 2 * len(got)), "second_half", flops=4 * rows * rows * height
    )(slots, placed, stay, back, *image_send, *got)
    jump, terms = call(second_kernel, [tall, wide], [VMEM] * (8 + len(got)), "second")(
        slots, placed, basis, half_jump, half_second, terms, got_near, near, *image_send
    )
    multipliers, amplitudes = call(
        final_kernel, [((loads, rows), f32), ((MODES * groups, loads), f32)], [VMEM] * 3, "final"
    )(total(terms), basis, jump)
    return multipliers, amplitudes.T


def general_body(dual_ops, mode_traces, route, mode_block, local_gap):
    own_index = lax.axis_index("sub")
    plane_index = lax.axis_index("rep")
    peer_count = lax.axis_size("sub")
    plane_count = lax.axis_size("rep")
    operator = dual_ops[0]
    traces = mode_traces[0]
    slot_rows = route[0]
    rows_here = operator.shape[0]
    load_cases = local_gap.shape[0]
    per_peer = rows_here // peer_count
    blocks = mode_block[:, 0]
    block_count = blocks.shape[0] // AGG_SUBS
    coarse = block_count * MODES
    positions = jnp.arange(rows_here, dtype=jnp.int32)
    inverse = jnp.zeros((rows_here,), jnp.int32).at[slot_rows].set(positions)
    slot_peer = positions // per_peer
    within = positions % per_peer
    flip_index = jnp.where(
        slot_peer == own_index, slot_peer * per_peer + per_peer - 1 - within, positions
    )
    peer_ids = jnp.arange(peer_count, dtype=jnp.int32)
    peer_blocks = blocks[peer_ids * plane_count + plane_index]
    own_block = blocks[own_index * plane_count + plane_index]
    labels = jnp.arange(block_count, dtype=jnp.int32)
    peer_onehot = (peer_blocks[:, None] == labels[None, :]).astype(jnp.float32)
    own_onehot = (labels == own_block).astype(jnp.float32)
    trace_slots = traces[:, slot_rows]
    receive_index = flip_index[inverse]

    def to_peers(values):
        return values[:, slot_rows]

    def from_peers(values):
        return values[:, inverse]

    gap_peers = to_peers(local_gap)
    got_traces = lax.all_to_all(trace_slots, "sub", split_axis=1, concat_axis=1, tiled=True)
    got_gap = lax.all_to_all(gap_peers, "sub", split_axis=1, concat_axis=1, tiled=True)
    partner_traces = got_traces[:, flip_index]
    residual = local_gap - got_gap[:, receive_index]
    own_gram = jnp.dot(traces, traces.T, precision=HIGHEST)
    paired = (trace_slots[:, None, :] * partner_traces[None, :, :]).reshape(
        MODES, MODES, peer_count, per_peer
    )
    cross_terms = jnp.sum(paired, axis=3)
    cross_blocks = jnp.einsum("klq,qb->kbl", cross_terms, peer_onehot, precision=HIGHEST)
    own_blocks = own_gram[:, None, :] * own_onehot[None, :, None]
    row_term = 2.0 * (own_blocks - cross_blocks).reshape(MODES, coarse)
    gram_term = (own_onehot[:, None, None] * row_term[None]).reshape(coarse, coarse)

    def coarse_term(values):
        own_part = 2.0 * jnp.dot(values, traces.T, precision=HIGHEST)
        return (own_part[:, None, :] * own_onehot[None, :, None]).reshape(load_cases, coarse)

    def expand(amounts):
        grouped = amounts.reshape(load_cases, block_count, MODES)
        own_amounts = lax.dynamic_index_in_dim(grouped, own_block, 1, keepdims=False)
        own_part = jnp.dot(own_amounts, traces, precision=HIGHEST)
        peer_amounts = jnp.einsum("qb,rbk->rkq", peer_onehot, grouped, precision=HIGHEST)
        spread = jnp.repeat(peer_amounts, per_peer, axis=2)
        peer_part = jnp.sum(spread * partner_traces[None, :, :], axis=1)
        return own_part - from_peers(peer_part)

    squares = jnp.sum(residual * residual, axis=1)
    gram_matrix, coarse_res, norm_res = lax.psum(
        (gram_term, coarse_term(residual), squares), ("sub", "rep")
    )
    factor = jnp.linalg.cholesky(gram_matrix)

    def solve_coarse(right):
        return jax.scipy.linalg.cho_solve((factor, True), right.T).T

    amplitudes = solve_coarse(coarse_res)
    projected = residual - expand(amplitudes)
    inner_sum = norm_res - jnp.sum(amplitudes * coarse_res, axis=1)
    direction = projected
    multipliers = jnp.zeros_like(residual)
    for iteration in range(ITERS):
        product = lax.dot_general(
            direction.astype(jnp.bfloat16),
            operator,
            (((1,), (1,)), ((), ())),
            preferred_element_type=jnp.float32,
        )
        got_product = lax.all_to_all(
            to_peers(product), "sub", split_axis=1, concat_axis=1, tiled=True
        )
        image_jump = product - got_product[:, receive_index]
        coarse_jump, jump_squares, residual_cross, curvature = lax.psum(
            (
                coarse_term(image_jump),
                jnp.sum(image_jump * image_jump, axis=1),
                jnp.sum(residual * image_jump, axis=1),
                jnp.sum(direction * image_jump, axis=1),
            ),
            ("sub", "rep"),
        )
        step_size = inner_sum / curvature
        multipliers = multipliers + step_size[:, None] * direction
        residual = residual - step_size[:, None] * image_jump
        coarse_res = coarse_res - step_size[:, None] * coarse_jump
        norm_res = (
            norm_res - 2.0 * step_size * residual_cross + step_size * step_size * jump_squares
        )
        amplitudes = solve_coarse(coarse_res)
        if iteration + 1 < ITERS:
            projected = residual - expand(amplitudes)
            renewed = norm_res - jnp.sum(amplitudes * coarse_res, axis=1)
            direction = projected + (renewed / inner_sum)[:, None] * direction
            inner_sum = renewed
    return (multipliers, amplitudes)


def fits(mesh, dual_ops, mode_block, local_gap):
    peers, planes = mesh.shape["sub"], mesh.shape["rep"]
    powers = all(size & (size - 1) == 0 for size in (peers, planes))
    whole = dual_ops.shape[1] % (128 * peers) == 0 and local_gap.shape[0] % 16 == 0
    return powers and whole and 8 * GROUP * (mode_block.shape[0] // AGG_SUBS) == 128


def solution(mesh):
    placed = (
        P(("sub", "rep"), None, None),
        P(("sub", "rep"), None, None),
        P(("sub", "rep"), None),
        P(),
        P(None, ("sub", "rep")),
    )

    def run(dual_ops, mode_traces, route, mode_block, local_gap):
        body = fused_body if fits(mesh, dual_ops, mode_block, local_gap) else general_body
        return jax.shard_map(
            body, mesh=mesh, in_specs=placed, out_specs=(P(None, ("sub", "rep")), P()), check_vma=False
        )(dual_ops, mode_traces, route, mode_block, local_gap)

    return run
```

```python
import functools

import jax
import jax.numpy as jnp
from jax import lax
from jax.experimental import pallas as pl
from jax.experimental.pallas import tpu as pltpu
from jax.sharding import PartitionSpec as P

MODES = 6
AGG_SUBS = 16
ITERS = 2
GROUP = 8
SCALAR_LANES = (MODES, MODES + 1, GROUP + MODES, GROUP + MODES + 1, 2 * GROUP + MODES)
OPERATOR_PARTS = 8
FINAL_PARTS = 4
DIGIT = 32

HIGHEST = lax.Precision.HIGHEST
VMEM = pl.BlockSpec(memory_space=pltpu.VMEM)
HBM = pl.BlockSpec(memory_space=pltpu.HBM)
NN = (((1,), (0,)), ((), ()))
NT = (((1,), (1,)), ((), ()))


def split(values):
    high = values.astype(jnp.bfloat16).astype(jnp.float32)
    return jnp.concatenate([high, values - high], axis=0).astype(jnp.bfloat16)


def split_dot(values, matrix, dims):
    rows = values.shape[0]
    both = lax.dot_general(split(values), matrix, dims, preferred_element_type=jnp.float32)
    return both[:rows] + both[rows:]


def small_dot(left, right):
    return jnp.dot(left, right, precision=HIGHEST, preferred_element_type=jnp.float32)


def send_far(values, far_ref, *pair_refs):
    height = values.shape[0]
    per_peer = pair_refs[0].shape[1]
    values = split(values)
    for at, ref in enumerate(pair_refs):
        columns = far_ref[:, 2 * at * per_peer : (2 * at + 2) * per_peer]
        slots = jnp.dot(values, columns, preferred_element_type=jnp.float32)
        slots = slots[:height] + slots[height:]
        ref[:height] = slots[:, :per_peer]
        ref[height:] = slots[:, per_peer:]


def send_near(values, edge_ref, near_ref, back_ref, stay_ref):
    per_peer = back_ref.shape[1]
    slots = split_dot(values, edge_ref[...], NN)
    for at, ref in enumerate((near_ref, back_ref, stay_ref)):
        ref[...] = slots[:, at * per_peer : (at + 1) * per_peer]


def straight(last_ref, pair_refs):
    height = last_ref.shape[0]
    return jnp.concatenate([*(ref[:height] for ref in pair_refs), last_ref[...]], axis=1)


def for_other(near_ref, pair_refs):
    height = near_ref.shape[0]
    return jnp.concatenate([near_ref[...], *(ref[height:] for ref in pair_refs)], axis=1)


def handed(got_ref, height):
    return jnp.concatenate([got_ref[at : at + height] for at in range(0, got_ref.shape[0], height)], axis=1)


def spread(values, loads, groups):
    modes = values[loads:]
    label = modes[MODES : MODES + 1]
    used = lax.broadcasted_iota(jnp.int32, modes.shape, 0) < MODES
    parts = [jnp.where(used & (label == group), modes, 0.0) for group in range(groups)]
    return jnp.concatenate([values[:loads], *parts], axis=0)


def one_hot(route_ref, peer, per_peer):
    start = pl.multiple_of(peer * per_peer, per_peer)
    route = route_ref[:, pl.ds(start, per_peer)]
    shape = (DIGIT, per_peer)
    low, high = (
        jnp.broadcast_to(digit.astype(jnp.float32), shape).astype(jnp.bfloat16)
        for digit in (route % DIGIT, route // DIGIT)
    )
    row = lax.broadcasted_iota(jnp.int32, shape, 0).astype(jnp.float32).astype(jnp.bfloat16)
    zero = jnp.zeros(shape, jnp.bfloat16)
    match = jnp.where(low == row, jnp.ones(shape, jnp.bfloat16), zero)
    pieces = [jnp.where(high == piece, match, zero) for piece in range(route_ref.shape[1] // DIGIT)]
    return jnp.concatenate(pieces, axis=0)


def place_kernel(
    route_hbm, block_hbm, gap_hbm, traces_hbm, operator_hbm,
    far_ref, values_ref, operator_ref, route_ref, *refs,
):
    *pair_refs, block_ref, traces_ref, sems = refs
    loads, rows = gap_hbm.shape
    per_peer = pair_refs[0].shape[1]
    peers = rows // per_peer
    height = rows // OPERATOR_PARTS
    parts = [pl.ds(start, height) for start in range(0, rows, height)]
    copies = [
        pltpu.make_async_copy(source, target, sems.at[at])
        for at, (source, target) in enumerate(
            (
                (route_hbm, route_ref),
                (block_hbm, block_ref),
                (traces_hbm, traces_ref),
                (gap_hbm, values_ref.at[pl.ds(0, loads)]),
                *((operator_hbm.at[:, part], operator_ref.at[:, part]) for part in parts),
            )
        )
    ]

    def build(at):
        peer = own_index ^ (peers - 1 - at)
        far_ref[:, at * per_peer : (at + 1) * per_peer] = one_hot(route_ref, peer, per_peer)

    for copy in copies:
        copy.start()
    own_index = lax.axis_index("sub")
    device = own_index * lax.axis_size("rep") + lax.axis_index("rep")
    copies[0].wait()
    for at in range(peers - 4):
        build(at)
    copies[1].wait()
    copies[2].wait()
    blocks = block_ref[...]
    lane = lax.broadcasted_iota(jnp.int32, blocks.shape, 1)
    own_block = jnp.sum(jnp.where(lane == device, blocks, 0), axis=1, keepdims=True)
    modes = traces_ref.shape[0]
    label = jnp.broadcast_to(own_block.astype(jnp.float32), (1, rows))
    for mode in range(modes):
        values_ref[loads + mode : loads + mode + 1] = traces_ref[mode]
    values_ref[loads + modes : loads + modes + 1] = label
    values_ref[loads + modes + 1 :] = jnp.zeros((GROUP - modes - 1, rows), jnp.float32)
    copies[3].wait()
    for at in range(peers - 4, peers - 2):
        build(at)
    send_far(values_ref[...], far_ref, *pair_refs)
    for copy in copies[4:]:
        copy.wait()


def ready_kernel(
    route_ref, far_ref, values_ref, operator_ref,
    edge_ref, slots_ref, placed_ref, near_ref, back_ref, stay_ref,
):
    per_peer = back_ref.shape[1]
    peers = far_ref.shape[1] // per_peer + 2
    own_index = lax.axis_index("sub")
    low = lax.broadcasted_iota(jnp.int32, (per_peer, per_peer), 0)
    high = lax.broadcasted_iota(jnp.int32, (per_peer, per_peer), 1)
    reverse = jnp.where(low + high == per_peer - 1, 1.0, 0.0).astype(jnp.bfloat16)
    own_columns = one_hot(route_ref, own_index, per_peer)
    near_columns = one_hot(route_ref, own_index ^ 1, per_peer)
    reversed_columns = jnp.dot(own_columns, reverse, preferred_element_type=jnp.float32).astype(jnp.bfloat16)
    edge_ref[...] = jnp.concatenate([near_columns, reversed_columns, own_columns], axis=1)
    for at in range(peers // 2 - 1):
        start = 2 * at * per_peer
        slots_ref[0, :, at * per_peer : (at + 1) * per_peer] = far_ref[:, start : start + per_peer]
        slots_ref[1, :, (at + 1) * per_peer : (at + 2) * per_peer] = far_ref[:, start + per_peer : start + 2 * per_peer]
    slots_ref[0, :, (peers // 2 - 1) * per_peer :] = own_columns
    slots_ref[1, :, :per_peer] = near_columns
    send_near(values_ref[...], edge_ref, near_ref, back_ref, stay_ref)
    operator = operator_ref[0]
    for half in range(2):
        placed_ref[half] = jnp.dot(
            operator, slots_ref[half], preferred_element_type=jnp.float32
        ).astype(operator.dtype)


def first_half_kernel(placed_ref, stay_ref, back_ref, *refs):
    *pair_refs, jump_ref, image_ref = refs
    sent_refs, got_refs = pair_refs[: len(pair_refs) // 2], pair_refs[len(pair_refs) // 2 :]
    loads = stay_ref.shape[0] - GROUP
    groups = (jump_ref.shape[0] - loads) // GROUP
    own, got = (spread(straight(*refs), loads, groups) for refs in ((stay_ref, sent_refs), (back_ref, got_refs)))
    jump_ref[...] = own - got
    image_ref[...] = split_dot(own - got, placed_ref[0], NT)


def first_kernel(far_ref, placed_ref, half_ref, got_ref, near_ref, *refs):
    sent_refs, (jump_ref, image_ref, *pair_refs) = refs[: len(refs) // 2 - 1], refs[len(refs) // 2 - 1 :]
    height = near_ref.shape[0]
    loads = height - GROUP
    groups = (image_ref.shape[0] - loads) // GROUP
    own, got = (spread(value, loads, groups) for value in (for_other(near_ref, sent_refs), handed(got_ref, height)))
    jump_ref[...] = own - got
    image = half_ref[...] + split_dot(own - got, placed_ref[1], NT)
    image_ref[...] = image
    send_far(image, far_ref, *pair_refs)


def products_of(left, right):
    both = lax.dot_general(split(left), split(right), NT, preferred_element_type=jnp.float32)
    both = both[: left.shape[0]] + both[left.shape[0] :]
    return both + pltpu.roll(both, right.shape[0], 1)


def with_scalars(top, products, lanes):
    lane = lax.broadcasted_iota(jnp.int32, top.shape, 1)
    for at, product in zip(lanes, products):
        top = jnp.where(lane == at, jnp.sum(product, axis=1, keepdims=True), top)
    return top


def middle_kernel(
    edge_ref, slots_ref, straight_ref, handed_ref, image_ref, basis_ref, terms_ref, near_ref, back_ref, stay_ref
):
    image = image_ref[...]
    send_near(image, edge_ref, near_ref, back_ref, stay_ref)
    coarse = terms_ref.shape[1] // 8
    loads = image.shape[0] - coarse
    basis = split_dot(straight_ref[...], slots_ref[0], NT) + split_dot(handed_ref[...], slots_ref[1], NT)
    basis_ref[...] = basis
    left = jnp.concatenate([basis[:loads], image[:loads], basis[loads:]])
    empty = jnp.zeros((2 * coarse, basis.shape[1]), jnp.float32)
    both = products_of(left, jnp.concatenate([basis[loads:], image[loads:], empty]))
    strip = lax.broadcasted_iota(jnp.int32, (loads, 8 * coarse), 1) // coarse
    top = jnp.where(strip < 2, both[:loads], 0.0)
    top = jnp.where(strip == 4, both[loads : 2 * loads], top)
    residual = basis[:loads]
    terms_ref[:loads] = with_scalars(top, (residual * residual, residual * image[:loads]), SCALAR_LANES[:2])
    strip = lax.broadcasted_iota(jnp.int32, (coarse, 8 * coarse), 1) // coarse
    terms_ref[loads:] = jnp.where(strip < 2, both[2 * loads :], 0.0)


def second_half_kernel(slots_ref, placed_ref, stay_ref, back_ref, *refs):
    *pair_refs, jump_ref, second_ref = refs
    sent_refs, got_refs = pair_refs[: len(pair_refs) // 2], pair_refs[len(pair_refs) // 2 :]
    jump = straight(stay_ref, sent_refs) - straight(back_ref, got_refs)
    jump_ref[...] = split_dot(jump, slots_ref[0], NT)
    second_ref[...] = split_dot(jump, placed_ref[0], NT)


def second_kernel(slots_ref, placed_ref, basis_ref, half_jump_ref, half_second_ref, early_ref, got_ref, near_ref, *refs):
    *sent_refs, jump_ref, terms_ref = refs
    coarse = terms_ref.shape[1] // 8
    loads = basis_ref.shape[0] - coarse
    jump = for_other(near_ref, sent_refs) - handed(got_ref, loads + coarse)
    second = half_second_ref[...] + split_dot(jump, placed_ref[1], NT)
    jump = half_jump_ref[...] + split_dot(jump, slots_ref[1], NT)
    jump_ref[...] = jump
    basis = basis_ref[...]
    left = jnp.concatenate([basis[:loads], jump[:loads], second[:loads], basis[loads:], jump[loads:]])
    empty = jnp.zeros((coarse, basis.shape[1]), jnp.float32)
    both = products_of(left, jnp.concatenate([basis[loads:], empty, jump[loads:], second[loads:]]))
    along, jumped, doubled = (both[at * loads : (at + 1) * loads] for at in range(3))
    base, far = both[3 * loads : 3 * loads + coarse], both[3 * loads + coarse :]
    strip = lax.broadcasted_iota(jnp.int32, (loads, 8 * coarse), 1) // coarse
    top = jnp.where(strip == 2, doubled, 0.0)
    top = jnp.where(strip == 3, along, top)
    top = jnp.where(strip == 5, pltpu.roll(doubled, coarse, 1), top)
    top = jnp.where(strip >= 6, jumped, top)
    residual, jump_loads, second_loads = basis[:loads], jump[:loads], second[:loads]
    products = (jump_loads * jump_loads, jump_loads * second_loads, residual * second_loads)
    terms_ref[:loads] = early_ref[:loads] + with_scalars(top, products, SCALAR_LANES[2:])
    strip = lax.broadcasted_iota(jnp.int32, (coarse, 8 * coarse), 1) // coarse
    base = jnp.where((strip == 2) | (strip == 3), base, 0.0)
    terms_ref[loads:] = early_ref[loads:] + jnp.where(strip < 4, base, far)


def sum_kernel(count, *refs):
    parts = [ref[...] for ref in reversed(refs[:count])]
    while len(parts) > 1:
        parts = [low + high for low, high in zip(parts[::2], parts[1::2])]
    for ref in refs[count:]:
        ref[...] = parts[0]


def eliminate(work, coarse):
    row = lax.broadcasted_iota(jnp.int32, work.shape, 0)
    for start in range(0, coarse, GROUP):
        pivots = range(start, start + MODES)
        columns = [jnp.broadcast_to(work[:, pivot : pivot + 1], work.shape) for pivot in pivots]
        square = [[column[pivot : pivot + 1] for column in columns] for pivot in pivots]
        rows = [work[pivot : pivot + 1] for pivot in pivots]
        for at in range(MODES):
            scale = 1.0 / square[at][at]
            rows[at] = rows[at] * scale
            square[at] = [value * scale for value in square[at]]
            for other in range(MODES):
                if other != at:
                    factor = square[other][at]
                    rows[other] = rows[other] - factor * rows[at]
                    square[other] = [
                        value if to <= at else value - factor * square[at][to]
                        for to, value in enumerate(square[other])
                    ]
        for column, solved in zip(columns, rows):
            work = work - column * solved
        for pivot, solved in zip(pivots, rows):
            work = jnp.where(row == pivot, solved, work)
    return work


def thin_dot(left, right):
    high, right_high = (value.astype(jnp.bfloat16).astype(jnp.float32) for value in (left, right))
    return jnp.dot(
        jnp.concatenate([high, left - high, high], axis=1).astype(jnp.bfloat16),
        jnp.concatenate([right_high, right_high, right - right_high], axis=0).astype(jnp.bfloat16),
        preferred_element_type=jnp.float32,
    )


def final_kernel(
    terms_ref, basis_ref, jump_ref, multipliers_hbm, amplitudes_hbm, multipliers_ref, amplitudes_ref, sems
):
    coarse = terms_ref.shape[1] // 8
    loads = basis_ref.shape[0] - coarse
    groups = coarse // GROUP
    by_load = terms_ref[:loads].T
    used = lax.broadcasted_iota(jnp.int32, (coarse, loads), 0) % GROUP < MODES

    def strip(at):
        return by_load[at * coarse : (at + 1) * coarse]

    def block(at):
        return terms_ref[loads:, at * coarse : (at + 1) * coarse]

    def total(values):
        return jnp.sum(values, axis=0, keepdims=True)

    res_res, res_image, jump_jump, jump_second, res_second = (by_load[at : at + 1] for at in SCALAR_LANES)
    coarse_res, res_h = (jnp.where(used, strip(at), 0.0) for at in (0, 1))
    second_z, res_dz, image_g, second_g, jump_z, jump_dz = (strip(at) for at in range(2, 8))
    g_h, g_dz, z_z, z_dz = block(1), block(3), block(6), block(7)
    row = lax.broadcasted_iota(jnp.int32, (coarse, coarse), 0)
    unit = jnp.where(row == lax.broadcasted_iota(jnp.int32, (coarse, coarse), 1), 1.0, 0.0)
    empty = jnp.zeros((coarse, 5 * coarse - 2 * loads), jnp.float32)
    solved = eliminate(
        jnp.concatenate([terms_ref[loads:, : 2 * coarse], coarse_res, image_g, unit, empty], axis=1), coarse
    )
    inverse_h = solved[:, coarse : 2 * coarse]
    amounts = solved[:, 2 * coarse : 2 * coarse + loads]
    inverse_image = solved[:, 2 * coarse + loads : 2 * coarse + 2 * loads]
    inverse = solved[:, 2 * coarse + 2 * loads : 3 * coarse + 2 * loads]
    products = small_dot(jnp.concatenate([inverse_h, g_h, z_z, g_dz, z_dz], axis=0), amounts)
    inverse_h_amounts, h_amounts, z_amounts, g_dz_amounts, z_dz_amounts = (
        products[at * coarse : (at + 1) * coarse] for at in range(5)
    )
    shares = 2.0 * (inverse_image - inverse_h_amounts)
    both = jnp.concatenate([amounts, shares], axis=0).T
    basis_g, jump_z_rows = basis_ref[loads:], jump_ref[loads:]
    d = basis_ref[:loads] - thin_dot(both[:, :coarse], basis_g)
    u = jump_ref[:loads] - thin_dot(both, jnp.concatenate([jump_z_rows, basis_g], axis=0))
    products = small_dot(jnp.concatenate([g_h, z_z], axis=0), shares)
    image_d = image_g - h_amounts
    inner = res_res - total(amounts * coarse_res)
    curvature = 2.0 * (res_image - total(amounts * (res_h + image_d)))
    u_u = jump_jump - total(amounts * (2.0 * jump_z - z_amounts) + 2.0 * image_d * shares)
    second_u = second_g - g_dz_amounts - products[:coarse]
    jump_u = second_z - z_dz_amounts - 0.5 * products[coarse:]
    d_second = res_second - total(amounts * (res_dz + second_u) + shares * res_h)
    u_second = jump_second - total(amounts * (jump_dz + jump_u) + shares * (0.5 * jump_z + second_u))
    step = inner / curvature
    renewed = step * step * u_u - inner
    grown = 1.0 + renewed / inner
    curvature = grown * grown * curvature - grown * step * (2.0 * d_second + u_u) + 2.0 * step * step * u_second
    second_step = renewed / curvature
    on_d, on_u = step + second_step * grown, second_step * step
    amplitudes = amounts - on_d * shares + 2.0 * on_u * small_dot(inverse, second_u)
    amplitudes_ref[...] = jnp.concatenate(
        [amplitudes[label * GROUP : label * GROUP + MODES] for label in range(groups)], axis=0
    )
    copies = [pltpu.make_async_copy(amplitudes_ref, amplitudes_hbm, sems.at[0])]
    copies[0].start()
    weights = jnp.concatenate([on_d, on_u, jnp.zeros((6, loads), jnp.float32)], axis=0).T
    height = loads // FINAL_PARTS
    for part in range(FINAL_PARTS):
        rows = pl.ds(part * height, height)
        here = slice(part * height, (part + 1) * height)
        multipliers_ref[rows] = weights[here, 0:1] * d[here] - weights[here, 1:2] * u[here]
        copies.append(pltpu.make_async_copy(multipliers_ref.at[rows], multipliers_hbm.at[rows], sems.at[part + 1]))
        copies[-1].start()
    for copy in copies:
        copy.wait()


def call(kernel, shapes, in_specs, name, scratch=(), flops=0, out_spec=VMEM):
    return pl.pallas_call(
        kernel,
        out_shape=[jax.ShapeDtypeStruct(*shape) for shape in shapes],
        in_specs=in_specs,
        out_specs=[out_spec] * len(shapes),
        scratch_shapes=scratch,
        compiler_params=pltpu.CompilerParams(vmem_limit_bytes=24 * 1024 * 1024),
        cost_estimate=pl.CostEstimate(flops=flops, bytes_accessed=2**20, transcendentals=0),
        name=name,
    )


def permute(values, offset, plane_offset=0):
    peers, planes = lax.axis_size("sub"), lax.axis_size("rep")
    offset = offset * planes + plane_offset
    return lax.ppermute(values, ("sub", "rep"), [(at, at ^ offset) for at in range(peers * planes)])


def to_chips(*pairs):
    return [permute(pair, 2 * (len(pairs) - at) + 1) for at, pair in enumerate(pairs)]


def to_core(near, *pairs):
    return permute(jnp.concatenate([near, *(pair[near.shape[0] :] for pair in pairs)], axis=0), 1)


def total(terms):
    chips = [(offset + 1, 0) for offset in reversed(range(2, lax.axis_size("sub"), 2))]
    chips = chips[-1:] + chips[:-1]
    planes = [(1, offset) for offset in reversed(range(1, lax.axis_size("rep")))]
    copies = [terms]
    for offsets, following in (([(1, 0)], len(chips)), (chips, len(planes)), (planes, 1)):
        parts = [permute(copy, *offset) for copy, offset in zip(copies, offsets)]
        kernel = functools.partial(sum_kernel, len(parts) + 1)
        copies = call(kernel, [(terms.shape, terms.dtype)] * following, [VMEM] * (len(parts) + 1), "sum")(
            *parts, copies[0]
        )
    return copies[0]


def fused_body(dual_ops, mode_traces, route, mode_block, local_gap):
    peers = lax.axis_size("sub")
    loads, rows = local_gap.shape
    modes = mode_traces.shape[1]
    subs = mode_block.shape[0]
    groups = subs // AGG_SUBS
    per_peer = rows // peers
    height = loads + GROUP * groups
    f32, i32 = jnp.float32, jnp.int32
    tall = ((height, rows), f32)
    wide = ((height, 8 * GROUP * groups), f32)

    def pairs(height):
        return [((2 * height, per_peer), f32)] * (peers // 2 - 1)

    def singles(height):
        return [((height, per_peer), f32)] * 3

    def held(value):
        return pltpu.with_memory_space_constraint(value, pltpu.HBM)

    inputs = [route, mode_block.reshape(1, subs), local_gap, mode_traces.transpose(1, 0, 2), dual_ops]
    short = loads + GROUP
    far, values, operator, route, *send = call(
        place_kernel,
        [
            ((rows, rows - 2 * per_peer), jnp.bfloat16),
            ((short, rows), f32),
            (dual_ops.shape, dual_ops.dtype),
            (route.shape, i32),
            *pairs(short),
        ],
        [HBM] * 5,
        "place",
        [pltpu.VMEM((1, subs), i32), pltpu.VMEM((modes, 1, rows), f32), pltpu.SemaphoreType.DMA((4 + OPERATOR_PARTS,))],
    )(*(held(value) for value in inputs))
    got = to_chips(*send)
    halves = ((2, rows, rows // 2), dual_ops.dtype)
    edge, slots, placed, near, back, stay = call(
        ready_kernel,
        [((rows, 3 * per_peer), jnp.bfloat16), halves, halves, *singles(short)],
        [VMEM] * 4,
        "ready",
        flops=2 * rows * rows * rows,
    )(route, far, values, operator)
    got_near = to_core(near, *got)
    half = ((height, rows // 2), f32)
    straight_jump, half_image = call(
        first_half_kernel, [half, tall], [VMEM] * (3 + 2 * len(got)), "first_half", flops=2 * rows * rows * height
    )(placed, stay, back, *send, *got)
    handed_jump, image, *image_send = call(
        first_kernel, [half, tall, *pairs(height)], [VMEM] * (5 + len(send)), "first"
    )(far, placed, half_image, got_near, near, *send)
    got = to_chips(*image_send)
    basis, terms, near, back, stay = call(
        middle_kernel, [tall, wide, *singles(height)], [VMEM] * 5, "middle", flops=4 * rows * rows * height
    )(edge, slots, straight_jump, handed_jump, image)
    got_near = to_core(near, *got)
    half_jump, half_second = call(
        second_half_kernel, [tall, tall], [VMEM] * (4 + 2 * len(got)), "second_half", flops=4 * rows * rows * height
    )(slots, placed, stay, back, *image_send, *got)
    jump, terms = call(second_kernel, [tall, wide], [VMEM] * (8 + len(got)), "second")(
        slots, placed, basis, half_jump, half_second, terms, got_near, near, *image_send
    )
    outputs = [((loads, rows), f32), ((MODES * groups, loads), f32)]
    multipliers, amplitudes = call(
        final_kernel,
        outputs,
        [VMEM] * 3,
        "final",
        [*(pltpu.VMEM(*output) for output in outputs), pltpu.SemaphoreType.DMA((FINAL_PARTS + 1,))],
        out_spec=HBM,
    )(total(terms), basis, jump)
    return multipliers, amplitudes.T


def general_body(dual_ops, mode_traces, route, mode_block, local_gap):
    own_index = lax.axis_index("sub")
    plane_index = lax.axis_index("rep")
    peer_count = lax.axis_size("sub")
    plane_count = lax.axis_size("rep")
    operator = dual_ops[0]
    traces = mode_traces[0]
    slot_rows = route[0]
    rows_here = operator.shape[0]
    load_cases = local_gap.shape[0]
    per_peer = rows_here // peer_count
    blocks = mode_block[:, 0]
    block_count = blocks.shape[0] // AGG_SUBS
    coarse = block_count * MODES
    positions = jnp.arange(rows_here, dtype=jnp.int32)
    inverse = jnp.zeros((rows_here,), jnp.int32).at[slot_rows].set(positions)
    slot_peer = positions // per_peer
    within = positions % per_peer
    flip_index = jnp.where(
        slot_peer == own_index, slot_peer * per_peer + per_peer - 1 - within, positions
    )
    peer_ids = jnp.arange(peer_count, dtype=jnp.int32)
    peer_blocks = blocks[peer_ids * plane_count + plane_index]
    own_block = blocks[own_index * plane_count + plane_index]
    labels = jnp.arange(block_count, dtype=jnp.int32)
    peer_onehot = (peer_blocks[:, None] == labels[None, :]).astype(jnp.float32)
    own_onehot = (labels == own_block).astype(jnp.float32)
    trace_slots = traces[:, slot_rows]
    receive_index = flip_index[inverse]

    def to_peers(values):
        return values[:, slot_rows]

    def from_peers(values):
        return values[:, inverse]

    gap_peers = to_peers(local_gap)
    got_traces = lax.all_to_all(trace_slots, "sub", split_axis=1, concat_axis=1, tiled=True)
    got_gap = lax.all_to_all(gap_peers, "sub", split_axis=1, concat_axis=1, tiled=True)
    partner_traces = got_traces[:, flip_index]
    residual = local_gap - got_gap[:, receive_index]
    own_gram = jnp.dot(traces, traces.T, precision=HIGHEST)
    paired = (trace_slots[:, None, :] * partner_traces[None, :, :]).reshape(
        MODES, MODES, peer_count, per_peer
    )
    cross_terms = jnp.sum(paired, axis=3)
    cross_blocks = jnp.einsum("klq,qb->kbl", cross_terms, peer_onehot, precision=HIGHEST)
    own_blocks = own_gram[:, None, :] * own_onehot[None, :, None]
    row_term = 2.0 * (own_blocks - cross_blocks).reshape(MODES, coarse)
    gram_term = (own_onehot[:, None, None] * row_term[None]).reshape(coarse, coarse)

    def coarse_term(values):
        own_part = 2.0 * jnp.dot(values, traces.T, precision=HIGHEST)
        return (own_part[:, None, :] * own_onehot[None, :, None]).reshape(load_cases, coarse)

    def expand(amounts):
        grouped = amounts.reshape(load_cases, block_count, MODES)
        own_amounts = lax.dynamic_index_in_dim(grouped, own_block, 1, keepdims=False)
        own_part = jnp.dot(own_amounts, traces, precision=HIGHEST)
        peer_amounts = jnp.einsum("qb,rbk->rkq", peer_onehot, grouped, precision=HIGHEST)
        spread = jnp.repeat(peer_amounts, per_peer, axis=2)
        peer_part = jnp.sum(spread * partner_traces[None, :, :], axis=1)
        return own_part - from_peers(peer_part)

    squares = jnp.sum(residual * residual, axis=1)
    gram_matrix, coarse_res, norm_res = lax.psum(
        (gram_term, coarse_term(residual), squares), ("sub", "rep")
    )
    factor = jnp.linalg.cholesky(gram_matrix)

    def solve_coarse(right):
        return jax.scipy.linalg.cho_solve((factor, True), right.T).T

    amplitudes = solve_coarse(coarse_res)
    projected = residual - expand(amplitudes)
    inner_sum = norm_res - jnp.sum(amplitudes * coarse_res, axis=1)
    direction = projected
    multipliers = jnp.zeros_like(residual)
    for iteration in range(ITERS):
        product = lax.dot_general(
            direction.astype(jnp.bfloat16),
            operator,
            (((1,), (1,)), ((), ())),
            preferred_element_type=jnp.float32,
        )
        got_product = lax.all_to_all(
            to_peers(product), "sub", split_axis=1, concat_axis=1, tiled=True
        )
        image_jump = product - got_product[:, receive_index]
        coarse_jump, jump_squares, residual_cross, curvature = lax.psum(
            (
                coarse_term(image_jump),
                jnp.sum(image_jump * image_jump, axis=1),
                jnp.sum(residual * image_jump, axis=1),
                jnp.sum(direction * image_jump, axis=1),
            ),
            ("sub", "rep"),
        )
        step_size = inner_sum / curvature
        multipliers = multipliers + step_size[:, None] * direction
        residual = residual - step_size[:, None] * image_jump
        coarse_res = coarse_res - step_size[:, None] * coarse_jump
        norm_res = (
            norm_res - 2.0 * step_size * residual_cross + step_size * step_size * jump_squares
        )
        amplitudes = solve_coarse(coarse_res)
        if iteration + 1 < ITERS:
            projected = residual - expand(amplitudes)
            renewed = norm_res - jnp.sum(amplitudes * coarse_res, axis=1)
            direction = projected + (renewed / inner_sum)[:, None] * direction
            inner_sum = renewed
    return (multipliers, amplitudes)


def fits(mesh, dual_ops, mode_block, local_gap):
    peers, planes = mesh.shape["sub"], mesh.shape["rep"]
    powers = all(size & (size - 1) == 0 for size in (peers, planes))
    whole = dual_ops.shape[1] % (128 * peers) == 0 and local_gap.shape[0] % 16 == 0
    return powers and whole and 8 * GROUP * (mode_block.shape[0] // AGG_SUBS) == 128


def solution(mesh):
    placed = (
        P(("sub", "rep"), None, None),
        P(("sub", "rep"), None, None),
        P(("sub", "rep"), None),
        P(),
        P(None, ("sub", "rep")),
    )

    def run(dual_ops, mode_traces, route, mode_block, local_gap):
        body = fused_body if fits(mesh, dual_ops, mode_block, local_gap) else general_body
        return jax.shard_map(
            body, mesh=mesh, in_specs=placed, out_specs=(P(None, ("sub", "rep")), P()), check_vma=False
        )(dual_ops, mode_traces, route, mode_block, local_gap)

    return run
```

```python
import functools

import jax
import jax.numpy as jnp
from jax import lax
from jax.experimental import pallas as pl
from jax.experimental.pallas import tpu as pltpu
from jax.sharding import PartitionSpec as P

MODES = 6
AGG_SUBS = 16
ITERS = 2
GROUP = 8
SCALAR_LANES = (MODES, MODES + 1, GROUP + MODES, GROUP + MODES + 1, 2 * GROUP + MODES)
OPERATOR_PARTS = 8
FINAL_PARTS = 4
DIGIT = 32

HIGHEST = lax.Precision.HIGHEST
VMEM = pl.BlockSpec(memory_space=pltpu.VMEM)
HBM = pl.BlockSpec(memory_space=pltpu.HBM)
NN = (((1,), (0,)), ((), ()))
NT = (((1,), (1,)), ((), ()))


def split(values):
    high = values.astype(jnp.bfloat16).astype(jnp.float32)
    return jnp.concatenate([high, values - high], axis=0).astype(jnp.bfloat16)


def split_dot(values, matrix, dims):
    rows = values.shape[0]
    both = lax.dot_general(split(values), matrix, dims, preferred_element_type=jnp.float32)
    return both[:rows] + both[rows:]


def small_dot(left, right):
    return jnp.dot(left, right, precision=HIGHEST, preferred_element_type=jnp.float32)


def send_far(values, far_ref, *pair_refs):
    height = values.shape[0]
    per_peer = pair_refs[0].shape[1]
    values = split(values)
    for at, ref in enumerate(pair_refs):
        columns = far_ref[:, 2 * at * per_peer : (2 * at + 2) * per_peer]
        slots = jnp.dot(values, columns, preferred_element_type=jnp.float32)
        slots = slots[:height] + slots[height:]
        ref[:height] = slots[:, :per_peer]
        ref[height:] = slots[:, per_peer:]


def send_near(values, edge_ref, near_ref, back_ref, stay_ref):
    per_peer = back_ref.shape[1]
    slots = split_dot(values, edge_ref[...], NN)
    for at, ref in enumerate((near_ref, back_ref, stay_ref)):
        ref[...] = slots[:, at * per_peer : (at + 1) * per_peer]


def straight(last_ref, pair_refs):
    height = last_ref.shape[0]
    return jnp.concatenate([*(ref[:height] for ref in pair_refs), last_ref[...]], axis=1)


def for_other(near_ref, pair_refs):
    height = near_ref.shape[0]
    return jnp.concatenate([near_ref[...], *(ref[height:] for ref in pair_refs)], axis=1)


def handed(got_ref, height):
    return jnp.concatenate([got_ref[at : at + height] for at in range(0, got_ref.shape[0], height)], axis=1)


def spread(values, loads, groups):
    modes = values[loads:]
    label = modes[MODES : MODES + 1]
    used = lax.broadcasted_iota(jnp.int32, modes.shape, 0) < MODES
    parts = [jnp.where(used & (label == group), modes, 0.0) for group in range(groups)]
    return jnp.concatenate([values[:loads], *parts], axis=0)


def one_hot(route_ref, peer, per_peer):
    start = pl.multiple_of(peer * per_peer, per_peer)
    route = route_ref[:, pl.ds(start, per_peer)]
    shape = (DIGIT, per_peer)
    low, high = (
        jnp.broadcast_to(digit.astype(jnp.float32), shape).astype(jnp.bfloat16)
        for digit in (route % DIGIT, route // DIGIT)
    )
    row = lax.broadcasted_iota(jnp.int32, shape, 0).astype(jnp.float32).astype(jnp.bfloat16)
    zero = jnp.zeros(shape, jnp.bfloat16)
    match = jnp.where(low == row, jnp.ones(shape, jnp.bfloat16), zero)
    pieces = [jnp.where(high == piece, match, zero) for piece in range(route_ref.shape[1] // DIGIT)]
    return jnp.concatenate(pieces, axis=0)


def place_kernel(
    route_hbm, block_hbm, gap_hbm, traces_hbm, operator_hbm,
    far_ref, values_ref, operator_ref, route_ref, *refs,
):
    *pair_refs, block_ref, traces_ref, sems = refs
    loads, rows = gap_hbm.shape
    per_peer = pair_refs[0].shape[1]
    peers = rows // per_peer
    height = rows // OPERATOR_PARTS
    parts = [pl.ds(start, height) for start in range(0, rows, height)]
    gap_parts = [pl.ds(start, GROUP) for start in range(0, loads, GROUP)]
    copies = [
        pltpu.make_async_copy(source, target, sems.at[at])
        for at, (source, target) in enumerate(
            (
                (route_hbm, route_ref),
                (block_hbm, block_ref),
                (traces_hbm, traces_ref),
                *((gap_hbm.at[part], values_ref.at[part]) for part in gap_parts),
                *((operator_hbm.at[:, part], operator_ref.at[:, part]) for part in parts),
            )
        )
    ]

    def build(at):
        peer = own_index ^ (peers - 1 - at)
        far_ref[:, at * per_peer : (at + 1) * per_peer] = one_hot(route_ref, peer, per_peer)

    for copy in copies:
        copy.start()
    own_index = lax.axis_index("sub")
    device = own_index * lax.axis_size("rep") + lax.axis_index("rep")
    copies[0].wait()
    for at in range(peers - 4):
        build(at)
    copies[1].wait()
    copies[2].wait()
    blocks = block_ref[...]
    lane = lax.broadcasted_iota(jnp.int32, blocks.shape, 1)
    own_block = jnp.sum(jnp.where(lane == device, blocks, 0), axis=1, keepdims=True)
    modes = traces_ref.shape[0]
    label = jnp.broadcast_to(own_block.astype(jnp.float32), (1, rows))
    for mode in range(modes):
        values_ref[loads + mode : loads + mode + 1] = traces_ref[mode]
    values_ref[loads + modes : loads + modes + 1] = label
    values_ref[loads + modes + 1 :] = jnp.zeros((GROUP - modes - 1, rows), jnp.float32)
    for copy in copies[3 : 3 + len(gap_parts)]:
        copy.wait()
    for at in range(peers - 4, peers - 2):
        build(at)
    send_far(values_ref[...], far_ref, *pair_refs)
    for copy in copies[3 + len(gap_parts) :]:
        copy.wait()


def ready_kernel(
    route_ref, far_ref, values_ref, operator_ref,
    edge_ref, slots_ref, placed_ref, near_ref, back_ref, stay_ref,
):
    per_peer = back_ref.shape[1]
    peers = far_ref.shape[1] // per_peer + 2
    own_index = lax.axis_index("sub")
    low = lax.broadcasted_iota(jnp.int32, (per_peer, per_peer), 0)
    high = lax.broadcasted_iota(jnp.int32, (per_peer, per_peer), 1)
    reverse = jnp.where(low + high == per_peer - 1, 1.0, 0.0).astype(jnp.bfloat16)
    own_columns = one_hot(route_ref, own_index, per_peer)
    near_columns = one_hot(route_ref, own_index ^ 1, per_peer)
    reversed_columns = jnp.dot(own_columns, reverse, preferred_element_type=jnp.float32).astype(jnp.bfloat16)
    edge_ref[...] = jnp.concatenate([near_columns, reversed_columns, own_columns], axis=1)
    for at in range(peers // 2 - 1):
        start = 2 * at * per_peer
        slots_ref[0, :, at * per_peer : (at + 1) * per_peer] = far_ref[:, start : start + per_peer]
        slots_ref[1, :, (at + 1) * per_peer : (at + 2) * per_peer] = far_ref[:, start + per_peer : start + 2 * per_peer]
    slots_ref[0, :, (peers // 2 - 1) * per_peer :] = own_columns
    slots_ref[1, :, :per_peer] = near_columns
    send_near(values_ref[...], edge_ref, near_ref, back_ref, stay_ref)
    operator = operator_ref[0]
    for half in range(2):
        placed_ref[half] = jnp.dot(
            operator, slots_ref[half], preferred_element_type=jnp.float32
        ).astype(operator.dtype)


def first_half_kernel(placed_ref, stay_ref, back_ref, *refs):
    *pair_refs, jump_ref, image_ref = refs
    sent_refs, got_refs = pair_refs[: len(pair_refs) // 2], pair_refs[len(pair_refs) // 2 :]
    loads = stay_ref.shape[0] - GROUP
    groups = (jump_ref.shape[0] - loads) // GROUP
    own, got = (spread(straight(*refs), loads, groups) for refs in ((stay_ref, sent_refs), (back_ref, got_refs)))
    jump_ref[...] = own - got
    image_ref[...] = split_dot(own - got, placed_ref[0], NT)


def first_kernel(far_ref, placed_ref, half_ref, got_ref, near_ref, *refs):
    sent_refs, (jump_ref, image_ref, *pair_refs) = refs[: len(refs) // 2 - 1], refs[len(refs) // 2 - 1 :]
    height = near_ref.shape[0]
    loads = height - GROUP
    groups = (image_ref.shape[0] - loads) // GROUP
    own, got = (spread(value, loads, groups) for value in (for_other(near_ref, sent_refs), handed(got_ref, height)))
    jump_ref[...] = own - got
    image = half_ref[...] + split_dot(own - got, placed_ref[1], NT)
    image_ref[...] = image
    send_far(image, far_ref, *pair_refs)


def products_of(left, right):
    both = lax.dot_general(split(left), split(right), NT, preferred_element_type=jnp.float32)
    both = both[: left.shape[0]] + both[left.shape[0] :]
    return both + pltpu.roll(both, right.shape[0], 1)


def with_scalars(top, products, lanes):
    lane = lax.broadcasted_iota(jnp.int32, top.shape, 1)
    for at, product in zip(lanes, products):
        top = jnp.where(lane == at, jnp.sum(product, axis=1, keepdims=True), top)
    return top


def middle_kernel(
    edge_ref, slots_ref, straight_ref, handed_ref, image_ref, basis_ref, terms_ref, near_ref, back_ref, stay_ref
):
    image = image_ref[...]
    send_near(image, edge_ref, near_ref, back_ref, stay_ref)
    coarse = terms_ref.shape[1] // 8
    loads = image.shape[0] - coarse
    basis = split_dot(straight_ref[...], slots_ref[0], NT) + split_dot(handed_ref[...], slots_ref[1], NT)
    basis_ref[...] = basis
    left = jnp.concatenate([basis[:loads], image[:loads], basis[loads:]])
    empty = jnp.zeros((2 * coarse, basis.shape[1]), jnp.float32)
    both = products_of(left, jnp.concatenate([basis[loads:], image[loads:], empty]))
    strip = lax.broadcasted_iota(jnp.int32, (loads, 8 * coarse), 1) // coarse
    top = jnp.where(strip < 2, both[:loads], 0.0)
    top = jnp.where(strip == 4, both[loads : 2 * loads], top)
    residual = basis[:loads]
    terms_ref[:loads] = with_scalars(top, (residual * residual, residual * image[:loads]), SCALAR_LANES[:2])
    strip = lax.broadcasted_iota(jnp.int32, (coarse, 8 * coarse), 1) // coarse
    terms_ref[loads:] = jnp.where(strip < 2, both[2 * loads :], 0.0)


def second_half_kernel(slots_ref, placed_ref, stay_ref, back_ref, *refs):
    *pair_refs, jump_ref, second_ref = refs
    sent_refs, got_refs = pair_refs[: len(pair_refs) // 2], pair_refs[len(pair_refs) // 2 :]
    jump = straight(stay_ref, sent_refs) - straight(back_ref, got_refs)
    jump_ref[...] = split_dot(jump, slots_ref[0], NT)
    second_ref[...] = split_dot(jump, placed_ref[0], NT)


def second_kernel(slots_ref, placed_ref, basis_ref, half_jump_ref, half_second_ref, early_ref, got_ref, near_ref, *refs):
    *sent_refs, jump_ref, terms_ref = refs
    coarse = terms_ref.shape[1] // 8
    loads = basis_ref.shape[0] - coarse
    jump = for_other(near_ref, sent_refs) - handed(got_ref, loads + coarse)
    second = half_second_ref[...] + split_dot(jump, placed_ref[1], NT)
    jump = half_jump_ref[...] + split_dot(jump, slots_ref[1], NT)
    jump_ref[...] = jump
    basis = basis_ref[...]
    left = jnp.concatenate([basis[:loads], jump[:loads], second[:loads], basis[loads:], jump[loads:]])
    empty = jnp.zeros((coarse, basis.shape[1]), jnp.float32)
    both = products_of(left, jnp.concatenate([basis[loads:], empty, jump[loads:], second[loads:]]))
    along, jumped, doubled = (both[at * loads : (at + 1) * loads] for at in range(3))
    base, far = both[3 * loads : 3 * loads + coarse], both[3 * loads + coarse :]
    strip = lax.broadcasted_iota(jnp.int32, (loads, 8 * coarse), 1) // coarse
    top = jnp.where(strip == 2, doubled, 0.0)
    top = jnp.where(strip == 3, along, top)
    top = jnp.where(strip == 5, pltpu.roll(doubled, coarse, 1), top)
    top = jnp.where(strip >= 6, jumped, top)
    residual, jump_loads, second_loads = basis[:loads], jump[:loads], second[:loads]
    products = (jump_loads * jump_loads, jump_loads * second_loads, residual * second_loads)
    terms_ref[:loads] = early_ref[:loads] + with_scalars(top, products, SCALAR_LANES[2:])
    strip = lax.broadcasted_iota(jnp.int32, (coarse, 8 * coarse), 1) // coarse
    base = jnp.where((strip == 2) | (strip == 3), base, 0.0)
    terms_ref[loads:] = early_ref[loads:] + jnp.where(strip < 4, base, far)


def sum_kernel(count, *refs):
    parts = [ref[...] for ref in reversed(refs[:count])]
    while len(parts) > 1:
        parts = [low + high for low, high in zip(parts[::2], parts[1::2])]
    for ref in refs[count:]:
        ref[...] = parts[0]


def inverse_of(value):
    guess = pl.reciprocal(value, approx=True)
    for _ in range(2):
        guess = guess * (2.0 - value * guess)
    return guess


def eliminate(work, coarse):
    row = lax.broadcasted_iota(jnp.int32, work.shape, 0)
    for start in range(0, coarse, GROUP):
        pivots = range(start, start + MODES)
        columns = [jnp.broadcast_to(work[:, pivot : pivot + 1], work.shape) for pivot in pivots]
        square = [[column[pivot : pivot + 1] for column in columns] for pivot in pivots]
        rows = [work[pivot : pivot + 1] for pivot in pivots]
        for at in range(MODES):
            scale = inverse_of(square[at][at])
            rows[at] = rows[at] * scale
            square[at] = [value * scale for value in square[at]]
            for other in range(MODES):
                if other != at:
                    factor = square[other][at]
                    rows[other] = rows[other] - factor * rows[at]
                    square[other] = [
                        value if to <= at else value - factor * square[at][to]
                        for to, value in enumerate(square[other])
                    ]
        for column, solved in zip(columns, rows):
            work = work - column * solved
        for pivot, solved in zip(pivots, rows):
            work = jnp.where(row == pivot, solved, work)
    return work


def thin_dot(left, right):
    high, right_high = (value.astype(jnp.bfloat16).astype(jnp.float32) for value in (left, right))
    return jnp.dot(
        jnp.concatenate([high, left - high, high], axis=1).astype(jnp.bfloat16),
        jnp.concatenate([right_high, right_high, right - right_high], axis=0).astype(jnp.bfloat16),
        preferred_element_type=jnp.float32,
    )


def final_kernel(
    terms_ref, basis_ref, jump_ref, multipliers_hbm, amplitudes_hbm, multipliers_ref, amplitudes_ref, sems
):
    coarse = terms_ref.shape[1] // 8
    loads = basis_ref.shape[0] - coarse
    groups = coarse // GROUP
    by_load = terms_ref[:loads].T
    used = lax.broadcasted_iota(jnp.int32, (coarse, loads), 0) % GROUP < MODES

    def strip(at):
        return by_load[at * coarse : (at + 1) * coarse]

    def block(at):
        return terms_ref[loads:, at * coarse : (at + 1) * coarse]

    def total(values):
        return jnp.sum(values, axis=0, keepdims=True)

    res_res, res_image, jump_jump, jump_second, res_second = (by_load[at : at + 1] for at in SCALAR_LANES)
    coarse_res, res_h = (jnp.where(used, strip(at), 0.0) for at in (0, 1))
    second_z, res_dz, image_g, second_g, jump_z, jump_dz = (strip(at) for at in range(2, 8))
    g_h, g_dz, z_z, z_dz = block(1), block(3), block(6), block(7)
    row = lax.broadcasted_iota(jnp.int32, (coarse, coarse), 0)
    unit = jnp.where(row == lax.broadcasted_iota(jnp.int32, (coarse, coarse), 1), 1.0, 0.0)
    empty = jnp.zeros((coarse, 5 * coarse - 2 * loads), jnp.float32)
    solved = eliminate(
        jnp.concatenate([terms_ref[loads:, : 2 * coarse], coarse_res, image_g, unit, empty], axis=1), coarse
    )
    inverse_h = solved[:, coarse : 2 * coarse]
    amounts = solved[:, 2 * coarse : 2 * coarse + loads]
    inverse_image = solved[:, 2 * coarse + loads : 2 * coarse + 2 * loads]
    inverse = solved[:, 2 * coarse + 2 * loads : 3 * coarse + 2 * loads]
    products = small_dot(jnp.concatenate([inverse_h, g_h, z_z, g_dz, z_dz], axis=0), amounts)
    inverse_h_amounts, h_amounts, z_amounts, g_dz_amounts, z_dz_amounts = (
        products[at * coarse : (at + 1) * coarse] for at in range(5)
    )
    shares = 2.0 * (inverse_image - inverse_h_amounts)
    both = jnp.concatenate([amounts, shares], axis=0).T
    basis_g, jump_z_rows = basis_ref[loads:], jump_ref[loads:]
    d = basis_ref[:loads] - thin_dot(both[:, :coarse], basis_g)
    u = jump_ref[:loads] - thin_dot(both, jnp.concatenate([jump_z_rows, basis_g], axis=0))
    products = small_dot(jnp.concatenate([g_h, z_z], axis=0), shares)
    image_d = image_g - h_amounts
    inner = res_res - total(amounts * coarse_res)
    curvature = 2.0 * (res_image - total(amounts * (res_h + image_d)))
    u_u = jump_jump - total(amounts * (2.0 * jump_z - z_amounts) + 2.0 * image_d * shares)
    second_u = second_g - g_dz_amounts - products[:coarse]
    jump_u = second_z - z_dz_amounts - 0.5 * products[coarse:]
    d_second = res_second - total(amounts * (res_dz + second_u) + shares * res_h)
    u_second = jump_second - total(amounts * (jump_dz + jump_u) + shares * (0.5 * jump_z + second_u))
    step = inner * inverse_of(curvature)
    renewed = step * step * u_u - inner
    grown = 1.0 + renewed * inverse_of(inner)
    curvature = grown * grown * curvature - grown * step * (2.0 * d_second + u_u) + 2.0 * step * step * u_second
    second_step = renewed * inverse_of(curvature)
    on_d, on_u = step + second_step * grown, second_step * step
    amplitudes = amounts - on_d * shares + 2.0 * on_u * small_dot(inverse, second_u)
    amplitudes_ref[...] = jnp.concatenate(
        [amplitudes[label * GROUP : label * GROUP + MODES] for label in range(groups)], axis=0
    )
    copies = [pltpu.make_async_copy(amplitudes_ref, amplitudes_hbm, sems.at[0])]
    copies[0].start()
    weights = jnp.concatenate([on_d, on_u, jnp.zeros((6, loads), jnp.float32)], axis=0).T
    height = loads // FINAL_PARTS
    for part in range(FINAL_PARTS):
        rows = pl.ds(part * height, height)
        here = slice(part * height, (part + 1) * height)
        multipliers_ref[rows] = weights[here, 0:1] * d[here] - weights[here, 1:2] * u[here]
        copies.append(pltpu.make_async_copy(multipliers_ref.at[rows], multipliers_hbm.at[rows], sems.at[part + 1]))
        copies[-1].start()
    for copy in copies:
        copy.wait()


def call(kernel, shapes, in_specs, name, scratch=(), flops=0, out_spec=VMEM):
    return pl.pallas_call(
        kernel,
        out_shape=[jax.ShapeDtypeStruct(*shape) for shape in shapes],
        in_specs=in_specs,
        out_specs=[out_spec] * len(shapes),
        scratch_shapes=scratch,
        compiler_params=pltpu.CompilerParams(vmem_limit_bytes=24 * 1024 * 1024),
        cost_estimate=pl.CostEstimate(flops=flops, bytes_accessed=2**20, transcendentals=0),
        name=name,
    )


def permute(values, offset, plane_offset=0):
    peers, planes = lax.axis_size("sub"), lax.axis_size("rep")
    offset = offset * planes + plane_offset
    return lax.ppermute(values, ("sub", "rep"), [(at, at ^ offset) for at in range(peers * planes)])


def to_chips(*pairs):
    return [permute(pair, 2 * (len(pairs) - at) + 1) for at, pair in enumerate(pairs)]


def to_core(near, *pairs):
    return permute(jnp.concatenate([near, *(pair[near.shape[0] :] for pair in pairs)], axis=0), 1)


def total(terms):
    chips = [(offset + 1, 0) for offset in reversed(range(2, lax.axis_size("sub"), 2))]
    chips = chips[-1:] + chips[:-1]
    planes = [(1, offset) for offset in reversed(range(1, lax.axis_size("rep")))]
    planes[:2] = planes[1::-1]
    copies = [terms]
    for offsets, following in (([(1, 0)], len(chips)), (chips, len(planes)), (planes, 1)):
        parts = [permute(copy, *offset) for copy, offset in zip(copies, offsets)]
        kernel = functools.partial(sum_kernel, len(parts) + 1)
        copies = call(kernel, [(terms.shape, terms.dtype)] * following, [VMEM] * (len(parts) + 1), "sum")(
            *parts, copies[0]
        )
    return copies[0]


def fused_body(dual_ops, mode_traces, route, mode_block, local_gap):
    peers = lax.axis_size("sub")
    loads, rows = local_gap.shape
    modes = mode_traces.shape[1]
    subs = mode_block.shape[0]
    groups = subs // AGG_SUBS
    per_peer = rows // peers
    height = loads + GROUP * groups
    f32, i32 = jnp.float32, jnp.int32
    tall = ((height, rows), f32)
    wide = ((height, 8 * GROUP * groups), f32)

    def pairs(height):
        return [((2 * height, per_peer), f32)] * (peers // 2 - 1)

    def singles(height):
        return [((height, per_peer), f32)] * 3

    def held(value):
        return pltpu.with_memory_space_constraint(value, pltpu.HBM)

    inputs = [route, mode_block.reshape(1, subs), local_gap, mode_traces.transpose(1, 0, 2), dual_ops]
    short = loads + GROUP
    far, values, operator, route, *send = call(
        place_kernel,
        [
            ((rows, rows - 2 * per_peer), jnp.bfloat16),
            ((short, rows), f32),
            (dual_ops.shape, dual_ops.dtype),
            (route.shape, i32),
            *pairs(short),
        ],
        [HBM] * 5,
        "place",
        [pltpu.VMEM((1, subs), i32), pltpu.VMEM((modes, 1, rows), f32), pltpu.SemaphoreType.DMA((3 + loads // GROUP + OPERATOR_PARTS,))],
    )(*(held(value) for value in inputs))
    got = to_chips(*send)
    halves = ((2, rows, rows // 2), dual_ops.dtype)
    edge, slots, placed, near, back, stay = call(
        ready_kernel,
        [((rows, 3 * per_peer), jnp.bfloat16), halves, halves, *singles(short)],
        [VMEM] * 4,
        "ready",
        flops=2 * rows * rows * rows,
    )(route, far, values, operator)
    got_near = to_core(near, *got)
    half = ((height, rows // 2), f32)
    straight_jump, half_image = call(
        first_half_kernel, [half, tall], [VMEM] * (3 + 2 * len(got)), "first_half", flops=2 * rows * rows * height
    )(placed, stay, back, *send, *got)
    handed_jump, image, *image_send = call(
        first_kernel, [half, tall, *pairs(height)], [VMEM] * (5 + len(send)), "first"
    )(far, placed, half_image, got_near, near, *send)
    got = to_chips(*image_send)
    basis, terms, near, back, stay = call(
        middle_kernel, [tall, wide, *singles(height)], [VMEM] * 5, "middle", flops=4 * rows * rows * height
    )(edge, slots, straight_jump, handed_jump, image)
    got_near = to_core(near, *got)
    half_jump, half_second = call(
        second_half_kernel, [tall, tall], [VMEM] * (4 + 2 * len(got)), "second_half", flops=4 * rows * rows * height
    )(slots, placed, stay, back, *image_send, *got)
    jump, terms = call(second_kernel, [tall, wide], [VMEM] * (8 + len(got)), "second")(
        slots, placed, basis, half_jump, half_second, terms, got_near, near, *image_send
    )
    outputs = [((loads, rows), f32), ((MODES * groups, loads), f32)]
    multipliers, amplitudes = call(
        final_kernel,
        outputs,
        [VMEM] * 3,
        "final",
        [*(pltpu.VMEM(*output) for output in outputs), pltpu.SemaphoreType.DMA((FINAL_PARTS + 1,))],
        out_spec=HBM,
    )(total(terms), basis, jump)
    return multipliers, amplitudes.T


def general_body(dual_ops, mode_traces, route, mode_block, local_gap):
    own_index = lax.axis_index("sub")
    plane_index = lax.axis_index("rep")
    peer_count = lax.axis_size("sub")
    plane_count = lax.axis_size("rep")
    operator = dual_ops[0]
    traces = mode_traces[0]
    slot_rows = route[0]
    rows_here = operator.shape[0]
    load_cases = local_gap.shape[0]
    per_peer = rows_here // peer_count
    blocks = mode_block[:, 0]
    block_count = blocks.shape[0] // AGG_SUBS
    coarse = block_count * MODES
    positions = jnp.arange(rows_here, dtype=jnp.int32)
    inverse = jnp.zeros((rows_here,), jnp.int32).at[slot_rows].set(positions)
    slot_peer = positions // per_peer
    within = positions % per_peer
    flip_index = jnp.where(
        slot_peer == own_index, slot_peer * per_peer + per_peer - 1 - within, positions
    )
    peer_ids = jnp.arange(peer_count, dtype=jnp.int32)
    peer_blocks = blocks[peer_ids * plane_count + plane_index]
    own_block = blocks[own_index * plane_count + plane_index]
    labels = jnp.arange(block_count, dtype=jnp.int32)
    peer_onehot = (peer_blocks[:, None] == labels[None, :]).astype(jnp.float32)
    own_onehot = (labels == own_block).astype(jnp.float32)
    trace_slots = traces[:, slot_rows]
    receive_index = flip_index[inverse]

    def to_peers(values):
        return values[:, slot_rows]

    def from_peers(values):
        return values[:, inverse]

    gap_peers = to_peers(local_gap)
    got_traces = lax.all_to_all(trace_slots, "sub", split_axis=1, concat_axis=1, tiled=True)
    got_gap = lax.all_to_all(gap_peers, "sub", split_axis=1, concat_axis=1, tiled=True)
    partner_traces = got_traces[:, flip_index]
    residual = local_gap - got_gap[:, receive_index]
    own_gram = jnp.dot(traces, traces.T, precision=HIGHEST)
    paired = (trace_slots[:, None, :] * partner_traces[None, :, :]).reshape(
        MODES, MODES, peer_count, per_peer
    )
    cross_terms = jnp.sum(paired, axis=3)
    cross_blocks = jnp.einsum("klq,qb->kbl", cross_terms, peer_onehot, precision=HIGHEST)
    own_blocks = own_gram[:, None, :] * own_onehot[None, :, None]
    row_term = 2.0 * (own_blocks - cross_blocks).reshape(MODES, coarse)
    gram_term = (own_onehot[:, None, None] * row_term[None]).reshape(coarse, coarse)

    def coarse_term(values):
        own_part = 2.0 * jnp.dot(values, traces.T, precision=HIGHEST)
        return (own_part[:, None, :] * own_onehot[None, :, None]).reshape(load_cases, coarse)

    def expand(amounts):
        grouped = amounts.reshape(load_cases, block_count, MODES)
        own_amounts = lax.dynamic_index_in_dim(grouped, own_block, 1, keepdims=False)
        own_part = jnp.dot(own_amounts, traces, precision=HIGHEST)
        peer_amounts = jnp.einsum("qb,rbk->rkq", peer_onehot, grouped, precision=HIGHEST)
        spread = jnp.repeat(peer_amounts, per_peer, axis=2)
        peer_part = jnp.sum(spread * partner_traces[None, :, :], axis=1)
        return own_part - from_peers(peer_part)

    squares = jnp.sum(residual * residual, axis=1)
    gram_matrix, coarse_res, norm_res = lax.psum(
        (gram_term, coarse_term(residual), squares), ("sub", "rep")
    )
    factor = jnp.linalg.cholesky(gram_matrix)

    def solve_coarse(right):
        return jax.scipy.linalg.cho_solve((factor, True), right.T).T

    amplitudes = solve_coarse(coarse_res)
    projected = residual - expand(amplitudes)
    inner_sum = norm_res - jnp.sum(amplitudes * coarse_res, axis=1)
    direction = projected
    multipliers = jnp.zeros_like(residual)
    for iteration in range(ITERS):
        product = lax.dot_general(
            direction.astype(jnp.bfloat16),
            operator,
            (((1,), (1,)), ((), ())),
            preferred_element_type=jnp.float32,
        )
        got_product = lax.all_to_all(
            to_peers(product), "sub", split_axis=1, concat_axis=1, tiled=True
        )
        image_jump = product - got_product[:, receive_index]
        coarse_jump, jump_squares, residual_cross, curvature = lax.psum(
            (
                coarse_term(image_jump),
                jnp.sum(image_jump * image_jump, axis=1),
                jnp.sum(residual * image_jump, axis=1),
                jnp.sum(direction * image_jump, axis=1),
            ),
            ("sub", "rep"),
        )
        step_size = inner_sum / curvature
        multipliers = multipliers + step_size[:, None] * direction
        residual = residual - step_size[:, None] * image_jump
        coarse_res = coarse_res - step_size[:, None] * coarse_jump
        norm_res = (
            norm_res - 2.0 * step_size * residual_cross + step_size * step_size * jump_squares
        )
        amplitudes = solve_coarse(coarse_res)
        if iteration + 1 < ITERS:
            projected = residual - expand(amplitudes)
            renewed = norm_res - jnp.sum(amplitudes * coarse_res, axis=1)
            direction = projected + (renewed / inner_sum)[:, None] * direction
            inner_sum = renewed
    return (multipliers, amplitudes)


def fits(mesh, dual_ops, mode_block, local_gap):
    peers, planes = mesh.shape["sub"], mesh.shape["rep"]
    powers = all(size & (size - 1) == 0 for size in (peers, planes))
    whole = dual_ops.shape[1] % (128 * peers) == 0 and local_gap.shape[0] % 16 == 0
    return powers and whole and 8 * GROUP * (mode_block.shape[0] // AGG_SUBS) == 128


def solution(mesh):
    placed = (
        P(("sub", "rep"), None, None),
        P(("sub", "rep"), None, None),
        P(("sub", "rep"), None),
        P(),
        P(None, ("sub", "rep")),
    )

    def run(dual_ops, mode_traces, route, mode_block, local_gap):
        body = fused_body if fits(mesh, dual_ops, mode_block, local_gap) else general_body
        return jax.shard_map(
            body, mesh=mesh, in_specs=placed, out_specs=(P(None, ("sub", "rep")), P()), check_vma=False
        )(dual_ops, mode_traces, route, mode_block, local_gap)

    return run
```

```python
import functools

import jax
import jax.numpy as jnp
from jax import lax
from jax.experimental import pallas as pl
from jax.experimental.pallas import tpu as pltpu
from jax.sharding import PartitionSpec as P

MODES = 6
AGG_SUBS = 16
ITERS = 2
GROUP = 8

HIGHEST = lax.Precision.HIGHEST
VMEM = pl.BlockSpec(memory_space=pltpu.VMEM)
HBM = pl.BlockSpec(memory_space=pltpu.HBM)
NN = (((1,), (0,)), ((), ()))
NT = (((1,), (1,)), ((), ()))


def split(values):
    high = values.astype(jnp.bfloat16).astype(jnp.float32)
    return jnp.concatenate([high, values - high], axis=0).astype(jnp.bfloat16)


def split_dot(values, matrix, dims):
    rows = values.shape[0]
    both = lax.dot_general(split(values), matrix, dims, preferred_element_type=jnp.float32)
    return both[:rows] + both[rows:]


def small_dot(left, right):
    return jnp.dot(left, right, precision=HIGHEST, preferred_element_type=jnp.float32)


def send_far(values, far_ref, *pair_refs):
    height = values.shape[0]
    per_peer = pair_refs[0].shape[1]
    values = split(values)
    for at, ref in enumerate(pair_refs):
        columns = far_ref[:, 2 * at * per_peer : (2 * at + 2) * per_peer]
        slots = jnp.dot(values, columns, preferred_element_type=jnp.float32)
        slots = slots[:height] + slots[height:]
        ref[:height] = slots[:, :per_peer]
        ref[height:] = slots[:, per_peer:]


def send_near(values, edge_ref, near_ref, back_ref, stay_ref):
    per_peer = back_ref.shape[1]
    slots = split_dot(values, edge_ref[...], NN)
    for at, ref in enumerate((near_ref, back_ref, stay_ref)):
        ref[...] = slots[:, at * per_peer : (at + 1) * per_peer]


def straight(last_ref, pair_refs):
    height = last_ref.shape[0]
    return jnp.concatenate([*(ref[:height] for ref in pair_refs), last_ref[...]], axis=1)


def for_other(near_ref, pair_refs):
    height = near_ref.shape[0]
    return jnp.concatenate([near_ref[...], *(ref[height:] for ref in pair_refs)], axis=1)


def handed(got_ref, height):
    return jnp.concatenate([got_ref[at : at + height] for at in range(0, got_ref.shape[0], height)], axis=1)


def spread(values, loads, groups):
    modes = values[loads:]
    label = modes[MODES : MODES + 1]
    used = lax.broadcasted_iota(jnp.int32, modes.shape, 0) < MODES
    parts = [jnp.where(used & (label == group), modes, 0.0) for group in range(groups)]
    return jnp.concatenate([values[:loads], *parts], axis=0)


def one_hot(route_ref, peer, per_peer):
    start = pl.multiple_of(peer * per_peer, per_peer)
    row_ids = lax.broadcasted_iota(jnp.int32, (route_ref.shape[1], per_peer), 0)
    return jnp.where(row_ids == route_ref[:, pl.ds(start, per_peer)], 1.0, 0.0).astype(jnp.bfloat16)


def place_kernel(
    route_hbm, block_hbm, gap_hbm, traces_hbm, operator_hbm,
    far_ref, values_ref, operator_ref, route_ref, *refs,
):
    *pair_refs, block_ref, traces_ref, sems = refs
    loads, rows = gap_hbm.shape
    per_peer = pair_refs[0].shape[1]
    peers = rows // per_peer
    copies = [
        pltpu.make_async_copy(source, target, sems.at[at])
        for at, (source, target) in enumerate(
            (
                (route_hbm, route_ref),
                (block_hbm, block_ref),
                (traces_hbm, traces_ref),
                (gap_hbm, values_ref.at[pl.ds(0, loads)]),
                (operator_hbm, operator_ref),
            )
        )
    ]

    def build(at):
        peer = own_index ^ (peers - 1 - at)
        far_ref[:, at * per_peer : (at + 1) * per_peer] = one_hot(route_ref, peer, per_peer)

    for copy in copies:
        copy.start()
    own_index = lax.axis_index("sub")
    device = own_index * lax.axis_size("rep") + lax.axis_index("rep")
    copies[0].wait()
    for at in range(peers - 4):
        build(at)
    copies[1].wait()
    copies[2].wait()
    blocks = block_ref[...]
    lane = lax.broadcasted_iota(jnp.int32, blocks.shape, 1)
    own_block = jnp.sum(jnp.where(lane == device, blocks, 0), axis=1, keepdims=True)
    modes = traces_ref.shape[0]
    label = jnp.broadcast_to(own_block.astype(jnp.float32), (1, rows))
    for mode in range(modes):
        values_ref[loads + mode : loads + mode + 1] = traces_ref[mode]
    values_ref[loads + modes : loads + modes + 1] = label
    values_ref[loads + modes + 1 :] = jnp.zeros((GROUP - modes - 1, rows), jnp.float32)
    copies[3].wait()
    for at in range(peers - 4, peers - 2):
        build(at)
    send_far(values_ref[...], far_ref, *pair_refs)
    copies[4].wait()


def ready_kernel(
    route_ref, far_ref, values_ref, operator_ref,
    edge_ref, slots_ref, placed_ref, near_ref, back_ref, stay_ref,
):
    per_peer = back_ref.shape[1]
    peers = far_ref.shape[1] // per_peer + 2
    own_index = lax.axis_index("sub")
    low = lax.broadcasted_iota(jnp.int32, (per_peer, per_peer), 0)
    high = lax.broadcasted_iota(jnp.int32, (per_peer, per_peer), 1)
    reverse = jnp.where(low + high == per_peer - 1, 1.0, 0.0).astype(jnp.bfloat16)
    own_columns = one_hot(route_ref, own_index, per_peer)
    near_columns = one_hot(route_ref, own_index ^ 1, per_peer)
    reversed_columns = jnp.dot(own_columns, reverse, preferred_element_type=jnp.float32).astype(jnp.bfloat16)
    edge_ref[...] = jnp.concatenate([near_columns, reversed_columns, own_columns], axis=1)
    for at in range(peers // 2 - 1):
        start = 2 * at * per_peer
        slots_ref[0, :, at * per_peer : (at + 1) * per_peer] = far_ref[:, start : start + per_peer]
        slots_ref[1, :, (at + 1) * per_peer : (at + 2) * per_peer] = far_ref[:, start + per_peer : start + 2 * per_peer]
    slots_ref[0, :, (peers // 2 - 1) * per_peer :] = own_columns
    slots_ref[1, :, :per_peer] = near_columns
    send_near(values_ref[...], edge_ref, near_ref, back_ref, stay_ref)
    operator = operator_ref[0]
    for half in range(2):
        placed_ref[half] = jnp.dot(
            operator, slots_ref[half], preferred_element_type=jnp.float32
        ).astype(operator.dtype)


def first_half_kernel(placed_ref, stay_ref, back_ref, *refs):
    *pair_refs, jump_ref, image_ref = refs
    sent_refs, got_refs = pair_refs[: len(pair_refs) // 2], pair_refs[len(pair_refs) // 2 :]
    loads = stay_ref.shape[0] - GROUP
    groups = (jump_ref.shape[0] - loads) // GROUP
    own, got = (spread(straight(*refs), loads, groups) for refs in ((stay_ref, sent_refs), (back_ref, got_refs)))
    jump_ref[...] = own - got
    image_ref[...] = split_dot(own - got, placed_ref[0], NT)


def first_kernel(far_ref, placed_ref, half_ref, got_ref, near_ref, *refs):
    sent_refs, (jump_ref, image_ref, *pair_refs) = refs[: len(refs) // 2 - 1], refs[len(refs) // 2 - 1 :]
    height = near_ref.shape[0]
    loads = height - GROUP
    groups = (image_ref.shape[0] - loads) // GROUP
    own, got = (spread(value, loads, groups) for value in (for_other(near_ref, sent_refs), handed(got_ref, height)))
    jump_ref[...] = own - got
    image = half_ref[...] + split_dot(own - got, placed_ref[1], NT)
    image_ref[...] = image
    send_far(image, far_ref, *pair_refs)


def products_of(left, right):
    rows, columns = left.shape[0], right.shape[0]
    both = lax.dot_general(split(left), split(right), NT, preferred_element_type=jnp.float32)
    both = both[:rows] + both[rows:]
    return both[:, :columns] + both[:, columns:]


def by_load(products):
    sums = [jnp.sum(product, axis=1, keepdims=True) for product in products]
    empty = [jnp.zeros_like(sums[0])] * (GROUP - len(sums))
    return jnp.concatenate(sums + empty, axis=1).T


def middle_kernel(
    edge_ref, slots_ref, straight_ref, handed_ref, image_ref, basis_ref, terms_ref, near_ref, back_ref, stay_ref
):
    image = image_ref[...]
    send_near(image, edge_ref, near_ref, back_ref, stay_ref)
    coarse = terms_ref.shape[0] // 3
    loads = image.shape[0] - coarse
    basis = split_dot(straight_ref[...], slots_ref[0], NT) + split_dot(handed_ref[...], slots_ref[1], NT)
    basis_ref[...] = basis
    residual, residual_image = basis[:loads], image[:loads]
    lanes = terms_ref.shape[1]
    empty = jnp.zeros((lanes - 2 * loads - 2 * coarse, basis.shape[1]), jnp.float32)
    both = products_of(
        jnp.concatenate([basis[loads:], image[loads:]]),
        jnp.concatenate([residual, basis[loads:], image[loads:], empty, residual_image]),
    )
    by_g, by_h = both[:coarse], both[coarse:]
    lane = lax.broadcasted_iota(jnp.int32, (coarse, lanes), 1)
    first, last = lane < loads, lane >= lanes - loads
    terms_ref[:coarse] = jnp.where(first | last, by_g, 0.0)
    terms_ref[coarse : 2 * coarse] = jnp.where(last, pltpu.roll(by_h, lanes - loads, 1), 0.0)
    terms_ref[2 * coarse :] = jnp.where((lane >= loads) & (lane < loads + 2 * coarse), by_g, 0.0)
    terms_ref[2 * coarse : 2 * coarse + GROUP, :loads] = by_load(
        [residual * residual, residual * residual_image]
    )


def second_half_kernel(slots_ref, placed_ref, stay_ref, back_ref, *refs):
    *pair_refs, jump_ref, second_ref = refs
    sent_refs, got_refs = pair_refs[: len(pair_refs) // 2], pair_refs[len(pair_refs) // 2 :]
    jump = straight(stay_ref, sent_refs) - straight(back_ref, got_refs)
    jump_ref[...] = split_dot(jump, slots_ref[0], NT)
    second_ref[...] = split_dot(jump, placed_ref[0], NT)


def second_kernel(slots_ref, placed_ref, basis_ref, half_jump_ref, half_second_ref, early_ref, got_ref, near_ref, *refs):
    *sent_refs, jump_ref, terms_ref = refs
    coarse = terms_ref.shape[0] // 3
    loads = basis_ref.shape[0] - coarse
    jump = for_other(near_ref, sent_refs) - handed(got_ref, loads + coarse)
    second = half_second_ref[...] + split_dot(jump, placed_ref[1], NT)
    jump = half_jump_ref[...] + split_dot(jump, slots_ref[1], NT)
    jump_ref[...] = jump
    basis = basis_ref[...]
    residual, jump_loads, second_loads = basis[:loads], jump[:loads], second[:loads]
    both = products_of(
        jnp.concatenate([basis[loads:], jump[loads:], second[loads:]]),
        jnp.concatenate([residual, jump_loads, second_loads, jump[loads:], second[loads:]]),
    )
    by_g, by_z, by_dz = (both[at * coarse : (at + 1) * coarse] for at in range(3))
    lanes = terms_ref.shape[1]
    lane = lax.broadcasted_iota(jnp.int32, (coarse, lanes), 1)
    group = lane // loads
    top = jnp.where(group == 1, by_z, jnp.where(group == 2, by_g, 0.0))
    low = jnp.where(group < 2, by_dz, jnp.where(group == 2, by_z, 0.0))
    last = jnp.where(group == 2, pltpu.roll(by_z, lanes - loads, 1), jnp.where(lane >= lanes - coarse, by_g, 0.0))
    terms_ref[:coarse] = early_ref[:coarse] + top
    terms_ref[coarse : 2 * coarse] = early_ref[coarse : 2 * coarse] + low
    terms_ref[2 * coarse :] = early_ref[2 * coarse :] + last
    sums = by_load([jump_loads * jump_loads, jump_loads * second_loads, residual * second_loads])
    start = 2 * coarse + GROUP
    terms_ref[start : start + GROUP, :loads] = sums


def sum_kernel(count, *refs):
    parts = [ref[...] for ref in reversed(refs[:count])]
    while len(parts) > 1:
        parts = [low + high for low, high in zip(parts[::2], parts[1::2])]
    for ref in refs[count:]:
        ref[...] = parts[0]


def eliminate(work, coarse):
    row = lax.broadcasted_iota(jnp.int32, work.shape, 0)
    for start in range(0, coarse, GROUP):
        pivots = range(start, start + MODES)
        columns = [jnp.broadcast_to(work[:, pivot : pivot + 1], work.shape) for pivot in pivots]
        square = [[column[pivot : pivot + 1] for column in columns] for pivot in pivots]
        rows = [work[pivot : pivot + 1] for pivot in pivots]
        for at in range(MODES):
            scale = 1.0 / square[at][at]
            rows[at] = rows[at] * scale
            square[at] = [value * scale for value in square[at]]
            for other in range(MODES):
                if other != at:
                    factor = square[other][at]
                    rows[other] = rows[other] - factor * rows[at]
                    square[other] = [
                        value if to <= at else value - factor * square[at][to]
                        for to, value in enumerate(square[other])
                    ]
        for column, solved in zip(columns, rows):
            work = work - column * solved
        for pivot, solved in zip(pivots, rows):
            work = jnp.where(row == pivot, solved, work)
    return work


def thin_dot(left, right):
    high, right_high = (value.astype(jnp.bfloat16).astype(jnp.float32) for value in (left, right))
    return jnp.dot(
        jnp.concatenate([high, left - high, high], axis=1).astype(jnp.bfloat16),
        jnp.concatenate([right_high, right_high, right - right_high], axis=0).astype(jnp.bfloat16),
        preferred_element_type=jnp.float32,
    )


def final_kernel(terms_ref, basis_ref, jump_ref, multipliers_ref, amplitudes_ref):
    coarse = terms_ref.shape[0] // 3
    loads = basis_ref.shape[0] - coarse
    groups = coarse // GROUP

    def part(block, start, width):
        return terms_ref[block * coarse : (block + 1) * coarse, start : start + width]

    def total(values):
        return jnp.sum(values, axis=0, keepdims=True)

    def scalar(at):
        return terms_ref[2 * coarse + at : 2 * coarse + at + 1, :loads]

    res_res, res_image, jump_jump, jump_second, res_second = (scalar(at) for at in (0, 1, 8, 9, 10))
    coarse_res, jump_z, second_g, image_g = (part(0, at * loads, loads) for at in range(4))
    res_dz, jump_dz, second_z, res_h = (part(1, at * loads, loads) for at in range(4))
    gram, g_h, z_z, z_dz = (part(2, loads + at * coarse, coarse) for at in range(4))
    g_dz = part(2, terms_ref.shape[1] - coarse, coarse)
    row = lax.broadcasted_iota(jnp.int32, (coarse, coarse), 0)
    unit = jnp.where(row == lax.broadcasted_iota(jnp.int32, (coarse, coarse), 1), 1.0, 0.0)
    empty = jnp.zeros((coarse, 5 * coarse - 2 * loads), jnp.float32)
    solved = eliminate(
        jnp.concatenate([gram, g_h, coarse_res, image_g, unit, empty], axis=1), coarse
    )
    inverse_h = solved[:, coarse : 2 * coarse]
    amounts = solved[:, 2 * coarse : 2 * coarse + loads]
    inverse_image = solved[:, 2 * coarse + loads : 2 * coarse + 2 * loads]
    inverse = solved[:, 2 * coarse + 2 * loads : 3 * coarse + 2 * loads]
    products = small_dot(jnp.concatenate([inverse_h, g_h, z_z, g_dz, z_dz], axis=0), amounts)
    inverse_h_amounts, h_amounts, z_amounts, g_dz_amounts, z_dz_amounts = (
        products[at * coarse : (at + 1) * coarse] for at in range(5)
    )
    shares = 2.0 * (inverse_image - inverse_h_amounts)
    both = jnp.concatenate([amounts, shares], axis=0).T
    basis_g, jump_z_rows = basis_ref[loads:], jump_ref[loads:]
    d = basis_ref[:loads] - thin_dot(both[:, :coarse], basis_g)
    u = jump_ref[:loads] - thin_dot(both, jnp.concatenate([jump_z_rows, basis_g], axis=0))
    products = small_dot(jnp.concatenate([g_h, z_z], axis=0), shares)
    image_d = image_g - h_amounts
    inner = res_res - total(amounts * coarse_res)
    curvature = 2.0 * (res_image - total(amounts * (res_h + image_d)))
    u_u = jump_jump - total(amounts * (2.0 * jump_z - z_amounts) + 2.0 * image_d * shares)
    second_u = second_g - g_dz_amounts - products[:coarse]
    jump_u = second_z - z_dz_amounts - 0.5 * products[coarse:]
    d_second = res_second - total(amounts * (res_dz + second_u) + shares * res_h)
    u_second = jump_second - total(amounts * (jump_dz + jump_u) + shares * (0.5 * jump_z + second_u))
    step = inner / curvature
    renewed = step * step * u_u - inner
    grown = 1.0 + renewed / inner
    curvature = grown * grown * curvature - grown * step * (2.0 * d_second + u_u) + 2.0 * step * step * u_second
    second_step = renewed / curvature
    on_d, on_u = step + second_step * grown, second_step * step
    amplitudes = amounts - on_d * shares + 2.0 * on_u * small_dot(inverse, second_u)
    amplitudes_ref[...] = jnp.concatenate(
        [amplitudes[label * GROUP : label * GROUP + MODES] for label in range(groups)], axis=0
    )
    weights = jnp.concatenate([on_d, on_u, jnp.zeros((6, loads), jnp.float32)], axis=0).T
    multipliers_ref[...] = weights[:, 0:1] * d - weights[:, 1:2] * u


def call(kernel, shapes, in_specs, name, scratch=(), flops=0):
    return pl.pallas_call(
        kernel,
        out_shape=[jax.ShapeDtypeStruct(*shape) for shape in shapes],
        in_specs=in_specs,
        out_specs=[VMEM] * len(shapes),
        scratch_shapes=scratch,
        compiler_params=pltpu.CompilerParams(vmem_limit_bytes=24 * 1024 * 1024),
        cost_estimate=pl.CostEstimate(flops=flops, bytes_accessed=2**20, transcendentals=0),
        name=name,
    )


def permute(values, offset, plane_offset=0):
    peers, planes = lax.axis_size("sub"), lax.axis_size("rep")
    offset = offset * planes + plane_offset
    return lax.ppermute(values, ("sub", "rep"), [(at, at ^ offset) for at in range(peers * planes)])


def to_chips(*pairs):
    return [permute(pair, 2 * (len(pairs) - at) + 1) for at, pair in enumerate(pairs)]


def to_core(near, *pairs):
    return permute(jnp.concatenate([near, *(pair[near.shape[0] :] for pair in pairs)], axis=0), 1)


def total(terms):
    chips = [(offset + 1, 0) for offset in reversed(range(2, lax.axis_size("sub"), 2))]
    chips = chips[-1:] + chips[:-1]
    planes = [(1, offset) for offset in reversed(range(1, lax.axis_size("rep")))]
    copies = [terms]
    for offsets, following in (([(1, 0)], len(chips)), (chips, len(planes)), (planes, 1)):
        parts = [permute(copy, *offset) for copy, offset in zip(copies, offsets)]
        kernel = functools.partial(sum_kernel, len(parts) + 1)
        copies = call(kernel, [(terms.shape, terms.dtype)] * following, [VMEM] * (len(parts) + 1), "sum")(
            *parts, copies[0]
        )
    return copies[0]


def fused_body(dual_ops, mode_traces, route, mode_block, local_gap):
    peers = lax.axis_size("sub")
    loads, rows = local_gap.shape
    modes = mode_traces.shape[1]
    subs = mode_block.shape[0]
    groups = subs // AGG_SUBS
    per_peer = rows // peers
    height = loads + GROUP * groups
    f32, i32 = jnp.float32, jnp.int32
    tall = ((height, rows), f32)
    wide = ((3 * GROUP * groups, 4 * loads), f32)

    def pairs(height):
        return [((2 * height, per_peer), f32)] * (peers // 2 - 1)

    def singles(height):
        return [((height, per_peer), f32)] * 3

    def held(value):
        return pltpu.with_memory_space_constraint(value, pltpu.HBM)

    inputs = [route, mode_block.reshape(1, subs), local_gap, mode_traces.transpose(1, 0, 2), dual_ops]
    short = loads + GROUP
    far, values, operator, route, *send = call(
        place_kernel,
        [
            ((rows, rows - 2 * per_peer), jnp.bfloat16),
            ((short, rows), f32),
            (dual_ops.shape, dual_ops.dtype),
            (route.shape, i32),
            *pairs(short),
        ],
        [HBM] * 5,
        "place",
        [pltpu.VMEM((1, subs), i32), pltpu.VMEM((modes, 1, rows), f32), pltpu.SemaphoreType.DMA((5,))],
    )(*(held(value) for value in inputs))
    got = to_chips(*send)
    halves = ((2, rows, rows // 2), dual_ops.dtype)
    edge, slots, placed, near, back, stay = call(
        ready_kernel,
        [((rows, 3 * per_peer), jnp.bfloat16), halves, halves, *singles(short)],
        [VMEM] * 4,
        "ready",
        flops=2 * rows * rows * rows,
    )(route, far, values, operator)
    got_near = to_core(near, *got)
    half = ((height, rows // 2), f32)
    straight_jump, half_image = call(
        first_half_kernel, [half, tall], [VMEM] * (3 + 2 * len(got)), "first_half", flops=2 * rows * rows * height
    )(placed, stay, back, *send, *got)
    handed_jump, image, *image_send = call(
        first_kernel, [half, tall, *pairs(height)], [VMEM] * (5 + len(send)), "first"
    )(far, placed, half_image, got_near, near, *send)
    got = to_chips(*image_send)
    basis, terms, near, back, stay = call(
        middle_kernel, [tall, wide, *singles(height)], [VMEM] * 5, "middle", flops=4 * rows * rows * height
    )(edge, slots, straight_jump, handed_jump, image)
    got_near = to_core(near, *got)
    half_jump, half_second = call(
        second_half_kernel, [tall, tall], [VMEM] * (4 + 2 * len(got)), "second_half", flops=4 * rows * rows * height
    )(slots, placed, stay, back, *image_send, *got)
    jump, terms = call(second_kernel, [tall, wide], [VMEM] * (8 + len(got)), "second")(
        slots, placed, basis, half_jump, half_second, terms, got_near, near, *image_send
    )
    multipliers, amplitudes = call(
        final_kernel, [((loads, rows), f32), ((MODES * groups, loads), f32)], [VMEM] * 3, "final"
    )(total(terms), basis, jump)
    return multipliers, amplitudes.T


def general_body(dual_ops, mode_traces, route, mode_block, local_gap):
    own_index = lax.axis_index("sub")
    plane_index = lax.axis_index("rep")
    peer_count = lax.axis_size("sub")
    plane_count = lax.axis_size("rep")
    operator = dual_ops[0]
    traces = mode_traces[0]
    slot_rows = route[0]
    rows_here = operator.shape[0]
    load_cases = local_gap.shape[0]
    per_peer = rows_here // peer_count
    blocks = mode_block[:, 0]
    block_count = blocks.shape[0] // AGG_SUBS
    coarse = block_count * MODES
    positions = jnp.arange(rows_here, dtype=jnp.int32)
    inverse = jnp.zeros((rows_here,), jnp.int32).at[slot_rows].set(positions)
    slot_peer = positions // per_peer
    within = positions % per_peer
    flip_index = jnp.where(
        slot_peer == own_index, slot_peer * per_peer + per_peer - 1 - within, positions
    )
    peer_ids = jnp.arange(peer_count, dtype=jnp.int32)
    peer_blocks = blocks[peer_ids * plane_count + plane_index]
    own_block = blocks[own_index * plane_count + plane_index]
    labels = jnp.arange(block_count, dtype=jnp.int32)
    peer_onehot = (peer_blocks[:, None] == labels[None, :]).astype(jnp.float32)
    own_onehot = (labels == own_block).astype(jnp.float32)
    trace_slots = traces[:, slot_rows]
    receive_index = flip_index[inverse]

    def to_peers(values):
        return values[:, slot_rows]

    def from_peers(values):
        return values[:, inverse]

    gap_peers = to_peers(local_gap)
    got_traces = lax.all_to_all(trace_slots, "sub", split_axis=1, concat_axis=1, tiled=True)
    got_gap = lax.all_to_all(gap_peers, "sub", split_axis=1, concat_axis=1, tiled=True)
    partner_traces = got_traces[:, flip_index]
    residual = local_gap - got_gap[:, receive_index]
    own_gram = jnp.dot(traces, traces.T, precision=HIGHEST)
    paired = (trace_slots[:, None, :] * partner_traces[None, :, :]).reshape(
        MODES, MODES, peer_count, per_peer
    )
    cross_terms = jnp.sum(paired, axis=3)
    cross_blocks = jnp.einsum("klq,qb->kbl", cross_terms, peer_onehot, precision=HIGHEST)
    own_blocks = own_gram[:, None, :] * own_onehot[None, :, None]
    row_term = 2.0 * (own_blocks - cross_blocks).reshape(MODES, coarse)
    gram_term = (own_onehot[:, None, None] * row_term[None]).reshape(coarse, coarse)

    def coarse_term(values):
        own_part = 2.0 * jnp.dot(values, traces.T, precision=HIGHEST)
        return (own_part[:, None, :] * own_onehot[None, :, None]).reshape(load_cases, coarse)

    def expand(amounts):
        grouped = amounts.reshape(load_cases, block_count, MODES)
        own_amounts = lax.dynamic_index_in_dim(grouped, own_block, 1, keepdims=False)
        own_part = jnp.dot(own_amounts, traces, precision=HIGHEST)
        peer_amounts = jnp.einsum("qb,rbk->rkq", peer_onehot, grouped, precision=HIGHEST)
        spread = jnp.repeat(peer_amounts, per_peer, axis=2)
        peer_part = jnp.sum(spread * partner_traces[None, :, :], axis=1)
        return own_part - from_peers(peer_part)

    squares = jnp.sum(residual * residual, axis=1)
    gram_matrix, coarse_res, norm_res = lax.psum(
        (gram_term, coarse_term(residual), squares), ("sub", "rep")
    )
    factor = jnp.linalg.cholesky(gram_matrix)

    def solve_coarse(right):
        return jax.scipy.linalg.cho_solve((factor, True), right.T).T

    amplitudes = solve_coarse(coarse_res)
    projected = residual - expand(amplitudes)
    inner_sum = norm_res - jnp.sum(amplitudes * coarse_res, axis=1)
    direction = projected
    multipliers = jnp.zeros_like(residual)
    for iteration in range(ITERS):
        product = lax.dot_general(
            direction.astype(jnp.bfloat16),
            operator,
            (((1,), (1,)), ((), ())),
            preferred_element_type=jnp.float32,
        )
        got_product = lax.all_to_all(
            to_peers(product), "sub", split_axis=1, concat_axis=1, tiled=True
        )
        image_jump = product - got_product[:, receive_index]
        coarse_jump, jump_squares, residual_cross, curvature = lax.psum(
            (
                coarse_term(image_jump),
                jnp.sum(image_jump * image_jump, axis=1),
                jnp.sum(residual * image_jump, axis=1),
                jnp.sum(direction * image_jump, axis=1),
            ),
            ("sub", "rep"),
        )
        step_size = inner_sum / curvature
        multipliers = multipliers + step_size[:, None] * direction
        residual = residual - step_size[:, None] * image_jump
        coarse_res = coarse_res - step_size[:, None] * coarse_jump
        norm_res = (
            norm_res - 2.0 * step_size * residual_cross + step_size * step_size * jump_squares
        )
        amplitudes = solve_coarse(coarse_res)
        if iteration + 1 < ITERS:
            projected = residual - expand(amplitudes)
            renewed = norm_res - jnp.sum(amplitudes * coarse_res, axis=1)
            direction = projected + (renewed / inner_sum)[:, None] * direction
            inner_sum = renewed
    return (multipliers, amplitudes)


def fits(mesh, dual_ops, mode_block, local_gap):
    peers, planes = mesh.shape["sub"], mesh.shape["rep"]
    powers = all(size & (size - 1) == 0 for size in (peers, planes))
    whole = dual_ops.shape[1] % (128 * peers) == 0 and local_gap.shape[0] % 16 == 0
    coarse = GROUP * (mode_block.shape[0] // AGG_SUBS)
    return powers and whole and 4 * local_gap.shape[0] == 128 and 8 * coarse == 128


def solution(mesh):
    placed = (
        P(("sub", "rep"), None, None),
        P(("sub", "rep"), None, None),
        P(("sub", "rep"), None),
        P(),
        P(None, ("sub", "rep")),
    )

    def run(dual_ops, mode_traces, route, mode_block, local_gap):
        body = fused_body if fits(mesh, dual_ops, mode_block, local_gap) else general_body
        return jax.shard_map(
            body, mesh=mesh, in_specs=placed, out_specs=(P(None, ("sub", "rep")), P()), check_vma=False
        )(dual_ops, mode_traces, route, mode_block, local_gap)

    return run
```

```python
import functools

import jax
import jax.numpy as jnp
from jax import lax
from jax.experimental import pallas as pl
from jax.experimental.pallas import tpu as pltpu
from jax.sharding import PartitionSpec as P

MODES = 6
AGG_SUBS = 16
ITERS = 2
GROUP = 8

HIGHEST = lax.Precision.HIGHEST
VMEM = pl.BlockSpec(memory_space=pltpu.VMEM)
HBM = pl.BlockSpec(memory_space=pltpu.HBM)
NN = (((1,), (0,)), ((), ()))
NT = (((1,), (1,)), ((), ()))


def split(values):
    high = values.astype(jnp.bfloat16).astype(jnp.float32)
    return jnp.concatenate([high, values - high], axis=0).astype(jnp.bfloat16)


def split_dot(values, matrix, dims):
    rows = values.shape[0]
    both = lax.dot_general(split(values), matrix, dims, preferred_element_type=jnp.float32)
    return both[:rows] + both[rows:]


def small_dot(left, right):
    return jnp.dot(left, right, precision=HIGHEST, preferred_element_type=jnp.float32)


def send_far(values, far_ref, *pair_refs):
    height = values.shape[0]
    per_peer = pair_refs[0].shape[1]
    values = split(values)
    for at, ref in enumerate(pair_refs):
        columns = far_ref[:, 2 * at * per_peer : (2 * at + 2) * per_peer]
        slots = jnp.dot(values, columns, preferred_element_type=jnp.float32)
        slots = slots[:height] + slots[height:]
        ref[:height] = slots[:, :per_peer]
        ref[height:] = slots[:, per_peer:]


def send_near(values, edge_ref, near_ref, back_ref, stay_ref):
    per_peer = back_ref.shape[1]
    slots = split_dot(values, edge_ref[...], NN)
    for at, ref in enumerate((near_ref, back_ref, stay_ref)):
        ref[...] = slots[:, at * per_peer : (at + 1) * per_peer]


def straight(last_ref, pair_refs):
    height = last_ref.shape[0]
    return jnp.concatenate([*(ref[:height] for ref in pair_refs), last_ref[...]], axis=1)


def for_other(near_ref, pair_refs):
    height = near_ref.shape[0]
    return jnp.concatenate([near_ref[...], *(ref[height:] for ref in pair_refs)], axis=1)


def handed(got_ref, height):
    return jnp.concatenate([got_ref[at : at + height] for at in range(0, got_ref.shape[0], height)], axis=1)


def spread(values, loads, groups):
    modes = values[loads:]
    label = modes[MODES : MODES + 1]
    used = lax.broadcasted_iota(jnp.int32, modes.shape, 0) < MODES
    parts = [jnp.where(used & (label == group), modes, 0.0) for group in range(groups)]
    return jnp.concatenate([values[:loads], *parts], axis=0)


def one_hot(route_ref, peer, per_peer):
    start = pl.multiple_of(peer * per_peer, per_peer)
    row_ids = lax.broadcasted_iota(jnp.int32, (route_ref.shape[1], per_peer), 0)
    return jnp.where(row_ids == route_ref[:, pl.ds(start, per_peer)], 1.0, 0.0).astype(jnp.bfloat16)


def place_kernel(
    route_hbm, block_hbm, gap_hbm, traces_hbm, operator_hbm,
    far_ref, values_ref, operator_ref, route_ref, *refs,
):
    *pair_refs, block_ref, traces_ref, sems = refs
    loads, rows = gap_hbm.shape
    per_peer = pair_refs[0].shape[1]
    peers = rows // per_peer
    copies = [
        pltpu.make_async_copy(source, target, sems.at[at])
        for at, (source, target) in enumerate(
            (
                (route_hbm, route_ref),
                (block_hbm, block_ref),
                (traces_hbm, traces_ref),
                (gap_hbm, values_ref.at[pl.ds(0, loads)]),
                (operator_hbm, operator_ref),
            )
        )
    ]

    def build(at):
        peer = own_index ^ (peers - 1 - at)
        far_ref[:, at * per_peer : (at + 1) * per_peer] = one_hot(route_ref, peer, per_peer)

    for copy in copies:
        copy.start()
    own_index = lax.axis_index("sub")
    device = own_index * lax.axis_size("rep") + lax.axis_index("rep")
    copies[0].wait()
    for at in range(peers - 4):
        build(at)
    copies[1].wait()
    copies[2].wait()
    blocks = block_ref[...]
    lane = lax.broadcasted_iota(jnp.int32, blocks.shape, 1)
    own_block = jnp.sum(jnp.where(lane == device, blocks, 0), axis=1, keepdims=True)
    modes = traces_ref.shape[0]
    label = jnp.broadcast_to(own_block.astype(jnp.float32), (1, rows))
    for mode in range(modes):
        values_ref[loads + mode : loads + mode + 1] = traces_ref[mode]
    values_ref[loads + modes : loads + modes + 1] = label
    values_ref[loads + modes + 1 :] = jnp.zeros((GROUP - modes - 1, rows), jnp.float32)
    copies[3].wait()
    for at in range(peers - 4, peers - 2):
        build(at)
    send_far(values_ref[...], far_ref, *pair_refs)
    copies[4].wait()


def ready_kernel(
    route_ref, far_ref, values_ref, operator_ref,
    edge_ref, slots_ref, placed_ref, near_ref, back_ref, stay_ref,
):
    per_peer = back_ref.shape[1]
    peers = far_ref.shape[1] // per_peer + 2
    own_index = lax.axis_index("sub")
    low = lax.broadcasted_iota(jnp.int32, (per_peer, per_peer), 0)
    high = lax.broadcasted_iota(jnp.int32, (per_peer, per_peer), 1)
    reverse = jnp.where(low + high == per_peer - 1, 1.0, 0.0).astype(jnp.bfloat16)
    own_columns = one_hot(route_ref, own_index, per_peer)
    near_columns = one_hot(route_ref, own_index ^ 1, per_peer)
    reversed_columns = jnp.dot(own_columns, reverse, preferred_element_type=jnp.float32).astype(jnp.bfloat16)
    edge_ref[...] = jnp.concatenate([near_columns, reversed_columns, own_columns], axis=1)
    for at in range(peers // 2 - 1):
        start = 2 * at * per_peer
        slots_ref[0, :, at * per_peer : (at + 1) * per_peer] = far_ref[:, start : start + per_peer]
        slots_ref[1, :, (at + 1) * per_peer : (at + 2) * per_peer] = far_ref[:, start + per_peer : start + 2 * per_peer]
    slots_ref[0, :, (peers // 2 - 1) * per_peer :] = own_columns
    slots_ref[1, :, :per_peer] = near_columns
    send_near(values_ref[...], edge_ref, near_ref, back_ref, stay_ref)
    operator = operator_ref[0]
    for half in range(2):
        placed_ref[half] = jnp.dot(
            operator, slots_ref[half], preferred_element_type=jnp.float32
        ).astype(operator.dtype)


def first_half_kernel(placed_ref, stay_ref, back_ref, *refs):
    *pair_refs, jump_ref, image_ref = refs
    sent_refs, got_refs = pair_refs[: len(pair_refs) // 2], pair_refs[len(pair_refs) // 2 :]
    loads = stay_ref.shape[0] - GROUP
    groups = (jump_ref.shape[0] - loads) // GROUP
    own, got = (spread(straight(*refs), loads, groups) for refs in ((stay_ref, sent_refs), (back_ref, got_refs)))
    jump_ref[...] = own - got
    image_ref[...] = split_dot(own - got, placed_ref[0], NT)


def first_kernel(far_ref, placed_ref, half_ref, got_ref, near_ref, *refs):
    sent_refs, (jump_ref, image_ref, *pair_refs) = refs[: len(refs) // 2 - 1], refs[len(refs) // 2 - 1 :]
    height = near_ref.shape[0]
    loads = height - GROUP
    groups = (image_ref.shape[0] - loads) // GROUP
    own, got = (spread(value, loads, groups) for value in (for_other(near_ref, sent_refs), handed(got_ref, height)))
    jump_ref[...] = own - got
    image = half_ref[...] + split_dot(own - got, placed_ref[1], NT)
    image_ref[...] = image
    send_far(image, far_ref, *pair_refs)


def products_of(left, right):
    rows, columns = left.shape[0], right.shape[0]
    both = lax.dot_general(split(left), split(right), NT, preferred_element_type=jnp.float32)
    both = both[:rows] + both[rows:]
    return both[:, :columns] + both[:, columns:]


def by_load(products):
    sums = [jnp.sum(product, axis=1, keepdims=True) for product in products]
    empty = [jnp.zeros_like(sums[0])] * (GROUP - len(sums))
    return jnp.concatenate(sums + empty, axis=1).T


def pack(by_mode, scalars, blocks):
    by_mode = by_mode + pltpu.roll(by_mode, by_mode.shape[1] // 2, 1)
    upper, lower = by_mode[:GROUP], by_mode[GROUP:]
    row = lax.broadcasted_iota(jnp.int32, upper.shape, 0)
    left = lax.broadcasted_iota(jnp.int32, upper.shape, 1) < upper.shape[1] // 2
    spare = [
        jnp.where(left, pltpu.roll(upper, 6, 0), pltpu.roll(upper, 4, 0)),
        jnp.where(left, pltpu.roll(upper, 2, 0), pltpu.roll(lower, 6, 0)),
        jnp.where(left, pltpu.roll(lower, 4, 0), pltpu.roll(lower, 2, 0)),
        jnp.where(row == MODES, *scalars),
    ]
    rows = jnp.concatenate(blocks, axis=0)
    parts = [jnp.where(row < MODES, rows[at * GROUP : (at + 1) * GROUP], spare[at]) for at in range(4)]
    return jnp.concatenate(parts, axis=0)


def unpack(terms):
    parts = [terms[at * GROUP : (at + 1) * GROUP] for at in range(4)]
    row = lax.broadcasted_iota(jnp.int32, parts[0].shape, 0)
    lane = lax.broadcasted_iota(jnp.int32, parts[0].shape, 1)
    half = terms.shape[1] // 2
    turned = [pltpu.roll(part, half, 1) for part in parts[:3]]
    upper = jnp.where(
        row < 2, pltpu.roll(parts[0], 2, 0), jnp.where(row < 4, pltpu.roll(turned[0], 4, 0), pltpu.roll(parts[1], 6, 0))
    )
    lower = jnp.where(
        row < 2, pltpu.roll(turned[1], 2, 0), jnp.where(row < 4, pltpu.roll(parts[2], 4, 0), pltpu.roll(turned[2], 6, 0))
    )
    by_mode = [jnp.where((row < MODES) & (lane < half), part, 0.0) for part in (upper, lower)]
    blocks = [jnp.where(row < MODES, part, 0.0) for part in parts]
    scalars = parts[3][MODES : MODES + 1], parts[3][MODES + 1 : MODES + 2]
    return jnp.concatenate(by_mode, axis=0), scalars, [jnp.concatenate(blocks[at : at + 2], axis=0) for at in (0, 2)]


def middle_kernel(
    edge_ref, slots_ref, straight_ref, handed_ref, image_ref, basis_ref, terms_ref, sums_ref, near_ref, back_ref, stay_ref
):
    image = image_ref[...]
    send_near(image, edge_ref, near_ref, back_ref, stay_ref)
    coarse = terms_ref.shape[0] // 3
    loads = image.shape[0] - coarse
    basis = split_dot(straight_ref[...], slots_ref[0], NT) + split_dot(handed_ref[...], slots_ref[1], NT)
    basis_ref[...] = basis
    residual, residual_image = basis[:loads], image[:loads]
    lanes = terms_ref.shape[1]
    empty = jnp.zeros((lanes - 2 * loads - 2 * coarse, basis.shape[1]), jnp.float32)
    both = products_of(
        jnp.concatenate([basis[loads:], image[loads:]]),
        jnp.concatenate([residual, basis[loads:], image[loads:], empty, residual_image]),
    )
    by_g, by_h = both[:coarse], both[coarse:]
    lane = lax.broadcasted_iota(jnp.int32, (coarse, lanes), 1)
    first, last = lane < loads, lane >= lanes - loads
    terms_ref[:coarse] = jnp.where(first | last, by_g, 0.0)
    terms_ref[coarse : 2 * coarse] = jnp.where(last, pltpu.roll(by_h, lanes - loads, 1), 0.0)
    row = lax.broadcasted_iota(jnp.int32, (coarse, lanes), 0)
    by_mode = jnp.where((lane <= row) | ((lane >= coarse) & (lane < 2 * coarse)), pltpu.roll(by_g, lanes - loads, 1), 0.0)
    terms_ref[2 * coarse :] = by_mode
    sums_ref[...] = by_load([residual * residual, residual * residual_image])


def second_half_kernel(slots_ref, placed_ref, stay_ref, back_ref, *refs):
    *pair_refs, jump_ref, second_ref = refs
    sent_refs, got_refs = pair_refs[: len(pair_refs) // 2], pair_refs[len(pair_refs) // 2 :]
    jump = straight(stay_ref, sent_refs) - straight(back_ref, got_refs)
    jump_ref[...] = split_dot(jump, slots_ref[0], NT)
    second_ref[...] = split_dot(jump, placed_ref[0], NT)


def second_kernel(
    slots_ref, placed_ref, basis_ref, half_jump_ref, half_second_ref, early_ref, sums_ref, got_ref, near_ref, *refs
):
    *sent_refs, jump_ref, terms_ref = refs
    coarse = terms_ref.shape[0] // 2
    loads = basis_ref.shape[0] - coarse
    jump = for_other(near_ref, sent_refs) - handed(got_ref, loads + coarse)
    second = half_second_ref[...] + split_dot(jump, placed_ref[1], NT)
    jump = half_jump_ref[...] + split_dot(jump, slots_ref[1], NT)
    jump_ref[...] = jump
    basis = basis_ref[...]
    residual, jump_loads, second_loads = basis[:loads], jump[:loads], second[:loads]
    both = products_of(
        jnp.concatenate([basis[loads:], jump[loads:], second[loads:]]),
        jnp.concatenate([residual, jump_loads, second_loads, jump[loads:], second[loads:]]),
    )
    by_g, by_z, by_dz = (both[at * coarse : (at + 1) * coarse] for at in range(3))
    lanes = terms_ref.shape[1]
    lane = lax.broadcasted_iota(jnp.int32, (coarse, lanes), 1)
    group = lane // loads
    top = jnp.where(group == 1, by_z, jnp.where(group == 2, by_g, 0.0))
    low = jnp.where(group < 2, by_dz, jnp.where(group == 2, by_z, 0.0))
    row = lax.broadcasted_iota(jnp.int32, (coarse, lanes), 0)
    z_z = pltpu.roll(by_z, 2 * coarse, 1)
    strip = lane // coarse
    by_mode = jnp.where((lane > row) & (strip == 0), z_z, 0.0)
    by_mode = jnp.where(strip == 2, pltpu.roll(by_z, 3 * coarse, 1), by_mode)
    by_mode = jnp.where(strip == 3, pltpu.roll(by_g, 4 * coarse, 1), by_mode)
    diagonal = jnp.sum(jnp.where(lane == row, z_z, 0.0), axis=0, keepdims=True)
    sums = by_load([jump_loads * jump_loads, jump_loads * second_loads, residual * second_loads])
    scalars = (
        jnp.concatenate([sums_ref[0:1], sums_ref[1:2], sums[0:1], sums[1:2]], axis=1),
        jnp.concatenate([sums[2:3], diagonal[:, : lanes - loads]], axis=1),
    )
    terms_ref[...] = pack(
        early_ref[2 * coarse :] + by_mode, scalars, [early_ref[:coarse] + top, early_ref[coarse : 2 * coarse] + low]
    )


def sum_kernel(count, *refs):
    parts = [ref[...] for ref in reversed(refs[:count])]
    while len(parts) > 1:
        parts = [low + high for low, high in zip(parts[::2], parts[1::2])]
    for ref in refs[count:]:
        ref[...] = parts[0]


def eliminate(work, coarse):
    row = lax.broadcasted_iota(jnp.int32, work.shape, 0)
    for start in range(0, coarse, GROUP):
        pivots = range(start, start + MODES)
        columns = [jnp.broadcast_to(work[:, pivot : pivot + 1], work.shape) for pivot in pivots]
        square = [[column[pivot : pivot + 1] for column in columns] for pivot in pivots]
        rows = [work[pivot : pivot + 1] for pivot in pivots]
        for at in range(MODES):
            scale = 1.0 / square[at][at]
            rows[at] = rows[at] * scale
            square[at] = [value * scale for value in square[at]]
            for other in range(MODES):
                if other != at:
                    factor = square[other][at]
                    rows[other] = rows[other] - factor * rows[at]
                    square[other] = [
                        value if to <= at else value - factor * square[at][to]
                        for to, value in enumerate(square[other])
                    ]
        for column, solved in zip(columns, rows):
            work = work - column * solved
        for pivot, solved in zip(pivots, rows):
            work = jnp.where(row == pivot, solved, work)
    return work


def thin_dot(left, right):
    high, right_high = (value.astype(jnp.bfloat16).astype(jnp.float32) for value in (left, right))
    return jnp.dot(
        jnp.concatenate([high, left - high, high], axis=1).astype(jnp.bfloat16),
        jnp.concatenate([right_high, right_high, right - right_high], axis=0).astype(jnp.bfloat16),
        preferred_element_type=jnp.float32,
    )


def final_kernel(terms_ref, basis_ref, jump_ref, multipliers_ref, amplitudes_ref):
    coarse = terms_ref.shape[0] // 2
    loads = basis_ref.shape[0] - coarse
    groups = coarse // GROUP

    def total(values):
        return jnp.sum(values, axis=0, keepdims=True)

    by_mode, (sums, last_sums), (top, low) = unpack(terms_ref[...])
    res_res, res_image, jump_jump, jump_second = (sums[:, at * loads : (at + 1) * loads] for at in range(4))
    res_second, diagonal = last_sums[:, :loads], last_sums[:, loads : loads + coarse]
    coarse_res, jump_z, second_g, image_g = (top[:, at * loads : (at + 1) * loads] for at in range(4))
    res_dz, jump_dz, second_z, res_h = (low[:, at * loads : (at + 1) * loads] for at in range(4))
    triangles, g_h, z_dz, g_dz = (by_mode[:, at * coarse : (at + 1) * coarse] for at in range(4))
    row = lax.broadcasted_iota(jnp.int32, (coarse, coarse), 0)
    column = lax.broadcasted_iota(jnp.int32, (coarse, coarse), 1)
    unit = jnp.where(row == column, 1.0, 0.0)
    other = triangles.T
    gram = jnp.where(row >= column, triangles, other)
    z_z = jnp.where(row < column, triangles, jnp.where(row == column, diagonal, other))
    empty = jnp.zeros((coarse, 5 * coarse - 2 * loads), jnp.float32)
    solved = eliminate(
        jnp.concatenate([gram, g_h, coarse_res, image_g, unit, empty], axis=1), coarse
    )
    inverse_h = solved[:, coarse : 2 * coarse]
    amounts = solved[:, 2 * coarse : 2 * coarse + loads]
    inverse_image = solved[:, 2 * coarse + loads : 2 * coarse + 2 * loads]
    inverse = solved[:, 2 * coarse + 2 * loads : 3 * coarse + 2 * loads]
    products = small_dot(jnp.concatenate([inverse_h, g_h, z_z, g_dz, z_dz], axis=0), amounts)
    inverse_h_amounts, h_amounts, z_amounts, g_dz_amounts, z_dz_amounts = (
        products[at * coarse : (at + 1) * coarse] for at in range(5)
    )
    shares = 2.0 * (inverse_image - inverse_h_amounts)
    both = jnp.concatenate([amounts, shares], axis=0).T
    basis_g, jump_z_rows = basis_ref[loads:], jump_ref[loads:]
    d = basis_ref[:loads] - thin_dot(both[:, :coarse], basis_g)
    u = jump_ref[:loads] - thin_dot(both, jnp.concatenate([jump_z_rows, basis_g], axis=0))
    products = small_dot(jnp.concatenate([g_h, z_z], axis=0), shares)
    image_d = image_g - h_amounts
    inner = res_res - total(amounts * coarse_res)
    curvature = 2.0 * (res_image - total(amounts * (res_h + image_d)))
    u_u = jump_jump - total(amounts * (2.0 * jump_z - z_amounts) + 2.0 * image_d * shares)
    second_u = second_g - g_dz_amounts - products[:coarse]
    jump_u = second_z - z_dz_amounts - 0.5 * products[coarse:]
    d_second = res_second - total(amounts * (res_dz + second_u) + shares * res_h)
    u_second = jump_second - total(amounts * (jump_dz + jump_u) + shares * (0.5 * jump_z + second_u))
    step = inner / curvature
    renewed = step * step * u_u - inner
    grown = 1.0 + renewed / inner
    curvature = grown * grown * curvature - grown * step * (2.0 * d_second + u_u) + 2.0 * step * step * u_second
    second_step = renewed / curvature
    on_d, on_u = step + second_step * grown, second_step * step
    amplitudes = amounts - on_d * shares + 2.0 * on_u * small_dot(inverse, second_u)
    amplitudes_ref[...] = jnp.concatenate(
        [amplitudes[label * GROUP : label * GROUP + MODES] for label in range(groups)], axis=0
    )
    weights = jnp.concatenate([on_d, on_u, jnp.zeros((6, loads), jnp.float32)], axis=0).T
    multipliers_ref[...] = weights[:, 0:1] * d - weights[:, 1:2] * u


def call(kernel, shapes, in_specs, name, scratch=(), flops=0):
    return pl.pallas_call(
        kernel,
        out_shape=[jax.ShapeDtypeStruct(*shape) for shape in shapes],
        in_specs=in_specs,
        out_specs=[VMEM] * len(shapes),
        scratch_shapes=scratch,
        compiler_params=pltpu.CompilerParams(vmem_limit_bytes=24 * 1024 * 1024),
        cost_estimate=pl.CostEstimate(flops=flops, bytes_accessed=2**20, transcendentals=0),
        name=name,
    )


def permute(values, offset, plane_offset=0):
    peers, planes = lax.axis_size("sub"), lax.axis_size("rep")
    offset = offset * planes + plane_offset
    return lax.ppermute(values, ("sub", "rep"), [(at, at ^ offset) for at in range(peers * planes)])


def to_chips(*pairs):
    return [permute(pair, 2 * (len(pairs) - at) + 1) for at, pair in enumerate(pairs)]


def to_core(near, *pairs):
    return permute(jnp.concatenate([near, *(pair[near.shape[0] :] for pair in pairs)], axis=0), 1)


def total(terms):
    chips = [(offset + 1, 0) for offset in reversed(range(2, lax.axis_size("sub"), 2))]
    chips = chips[-1:] + chips[:-1]
    planes = [(1, offset) for offset in reversed(range(1, lax.axis_size("rep")))]
    copies = [terms]
    for offsets, following in (([(1, 0)], len(chips)), (chips, len(planes)), (planes, 1)):
        parts = [permute(copy, *offset) for copy, offset in zip(copies, offsets)]
        kernel = functools.partial(sum_kernel, len(parts) + 1)
        copies = call(kernel, [(terms.shape, terms.dtype)] * following, [VMEM] * (len(parts) + 1), "sum")(
            *parts, copies[0]
        )
    return copies[0]


def fused_body(dual_ops, mode_traces, route, mode_block, local_gap):
    peers = lax.axis_size("sub")
    loads, rows = local_gap.shape
    modes = mode_traces.shape[1]
    subs = mode_block.shape[0]
    groups = subs // AGG_SUBS
    per_peer = rows // peers
    height = loads + GROUP * groups
    f32, i32 = jnp.float32, jnp.int32
    tall = ((height, rows), f32)
    wide = ((3 * GROUP * groups, 4 * loads), f32)

    def pairs(height):
        return [((2 * height, per_peer), f32)] * (peers // 2 - 1)

    def singles(height):
        return [((height, per_peer), f32)] * 3

    def held(value):
        return pltpu.with_memory_space_constraint(value, pltpu.HBM)

    inputs = [route, mode_block.reshape(1, subs), local_gap, mode_traces.transpose(1, 0, 2), dual_ops]
    short = loads + GROUP
    far, values, operator, route, *send = call(
        place_kernel,
        [
            ((rows, rows - 2 * per_peer), jnp.bfloat16),
            ((short, rows), f32),
            (dual_ops.shape, dual_ops.dtype),
            (route.shape, i32),
            *pairs(short),
        ],
        [HBM] * 5,
        "place",
        [pltpu.VMEM((1, subs), i32), pltpu.VMEM((modes, 1, rows), f32), pltpu.SemaphoreType.DMA((5,))],
    )(*(held(value) for value in inputs))
    got = to_chips(*send)
    halves = ((2, rows, rows // 2), dual_ops.dtype)
    edge, slots, placed, near, back, stay = call(
        ready_kernel,
        [((rows, 3 * per_peer), jnp.bfloat16), halves, halves, *singles(short)],
        [VMEM] * 4,
        "ready",
        flops=2 * rows * rows * rows,
    )(route, far, values, operator)
    got_near = to_core(near, *got)
    half = ((height, rows // 2), f32)
    straight_jump, half_image = call(
        first_half_kernel, [half, tall], [VMEM] * (3 + 2 * len(got)), "first_half", flops=2 * rows * rows * height
    )(placed, stay, back, *send, *got)
    handed_jump, image, *image_send = call(
        first_kernel, [half, tall, *pairs(height)], [VMEM] * (5 + len(send)), "first"
    )(far, placed, half_image, got_near, near, *send)
    got = to_chips(*image_send)
    basis, terms, sums, near, back, stay = call(
        middle_kernel, [tall, wide, ((GROUP, loads), f32), *singles(height)], [VMEM] * 5, "middle", flops=4 * rows * rows * height
    )(edge, slots, straight_jump, handed_jump, image)
    got_near = to_core(near, *got)
    half_jump, half_second = call(
        second_half_kernel, [tall, tall], [VMEM] * (4 + 2 * len(got)), "second_half", flops=4 * rows * rows * height
    )(slots, placed, stay, back, *image_send, *got)
    packed = ((2 * GROUP * groups, 4 * loads), f32)
    jump, terms = call(second_kernel, [tall, packed], [VMEM] * (9 + len(got)), "second")(
        slots, placed, basis, half_jump, half_second, terms, sums, got_near, near, *image_send
    )
    multipliers, amplitudes = call(
        final_kernel, [((loads, rows), f32), ((MODES * groups, loads), f32)], [VMEM] * 3, "final"
    )(total(terms), basis, jump)
    return multipliers, amplitudes.T


def general_body(dual_ops, mode_traces, route, mode_block, local_gap):
    own_index = lax.axis_index("sub")
    plane_index = lax.axis_index("rep")
    peer_count = lax.axis_size("sub")
    plane_count = lax.axis_size("rep")
    operator = dual_ops[0]
    traces = mode_traces[0]
    slot_rows = route[0]
    rows_here = operator.shape[0]
    load_cases = local_gap.shape[0]
    per_peer = rows_here // peer_count
    blocks = mode_block[:, 0]
    block_count = blocks.shape[0] // AGG_SUBS
    coarse = block_count * MODES
    positions = jnp.arange(rows_here, dtype=jnp.int32)
    inverse = jnp.zeros((rows_here,), jnp.int32).at[slot_rows].set(positions)
    slot_peer = positions // per_peer
    within = positions % per_peer
    flip_index = jnp.where(
        slot_peer == own_index, slot_peer * per_peer + per_peer - 1 - within, positions
    )
    peer_ids = jnp.arange(peer_count, dtype=jnp.int32)
    peer_blocks = blocks[peer_ids * plane_count + plane_index]
    own_block = blocks[own_index * plane_count + plane_index]
    labels = jnp.arange(block_count, dtype=jnp.int32)
    peer_onehot = (peer_blocks[:, None] == labels[None, :]).astype(jnp.float32)
    own_onehot = (labels == own_block).astype(jnp.float32)
    trace_slots = traces[:, slot_rows]
    receive_index = flip_index[inverse]

    def to_peers(values):
        return values[:, slot_rows]

    def from_peers(values):
        return values[:, inverse]

    gap_peers = to_peers(local_gap)
    got_traces = lax.all_to_all(trace_slots, "sub", split_axis=1, concat_axis=1, tiled=True)
    got_gap = lax.all_to_all(gap_peers, "sub", split_axis=1, concat_axis=1, tiled=True)
    partner_traces = got_traces[:, flip_index]
    residual = local_gap - got_gap[:, receive_index]
    own_gram = jnp.dot(traces, traces.T, precision=HIGHEST)
    paired = (trace_slots[:, None, :] * partner_traces[None, :, :]).reshape(
        MODES, MODES, peer_count, per_peer
    )
    cross_terms = jnp.sum(paired, axis=3)
    cross_blocks = jnp.einsum("klq,qb->kbl", cross_terms, peer_onehot, precision=HIGHEST)
    own_blocks = own_gram[:, None, :] * own_onehot[None, :, None]
    row_term = 2.0 * (own_blocks - cross_blocks).reshape(MODES, coarse)
    gram_term = (own_onehot[:, None, None] * row_term[None]).reshape(coarse, coarse)

    def coarse_term(values):
        own_part = 2.0 * jnp.dot(values, traces.T, precision=HIGHEST)
        return (own_part[:, None, :] * own_onehot[None, :, None]).reshape(load_cases, coarse)

    def expand(amounts):
        grouped = amounts.reshape(load_cases, block_count, MODES)
        own_amounts = lax.dynamic_index_in_dim(grouped, own_block, 1, keepdims=False)
        own_part = jnp.dot(own_amounts, traces, precision=HIGHEST)
        peer_amounts = jnp.einsum("qb,rbk->rkq", peer_onehot, grouped, precision=HIGHEST)
        spread = jnp.repeat(peer_amounts, per_peer, axis=2)
        peer_part = jnp.sum(spread * partner_traces[None, :, :], axis=1)
        return own_part - from_peers(peer_part)

    squares = jnp.sum(residual * residual, axis=1)
    gram_matrix, coarse_res, norm_res = lax.psum(
        (gram_term, coarse_term(residual), squares), ("sub", "rep")
    )
    factor = jnp.linalg.cholesky(gram_matrix)

    def solve_coarse(right):
        return jax.scipy.linalg.cho_solve((factor, True), right.T).T

    amplitudes = solve_coarse(coarse_res)
    projected = residual - expand(amplitudes)
    inner_sum = norm_res - jnp.sum(amplitudes * coarse_res, axis=1)
    direction = projected
    multipliers = jnp.zeros_like(residual)
    for iteration in range(ITERS):
        product = lax.dot_general(
            direction.astype(jnp.bfloat16),
            operator,
            (((1,), (1,)), ((), ())),
            preferred_element_type=jnp.float32,
        )
        got_product = lax.all_to_all(
            to_peers(product), "sub", split_axis=1, concat_axis=1, tiled=True
        )
        image_jump = product - got_product[:, receive_index]
        coarse_jump, jump_squares, residual_cross, curvature = lax.psum(
            (
                coarse_term(image_jump),
                jnp.sum(image_jump * image_jump, axis=1),
                jnp.sum(residual * image_jump, axis=1),
                jnp.sum(direction * image_jump, axis=1),
            ),
            ("sub", "rep"),
        )
        step_size = inner_sum / curvature
        multipliers = multipliers + step_size[:, None] * direction
        residual = residual - step_size[:, None] * image_jump
        coarse_res = coarse_res - step_size[:, None] * coarse_jump
        norm_res = (
            norm_res - 2.0 * step_size * residual_cross + step_size * step_size * jump_squares
        )
        amplitudes = solve_coarse(coarse_res)
        if iteration + 1 < ITERS:
            projected = residual - expand(amplitudes)
            renewed = norm_res - jnp.sum(amplitudes * coarse_res, axis=1)
            direction = projected + (renewed / inner_sum)[:, None] * direction
            inner_sum = renewed
    return (multipliers, amplitudes)


def fits(mesh, dual_ops, mode_block, local_gap):
    peers, planes = mesh.shape["sub"], mesh.shape["rep"]
    powers = all(size & (size - 1) == 0 for size in (peers, planes))
    whole = dual_ops.shape[1] % (128 * peers) == 0 and local_gap.shape[0] % 16 == 0
    coarse = GROUP * (mode_block.shape[0] // AGG_SUBS)
    return powers and whole and 4 * local_gap.shape[0] == 128 and 8 * coarse == 128


def solution(mesh):
    placed = (
        P(("sub", "rep"), None, None),
        P(("sub", "rep"), None, None),
        P(("sub", "rep"), None),
        P(),
        P(None, ("sub", "rep")),
    )

    def run(dual_ops, mode_traces, route, mode_block, local_gap):
        body = fused_body if fits(mesh, dual_ops, mode_block, local_gap) else general_body
        return jax.shard_map(
            body, mesh=mesh, in_specs=placed, out_specs=(P(None, ("sub", "rep")), P()), check_vma=False
        )(dual_ops, mode_traces, route, mode_block, local_gap)

    return run
```

```python
import functools

import jax
import jax.numpy as jnp
from jax import lax
from jax.experimental import pallas as pl
from jax.experimental.pallas import tpu as pltpu
from jax.sharding import PartitionSpec as P

MODES = 6
AGG_SUBS = 16
ITERS = 2
GROUP = 8

HIGHEST = lax.Precision.HIGHEST
VMEM = pl.BlockSpec(memory_space=pltpu.VMEM)
HBM = pl.BlockSpec(memory_space=pltpu.HBM)
NN = (((1,), (0,)), ((), ()))
NT = (((1,), (1,)), ((), ()))


def split(values):
    high = values.astype(jnp.bfloat16).astype(jnp.float32)
    return jnp.concatenate([high, values - high], axis=0).astype(jnp.bfloat16)


def split_dot(values, matrix, dims):
    rows = values.shape[0]
    both = lax.dot_general(split(values), matrix, dims, preferred_element_type=jnp.float32)
    return both[:rows] + both[rows:]


def small_dot(left, right):
    return jnp.dot(left, right, precision=HIGHEST, preferred_element_type=jnp.float32)


def send_far(values, far_ref, *pair_refs):
    height = values.shape[0]
    per_peer = pair_refs[0].shape[1]
    values = split(values)
    for at, ref in enumerate(pair_refs):
        columns = far_ref[:, 2 * at * per_peer : (2 * at + 2) * per_peer]
        slots = jnp.dot(values, columns, preferred_element_type=jnp.float32)
        slots = slots[:height] + slots[height:]
        ref[:height] = slots[:, :per_peer]
        ref[height:] = slots[:, per_peer:]


def send_near(values, edge_ref, near_ref, back_ref, stay_ref):
    per_peer = back_ref.shape[1]
    slots = split_dot(values, edge_ref[...], NN)
    for at, ref in enumerate((near_ref, back_ref, stay_ref)):
        ref[...] = slots[:, at * per_peer : (at + 1) * per_peer]


def straight(last_ref, pair_refs):
    height = last_ref.shape[0]
    return jnp.concatenate([*(ref[:height] for ref in pair_refs), last_ref[...]], axis=1)


def for_other(near_ref, pair_refs):
    height = near_ref.shape[0]
    return jnp.concatenate([near_ref[...], *(ref[height:] for ref in pair_refs)], axis=1)


def handed(got_ref, height, backwards=False):
    starts = list(range(height, got_ref.shape[0], height))
    starts = [0, *(starts[::-1] if backwards else starts)]
    return jnp.concatenate([got_ref[at : at + height] for at in starts], axis=1)


def spread(values, loads, groups):
    modes = values[loads:]
    label = modes[MODES : MODES + 1]
    used = lax.broadcasted_iota(jnp.int32, modes.shape, 0) < MODES
    parts = [jnp.where(used & (label == group), modes, 0.0) for group in range(groups)]
    return jnp.concatenate([values[:loads], *parts], axis=0)


def one_hot(route_ref, peer, per_peer):
    start = pl.multiple_of(peer * per_peer, per_peer)
    row_ids = lax.broadcasted_iota(jnp.int32, (route_ref.shape[1], per_peer), 0)
    return jnp.where(row_ids == route_ref[:, pl.ds(start, per_peer)], 1.0, 0.0).astype(jnp.bfloat16)


def place_kernel(
    route_hbm, block_hbm, gap_hbm, traces_hbm, operator_hbm,
    far_ref, values_ref, operator_ref, route_ref, *refs,
):
    *pair_refs, block_ref, traces_ref, sems = refs
    loads, rows = gap_hbm.shape
    per_peer = pair_refs[0].shape[1]
    peers = rows // per_peer
    copies = [
        pltpu.make_async_copy(source, target, sems.at[at])
        for at, (source, target) in enumerate(
            (
                (route_hbm, route_ref),
                (block_hbm, block_ref),
                (traces_hbm, traces_ref),
                (gap_hbm, values_ref.at[pl.ds(0, loads)]),
                (operator_hbm, operator_ref),
            )
        )
    ]

    def build(at):
        peer = own_index ^ (peers - 1 - at)
        far_ref[:, at * per_peer : (at + 1) * per_peer] = one_hot(route_ref, peer, per_peer)

    for copy in copies:
        copy.start()
    own_index = lax.axis_index("sub")
    device = own_index * lax.axis_size("rep") + lax.axis_index("rep")
    copies[0].wait()
    for at in range(peers - 4):
        build(at)
    copies[1].wait()
    copies[2].wait()
    blocks = block_ref[...]
    lane = lax.broadcasted_iota(jnp.int32, blocks.shape, 1)
    own_block = jnp.sum(jnp.where(lane == device, blocks, 0), axis=1, keepdims=True)
    modes = traces_ref.shape[0]
    label = jnp.broadcast_to(own_block.astype(jnp.float32), (1, rows))
    for mode in range(modes):
        values_ref[loads + mode : loads + mode + 1] = traces_ref[mode]
    values_ref[loads + modes : loads + modes + 1] = label
    values_ref[loads + modes + 1 :] = jnp.zeros((GROUP - modes - 1, rows), jnp.float32)
    copies[3].wait()
    for at in range(peers - 4, peers - 2):
        build(at)
    send_far(values_ref[...], far_ref, *pair_refs)
    copies[4].wait()


def ready_kernel(
    route_ref, far_ref, values_ref, operator_ref,
    edge_ref, slots_ref, placed_ref, near_ref, back_ref, stay_ref,
):
    per_peer = back_ref.shape[1]
    peers = far_ref.shape[1] // per_peer + 2
    own_index = lax.axis_index("sub")
    low = lax.broadcasted_iota(jnp.int32, (per_peer, per_peer), 0)
    high = lax.broadcasted_iota(jnp.int32, (per_peer, per_peer), 1)
    reverse = jnp.where(low + high == per_peer - 1, 1.0, 0.0).astype(jnp.bfloat16)
    own_columns = one_hot(route_ref, own_index, per_peer)
    near_columns = one_hot(route_ref, own_index ^ 1, per_peer)
    reversed_columns = jnp.dot(own_columns, reverse, preferred_element_type=jnp.float32).astype(jnp.bfloat16)
    edge_ref[...] = jnp.concatenate([near_columns, reversed_columns, own_columns], axis=1)
    for at in range(peers // 2 - 1):
        start = 2 * at * per_peer
        slots_ref[0, :, at * per_peer : (at + 1) * per_peer] = far_ref[:, start : start + per_peer]
        slots_ref[1, :, (at + 1) * per_peer : (at + 2) * per_peer] = far_ref[:, start + per_peer : start + 2 * per_peer]
    slots_ref[0, :, (peers // 2 - 1) * per_peer :] = own_columns
    slots_ref[1, :, :per_peer] = near_columns
    send_near(values_ref[...], edge_ref, near_ref, back_ref, stay_ref)
    operator = operator_ref[0]
    for half in range(2):
        placed_ref[half] = jnp.dot(
            operator, slots_ref[half], preferred_element_type=jnp.float32
        ).astype(operator.dtype)


def first_half_kernel(placed_ref, stay_ref, back_ref, *refs):
    *pair_refs, jump_ref, image_ref = refs
    sent_refs, got_refs = pair_refs[: len(pair_refs) // 2], pair_refs[len(pair_refs) // 2 :]
    loads = stay_ref.shape[0] - GROUP
    groups = (jump_ref.shape[0] - loads) // GROUP
    own, got = (spread(straight(*refs), loads, groups) for refs in ((stay_ref, sent_refs), (back_ref, got_refs)))
    jump_ref[...] = own - got
    image_ref[...] = split_dot(own - got, placed_ref[0], NT)


def first_kernel(far_ref, placed_ref, half_ref, got_ref, near_ref, *refs):
    sent_refs, (jump_ref, image_ref, *pair_refs) = refs[: len(refs) // 2 - 1], refs[len(refs) // 2 - 1 :]
    height = near_ref.shape[0]
    loads = height - GROUP
    groups = (image_ref.shape[0] - loads) // GROUP
    own, got = (spread(value, loads, groups) for value in (for_other(near_ref, sent_refs), handed(got_ref, height)))
    jump_ref[...] = own - got
    image = half_ref[...] + split_dot(own - got, placed_ref[1], NT)
    image_ref[...] = image
    send_far(image, far_ref, *pair_refs)


def products_of(left, right):
    rows, columns = left.shape[0], right.shape[0]
    both = lax.dot_general(split(left), split(right), NT, preferred_element_type=jnp.float32)
    both = both[:rows] + both[rows:]
    return both[:, :columns] + both[:, columns:]


def by_load(products):
    sums = [jnp.sum(product, axis=1, keepdims=True) for product in products]
    empty = [jnp.zeros_like(sums[0])] * (GROUP - len(sums))
    return jnp.concatenate(sums + empty, axis=1).T


def pack(by_mode, scalars, blocks):
    by_mode = by_mode + pltpu.roll(by_mode, by_mode.shape[1] // 2, 1)
    upper, lower = by_mode[:GROUP], by_mode[GROUP:]
    row = lax.broadcasted_iota(jnp.int32, upper.shape, 0)
    left = lax.broadcasted_iota(jnp.int32, upper.shape, 1) < upper.shape[1] // 2
    spare = [
        jnp.where(left, pltpu.roll(upper, 6, 0), pltpu.roll(upper, 4, 0)),
        jnp.where(left, pltpu.roll(upper, 2, 0), pltpu.roll(lower, 6, 0)),
        jnp.where(left, pltpu.roll(lower, 4, 0), pltpu.roll(lower, 2, 0)),
        jnp.where(row == MODES, *scalars),
    ]
    rows = jnp.concatenate(blocks, axis=0)
    parts = [jnp.where(row < MODES, rows[at * GROUP : (at + 1) * GROUP], spare[at]) for at in range(4)]
    return jnp.concatenate(parts, axis=0)


def unpack(terms):
    parts = [terms[at * GROUP : (at + 1) * GROUP] for at in range(4)]
    row = lax.broadcasted_iota(jnp.int32, parts[0].shape, 0)
    lane = lax.broadcasted_iota(jnp.int32, parts[0].shape, 1)
    half = terms.shape[1] // 2
    turned = [pltpu.roll(part, half, 1) for part in parts[:3]]
    upper = jnp.where(
        row < 2, pltpu.roll(parts[0], 2, 0), jnp.where(row < 4, pltpu.roll(turned[0], 4, 0), pltpu.roll(parts[1], 6, 0))
    )
    lower = jnp.where(
        row < 2, pltpu.roll(turned[1], 2, 0), jnp.where(row < 4, pltpu.roll(parts[2], 4, 0), pltpu.roll(turned[2], 6, 0))
    )
    by_mode = [jnp.where((row < MODES) & (lane < half), part, 0.0) for part in (upper, lower)]
    blocks = [jnp.where(row < MODES, part, 0.0) for part in parts]
    scalars = parts[3][MODES : MODES + 1], parts[3][MODES + 1 : MODES + 2]
    return jnp.concatenate(by_mode, axis=0), scalars, [jnp.concatenate(blocks[at : at + 2], axis=0) for at in (0, 2)]


def powers(coarse, loads):
    lane = lax.broadcasted_iota(jnp.int32, (coarse, 4 * loads), 1)
    row = lax.broadcasted_iota(jnp.int32, (coarse, 4 * loads), 0)

    def choose(at, *values):
        return functools.reduce(lambda rest, pair: jnp.where(at == pair[0], pair[1], rest), enumerate(values), 0.0 * lane)

    strip, group = lane // coarse, lane // loads
    by_mode = choose(strip, jnp.where(lane > row, 2.0, 0.0), 1.0, 3.0, 2.0)
    scalars = choose(group, 0.0, 1.0, 2.0, 3.0), choose(group, 2.0, 2.0)
    blocks = [choose(group, 0.0, 2.0, 2.0, 1.0), choose(group, 2.0, 3.0, 3.0, 1.0)]
    return pack(by_mode, [line[:1] for line in scalars], blocks)


def magnitude(operator_ref):
    tall = 2 * GROUP
    largest = jnp.zeros((tall, operator_ref.shape[2]), operator_ref.dtype)
    for start in range(0, operator_ref.shape[1], tall):
        part = operator_ref[0, start : start + tall]
        largest = jnp.maximum(largest, jnp.maximum(part, -part))
    largest = jnp.max(largest.astype(jnp.float32), axis=0, keepdims=True)
    return jnp.clip(jnp.max(largest, axis=1, keepdims=True), 1e-30, 1e30)


def scale_of(terms):
    last = terms[-GROUP:]
    half = last.shape[1] // 2
    lane = lax.broadcasted_iota(jnp.int32, last.shape, 1)
    return jnp.where(lane < half, pltpu.roll(last, half, 1), last)[GROUP - 1 :]


def middle_kernel(
    edge_ref, slots_ref, operator_ref, straight_ref, handed_ref, image_ref,
    basis_ref, scale_ref, powers_ref, terms_ref, sums_ref, near_ref, back_ref, stay_ref,
):
    image = image_ref[...]
    send_near(image, edge_ref, near_ref, back_ref, stay_ref)
    coarse = terms_ref.shape[0] // 3
    loads = image.shape[0] - coarse
    basis = split_dot(straight_ref[...], slots_ref[0], NT) + split_dot(handed_ref[...], slots_ref[1], NT)
    basis_ref[...] = basis
    scale = magnitude(operator_ref)
    scale_ref[...] = jnp.broadcast_to(scale, scale_ref.shape)
    image = image * (1.0 / scale)
    residual, residual_image = basis[:loads], image[:loads]
    lanes = terms_ref.shape[1]
    powers_ref[...] = powers(coarse, loads)
    empty = jnp.zeros((lanes - 2 * loads - 2 * coarse, basis.shape[1]), jnp.float32)
    both = products_of(
        jnp.concatenate([basis[loads:], image[loads:]]),
        jnp.concatenate([residual, basis[loads:], image[loads:], empty, residual_image]),
    )
    by_g, by_h = both[:coarse], both[coarse:]
    lane = lax.broadcasted_iota(jnp.int32, (coarse, lanes), 1)
    first, last = lane < loads, lane >= lanes - loads
    terms_ref[:coarse] = jnp.where(first | last, by_g, 0.0)
    terms_ref[coarse : 2 * coarse] = jnp.where(last, pltpu.roll(by_h, lanes - loads, 1), 0.0)
    row = lax.broadcasted_iota(jnp.int32, (coarse, lanes), 0)
    by_mode = jnp.where((lane <= row) | ((lane >= coarse) & (lane < 2 * coarse)), pltpu.roll(by_g, lanes - loads, 1), 0.0)
    terms_ref[2 * coarse :] = by_mode
    sums_ref[...] = by_load([residual * residual, residual * residual_image])


def second_half_kernel(slots_ref, placed_ref, stay_ref, back_ref, *refs):
    *pair_refs, jump_ref, second_ref = refs
    sent_refs, got_refs = pair_refs[: len(pair_refs) // 2], pair_refs[len(pair_refs) // 2 :]
    jump = straight(stay_ref, sent_refs) - straight(back_ref, got_refs)
    jump_ref[...] = split_dot(jump, slots_ref[0], NT)
    second_ref[...] = split_dot(jump, placed_ref[0], NT)


def second_kernel(
    slots_ref, placed_ref, basis_ref, half_jump_ref, half_second_ref, scale_ref, early_ref, sums_ref, got_ref,
    near_ref, *refs,
):
    *sent_refs, jump_ref, terms_ref = refs
    coarse = terms_ref.shape[0] // 2
    loads = basis_ref.shape[0] - coarse
    jump = for_other(near_ref, sent_refs) - handed(got_ref, loads + coarse, backwards=True)
    inverse = 1.0 / scale_ref[:1]
    second = (half_second_ref[...] + split_dot(jump, placed_ref[1], NT)) * inverse * inverse
    jump = (half_jump_ref[...] + split_dot(jump, slots_ref[1], NT)) * inverse
    jump_ref[...] = jump
    basis = basis_ref[...]
    residual, jump_loads, second_loads = basis[:loads], jump[:loads], second[:loads]
    both = products_of(
        jnp.concatenate([basis[loads:], jump[loads:], second[loads:]]),
        jnp.concatenate([residual, jump_loads, second_loads, jump[loads:], second[loads:]]),
    )
    by_g, by_z, by_dz = (both[at * coarse : (at + 1) * coarse] for at in range(3))
    lanes = terms_ref.shape[1]
    lane = lax.broadcasted_iota(jnp.int32, (coarse, lanes), 1)
    group = lane // loads
    top = jnp.where(group == 1, by_z, jnp.where(group == 2, by_g, 0.0))
    low = jnp.where(group < 2, by_dz, jnp.where(group == 2, by_z, 0.0))
    row = lax.broadcasted_iota(jnp.int32, (coarse, lanes), 0)
    z_z = pltpu.roll(by_z, 2 * coarse, 1)
    strip = lane // coarse
    by_mode = jnp.where((lane > row) & (strip == 0), z_z, 0.0)
    by_mode = jnp.where(strip == 2, pltpu.roll(by_z, 3 * coarse, 1), by_mode)
    by_mode = jnp.where(strip == 3, pltpu.roll(by_g, 4 * coarse, 1), by_mode)
    diagonal = jnp.sum(jnp.where(lane == row, z_z, 0.0), axis=0, keepdims=True)
    sums = by_load([jump_loads * jump_loads, jump_loads * second_loads, residual * second_loads])
    scalars = (
        jnp.concatenate([sums_ref[0:1], sums_ref[1:2], sums[0:1], sums[1:2]], axis=1),
        jnp.concatenate([sums[2:3], diagonal[:, :loads], scale_ref[:1, : 2 * loads]], axis=1),
    )
    terms_ref[...] = pack(
        early_ref[2 * coarse :] + by_mode, scalars, [early_ref[:coarse] + top, early_ref[coarse : 2 * coarse] + low]
    )


def sum_kernel(count, powers_ref, *refs):
    parts = [ref[...] for ref in reversed(refs[:count])]
    scales = [scale_of(part) for part in parts]
    largest = functools.reduce(jnp.maximum, scales)
    power = powers_ref[...]
    for at, scale in enumerate(scales):
        factor = scale / largest
        for least in range(3):
            parts[at] = parts[at] * jnp.where(power > least, factor, 1.0)
    while len(parts) > 1:
        parts = [low + high for low, high in zip(parts[::2], parts[1::2])]
    row = lax.broadcasted_iota(jnp.int32, power.shape, 0)
    lane = lax.broadcasted_iota(jnp.int32, power.shape, 1)
    total = jnp.where((row == power.shape[0] - 1) & (lane >= power.shape[1] // 2), largest, parts[0])
    for ref in refs[count:]:
        ref[...] = total


def eliminate(work, coarse):
    row = lax.broadcasted_iota(jnp.int32, work.shape, 0)
    for start in range(0, coarse, GROUP):
        pivots = range(start, start + MODES)
        columns = [jnp.broadcast_to(work[:, pivot : pivot + 1], work.shape) for pivot in pivots]
        square = [[column[pivot : pivot + 1] for column in columns] for pivot in pivots]
        rows = [work[pivot : pivot + 1] for pivot in pivots]
        for at in range(MODES):
            scale = 1.0 / square[at][at]
            rows[at] = rows[at] * scale
            square[at] = [value * scale for value in square[at]]
            for other in range(MODES):
                if other != at:
                    factor = square[other][at]
                    rows[other] = rows[other] - factor * rows[at]
                    square[other] = [
                        value if to <= at else value - factor * square[at][to]
                        for to, value in enumerate(square[other])
                    ]
        for column, solved in zip(columns, rows):
            work = work - column * solved
        for pivot, solved in zip(pivots, rows):
            work = jnp.where(row == pivot, solved, work)
    return work


def thin_dot(left, right):
    high, right_high = (value.astype(jnp.bfloat16).astype(jnp.float32) for value in (left, right))
    return jnp.dot(
        jnp.concatenate([high, left - high, high], axis=1).astype(jnp.bfloat16),
        jnp.concatenate([right_high, right_high, right - right_high], axis=0).astype(jnp.bfloat16),
        preferred_element_type=jnp.float32,
    )


def final_kernel(terms_ref, basis_ref, jump_ref, scale_ref, multipliers_ref, amplitudes_ref):
    coarse = terms_ref.shape[0] // 2
    loads = basis_ref.shape[0] - coarse
    groups = coarse // GROUP

    def total(values):
        return jnp.sum(values, axis=0, keepdims=True)

    scale = scale_of(terms_ref[...])
    ratio = scale_ref[:1, : scale.shape[1]] / scale
    jump = jump_ref[...] * jnp.concatenate([ratio] * (jump_ref.shape[1] // ratio.shape[1]), axis=1)
    by_mode, (sums, last_sums), (top, low) = unpack(terms_ref[...])
    res_res, res_image, jump_jump, jump_second = (sums[:, at * loads : (at + 1) * loads] for at in range(4))
    res_second, diagonal = last_sums[:, :loads], last_sums[:, loads : loads + coarse]
    coarse_res, jump_z, second_g, image_g = (top[:, at * loads : (at + 1) * loads] for at in range(4))
    res_dz, jump_dz, second_z, res_h = (low[:, at * loads : (at + 1) * loads] for at in range(4))
    triangles, g_h, z_dz, g_dz = (by_mode[:, at * coarse : (at + 1) * coarse] for at in range(4))
    row = lax.broadcasted_iota(jnp.int32, (coarse, coarse), 0)
    column = lax.broadcasted_iota(jnp.int32, (coarse, coarse), 1)
    unit = jnp.where(row == column, 1.0, 0.0)
    other = triangles.T
    gram = jnp.where(row >= column, triangles, other)
    z_z = jnp.where(row < column, triangles, jnp.where(row == column, diagonal, other))
    empty = jnp.zeros((coarse, 5 * coarse - 2 * loads), jnp.float32)
    solved = eliminate(
        jnp.concatenate([gram, g_h, coarse_res, image_g, unit, empty], axis=1), coarse
    )
    inverse_h = solved[:, coarse : 2 * coarse]
    amounts = solved[:, 2 * coarse : 2 * coarse + loads]
    inverse_image = solved[:, 2 * coarse + loads : 2 * coarse + 2 * loads]
    inverse = solved[:, 2 * coarse + 2 * loads : 3 * coarse + 2 * loads]
    products = small_dot(jnp.concatenate([inverse_h, g_h, z_z, g_dz, z_dz], axis=0), amounts)
    inverse_h_amounts, h_amounts, z_amounts, g_dz_amounts, z_dz_amounts = (
        products[at * coarse : (at + 1) * coarse] for at in range(5)
    )
    shares = 2.0 * (inverse_image - inverse_h_amounts)
    both = jnp.concatenate([amounts, shares], axis=0).T
    basis_g, jump_z_rows = basis_ref[loads:], jump[loads:]
    d = basis_ref[:loads] - thin_dot(both[:, :coarse], basis_g)
    u = jump[:loads] - thin_dot(both, jnp.concatenate([jump_z_rows, basis_g], axis=0))
    products = small_dot(jnp.concatenate([g_h, z_z], axis=0), shares)
    image_d = image_g - h_amounts
    inner = res_res - total(amounts * coarse_res)
    curvature = 2.0 * (res_image - total(amounts * (res_h + image_d)))
    u_u = jump_jump - total(amounts * (2.0 * jump_z - z_amounts) + 2.0 * image_d * shares)
    second_u = second_g - g_dz_amounts - products[:coarse]
    jump_u = second_z - z_dz_amounts - 0.5 * products[coarse:]
    d_second = res_second - total(amounts * (res_dz + second_u) + shares * res_h)
    u_second = jump_second - total(amounts * (jump_dz + jump_u) + shares * (0.5 * jump_z + second_u))
    step = inner / curvature
    renewed = step * step * u_u - inner
    grown = 1.0 + renewed / inner
    curvature = grown * grown * curvature - grown * step * (2.0 * d_second + u_u) + 2.0 * step * step * u_second
    second_step = renewed / curvature
    on_d, on_u = step + second_step * grown, second_step * step
    amplitudes = amounts - on_d * shares + 2.0 * on_u * small_dot(inverse, second_u)
    amplitudes_ref[...] = jnp.concatenate(
        [amplitudes[label * GROUP : label * GROUP + MODES] for label in range(groups)], axis=0
    )
    inverse = 1.0 / scale[:, :loads]
    weights = jnp.concatenate([on_d * inverse, on_u * inverse, jnp.zeros((6, loads), jnp.float32)], axis=0).T
    multipliers_ref[...] = weights[:, 0:1] * d - weights[:, 1:2] * u


def call(kernel, shapes, in_specs, name, scratch=(), flops=0):
    return pl.pallas_call(
        kernel,
        out_shape=[jax.ShapeDtypeStruct(*shape) for shape in shapes],
        in_specs=in_specs,
        out_specs=[VMEM] * len(shapes),
        scratch_shapes=scratch,
        compiler_params=pltpu.CompilerParams(vmem_limit_bytes=24 * 1024 * 1024),
        cost_estimate=pl.CostEstimate(flops=flops, bytes_accessed=2**20, transcendentals=0),
        name=name,
    )


def permute(values, offset, plane_offset=0):
    peers, planes = lax.axis_size("sub"), lax.axis_size("rep")
    offset = offset * planes + plane_offset
    return lax.ppermute(values, ("sub", "rep"), [(at, at ^ offset) for at in range(peers * planes)])


def to_chips(*pairs):
    return [permute(pair, 2 * (len(pairs) - at) + 1) for at, pair in enumerate(pairs)]


def to_core(near, *pairs):
    return permute(jnp.concatenate([near, *(pair[near.shape[0] :] for pair in pairs)], axis=0), 1)


def total(terms, powers):
    chips = [(offset + 1, 0) for offset in reversed(range(2, lax.axis_size("sub"), 2))]
    planes = [(1, offset) for offset in reversed(range(1, lax.axis_size("rep")))]
    copies = [terms]
    for offsets, following in (([(1, 0)], len(chips)), (chips, len(planes)), (planes, 1)):
        parts = [permute(copy, *offset) for copy, offset in zip(copies, offsets)]
        kernel = functools.partial(sum_kernel, len(parts) + 1)
        copies = call(kernel, [(terms.shape, terms.dtype)] * following, [VMEM] * (len(parts) + 2), "sum")(
            powers, *parts, copies[0]
        )
    return copies[0]


def fused_body(dual_ops, mode_traces, route, mode_block, local_gap):
    peers = lax.axis_size("sub")
    loads, rows = local_gap.shape
    modes = mode_traces.shape[1]
    subs = mode_block.shape[0]
    groups = subs // AGG_SUBS
    per_peer = rows // peers
    height = loads + GROUP * groups
    f32, i32 = jnp.float32, jnp.int32
    tall = ((height, rows), f32)
    wide = ((3 * GROUP * groups, 4 * loads), f32)

    def pairs(height):
        return [((2 * height, per_peer), f32)] * (peers // 2 - 1)

    def singles(height):
        return [((height, per_peer), f32)] * 3

    def held(value):
        return pltpu.with_memory_space_constraint(value, pltpu.HBM)

    inputs = [route, mode_block.reshape(1, subs), local_gap, mode_traces.transpose(1, 0, 2), dual_ops]
    short = loads + GROUP
    far, values, operator, route, *send = call(
        place_kernel,
        [
            ((rows, rows - 2 * per_peer), jnp.bfloat16),
            ((short, rows), f32),
            (dual_ops.shape, dual_ops.dtype),
            (route.shape, i32),
            *pairs(short),
        ],
        [HBM] * 5,
        "place",
        [pltpu.VMEM((1, subs), i32), pltpu.VMEM((modes, 1, rows), f32), pltpu.SemaphoreType.DMA((5,))],
    )(*(held(value) for value in inputs))
    got = to_chips(*send)
    halves = ((2, rows, rows // 2), dual_ops.dtype)
    edge, slots, placed, near, back, stay = call(
        ready_kernel,
        [((rows, 3 * per_peer), jnp.bfloat16), halves, halves, *singles(short)],
        [VMEM] * 4,
        "ready",
        flops=2 * rows * rows * rows,
    )(route, far, values, operator)
    got_near = to_core(near, *got)
    half = ((height, rows // 2), f32)
    straight_jump, half_image = call(
        first_half_kernel, [half, tall], [VMEM] * (3 + 2 * len(got)), "first_half", flops=2 * rows * rows * height
    )(placed, stay, back, *send, *got)
    handed_jump, image, *image_send = call(
        first_kernel, [half, tall, *pairs(height)], [VMEM] * (5 + len(send)), "first"
    )(far, placed, half_image, got_near, near, *send)
    got = to_chips(*image_send)
    packed = ((2 * GROUP * groups, 4 * loads), f32)
    basis, scale, powers, terms, sums, near, back, stay = call(
        middle_kernel,
        [tall, ((GROUP, rows), f32), packed, wide, ((GROUP, loads), f32), *singles(height)],
        [VMEM] * 6,
        "middle",
        flops=4 * rows * rows * height,
    )(edge, slots, operator, straight_jump, handed_jump, image)
    got_near = to_core(near, *got[::-1])
    half_jump, half_second = call(
        second_half_kernel, [tall, tall], [VMEM] * (4 + 2 * len(got)), "second_half", flops=4 * rows * rows * height
    )(slots, placed, stay, back, *image_send, *got)
    jump, terms = call(second_kernel, [tall, packed], [VMEM] * (10 + len(got)), "second")(
        slots, placed, basis, half_jump, half_second, scale, terms, sums, got_near, near, *image_send
    )
    multipliers, amplitudes = call(
        final_kernel, [((loads, rows), f32), ((MODES * groups, loads), f32)], [VMEM] * 4, "final"
    )(total(terms, powers), basis, jump, scale)
    return multipliers, amplitudes.T


def general_body(dual_ops, mode_traces, route, mode_block, local_gap):
    own_index = lax.axis_index("sub")
    plane_index = lax.axis_index("rep")
    peer_count = lax.axis_size("sub")
    plane_count = lax.axis_size("rep")
    operator = dual_ops[0]
    traces = mode_traces[0]
    slot_rows = route[0]
    rows_here = operator.shape[0]
    load_cases = local_gap.shape[0]
    per_peer = rows_here // peer_count
    blocks = mode_block[:, 0]
    block_count = blocks.shape[0] // AGG_SUBS
    coarse = block_count * MODES
    positions = jnp.arange(rows_here, dtype=jnp.int32)
    inverse = jnp.zeros((rows_here,), jnp.int32).at[slot_rows].set(positions)
    slot_peer = positions // per_peer
    within = positions % per_peer
    flip_index = jnp.where(
        slot_peer == own_index, slot_peer * per_peer + per_peer - 1 - within, positions
    )
    peer_ids = jnp.arange(peer_count, dtype=jnp.int32)
    peer_blocks = blocks[peer_ids * plane_count + plane_index]
    own_block = blocks[own_index * plane_count + plane_index]
    labels = jnp.arange(block_count, dtype=jnp.int32)
    peer_onehot = (peer_blocks[:, None] == labels[None, :]).astype(jnp.float32)
    own_onehot = (labels == own_block).astype(jnp.float32)
    trace_slots = traces[:, slot_rows]
    receive_index = flip_index[inverse]

    def to_peers(values):
        return values[:, slot_rows]

    def from_peers(values):
        return values[:, inverse]

    gap_peers = to_peers(local_gap)
    got_traces = lax.all_to_all(trace_slots, "sub", split_axis=1, concat_axis=1, tiled=True)
    got_gap = lax.all_to_all(gap_peers, "sub", split_axis=1, concat_axis=1, tiled=True)
    partner_traces = got_traces[:, flip_index]
    residual = local_gap - got_gap[:, receive_index]
    own_gram = jnp.dot(traces, traces.T, precision=HIGHEST)
    paired = (trace_slots[:, None, :] * partner_traces[None, :, :]).reshape(
        MODES, MODES, peer_count, per_peer
    )
    cross_terms = jnp.sum(paired, axis=3)
    cross_blocks = jnp.einsum("klq,qb->kbl", cross_terms, peer_onehot, precision=HIGHEST)
    own_blocks = own_gram[:, None, :] * own_onehot[None, :, None]
    row_term = 2.0 * (own_blocks - cross_blocks).reshape(MODES, coarse)
    gram_term = (own_onehot[:, None, None] * row_term[None]).reshape(coarse, coarse)

    def coarse_term(values):
        own_part = 2.0 * jnp.dot(values, traces.T, precision=HIGHEST)
        return (own_part[:, None, :] * own_onehot[None, :, None]).reshape(load_cases, coarse)

    def expand(amounts):
        grouped = amounts.reshape(load_cases, block_count, MODES)
        own_amounts = lax.dynamic_index_in_dim(grouped, own_block, 1, keepdims=False)
        own_part = jnp.dot(own_amounts, traces, precision=HIGHEST)
        peer_amounts = jnp.einsum("qb,rbk->rkq", peer_onehot, grouped, precision=HIGHEST)
        spread = jnp.repeat(peer_amounts, per_peer, axis=2)
        peer_part = jnp.sum(spread * partner_traces[None, :, :], axis=1)
        return own_part - from_peers(peer_part)

    squares = jnp.sum(residual * residual, axis=1)
    gram_matrix, coarse_res, norm_res = lax.psum(
        (gram_term, coarse_term(residual), squares), ("sub", "rep")
    )
    factor = jnp.linalg.cholesky(gram_matrix)

    def solve_coarse(right):
        return jax.scipy.linalg.cho_solve((factor, True), right.T).T

    amplitudes = solve_coarse(coarse_res)
    projected = residual - expand(amplitudes)
    inner_sum = norm_res - jnp.sum(amplitudes * coarse_res, axis=1)
    direction = projected
    multipliers = jnp.zeros_like(residual)
    for iteration in range(ITERS):
        product = lax.dot_general(
            direction.astype(jnp.bfloat16),
            operator,
            (((1,), (1,)), ((), ())),
            preferred_element_type=jnp.float32,
        )
        got_product = lax.all_to_all(
            to_peers(product), "sub", split_axis=1, concat_axis=1, tiled=True
        )
        image_jump = product - got_product[:, receive_index]
        coarse_jump, jump_squares, residual_cross, curvature = lax.psum(
            (
                coarse_term(image_jump),
                jnp.sum(image_jump * image_jump, axis=1),
                jnp.sum(residual * image_jump, axis=1),
                jnp.sum(direction * image_jump, axis=1),
            ),
            ("sub", "rep"),
        )
        step_size = inner_sum / curvature
        multipliers = multipliers + step_size[:, None] * direction
        residual = residual - step_size[:, None] * image_jump
        coarse_res = coarse_res - step_size[:, None] * coarse_jump
        norm_res = (
            norm_res - 2.0 * step_size * residual_cross + step_size * step_size * jump_squares
        )
        amplitudes = solve_coarse(coarse_res)
        if iteration + 1 < ITERS:
            projected = residual - expand(amplitudes)
            renewed = norm_res - jnp.sum(amplitudes * coarse_res, axis=1)
            direction = projected + (renewed / inner_sum)[:, None] * direction
            inner_sum = renewed
    return (multipliers, amplitudes)


def fits(mesh, dual_ops, mode_block, local_gap):
    peers, planes = mesh.shape["sub"], mesh.shape["rep"]
    powers = all(size & (size - 1) == 0 for size in (peers, planes))
    whole = dual_ops.shape[1] % (128 * peers) == 0 and local_gap.shape[0] % 16 == 0
    coarse = GROUP * (mode_block.shape[0] // AGG_SUBS)
    return powers and whole and 4 * local_gap.shape[0] == 128 and 8 * coarse == 128


def solution(mesh):
    placed = (
        P(("sub", "rep"), None, None),
        P(("sub", "rep"), None, None),
        P(("sub", "rep"), None),
        P(),
        P(None, ("sub", "rep")),
    )

    def run(dual_ops, mode_traces, route, mode_block, local_gap):
        body = fused_body if fits(mesh, dual_ops, mode_block, local_gap) else general_body
        return jax.shard_map(
            body, mesh=mesh, in_specs=placed, out_specs=(P(None, ("sub", "rep")), P()), check_vma=False
        )(dual_ops, mode_traces, route, mode_block, local_gap)

    return run
```

```python
import functools

import jax
import jax.numpy as jnp
from jax import lax
from jax.experimental import pallas as pl
from jax.experimental.pallas import tpu as pltpu
from jax.sharding import PartitionSpec as P

MODES = 6
AGG_SUBS = 16
ITERS = 2
GROUP = 8

HIGHEST = lax.Precision.HIGHEST
VMEM = pl.BlockSpec(memory_space=pltpu.VMEM)
HBM = pl.BlockSpec(memory_space=pltpu.HBM)
NN = (((1,), (0,)), ((), ()))
NT = (((1,), (1,)), ((), ()))


def split(values):
    high = values.astype(jnp.bfloat16).astype(jnp.float32)
    return jnp.concatenate([high, values - high], axis=0).astype(jnp.bfloat16)


def split_dot(values, matrix, dims):
    rows = values.shape[0]
    both = lax.dot_general(split(values), matrix, dims, preferred_element_type=jnp.float32)
    return both[:rows] + both[rows:]


def small_dot(left, right):
    return jnp.dot(left, right, precision=HIGHEST, preferred_element_type=jnp.float32)


def send_far(values, far_ref, *pair_refs):
    height = values.shape[0]
    per_peer = pair_refs[0].shape[1]
    values = split(values)
    for at, ref in enumerate(pair_refs):
        columns = far_ref[:, 2 * at * per_peer : (2 * at + 2) * per_peer]
        slots = jnp.dot(values, columns, preferred_element_type=jnp.float32)
        slots = slots[:height] + slots[height:]
        ref[:height] = slots[:, :per_peer]
        ref[height:] = slots[:, per_peer:]


def send_near(values, edge_ref, near_ref, back_ref, stay_ref):
    per_peer = back_ref.shape[1]
    slots = split_dot(values, edge_ref[...], NN)
    for at, ref in enumerate((near_ref, back_ref, stay_ref)):
        ref[...] = slots[:, at * per_peer : (at + 1) * per_peer]


def straight(last_ref, pair_refs):
    height = last_ref.shape[0]
    return jnp.concatenate([*(ref[:height] for ref in pair_refs), last_ref[...]], axis=1)


def for_other(near_ref, pair_refs):
    height = near_ref.shape[0]
    return jnp.concatenate([near_ref[...], *(ref[height:] for ref in pair_refs)], axis=1)


def handed(got_ref, height, backwards=False):
    starts = list(range(height, got_ref.shape[0], height))
    starts = [0, *(starts[::-1] if backwards else starts)]
    return jnp.concatenate([got_ref[at : at + height] for at in starts], axis=1)


def spread(values, loads, groups):
    modes = values[loads:]
    label = modes[MODES : MODES + 1]
    used = lax.broadcasted_iota(jnp.int32, modes.shape, 0) < MODES
    parts = [jnp.where(used & (label == group), modes, 0.0) for group in range(groups)]
    return jnp.concatenate([values[:loads], *parts], axis=0)


def one_hot(route_ref, peer, per_peer):
    start = pl.multiple_of(peer * per_peer, per_peer)
    row_ids = lax.broadcasted_iota(jnp.int32, (route_ref.shape[1], per_peer), 0)
    return jnp.where(row_ids == route_ref[:, pl.ds(start, per_peer)], 1.0, 0.0).astype(jnp.bfloat16)


def place_kernel(
    route_hbm, block_hbm, gap_hbm, traces_hbm, operator_hbm,
    far_ref, values_ref, operator_ref, route_ref, *refs,
):
    *pair_refs, block_ref, traces_ref, sems = refs
    loads, rows = gap_hbm.shape
    per_peer = pair_refs[0].shape[1]
    peers = rows // per_peer
    copies = [
        pltpu.make_async_copy(source, target, sems.at[at])
        for at, (source, target) in enumerate(
            (
                (route_hbm, route_ref),
                (block_hbm, block_ref),
                (traces_hbm, traces_ref),
                (gap_hbm, values_ref.at[pl.ds(0, loads)]),
                (operator_hbm, operator_ref),
            )
        )
    ]

    def build(at):
        peer = own_index ^ (peers - 1 - at)
        far_ref[:, at * per_peer : (at + 1) * per_peer] = one_hot(route_ref, peer, per_peer)

    for copy in copies:
        copy.start()
    own_index = lax.axis_index("sub")
    device = own_index * lax.axis_size("rep") + lax.axis_index("rep")
    copies[0].wait()
    for at in range(peers - 4):
        build(at)
    copies[1].wait()
    copies[2].wait()
    blocks = block_ref[...]
    lane = lax.broadcasted_iota(jnp.int32, blocks.shape, 1)
    own_block = jnp.sum(jnp.where(lane == device, blocks, 0), axis=1, keepdims=True)
    modes = traces_ref.shape[0]
    label = jnp.broadcast_to(own_block.astype(jnp.float32), (1, rows))
    for mode in range(modes):
        values_ref[loads + mode : loads + mode + 1] = traces_ref[mode]
    values_ref[loads + modes : loads + modes + 1] = label
    values_ref[loads + modes + 1 :] = jnp.zeros((GROUP - modes - 1, rows), jnp.float32)
    copies[3].wait()
    for at in range(peers - 4, peers - 2):
        build(at)
    send_far(values_ref[...], far_ref, *pair_refs)
    copies[4].wait()


def ready_kernel(
    route_ref, far_ref, values_ref, operator_ref,
    edge_ref, slots_ref, placed_ref, near_ref, back_ref, stay_ref,
):
    per_peer = back_ref.shape[1]
    peers = far_ref.shape[1] // per_peer + 2
    own_index = lax.axis_index("sub")
    low = lax.broadcasted_iota(jnp.int32, (per_peer, per_peer), 0)
    high = lax.broadcasted_iota(jnp.int32, (per_peer, per_peer), 1)
    reverse = jnp.where(low + high == per_peer - 1, 1.0, 0.0).astype(jnp.bfloat16)
    own_columns = one_hot(route_ref, own_index, per_peer)
    near_columns = one_hot(route_ref, own_index ^ 1, per_peer)
    reversed_columns = jnp.dot(own_columns, reverse, preferred_element_type=jnp.float32).astype(jnp.bfloat16)
    edge_ref[...] = jnp.concatenate([near_columns, reversed_columns, own_columns], axis=1)
    for at in range(peers // 2 - 1):
        start = 2 * at * per_peer
        slots_ref[0, :, at * per_peer : (at + 1) * per_peer] = far_ref[:, start : start + per_peer]
        slots_ref[1, :, (at + 1) * per_peer : (at + 2) * per_peer] = far_ref[:, start + per_peer : start + 2 * per_peer]
    slots_ref[0, :, (peers // 2 - 1) * per_peer :] = own_columns
    slots_ref[1, :, :per_peer] = near_columns
    send_near(values_ref[...], edge_ref, near_ref, back_ref, stay_ref)
    operator = operator_ref[0]
    for half in range(2):
        placed_ref[half] = jnp.dot(
            operator, slots_ref[half], preferred_element_type=jnp.float32
        ).astype(operator.dtype)


def first_half_kernel(placed_ref, stay_ref, back_ref, *refs):
    *pair_refs, jump_ref, image_ref = refs
    sent_refs, got_refs = pair_refs[: len(pair_refs) // 2], pair_refs[len(pair_refs) // 2 :]
    loads = stay_ref.shape[0] - GROUP
    groups = (jump_ref.shape[0] - loads) // GROUP
    own, got = (spread(straight(*refs), loads, groups) for refs in ((stay_ref, sent_refs), (back_ref, got_refs)))
    jump_ref[...] = own - got
    image_ref[...] = split_dot(own - got, placed_ref[0], NT)


def first_kernel(far_ref, placed_ref, half_ref, got_ref, near_ref, *refs):
    sent_refs, (jump_ref, image_ref, *pair_refs) = refs[: len(refs) // 2 - 1], refs[len(refs) // 2 - 1 :]
    height = near_ref.shape[0]
    loads = height - GROUP
    groups = (image_ref.shape[0] - loads) // GROUP
    own, got = (spread(value, loads, groups) for value in (for_other(near_ref, sent_refs), handed(got_ref, height)))
    jump_ref[...] = own - got
    image = half_ref[...] + split_dot(own - got, placed_ref[1], NT)
    image_ref[...] = image
    send_far(image, far_ref, *pair_refs)


def products_of(left, right):
    rows, columns = left.shape[0], right.shape[0]
    both = lax.dot_general(split(left), split(right), NT, preferred_element_type=jnp.float32)
    both = both[:rows] + both[rows:]
    return both[:, :columns] + both[:, columns:]


def by_load(products):
    sums = [jnp.sum(product, axis=1, keepdims=True) for product in products]
    empty = [jnp.zeros_like(sums[0])] * (GROUP - len(sums))
    return jnp.concatenate(sums + empty, axis=1).T


def pack(by_mode, scalars, blocks):
    by_mode = by_mode + pltpu.roll(by_mode, by_mode.shape[1] // 2, 1)
    upper, lower = by_mode[:GROUP], by_mode[GROUP:]
    row = lax.broadcasted_iota(jnp.int32, upper.shape, 0)
    left = lax.broadcasted_iota(jnp.int32, upper.shape, 1) < upper.shape[1] // 2
    spare = [
        jnp.where(left, pltpu.roll(upper, 6, 0), pltpu.roll(upper, 4, 0)),
        jnp.where(left, pltpu.roll(upper, 2, 0), pltpu.roll(lower, 6, 0)),
        jnp.where(left, pltpu.roll(lower, 4, 0), pltpu.roll(lower, 2, 0)),
        jnp.where(row == MODES, *scalars),
    ]
    rows = jnp.concatenate(blocks, axis=0)
    parts = [jnp.where(row < MODES, rows[at * GROUP : (at + 1) * GROUP], spare[at]) for at in range(4)]
    return jnp.concatenate(parts, axis=0)


def unpack(terms):
    parts = [terms[at * GROUP : (at + 1) * GROUP] for at in range(4)]
    row = lax.broadcasted_iota(jnp.int32, parts[0].shape, 0)
    lane = lax.broadcasted_iota(jnp.int32, parts[0].shape, 1)
    half = terms.shape[1] // 2
    turned = [pltpu.roll(part, half, 1) for part in parts[:3]]
    upper = jnp.where(
        row < 2, pltpu.roll(parts[0], 2, 0), jnp.where(row < 4, pltpu.roll(turned[0], 4, 0), pltpu.roll(parts[1], 6, 0))
    )
    lower = jnp.where(
        row < 2, pltpu.roll(turned[1], 2, 0), jnp.where(row < 4, pltpu.roll(parts[2], 4, 0), pltpu.roll(turned[2], 6, 0))
    )
    by_mode = [jnp.where((row < MODES) & (lane < half), part, 0.0) for part in (upper, lower)]
    blocks = [jnp.where(row < MODES, part, 0.0) for part in parts]
    scalars = parts[3][MODES : MODES + 1], parts[3][MODES + 1 : MODES + 2]
    return jnp.concatenate(by_mode, axis=0), scalars, [jnp.concatenate(blocks[at : at + 2], axis=0) for at in (0, 2)]


def powers(coarse, loads):
    lane = lax.broadcasted_iota(jnp.int32, (coarse, 4 * loads), 1)
    row = lax.broadcasted_iota(jnp.int32, (coarse, 4 * loads), 0)

    def choose(at, *values):
        return functools.reduce(lambda rest, pair: jnp.where(at == pair[0], pair[1], rest), enumerate(values), 0.0 * lane)

    strip, group = lane // coarse, lane // loads
    by_mode = choose(strip, jnp.where(lane > row, 2.0, 0.0), 1.0, 3.0, 2.0)
    scalars = choose(group, 0.0, 1.0, 2.0, 3.0), choose(group, 2.0, 2.0)
    blocks = [choose(group, 0.0, 2.0, 2.0, 1.0), choose(group, 2.0, 3.0, 3.0, 1.0)]
    return pack(by_mode, [line[:1] for line in scalars], blocks)


def magnitude(operator_ref):
    tall = 2 * GROUP
    largest = jnp.zeros((tall, operator_ref.shape[2]), operator_ref.dtype)
    for start in range(0, operator_ref.shape[1], tall):
        part = operator_ref[0, start : start + tall]
        largest = jnp.maximum(largest, jnp.maximum(part, -part))
    largest = jnp.max(largest.astype(jnp.float32), axis=0, keepdims=True)
    return jnp.clip(jnp.max(largest, axis=1, keepdims=True), 1e-30, 1e30)


def scale_of(terms):
    last = terms[-GROUP:]
    half = last.shape[1] // 2
    lane = lax.broadcasted_iota(jnp.int32, last.shape, 1)
    return jnp.where(lane < half, pltpu.roll(last, half, 1), last)[GROUP - 1 :]


def middle_kernel(
    edge_ref, slots_ref, operator_ref, straight_ref, handed_ref, image_ref,
    basis_ref, scale_ref, powers_ref, terms_ref, sums_ref, near_ref, back_ref, stay_ref,
):
    image = image_ref[...]
    send_near(image, edge_ref, near_ref, back_ref, stay_ref)
    coarse = terms_ref.shape[0] // 3
    loads = image.shape[0] - coarse
    basis = split_dot(straight_ref[...], slots_ref[0], NT) + split_dot(handed_ref[...], slots_ref[1], NT)
    basis_ref[...] = basis
    scale = magnitude(operator_ref)
    scale_ref[...] = jnp.broadcast_to(scale, scale_ref.shape)
    image = image * (1.0 / scale)
    residual, residual_image = basis[:loads], image[:loads]
    lanes = terms_ref.shape[1]
    powers_ref[...] = powers(coarse, loads)
    empty = jnp.zeros((lanes - 2 * loads - 2 * coarse, basis.shape[1]), jnp.float32)
    both = products_of(
        jnp.concatenate([basis[loads:], image[loads:]]),
        jnp.concatenate([residual, basis[loads:], image[loads:], empty, residual_image]),
    )
    by_g, by_h = both[:coarse], both[coarse:]
    lane = lax.broadcasted_iota(jnp.int32, (coarse, lanes), 1)
    first, last = lane < loads, lane >= lanes - loads
    terms_ref[:coarse] = jnp.where(first | last, by_g, 0.0)
    terms_ref[coarse : 2 * coarse] = jnp.where(last, pltpu.roll(by_h, lanes - loads, 1), 0.0)
    row = lax.broadcasted_iota(jnp.int32, (coarse, lanes), 0)
    by_mode = jnp.where((lane <= row) | ((lane >= coarse) & (lane < 2 * coarse)), pltpu.roll(by_g, lanes - loads, 1), 0.0)
    terms_ref[2 * coarse :] = by_mode
    sums_ref[...] = by_load([residual * residual, residual * residual_image])


def second_half_kernel(slots_ref, placed_ref, scale_ref, stay_ref, back_ref, *refs):
    *pair_refs, jump_ref, second_ref = refs
    sent_refs, got_refs = pair_refs[: len(pair_refs) // 2], pair_refs[len(pair_refs) // 2 :]
    jump = straight(stay_ref, sent_refs) - straight(back_ref, got_refs)
    jump = jump * (1.0 / scale_ref[:1, : jump.shape[1]])
    jump_ref[...] = split_dot(jump, slots_ref[0], NT)
    second_ref[...] = split_dot(jump, placed_ref[0], NT)


def second_kernel(
    slots_ref, placed_ref, basis_ref, half_jump_ref, half_second_ref, scale_ref, early_ref, sums_ref, got_ref,
    near_ref, *refs,
):
    *sent_refs, jump_ref, terms_ref = refs
    coarse = terms_ref.shape[0] // 2
    loads = basis_ref.shape[0] - coarse
    jump = for_other(near_ref, sent_refs) - handed(got_ref, loads + coarse, backwards=True)
    inverse = 1.0 / scale_ref[:1]
    jump = jump * inverse[:, : jump.shape[1]]
    second = (half_second_ref[...] + split_dot(jump, placed_ref[1], NT)) * inverse
    jump = half_jump_ref[...] + split_dot(jump, slots_ref[1], NT)
    jump_ref[...] = jump
    basis = basis_ref[...]
    residual, jump_loads, second_loads = basis[:loads], jump[:loads], second[:loads]
    both = products_of(
        jnp.concatenate([basis[loads:], jump[loads:], second[loads:]]),
        jnp.concatenate([residual, jump_loads, second_loads, jump[loads:], second[loads:]]),
    )
    by_g, by_z, by_dz = (both[at * coarse : (at + 1) * coarse] for at in range(3))
    lanes = terms_ref.shape[1]
    lane = lax.broadcasted_iota(jnp.int32, (coarse, lanes), 1)
    group = lane // loads
    top = jnp.where(group == 1, by_z, jnp.where(group == 2, by_g, 0.0))
    low = jnp.where(group < 2, by_dz, jnp.where(group == 2, by_z, 0.0))
    row = lax.broadcasted_iota(jnp.int32, (coarse, lanes), 0)
    z_z = pltpu.roll(by_z, 2 * coarse, 1)
    strip = lane // coarse
    by_mode = jnp.where((lane > row) & (strip == 0), z_z, 0.0)
    by_mode = jnp.where(strip == 2, pltpu.roll(by_z, 3 * coarse, 1), by_mode)
    by_mode = jnp.where(strip == 3, pltpu.roll(by_g, 4 * coarse, 1), by_mode)
    diagonal = jnp.sum(jnp.where(lane == row, z_z, 0.0), axis=0, keepdims=True)
    sums = by_load([jump_loads * jump_loads, jump_loads * second_loads, residual * second_loads])
    scalars = (
        jnp.concatenate([sums_ref[0:1], sums_ref[1:2], sums[0:1], sums[1:2]], axis=1),
        jnp.concatenate([sums[2:3], diagonal[:, :loads], scale_ref[:1, : 2 * loads]], axis=1),
    )
    terms_ref[...] = pack(
        early_ref[2 * coarse :] + by_mode, scalars, [early_ref[:coarse] + top, early_ref[coarse : 2 * coarse] + low]
    )


def sum_kernel(count, powers_ref, *refs):
    parts = [ref[...] for ref in reversed(refs[:count])]
    scales = [scale_of(part) for part in parts]
    largest = functools.reduce(jnp.maximum, scales)
    power = powers_ref[...]
    inverse = 1.0 / largest
    for at, scale in enumerate(scales):
        factor = scale * inverse
        square = factor * factor
        high = jnp.where(power > 2, square * factor, square)
        parts[at] = parts[at] * jnp.where(power > 1, high, jnp.where(power > 0, factor, 1.0))
    while len(parts) > 1:
        parts = [low + high for low, high in zip(parts[::2], parts[1::2])]
    row = lax.broadcasted_iota(jnp.int32, power.shape, 0)
    lane = lax.broadcasted_iota(jnp.int32, power.shape, 1)
    total = jnp.where((row == power.shape[0] - 1) & (lane >= power.shape[1] // 2), largest, parts[0])
    for ref in refs[count:]:
        ref[...] = total


def eliminate(work, coarse):
    row = lax.broadcasted_iota(jnp.int32, work.shape, 0)
    for start in range(0, coarse, GROUP):
        pivots = range(start, start + MODES)
        columns = [jnp.broadcast_to(work[:, pivot : pivot + 1], work.shape) for pivot in pivots]
        square = [[column[pivot : pivot + 1] for column in columns] for pivot in pivots]
        rows = [work[pivot : pivot + 1] for pivot in pivots]
        for at in range(MODES):
            scale = 1.0 / square[at][at]
            rows[at] = rows[at] * scale
            square[at] = [value * scale for value in square[at]]
            for other in range(MODES):
                if other != at:
                    factor = square[other][at]
                    rows[other] = rows[other] - factor * rows[at]
                    square[other] = [
                        value if to <= at else value - factor * square[at][to]
                        for to, value in enumerate(square[other])
                    ]
        for column, solved in zip(columns, rows):
            work = work - column * solved
        for pivot, solved in zip(pivots, rows):
            work = jnp.where(row == pivot, solved, work)
    return work


def thin_dot(left, right):
    high, right_high = (value.astype(jnp.bfloat16).astype(jnp.float32) for value in (left, right))
    return jnp.dot(
        jnp.concatenate([high, left - high, high], axis=1).astype(jnp.bfloat16),
        jnp.concatenate([right_high, right_high, right - right_high], axis=0).astype(jnp.bfloat16),
        preferred_element_type=jnp.float32,
    )


def final_kernel(terms_ref, basis_ref, jump_ref, scale_ref, multipliers_ref, amplitudes_ref):
    coarse = terms_ref.shape[0] // 2
    loads = basis_ref.shape[0] - coarse
    groups = coarse // GROUP

    def total(values):
        return jnp.sum(values, axis=0, keepdims=True)

    scale = scale_of(terms_ref[...])
    ratio = scale_ref[:1, : scale.shape[1]] / scale
    jump = jump_ref[...] * jnp.concatenate([ratio] * (jump_ref.shape[1] // ratio.shape[1]), axis=1)
    by_mode, (sums, last_sums), (top, low) = unpack(terms_ref[...])
    res_res, res_image, jump_jump, jump_second = (sums[:, at * loads : (at + 1) * loads] for at in range(4))
    res_second, diagonal = last_sums[:, :loads], last_sums[:, loads : loads + coarse]
    coarse_res, jump_z, second_g, image_g = (top[:, at * loads : (at + 1) * loads] for at in range(4))
    res_dz, jump_dz, second_z, res_h = (low[:, at * loads : (at + 1) * loads] for at in range(4))
    triangles, g_h, z_dz, g_dz = (by_mode[:, at * coarse : (at + 1) * coarse] for at in range(4))
    row = lax.broadcasted_iota(jnp.int32, (coarse, coarse), 0)
    column = lax.broadcasted_iota(jnp.int32, (coarse, coarse), 1)
    unit = jnp.where(row == column, 1.0, 0.0)
    other = triangles.T
    gram = jnp.where(row >= column, triangles, other)
    z_z = jnp.where(row < column, triangles, jnp.where(row == column, diagonal, other))
    empty = jnp.zeros((coarse, 5 * coarse - 2 * loads), jnp.float32)
    solved = eliminate(
        jnp.concatenate([gram, g_h, coarse_res, image_g, unit, empty], axis=1), coarse
    )
    inverse_h = solved[:, coarse : 2 * coarse]
    amounts = solved[:, 2 * coarse : 2 * coarse + loads]
    inverse_image = solved[:, 2 * coarse + loads : 2 * coarse + 2 * loads]
    inverse = solved[:, 2 * coarse + 2 * loads : 3 * coarse + 2 * loads]
    products = small_dot(jnp.concatenate([inverse_h, g_h, z_z, g_dz, z_dz], axis=0), amounts)
    inverse_h_amounts, h_amounts, z_amounts, g_dz_amounts, z_dz_amounts = (
        products[at * coarse : (at + 1) * coarse] for at in range(5)
    )
    shares = 2.0 * (inverse_image - inverse_h_amounts)
    both = jnp.concatenate([amounts, shares], axis=0).T
    basis_g, jump_z_rows = basis_ref[loads:], jump[loads:]
    d = basis_ref[:loads] - thin_dot(both[:, :coarse], basis_g)
    u = jump[:loads] - thin_dot(both, jnp.concatenate([jump_z_rows, basis_g], axis=0))
    products = small_dot(jnp.concatenate([g_h, z_z], axis=0), shares)
    image_d = image_g - h_amounts
    inner = res_res - total(amounts * coarse_res)
    curvature = 2.0 * (res_image - total(amounts * (res_h + image_d)))
    u_u = jump_jump - total(amounts * (2.0 * jump_z - z_amounts) + 2.0 * image_d * shares)
    second_u = second_g - g_dz_amounts - products[:coarse]
    jump_u = second_z - z_dz_amounts - 0.5 * products[coarse:]
    d_second = res_second - total(amounts * (res_dz + second_u) + shares * res_h)
    u_second = jump_second - total(amounts * (jump_dz + jump_u) + shares * (0.5 * jump_z + second_u))
    step = inner / curvature
    renewed = step * step * u_u - inner
    grown = 1.0 + renewed / inner
    curvature = grown * grown * curvature - grown * step * (2.0 * d_second + u_u) + 2.0 * step * step * u_second
    second_step = renewed / curvature
    on_d, on_u = step + second_step * grown, second_step * step
    amplitudes = amounts - on_d * shares + 2.0 * on_u * small_dot(inverse, second_u)
    amplitudes_ref[...] = jnp.concatenate(
        [amplitudes[label * GROUP : label * GROUP + MODES] for label in range(groups)], axis=0
    )
    inverse = 1.0 / scale[:, :loads]
    weights = jnp.concatenate([on_d * inverse, on_u * inverse, jnp.zeros((6, loads), jnp.float32)], axis=0).T
    multipliers_ref[...] = weights[:, 0:1] * d - weights[:, 1:2] * u


def call(kernel, shapes, in_specs, name, scratch=(), flops=0):
    return pl.pallas_call(
        kernel,
        out_shape=[jax.ShapeDtypeStruct(*shape) for shape in shapes],
        in_specs=in_specs,
        out_specs=[VMEM] * len(shapes),
        scratch_shapes=scratch,
        compiler_params=pltpu.CompilerParams(vmem_limit_bytes=24 * 1024 * 1024),
        cost_estimate=pl.CostEstimate(flops=flops, bytes_accessed=2**20, transcendentals=0),
        name=name,
    )


def permute(values, offset, plane_offset=0):
    peers, planes = lax.axis_size("sub"), lax.axis_size("rep")
    offset = offset * planes + plane_offset
    return lax.ppermute(values, ("sub", "rep"), [(at, at ^ offset) for at in range(peers * planes)])


def to_chips(*pairs):
    return [permute(pair, 2 * (len(pairs) - at) + 1) for at, pair in enumerate(pairs)]


def to_core(near, *pairs):
    return permute(jnp.concatenate([near, *(pair[near.shape[0] :] for pair in pairs)], axis=0), 1)


def total(terms, powers):
    chips = [(offset + 1, 0) for offset in reversed(range(2, lax.axis_size("sub"), 2))]
    planes = [(1, offset) for offset in reversed(range(1, lax.axis_size("rep")))]
    copies = [terms]
    for offsets, following in (([(1, 0)], len(chips)), (chips, len(planes)), (planes, 1)):
        parts = [permute(copy, *offset) for copy, offset in zip(copies, offsets)]
        kernel = functools.partial(sum_kernel, len(parts) + 1)
        copies = call(kernel, [(terms.shape, terms.dtype)] * following, [VMEM] * (len(parts) + 2), "sum")(
            powers, *parts, copies[0]
        )
    return copies[0]


def fused_body(dual_ops, mode_traces, route, mode_block, local_gap):
    peers = lax.axis_size("sub")
    loads, rows = local_gap.shape
    modes = mode_traces.shape[1]
    subs = mode_block.shape[0]
    groups = subs // AGG_SUBS
    per_peer = rows // peers
    height = loads + GROUP * groups
    f32, i32 = jnp.float32, jnp.int32
    tall = ((height, rows), f32)
    wide = ((3 * GROUP * groups, 4 * loads), f32)

    def pairs(height):
        return [((2 * height, per_peer), f32)] * (peers // 2 - 1)

    def singles(height):
        return [((height, per_peer), f32)] * 3

    def held(value):
        return pltpu.with_memory_space_constraint(value, pltpu.HBM)

    inputs = [route, mode_block.reshape(1, subs), local_gap, mode_traces.transpose(1, 0, 2), dual_ops]
    short = loads + GROUP
    far, values, operator, route, *send = call(
        place_kernel,
        [
            ((rows, rows - 2 * per_peer), jnp.bfloat16),
            ((short, rows), f32),
            (dual_ops.shape, dual_ops.dtype),
            (route.shape, i32),
            *pairs(short),
        ],
        [HBM] * 5,
        "place",
        [pltpu.VMEM((1, subs), i32), pltpu.VMEM((modes, 1, rows), f32), pltpu.SemaphoreType.DMA((5,))],
    )(*(held(value) for value in inputs))
    got = to_chips(*send)
    halves = ((2, rows, rows // 2), dual_ops.dtype)
    edge, slots, placed, near, back, stay = call(
        ready_kernel,
        [((rows, 3 * per_peer), jnp.bfloat16), halves, halves, *singles(short)],
        [VMEM] * 4,
        "ready",
        flops=2 * rows * rows * rows,
    )(route, far, values, operator)
    got_near = to_core(near, *got)
    half = ((height, rows // 2), f32)
    straight_jump, half_image = call(
        first_half_kernel, [half, tall], [VMEM] * (3 + 2 * len(got)), "first_half", flops=2 * rows * rows * height
    )(placed, stay, back, *send, *got)
    handed_jump, image, *image_send = call(
        first_kernel, [half, tall, *pairs(height)], [VMEM] * (5 + len(send)), "first"
    )(far, placed, half_image, got_near, near, *send)
    got = to_chips(*image_send)
    packed = ((2 * GROUP * groups, 4 * loads), f32)
    basis, scale, powers, terms, sums, near, back, stay = call(
        middle_kernel,
        [tall, ((GROUP, rows), f32), packed, wide, ((GROUP, loads), f32), *singles(height)],
        [VMEM] * 6,
        "middle",
        flops=4 * rows * rows * height,
    )(edge, slots, operator, straight_jump, handed_jump, image)
    got_near = to_core(near, *got[::-1])
    half_jump, half_second = call(
        second_half_kernel, [tall, tall], [VMEM] * (5 + 2 * len(got)), "second_half", flops=4 * rows * rows * height
    )(slots, placed, scale, stay, back, *image_send, *got)
    jump, terms = call(second_kernel, [tall, packed], [VMEM] * (10 + len(got)), "second")(
        slots, placed, basis, half_jump, half_second, scale, terms, sums, got_near, near, *image_send
    )
    multipliers, amplitudes = call(
        final_kernel, [((loads, rows), f32), ((MODES * groups, loads), f32)], [VMEM] * 4, "final"
    )(total(terms, powers), basis, jump, scale)
    return multipliers, amplitudes.T


def general_body(dual_ops, mode_traces, route, mode_block, local_gap):
    own_index = lax.axis_index("sub")
    plane_index = lax.axis_index("rep")
    peer_count = lax.axis_size("sub")
    plane_count = lax.axis_size("rep")
    operator = dual_ops[0]
    traces = mode_traces[0]
    slot_rows = route[0]
    rows_here = operator.shape[0]
    load_cases = local_gap.shape[0]
    per_peer = rows_here // peer_count
    blocks = mode_block[:, 0]
    block_count = blocks.shape[0] // AGG_SUBS
    coarse = block_count * MODES
    positions = jnp.arange(rows_here, dtype=jnp.int32)
    inverse = jnp.zeros((rows_here,), jnp.int32).at[slot_rows].set(positions)
    slot_peer = positions // per_peer
    within = positions % per_peer
    flip_index = jnp.where(
        slot_peer == own_index, slot_peer * per_peer + per_peer - 1 - within, positions
    )
    peer_ids = jnp.arange(peer_count, dtype=jnp.int32)
    peer_blocks = blocks[peer_ids * plane_count + plane_index]
    own_block = blocks[own_index * plane_count + plane_index]
    labels = jnp.arange(block_count, dtype=jnp.int32)
    peer_onehot = (peer_blocks[:, None] == labels[None, :]).astype(jnp.float32)
    own_onehot = (labels == own_block).astype(jnp.float32)
    trace_slots = traces[:, slot_rows]
    receive_index = flip_index[inverse]

    def to_peers(values):
        return values[:, slot_rows]

    def from_peers(values):
        return values[:, inverse]

    gap_peers = to_peers(local_gap)
    got_traces = lax.all_to_all(trace_slots, "sub", split_axis=1, concat_axis=1, tiled=True)
    got_gap = lax.all_to_all(gap_peers, "sub", split_axis=1, concat_axis=1, tiled=True)
    partner_traces = got_traces[:, flip_index]
    residual = local_gap - got_gap[:, receive_index]
    own_gram = jnp.dot(traces, traces.T, precision=HIGHEST)
    paired = (trace_slots[:, None, :] * partner_traces[None, :, :]).reshape(
        MODES, MODES, peer_count, per_peer
    )
    cross_terms = jnp.sum(paired, axis=3)
    cross_blocks = jnp.einsum("klq,qb->kbl", cross_terms, peer_onehot, precision=HIGHEST)
    own_blocks = own_gram[:, None, :] * own_onehot[None, :, None]
    row_term = 2.0 * (own_blocks - cross_blocks).reshape(MODES, coarse)
    gram_term = (own_onehot[:, None, None] * row_term[None]).reshape(coarse, coarse)

    def coarse_term(values):
        own_part = 2.0 * jnp.dot(values, traces.T, precision=HIGHEST)
        return (own_part[:, None, :] * own_onehot[None, :, None]).reshape(load_cases, coarse)

    def expand(amounts):
        grouped = amounts.reshape(load_cases, block_count, MODES)
        own_amounts = lax.dynamic_index_in_dim(grouped, own_block, 1, keepdims=False)
        own_part = jnp.dot(own_amounts, traces, precision=HIGHEST)
        peer_amounts = jnp.einsum("qb,rbk->rkq", peer_onehot, grouped, precision=HIGHEST)
        spread = jnp.repeat(peer_amounts, per_peer, axis=2)
        peer_part = jnp.sum(spread * partner_traces[None, :, :], axis=1)
        return own_part - from_peers(peer_part)

    squares = jnp.sum(residual * residual, axis=1)
    gram_matrix, coarse_res, norm_res = lax.psum(
        (gram_term, coarse_term(residual), squares), ("sub", "rep")
    )
    factor = jnp.linalg.cholesky(gram_matrix)

    def solve_coarse(right):
        return jax.scipy.linalg.cho_solve((factor, True), right.T).T

    amplitudes = solve_coarse(coarse_res)
    projected = residual - expand(amplitudes)
    inner_sum = norm_res - jnp.sum(amplitudes * coarse_res, axis=1)
    direction = projected
    multipliers = jnp.zeros_like(residual)
    for iteration in range(ITERS):
        product = lax.dot_general(
            direction.astype(jnp.bfloat16),
            operator,
            (((1,), (1,)), ((), ())),
            preferred_element_type=jnp.float32,
        )
        got_product = lax.all_to_all(
            to_peers(product), "sub", split_axis=1, concat_axis=1, tiled=True
        )
        image_jump = product - got_product[:, receive_index]
        coarse_jump, jump_squares, residual_cross, curvature = lax.psum(
            (
                coarse_term(image_jump),
                jnp.sum(image_jump * image_jump, axis=1),
                jnp.sum(residual * image_jump, axis=1),
                jnp.sum(direction * image_jump, axis=1),
            ),
            ("sub", "rep"),
        )
        step_size = inner_sum / curvature
        multipliers = multipliers + step_size[:, None] * direction
        residual = residual - step_size[:, None] * image_jump
        coarse_res = coarse_res - step_size[:, None] * coarse_jump
        norm_res = (
            norm_res - 2.0 * step_size * residual_cross + step_size * step_size * jump_squares
        )
        amplitudes = solve_coarse(coarse_res)
        if iteration + 1 < ITERS:
            projected = residual - expand(amplitudes)
            renewed = norm_res - jnp.sum(amplitudes * coarse_res, axis=1)
            direction = projected + (renewed / inner_sum)[:, None] * direction
            inner_sum = renewed
    return (multipliers, amplitudes)


def fits(mesh, dual_ops, mode_block, local_gap):
    peers, planes = mesh.shape["sub"], mesh.shape["rep"]
    powers = all(size & (size - 1) == 0 for size in (peers, planes))
    whole = dual_ops.shape[1] % (128 * peers) == 0 and local_gap.shape[0] % 16 == 0
    coarse = GROUP * (mode_block.shape[0] // AGG_SUBS)
    return powers and whole and 4 * local_gap.shape[0] == 128 and 8 * coarse == 128


def solution(mesh):
    placed = (
        P(("sub", "rep"), None, None),
        P(("sub", "rep"), None, None),
        P(("sub", "rep"), None),
        P(),
        P(None, ("sub", "rep")),
    )

    def run(dual_ops, mode_traces, route, mode_block, local_gap):
        body = fused_body if fits(mesh, dual_ops, mode_block, local_gap) else general_body
        return jax.shard_map(
            body, mesh=mesh, in_specs=placed, out_specs=(P(None, ("sub", "rep")), P()), check_vma=False
        )(dual_ops, mode_traces, route, mode_block, local_gap)

    return run
```

```python
import functools

import jax
import jax.numpy as jnp
from jax import lax
from jax.experimental import pallas as pl
from jax.experimental.pallas import tpu as pltpu
from jax.sharding import PartitionSpec as P

MODES = 6
AGG_SUBS = 16
ITERS = 2
GROUP = 8

HIGHEST = lax.Precision.HIGHEST
VMEM = pl.BlockSpec(memory_space=pltpu.VMEM)
HBM = pl.BlockSpec(memory_space=pltpu.HBM)
NN = (((1,), (0,)), ((), ()))
NT = (((1,), (1,)), ((), ()))


def split(values):
    high = values.astype(jnp.bfloat16).astype(jnp.float32)
    return jnp.concatenate([high, values - high], axis=0).astype(jnp.bfloat16)


def split_dot(values, matrix, dims):
    rows = values.shape[0]
    both = lax.dot_general(split(values), matrix, dims, preferred_element_type=jnp.float32)
    return both[:rows] + both[rows:]


def small_dot(left, right):
    return jnp.dot(left, right, precision=HIGHEST, preferred_element_type=jnp.float32)


def send_far(values, far_ref, *pair_refs):
    height = values.shape[0]
    per_peer = pair_refs[0].shape[1]
    values = split(values)
    for at, ref in enumerate(pair_refs):
        columns = far_ref[:, 2 * at * per_peer : (2 * at + 2) * per_peer]
        slots = jnp.dot(values, columns, preferred_element_type=jnp.float32)
        slots = slots[:height] + slots[height:]
        ref[:height] = slots[:, :per_peer]
        ref[height:] = slots[:, per_peer:]


def send_near(values, edge_ref, near_ref, back_ref, stay_ref):
    per_peer = back_ref.shape[1]
    slots = split_dot(values, edge_ref[...], NN)
    for at, ref in enumerate((near_ref, back_ref, stay_ref)):
        ref[...] = slots[:, at * per_peer : (at + 1) * per_peer]


def straight(last_ref, pair_refs):
    height = last_ref.shape[0]
    return jnp.concatenate([*(ref[:height] for ref in pair_refs), last_ref[...]], axis=1)


def for_other(near_ref, pair_refs):
    height = near_ref.shape[0]
    return jnp.concatenate([near_ref[...], *(ref[height:] for ref in pair_refs)], axis=1)


def handed(got_ref, height, backwards=False):
    starts = list(range(height, got_ref.shape[0], height))
    starts = [0, *(starts[::-1] if backwards else starts)]
    return jnp.concatenate([got_ref[at : at + height] for at in starts], axis=1)


def spread(values, loads, groups):
    modes = values[loads:]
    label = modes[MODES : MODES + 1]
    used = lax.broadcasted_iota(jnp.int32, modes.shape, 0) < MODES
    parts = [jnp.where(used & (label == group), modes, 0.0) for group in range(groups)]
    return jnp.concatenate([values[:loads], *parts], axis=0)


def one_hot(route_ref, peer, per_peer):
    start = pl.multiple_of(peer * per_peer, per_peer)
    row_ids = lax.broadcasted_iota(jnp.int32, (route_ref.shape[1], per_peer), 0)
    return jnp.where(row_ids == route_ref[:, pl.ds(start, per_peer)], 1.0, 0.0).astype(jnp.bfloat16)


def place_kernel(
    route_hbm, block_hbm, gap_hbm, traces_hbm, operator_hbm,
    far_ref, values_ref, operator_ref, route_ref, *refs,
):
    *pair_refs, block_ref, traces_ref, sems = refs
    loads, rows = gap_hbm.shape
    per_peer = pair_refs[0].shape[1]
    peers = rows // per_peer
    copies = [
        pltpu.make_async_copy(source, target, sems.at[at])
        for at, (source, target) in enumerate(
            (
                (route_hbm, route_ref),
                (block_hbm, block_ref),
                (traces_hbm, traces_ref),
                (gap_hbm, values_ref.at[pl.ds(0, loads)]),
                (operator_hbm, operator_ref),
            )
        )
    ]

    def build(at):
        peer = own_index ^ (peers - 1 - at)
        far_ref[:, at * per_peer : (at + 1) * per_peer] = one_hot(route_ref, peer, per_peer)

    for copy in copies:
        copy.start()
    own_index = lax.axis_index("sub")
    device = own_index * lax.axis_size("rep") + lax.axis_index("rep")
    copies[0].wait()
    for at in range(peers - 4):
        build(at)
    copies[1].wait()
    copies[2].wait()
    blocks = block_ref[...]
    lane = lax.broadcasted_iota(jnp.int32, blocks.shape, 1)
    own_block = jnp.sum(jnp.where(lane == device, blocks, 0), axis=1, keepdims=True)
    modes = traces_ref.shape[0]
    label = jnp.broadcast_to(own_block.astype(jnp.float32), (1, rows))
    for mode in range(modes):
        values_ref[loads + mode : loads + mode + 1] = traces_ref[mode]
    values_ref[loads + modes : loads + modes + 1] = label
    values_ref[loads + modes + 1 :] = jnp.zeros((GROUP - modes - 1, rows), jnp.float32)
    copies[3].wait()
    for at in range(peers - 4, peers - 2):
        build(at)
    send_far(values_ref[...], far_ref, *pair_refs)
    copies[4].wait()


def ready_kernel(
    route_ref, far_ref, values_ref, operator_ref,
    edge_ref, slots_ref, placed_ref, near_ref, back_ref, stay_ref,
):
    per_peer = back_ref.shape[1]
    peers = far_ref.shape[1] // per_peer + 2
    own_index = lax.axis_index("sub")
    low = lax.broadcasted_iota(jnp.int32, (per_peer, per_peer), 0)
    high = lax.broadcasted_iota(jnp.int32, (per_peer, per_peer), 1)
    reverse = jnp.where(low + high == per_peer - 1, 1.0, 0.0).astype(jnp.bfloat16)
    own_columns = one_hot(route_ref, own_index, per_peer)
    near_columns = one_hot(route_ref, own_index ^ 1, per_peer)
    reversed_columns = jnp.dot(own_columns, reverse, preferred_element_type=jnp.float32).astype(jnp.bfloat16)
    edge_ref[...] = jnp.concatenate([near_columns, reversed_columns, own_columns], axis=1)
    for at in range(peers // 2 - 1):
        start = 2 * at * per_peer
        slots_ref[0, :, at * per_peer : (at + 1) * per_peer] = far_ref[:, start : start + per_peer]
        slots_ref[1, :, (at + 1) * per_peer : (at + 2) * per_peer] = far_ref[:, start + per_peer : start + 2 * per_peer]
    slots_ref[0, :, (peers // 2 - 1) * per_peer :] = own_columns
    slots_ref[1, :, :per_peer] = near_columns
    send_near(values_ref[...], edge_ref, near_ref, back_ref, stay_ref)
    operator = operator_ref[0]
    for half in range(2):
        placed_ref[half] = jnp.dot(
            operator, slots_ref[half], preferred_element_type=jnp.float32
        ).astype(operator.dtype)


def first_half_kernel(placed_ref, stay_ref, back_ref, *refs):
    *pair_refs, jump_ref, image_ref = refs
    sent_refs, got_refs = pair_refs[: len(pair_refs) // 2], pair_refs[len(pair_refs) // 2 :]
    loads = stay_ref.shape[0] - GROUP
    groups = (jump_ref.shape[0] - loads) // GROUP
    own, got = (spread(straight(*refs), loads, groups) for refs in ((stay_ref, sent_refs), (back_ref, got_refs)))
    jump_ref[...] = own - got
    image_ref[...] = split_dot(own - got, placed_ref[0], NT)


def first_kernel(far_ref, placed_ref, half_ref, got_ref, near_ref, *refs):
    sent_refs, (jump_ref, image_ref, *pair_refs) = refs[: len(refs) // 2 - 1], refs[len(refs) // 2 - 1 :]
    height = near_ref.shape[0]
    loads = height - GROUP
    groups = (image_ref.shape[0] - loads) // GROUP
    own, got = (spread(value, loads, groups) for value in (for_other(near_ref, sent_refs), handed(got_ref, height)))
    jump_ref[...] = own - got
    image = half_ref[...] + split_dot(own - got, placed_ref[1], NT)
    image_ref[...] = image
    send_far(image, far_ref, *pair_refs)


def products_of(left, right):
    rows, columns = left.shape[0], right.shape[0]
    both = lax.dot_general(split(left), split(right), NT, preferred_element_type=jnp.float32)
    both = both[:rows] + both[rows:]
    return both[:, :columns] + both[:, columns:]


def by_load(products):
    sums = [jnp.sum(product, axis=1, keepdims=True) for product in products]
    empty = [jnp.zeros_like(sums[0])] * (GROUP - len(sums))
    return jnp.concatenate(sums + empty, axis=1).T


def pack(by_mode, scalars, blocks):
    by_mode = by_mode + pltpu.roll(by_mode, by_mode.shape[1] // 2, 1)
    upper, lower = by_mode[:GROUP], by_mode[GROUP:]
    row = lax.broadcasted_iota(jnp.int32, upper.shape, 0)
    left = lax.broadcasted_iota(jnp.int32, upper.shape, 1) < upper.shape[1] // 2
    spare = [
        jnp.where(left, pltpu.roll(upper, 6, 0), pltpu.roll(upper, 4, 0)),
        jnp.where(left, pltpu.roll(upper, 2, 0), pltpu.roll(lower, 6, 0)),
        jnp.where(left, pltpu.roll(lower, 4, 0), pltpu.roll(lower, 2, 0)),
        jnp.where(row == MODES, *scalars),
    ]
    rows = jnp.concatenate(blocks, axis=0)
    parts = [jnp.where(row < MODES, rows[at * GROUP : (at + 1) * GROUP], spare[at]) for at in range(4)]
    return jnp.concatenate(parts, axis=0)


def unpack(terms):
    parts = [terms[at * GROUP : (at + 1) * GROUP] for at in range(4)]
    row = lax.broadcasted_iota(jnp.int32, parts[0].shape, 0)
    lane = lax.broadcasted_iota(jnp.int32, parts[0].shape, 1)
    half = terms.shape[1] // 2
    turned = [pltpu.roll(part, half, 1) for part in parts[:3]]
    upper = jnp.where(
        row < 2, pltpu.roll(parts[0], 2, 0), jnp.where(row < 4, pltpu.roll(turned[0], 4, 0), pltpu.roll(parts[1], 6, 0))
    )
    lower = jnp.where(
        row < 2, pltpu.roll(turned[1], 2, 0), jnp.where(row < 4, pltpu.roll(parts[2], 4, 0), pltpu.roll(turned[2], 6, 0))
    )
    by_mode = [jnp.where((row < MODES) & (lane < half), part, 0.0) for part in (upper, lower)]
    blocks = [jnp.where(row < MODES, part, 0.0) for part in parts]
    scalars = parts[3][MODES : MODES + 1], parts[3][MODES + 1 : MODES + 2]
    return jnp.concatenate(by_mode, axis=0), scalars, [jnp.concatenate(blocks[at : at + 2], axis=0) for at in (0, 2)]


def powers(coarse, loads):
    lane = lax.broadcasted_iota(jnp.int32, (coarse, 4 * loads), 1)
    row = lax.broadcasted_iota(jnp.int32, (coarse, 4 * loads), 0)

    def choose(at, *values):
        return functools.reduce(lambda rest, pair: jnp.where(at == pair[0], pair[1], rest), enumerate(values), 0.0 * lane)

    strip, group = lane // coarse, lane // loads
    by_mode = choose(strip, jnp.where(lane > row, 2.0, 0.0), 1.0, 3.0, 2.0)
    scalars = choose(group, 0.0, 1.0, 2.0, 3.0), choose(group, 2.0, 2.0)
    blocks = [choose(group, 0.0, 2.0, 2.0, 1.0), choose(group, 2.0, 3.0, 3.0, 1.0)]
    return pack(by_mode, [line[:1] for line in scalars], blocks)


def magnitude(operator_ref):
    tall = 2 * GROUP
    largest = jnp.zeros((tall, operator_ref.shape[2]), operator_ref.dtype)
    for start in range(0, operator_ref.shape[1], tall):
        part = operator_ref[0, start : start + tall]
        largest = jnp.maximum(largest, jnp.maximum(part, -part))
    largest = jnp.max(largest.astype(jnp.float32), axis=0, keepdims=True)
    return jnp.clip(jnp.max(largest, axis=1, keepdims=True), 1e-30, 1e30)


def scale_of(terms):
    last = terms[-GROUP:]
    half = last.shape[1] // 2
    lane = lax.broadcasted_iota(jnp.int32, last.shape, 1)
    return jnp.where(lane < half, pltpu.roll(last, half, 1), last)[GROUP - 1 :]


def middle_kernel(
    edge_ref, slots_ref, operator_ref, straight_ref, handed_ref, image_ref,
    basis_ref, scale_ref, powers_ref, terms_ref, sums_ref, near_ref, back_ref, stay_ref,
):
    image = image_ref[...]
    send_near(image, edge_ref, near_ref, back_ref, stay_ref)
    coarse = terms_ref.shape[0] // 3
    loads = image.shape[0] - coarse
    basis = split_dot(straight_ref[...], slots_ref[0], NT) + split_dot(handed_ref[...], slots_ref[1], NT)
    basis_ref[...] = basis
    scale = magnitude(operator_ref)
    scale_ref[...] = jnp.broadcast_to(scale, scale_ref.shape)
    image = image * (1.0 / scale)
    residual, residual_image = basis[:loads], image[:loads]
    lanes = terms_ref.shape[1]
    powers_ref[...] = powers(coarse, loads)
    empty = jnp.zeros((lanes - 2 * loads - 2 * coarse, basis.shape[1]), jnp.float32)
    both = products_of(
        jnp.concatenate([basis[loads:], image[loads:]]),
        jnp.concatenate([residual, basis[loads:], image[loads:], empty, residual_image]),
    )
    by_g, by_h = both[:coarse], both[coarse:]
    lane = lax.broadcasted_iota(jnp.int32, (coarse, lanes), 1)
    first, last = lane < loads, lane >= lanes - loads
    terms_ref[:coarse] = jnp.where(first | last, by_g, 0.0)
    terms_ref[coarse : 2 * coarse] = jnp.where(last, pltpu.roll(by_h, lanes - loads, 1), 0.0)
    row = lax.broadcasted_iota(jnp.int32, (coarse, lanes), 0)
    by_mode = jnp.where((lane <= row) | ((lane >= coarse) & (lane < 2 * coarse)), pltpu.roll(by_g, lanes - loads, 1), 0.0)
    terms_ref[2 * coarse :] = by_mode
    sums_ref[...] = by_load([residual * residual, residual * residual_image])


def second_half_kernel(slots_ref, placed_ref, scale_ref, stay_ref, back_ref, *refs):
    *pair_refs, jump_ref, second_ref = refs
    sent_refs, got_refs = pair_refs[: len(pair_refs) // 2], pair_refs[len(pair_refs) // 2 :]
    jump = straight(stay_ref, sent_refs) - straight(back_ref, got_refs)
    jump = jump * (1.0 / scale_ref[:1, : jump.shape[1]])
    jump_ref[...] = split_dot(jump, slots_ref[0], NT)
    second_ref[...] = split_dot(jump, placed_ref[0], NT)


def second_kernel(
    slots_ref, placed_ref, basis_ref, half_jump_ref, half_second_ref, scale_ref, early_ref, sums_ref, got_ref,
    near_ref, *refs,
):
    *sent_refs, jump_ref, terms_ref = refs
    coarse = terms_ref.shape[0] // 2
    loads = basis_ref.shape[0] - coarse
    jump = for_other(near_ref, sent_refs) - handed(got_ref, loads + coarse, backwards=True)
    inverse = 1.0 / scale_ref[:1]
    jump = jump * inverse[:, : jump.shape[1]]
    second = (half_second_ref[...] + split_dot(jump, placed_ref[1], NT)) * inverse
    jump = half_jump_ref[...] + split_dot(jump, slots_ref[1], NT)
    jump_ref[...] = jump
    basis = basis_ref[...]
    residual, jump_loads, second_loads = basis[:loads], jump[:loads], second[:loads]
    both = products_of(
        jnp.concatenate([basis[loads:], jump[loads:], second[loads:]]),
        jnp.concatenate([residual, jump_loads, second_loads, jump[loads:], second[loads:]]),
    )
    by_g, by_z, by_dz = (both[at * coarse : (at + 1) * coarse] for at in range(3))
    lanes = terms_ref.shape[1]
    lane = lax.broadcasted_iota(jnp.int32, (coarse, lanes), 1)
    group = lane // loads
    top = jnp.where(group == 1, by_z, jnp.where(group == 2, by_g, 0.0))
    low = jnp.where(group < 2, by_dz, jnp.where(group == 2, by_z, 0.0))
    row = lax.broadcasted_iota(jnp.int32, (coarse, lanes), 0)
    z_z = pltpu.roll(by_z, 2 * coarse, 1)
    strip = lane // coarse
    by_mode = jnp.where((lane > row) & (strip == 0), z_z, 0.0)
    by_mode = jnp.where(strip == 2, pltpu.roll(by_z, 3 * coarse, 1), by_mode)
    by_mode = jnp.where(strip == 3, pltpu.roll(by_g, 4 * coarse, 1), by_mode)
    diagonal = jnp.sum(jnp.where(lane == row, z_z, 0.0), axis=0, keepdims=True)
    sums = by_load([jump_loads * jump_loads, jump_loads * second_loads, residual * second_loads])
    scalars = (
        jnp.concatenate([sums_ref[0:1], sums_ref[1:2], sums[0:1], sums[1:2]], axis=1),
        jnp.concatenate([sums[2:3], diagonal[:, :loads], scale_ref[:1, : 2 * loads]], axis=1),
    )
    terms_ref[...] = pack(
        early_ref[2 * coarse :] + by_mode, scalars, [early_ref[:coarse] + top, early_ref[coarse : 2 * coarse] + low]
    )


def summed(refs, power):
    parts = [ref[...] for ref in reversed(refs)]
    scales = [scale_of(part) for part in parts]
    largest = functools.reduce(jnp.maximum, scales)
    inverse = 1.0 / largest
    for at, scale in enumerate(scales):
        factor = scale * inverse
        square = factor * factor
        high = jnp.where(power > 2, square * factor, square)
        parts[at] = parts[at] * jnp.where(power > 1, high, jnp.where(power > 0, factor, 1.0))
    while len(parts) > 1:
        parts = [low + high for low, high in zip(parts[::2], parts[1::2])]
    return parts[0], largest


def sum_kernel(count, powers_ref, *refs):
    power = powers_ref[...]
    total, scale = summed(refs[:count], power)
    row = lax.broadcasted_iota(jnp.int32, power.shape, 0)
    lane = lax.broadcasted_iota(jnp.int32, power.shape, 1)
    total = jnp.where((row == power.shape[0] - 1) & (lane >= power.shape[1] // 2), scale, total)
    for ref in refs[count:]:
        ref[...] = total


def eliminate(work, coarse):
    row = lax.broadcasted_iota(jnp.int32, work.shape, 0)
    for start in range(0, coarse, GROUP):
        pivots = range(start, start + MODES)
        columns = [jnp.broadcast_to(work[:, pivot : pivot + 1], work.shape) for pivot in pivots]
        square = [[column[pivot : pivot + 1] for column in columns] for pivot in pivots]
        rows = [work[pivot : pivot + 1] for pivot in pivots]
        for at in range(MODES):
            scale = 1.0 / square[at][at]
            rows[at] = rows[at] * scale
            square[at] = [value * scale for value in square[at]]
            for other in range(MODES):
                if other != at:
                    factor = square[other][at]
                    rows[other] = rows[other] - factor * rows[at]
                    square[other] = [
                        value if to <= at else value - factor * square[at][to]
                        for to, value in enumerate(square[other])
                    ]
        for column, solved in zip(columns, rows):
            work = work - column * solved
        for pivot, solved in zip(pivots, rows):
            work = jnp.where(row == pivot, solved, work)
    return work


def thin_dot(left, right):
    high, right_high = (value.astype(jnp.bfloat16).astype(jnp.float32) for value in (left, right))
    return jnp.dot(
        jnp.concatenate([high, left - high, high], axis=1).astype(jnp.bfloat16),
        jnp.concatenate([right_high, right_high, right - right_high], axis=0).astype(jnp.bfloat16),
        preferred_element_type=jnp.float32,
    )


def final_kernel(powers_ref, *refs):
    *parts_refs, basis_ref, jump_ref, scale_ref, multipliers_ref, amplitudes_ref = refs
    terms, scale = summed(parts_refs, powers_ref[...])
    coarse = terms.shape[0] // 2
    loads = basis_ref.shape[0] - coarse
    groups = coarse // GROUP

    def total(values):
        return jnp.sum(values, axis=0, keepdims=True)

    ratio = scale_ref[:1, : scale.shape[1]] / scale
    jump = jump_ref[...] * jnp.concatenate([ratio] * (jump_ref.shape[1] // ratio.shape[1]), axis=1)
    by_mode, (sums, last_sums), (top, low) = unpack(terms)
    res_res, res_image, jump_jump, jump_second = (sums[:, at * loads : (at + 1) * loads] for at in range(4))
    res_second, diagonal = last_sums[:, :loads], last_sums[:, loads : loads + coarse]
    coarse_res, jump_z, second_g, image_g = (top[:, at * loads : (at + 1) * loads] for at in range(4))
    res_dz, jump_dz, second_z, res_h = (low[:, at * loads : (at + 1) * loads] for at in range(4))
    triangles, g_h, z_dz, g_dz = (by_mode[:, at * coarse : (at + 1) * coarse] for at in range(4))
    row = lax.broadcasted_iota(jnp.int32, (coarse, coarse), 0)
    column = lax.broadcasted_iota(jnp.int32, (coarse, coarse), 1)
    unit = jnp.where(row == column, 1.0, 0.0)
    other = triangles.T
    gram = jnp.where(row >= column, triangles, other)
    z_z = jnp.where(row < column, triangles, jnp.where(row == column, diagonal, other))
    empty = jnp.zeros((coarse, 5 * coarse - 2 * loads), jnp.float32)
    solved = eliminate(
        jnp.concatenate([gram, g_h, coarse_res, image_g, unit, empty], axis=1), coarse
    )
    inverse_h = solved[:, coarse : 2 * coarse]
    amounts = solved[:, 2 * coarse : 2 * coarse + loads]
    inverse_image = solved[:, 2 * coarse + loads : 2 * coarse + 2 * loads]
    inverse = solved[:, 2 * coarse + 2 * loads : 3 * coarse + 2 * loads]
    products = small_dot(jnp.concatenate([inverse_h, g_h, z_z, g_dz, z_dz], axis=0), amounts)
    inverse_h_amounts, h_amounts, z_amounts, g_dz_amounts, z_dz_amounts = (
        products[at * coarse : (at + 1) * coarse] for at in range(5)
    )
    shares = 2.0 * (inverse_image - inverse_h_amounts)
    both = jnp.concatenate([amounts, shares], axis=0).T
    basis_g, jump_z_rows = basis_ref[loads:], jump[loads:]
    d = basis_ref[:loads] - thin_dot(both[:, :coarse], basis_g)
    u = jump[:loads] - thin_dot(both, jnp.concatenate([jump_z_rows, basis_g], axis=0))
    products = small_dot(jnp.concatenate([g_h, z_z], axis=0), shares)
    image_d = image_g - h_amounts
    inner = res_res - total(amounts * coarse_res)
    curvature = 2.0 * (res_image - total(amounts * (res_h + image_d)))
    u_u = jump_jump - total(amounts * (2.0 * jump_z - z_amounts) + 2.0 * image_d * shares)
    second_u = second_g - g_dz_amounts - products[:coarse]
    jump_u = second_z - z_dz_amounts - 0.5 * products[coarse:]
    d_second = res_second - total(amounts * (res_dz + second_u) + shares * res_h)
    u_second = jump_second - total(amounts * (jump_dz + jump_u) + shares * (0.5 * jump_z + second_u))
    step = inner / curvature
    renewed = step * step * u_u - inner
    grown = 1.0 + renewed / inner
    curvature = grown * grown * curvature - grown * step * (2.0 * d_second + u_u) + 2.0 * step * step * u_second
    second_step = renewed / curvature
    on_d, on_u = step + second_step * grown, second_step * step
    amplitudes = amounts - on_d * shares + 2.0 * on_u * small_dot(inverse, second_u)
    amplitudes_ref[...] = jnp.concatenate(
        [amplitudes[label * GROUP : label * GROUP + MODES] for label in range(groups)], axis=0
    )
    inverse = 1.0 / scale[:, :loads]
    weights = jnp.concatenate([on_d * inverse, on_u * inverse, jnp.zeros((6, loads), jnp.float32)], axis=0).T
    multipliers_ref[...] = weights[:, 0:1] * d - weights[:, 1:2] * u


def call(kernel, shapes, in_specs, name, scratch=(), flops=0):
    return pl.pallas_call(
        kernel,
        out_shape=[jax.ShapeDtypeStruct(*shape) for shape in shapes],
        in_specs=in_specs,
        out_specs=[VMEM] * len(shapes),
        scratch_shapes=scratch,
        compiler_params=pltpu.CompilerParams(vmem_limit_bytes=24 * 1024 * 1024),
        cost_estimate=pl.CostEstimate(flops=flops, bytes_accessed=2**20, transcendentals=0),
        name=name,
    )


def permute(values, offset, plane_offset=0):
    peers, planes = lax.axis_size("sub"), lax.axis_size("rep")
    offset = offset * planes + plane_offset
    return lax.ppermute(values, ("sub", "rep"), [(at, at ^ offset) for at in range(peers * planes)])


def to_chips(*pairs):
    return [permute(pair, 2 * (len(pairs) - at) + 1) for at, pair in enumerate(pairs)]


def to_core(near, *pairs):
    return permute(jnp.concatenate([near, *(pair[near.shape[0] :] for pair in pairs)], axis=0), 1)


def last_parts(terms, powers):
    chips = [(offset + 1, 0) for offset in reversed(range(2, lax.axis_size("sub"), 2))]
    planes = [(1, offset) for offset in reversed(range(1, lax.axis_size("rep")))]
    copies = [terms]
    for offsets, following in (([(1, 0)], len(chips)), (chips, len(planes))):
        parts = [permute(copy, *offset) for copy, offset in zip(copies, offsets)]
        kernel = functools.partial(sum_kernel, len(parts) + 1)
        copies = call(kernel, [(terms.shape, terms.dtype)] * following, [VMEM] * (len(parts) + 2), "sum")(
            powers, *parts, copies[0]
        )
    return [*(permute(copy, *offset) for copy, offset in zip(copies, planes)), copies[0]]


def fused_body(dual_ops, mode_traces, route, mode_block, local_gap):
    peers = lax.axis_size("sub")
    loads, rows = local_gap.shape
    modes = mode_traces.shape[1]
    subs = mode_block.shape[0]
    groups = subs // AGG_SUBS
    per_peer = rows // peers
    height = loads + GROUP * groups
    f32, i32 = jnp.float32, jnp.int32
    tall = ((height, rows), f32)
    wide = ((3 * GROUP * groups, 4 * loads), f32)

    def pairs(height):
        return [((2 * height, per_peer), f32)] * (peers // 2 - 1)

    def singles(height):
        return [((height, per_peer), f32)] * 3

    def held(value):
        return pltpu.with_memory_space_constraint(value, pltpu.HBM)

    inputs = [route, mode_block.reshape(1, subs), local_gap, mode_traces.transpose(1, 0, 2), dual_ops]
    short = loads + GROUP
    far, values, operator, route, *send = call(
        place_kernel,
        [
            ((rows, rows - 2 * per_peer), jnp.bfloat16),
            ((short, rows), f32),
            (dual_ops.shape, dual_ops.dtype),
            (route.shape, i32),
            *pairs(short),
        ],
        [HBM] * 5,
        "place",
        [pltpu.VMEM((1, subs), i32), pltpu.VMEM((modes, 1, rows), f32), pltpu.SemaphoreType.DMA((5,))],
    )(*(held(value) for value in inputs))
    got = to_chips(*send)
    halves = ((2, rows, rows // 2), dual_ops.dtype)
    edge, slots, placed, near, back, stay = call(
        ready_kernel,
        [((rows, 3 * per_peer), jnp.bfloat16), halves, halves, *singles(short)],
        [VMEM] * 4,
        "ready",
        flops=2 * rows * rows * rows,
    )(route, far, values, operator)
    got_near = to_core(near, *got)
    half = ((height, rows // 2), f32)
    straight_jump, half_image = call(
        first_half_kernel, [half, tall], [VMEM] * (3 + 2 * len(got)), "first_half", flops=2 * rows * rows * height
    )(placed, stay, back, *send, *got)
    handed_jump, image, *image_send = call(
        first_kernel, [half, tall, *pairs(height)], [VMEM] * (5 + len(send)), "first"
    )(far, placed, half_image, got_near, near, *send)
    got = to_chips(*image_send)
    packed = ((2 * GROUP * groups, 4 * loads), f32)
    basis, scale, powers, terms, sums, near, back, stay = call(
        middle_kernel,
        [tall, ((GROUP, rows), f32), packed, wide, ((GROUP, loads), f32), *singles(height)],
        [VMEM] * 6,
        "middle",
        flops=4 * rows * rows * height,
    )(edge, slots, operator, straight_jump, handed_jump, image)
    got_near = to_core(near, *got[::-1])
    half_jump, half_second = call(
        second_half_kernel, [tall, tall], [VMEM] * (5 + 2 * len(got)), "second_half", flops=4 * rows * rows * height
    )(slots, placed, scale, stay, back, *image_send, *got)
    jump, terms = call(second_kernel, [tall, packed], [VMEM] * (10 + len(got)), "second")(
        slots, placed, basis, half_jump, half_second, scale, terms, sums, got_near, near, *image_send
    )
    parts = last_parts(terms, powers)
    multipliers, amplitudes = call(
        final_kernel, [((loads, rows), f32), ((MODES * groups, loads), f32)], [VMEM] * (4 + len(parts)), "final"
    )(powers, *parts, basis, jump, scale)
    return multipliers, amplitudes.T


def general_body(dual_ops, mode_traces, route, mode_block, local_gap):
    own_index = lax.axis_index("sub")
    plane_index = lax.axis_index("rep")
    peer_count = lax.axis_size("sub")
    plane_count = lax.axis_size("rep")
    operator = dual_ops[0]
    traces = mode_traces[0]
    slot_rows = route[0]
    rows_here = operator.shape[0]
    load_cases = local_gap.shape[0]
    per_peer = rows_here // peer_count
    blocks = mode_block[:, 0]
    block_count = blocks.shape[0] // AGG_SUBS
    coarse = block_count * MODES
    positions = jnp.arange(rows_here, dtype=jnp.int32)
    inverse = jnp.zeros((rows_here,), jnp.int32).at[slot_rows].set(positions)
    slot_peer = positions // per_peer
    within = positions % per_peer
    flip_index = jnp.where(
        slot_peer == own_index, slot_peer * per_peer + per_peer - 1 - within, positions
    )
    peer_ids = jnp.arange(peer_count, dtype=jnp.int32)
    peer_blocks = blocks[peer_ids * plane_count + plane_index]
    own_block = blocks[own_index * plane_count + plane_index]
    labels = jnp.arange(block_count, dtype=jnp.int32)
    peer_onehot = (peer_blocks[:, None] == labels[None, :]).astype(jnp.float32)
    own_onehot = (labels == own_block).astype(jnp.float32)
    trace_slots = traces[:, slot_rows]
    receive_index = flip_index[inverse]

    def to_peers(values):
        return values[:, slot_rows]

    def from_peers(values):
        return values[:, inverse]

    gap_peers = to_peers(local_gap)
    got_traces = lax.all_to_all(trace_slots, "sub", split_axis=1, concat_axis=1, tiled=True)
    got_gap = lax.all_to_all(gap_peers, "sub", split_axis=1, concat_axis=1, tiled=True)
    partner_traces = got_traces[:, flip_index]
    residual = local_gap - got_gap[:, receive_index]
    own_gram = jnp.dot(traces, traces.T, precision=HIGHEST)
    paired = (trace_slots[:, None, :] * partner_traces[None, :, :]).reshape(
        MODES, MODES, peer_count, per_peer
    )
    cross_terms = jnp.sum(paired, axis=3)
    cross_blocks = jnp.einsum("klq,qb->kbl", cross_terms, peer_onehot, precision=HIGHEST)
    own_blocks = own_gram[:, None, :] * own_onehot[None, :, None]
    row_term = 2.0 * (own_blocks - cross_blocks).reshape(MODES, coarse)
    gram_term = (own_onehot[:, None, None] * row_term[None]).reshape(coarse, coarse)

    def coarse_term(values):
        own_part = 2.0 * jnp.dot(values, traces.T, precision=HIGHEST)
        return (own_part[:, None, :] * own_onehot[None, :, None]).reshape(load_cases, coarse)

    def expand(amounts):
        grouped = amounts.reshape(load_cases, block_count, MODES)
        own_amounts = lax.dynamic_index_in_dim(grouped, own_block, 1, keepdims=False)
        own_part = jnp.dot(own_amounts, traces, precision=HIGHEST)
        peer_amounts = jnp.einsum("qb,rbk->rkq", peer_onehot, grouped, precision=HIGHEST)
        spread = jnp.repeat(peer_amounts, per_peer, axis=2)
        peer_part = jnp.sum(spread * partner_traces[None, :, :], axis=1)
        return own_part - from_peers(peer_part)

    squares = jnp.sum(residual * residual, axis=1)
    gram_matrix, coarse_res, norm_res = lax.psum(
        (gram_term, coarse_term(residual), squares), ("sub", "rep")
    )
    factor = jnp.linalg.cholesky(gram_matrix)

    def solve_coarse(right):
        return jax.scipy.linalg.cho_solve((factor, True), right.T).T

    amplitudes = solve_coarse(coarse_res)
    projected = residual - expand(amplitudes)
    inner_sum = norm_res - jnp.sum(amplitudes * coarse_res, axis=1)
    direction = projected
    multipliers = jnp.zeros_like(residual)
    for iteration in range(ITERS):
        product = lax.dot_general(
            direction.astype(jnp.bfloat16),
            operator,
            (((1,), (1,)), ((), ())),
            preferred_element_type=jnp.float32,
        )
        got_product = lax.all_to_all(
            to_peers(product), "sub", split_axis=1, concat_axis=1, tiled=True
        )
        image_jump = product - got_product[:, receive_index]
        coarse_jump, jump_squares, residual_cross, curvature = lax.psum(
            (
                coarse_term(image_jump),
                jnp.sum(image_jump * image_jump, axis=1),
                jnp.sum(residual * image_jump, axis=1),
                jnp.sum(direction * image_jump, axis=1),
            ),
            ("sub", "rep"),
        )
        step_size = inner_sum / curvature
        multipliers = multipliers + step_size[:, None] * direction
        residual = residual - step_size[:, None] * image_jump
        coarse_res = coarse_res - step_size[:, None] * coarse_jump
        norm_res = (
            norm_res - 2.0 * step_size * residual_cross + step_size * step_size * jump_squares
        )
        amplitudes = solve_coarse(coarse_res)
        if iteration + 1 < ITERS:
            projected = residual - expand(amplitudes)
            renewed = norm_res - jnp.sum(amplitudes * coarse_res, axis=1)
            direction = projected + (renewed / inner_sum)[:, None] * direction
            inner_sum = renewed
    return (multipliers, amplitudes)


def fits(mesh, dual_ops, mode_block, local_gap):
    peers, planes = mesh.shape["sub"], mesh.shape["rep"]
    powers = all(size & (size - 1) == 0 for size in (peers, planes))
    whole = dual_ops.shape[1] % (128 * peers) == 0 and local_gap.shape[0] % 16 == 0
    coarse = GROUP * (mode_block.shape[0] // AGG_SUBS)
    return powers and whole and 4 * local_gap.shape[0] == 128 and 8 * coarse == 128


def solution(mesh):
    placed = (
        P(("sub", "rep"), None, None),
        P(("sub", "rep"), None, None),
        P(("sub", "rep"), None),
        P(),
        P(None, ("sub", "rep")),
    )

    def run(dual_ops, mode_traces, route, mode_block, local_gap):
        body = fused_body if fits(mesh, dual_ops, mode_block, local_gap) else general_body
        return jax.shard_map(
            body, mesh=mesh, in_specs=placed, out_specs=(P(None, ("sub", "rep")), P()), check_vma=False
        )(dual_ops, mode_traces, route, mode_block, local_gap)

    return run
```

```python
import functools

import jax
import jax.numpy as jnp
from jax import lax
from jax.experimental import pallas as pl
from jax.experimental.pallas import tpu as pltpu
from jax.sharding import PartitionSpec as P

MODES = 6
AGG_SUBS = 16
ITERS = 2
GROUP = 8

HIGHEST = lax.Precision.HIGHEST
VMEM = pl.BlockSpec(memory_space=pltpu.VMEM)
HBM = pl.BlockSpec(memory_space=pltpu.HBM)
NN = (((1,), (0,)), ((), ()))
NT = (((1,), (1,)), ((), ()))


def split(values):
    high = values.astype(jnp.bfloat16).astype(jnp.float32)
    return jnp.concatenate([high, values - high], axis=0).astype(jnp.bfloat16)


def split_dot(values, matrix, dims):
    rows = values.shape[0]
    both = lax.dot_general(split(values), matrix, dims, preferred_element_type=jnp.float32)
    return both[:rows] + both[rows:]


def small_dot(left, right):
    return jnp.dot(left, right, precision=HIGHEST, preferred_element_type=jnp.float32)


def send_far(values, far_ref, *pair_refs):
    height = values.shape[0]
    per_peer = pair_refs[0].shape[1]
    values = split(values)
    for at, ref in enumerate(pair_refs):
        columns = far_ref[:, 2 * at * per_peer : (2 * at + 2) * per_peer]
        slots = jnp.dot(values, columns, preferred_element_type=jnp.float32)
        slots = slots[:height] + slots[height:]
        ref[:height] = slots[:, :per_peer]
        ref[height:] = slots[:, per_peer:]


def send_near(values, edge_ref, near_ref, back_ref, stay_ref):
    per_peer = back_ref.shape[1]
    slots = split_dot(values, edge_ref[...], NN)
    for at, ref in enumerate((near_ref, back_ref, stay_ref)):
        ref[...] = slots[:, at * per_peer : (at + 1) * per_peer]


def straight(last_ref, pair_refs):
    height = last_ref.shape[0]
    return jnp.concatenate([*(ref[:height] for ref in pair_refs), last_ref[...]], axis=1)


def for_other(near_ref, pair_refs):
    height = near_ref.shape[0]
    return jnp.concatenate([near_ref[...], *(ref[height:] for ref in pair_refs)], axis=1)


def handed(got_ref, height, backwards=False):
    starts = list(range(height, got_ref.shape[0] - height + 1, height))
    starts = [0, *(starts[::-1] if backwards else starts)]
    return jnp.concatenate([got_ref[at : at + height] for at in starts], axis=1)


def spread(values, loads, groups):
    modes = values[loads:]
    label = modes[MODES : MODES + 1]
    used = lax.broadcasted_iota(jnp.int32, modes.shape, 0) < MODES
    parts = [jnp.where(used & (label == group), modes, 0.0) for group in range(groups)]
    return jnp.concatenate([values[:loads], *parts], axis=0)


def one_hot(route_ref, peer, per_peer):
    start = pl.multiple_of(peer * per_peer, per_peer)
    row_ids = lax.broadcasted_iota(jnp.int32, (route_ref.shape[1], per_peer), 0)
    return jnp.where(row_ids == route_ref[:, pl.ds(start, per_peer)], 1.0, 0.0).astype(jnp.bfloat16)


def place_kernel(
    route_hbm, block_hbm, gap_hbm, traces_hbm, operator_hbm,
    far_ref, values_ref, operator_ref, route_ref, *refs,
):
    *pair_refs, block_ref, traces_ref, sems = refs
    loads, rows = gap_hbm.shape
    per_peer = pair_refs[0].shape[1]
    peers = rows // per_peer
    copies = [
        pltpu.make_async_copy(source, target, sems.at[at])
        for at, (source, target) in enumerate(
            (
                (route_hbm, route_ref),
                (block_hbm, block_ref),
                (traces_hbm, traces_ref),
                (gap_hbm, values_ref.at[pl.ds(0, loads)]),
                (operator_hbm, operator_ref),
            )
        )
    ]

    def build(at):
        peer = own_index ^ (peers - 1 - at)
        far_ref[:, at * per_peer : (at + 1) * per_peer] = one_hot(route_ref, peer, per_peer)

    for copy in copies:
        copy.start()
    own_index = lax.axis_index("sub")
    device = own_index * lax.axis_size("rep") + lax.axis_index("rep")
    copies[0].wait()
    for at in range(peers - 4):
        build(at)
    copies[1].wait()
    copies[2].wait()
    blocks = block_ref[...]
    lane = lax.broadcasted_iota(jnp.int32, blocks.shape, 1)
    own_block = jnp.sum(jnp.where(lane == device, blocks, 0), axis=1, keepdims=True)
    modes = traces_ref.shape[0]
    label = jnp.broadcast_to(own_block.astype(jnp.float32), (1, rows))
    for mode in range(modes):
        values_ref[loads + mode : loads + mode + 1] = traces_ref[mode]
    values_ref[loads + modes : loads + modes + 1] = label
    values_ref[loads + modes + 1 :] = jnp.zeros((GROUP - modes - 1, rows), jnp.float32)
    copies[3].wait()
    for at in range(peers - 4, peers - 2):
        build(at)
    send_far(values_ref[...], far_ref, *pair_refs)
    copies[4].wait()


def ready_kernel(
    route_ref, far_ref, values_ref, operator_ref,
    edge_ref, slots_ref, placed_ref, near_ref, back_ref, stay_ref,
):
    per_peer = back_ref.shape[1]
    peers = far_ref.shape[1] // per_peer + 2
    own_index = lax.axis_index("sub")
    low = lax.broadcasted_iota(jnp.int32, (per_peer, per_peer), 0)
    high = lax.broadcasted_iota(jnp.int32, (per_peer, per_peer), 1)
    reverse = jnp.where(low + high == per_peer - 1, 1.0, 0.0).astype(jnp.bfloat16)
    own_columns = one_hot(route_ref, own_index, per_peer)
    near_columns = one_hot(route_ref, own_index ^ 1, per_peer)
    reversed_columns = jnp.dot(own_columns, reverse, preferred_element_type=jnp.float32).astype(jnp.bfloat16)
    edge_ref[...] = jnp.concatenate([near_columns, reversed_columns, own_columns], axis=1)
    for at in range(peers // 2 - 1):
        start = 2 * at * per_peer
        slots_ref[0, :, at * per_peer : (at + 1) * per_peer] = far_ref[:, start : start + per_peer]
        slots_ref[1, :, (at + 1) * per_peer : (at + 2) * per_peer] = far_ref[:, start + per_peer : start + 2 * per_peer]
    slots_ref[0, :, (peers // 2 - 1) * per_peer :] = own_columns
    slots_ref[1, :, :per_peer] = near_columns
    send_near(values_ref[...], edge_ref, near_ref, back_ref, stay_ref)
    operator = operator_ref[0]
    for half in range(2):
        placed_ref[half] = jnp.dot(
            operator, slots_ref[half], preferred_element_type=jnp.float32
        ).astype(operator.dtype)


def first_half_kernel(placed_ref, stay_ref, back_ref, *refs):
    *pair_refs, jump_ref, image_ref = refs
    sent_refs, got_refs = pair_refs[: len(pair_refs) // 2], pair_refs[len(pair_refs) // 2 :]
    loads = stay_ref.shape[0] - GROUP
    groups = (jump_ref.shape[0] - loads) // GROUP
    own, got = (spread(straight(*refs), loads, groups) for refs in ((stay_ref, sent_refs), (back_ref, got_refs)))
    jump_ref[...] = own - got
    image_ref[...] = split_dot(own - got, placed_ref[0], NT)


def first_kernel(far_ref, placed_ref, half_ref, got_ref, near_ref, *refs):
    sent_refs, (jump_ref, image_ref, *pair_refs) = refs[: len(refs) // 2 - 1], refs[len(refs) // 2 - 1 :]
    height = near_ref.shape[0]
    loads = height - GROUP
    groups = (image_ref.shape[0] - loads) // GROUP
    own, got = (spread(value, loads, groups) for value in (for_other(near_ref, sent_refs), handed(got_ref, height)))
    jump_ref[...] = own - got
    image = half_ref[...] + split_dot(own - got, placed_ref[1], NT)
    image_ref[...] = image
    send_far(image, far_ref, *pair_refs)


def products_of(left, right):
    rows, columns = left.shape[0], right.shape[0]
    both = lax.dot_general(split(left), split(right), NT, preferred_element_type=jnp.float32)
    both = both[:rows] + both[rows:]
    return both[:, :columns] + both[:, columns:]


def by_load(products):
    sums = [jnp.sum(product, axis=1, keepdims=True) for product in products]
    empty = [jnp.zeros_like(sums[0])] * (GROUP - len(sums))
    return jnp.concatenate(sums + empty, axis=1).T


def pack(by_mode, scalars, blocks):
    by_mode = by_mode + pltpu.roll(by_mode, by_mode.shape[1] // 2, 1)
    upper, lower = by_mode[:GROUP], by_mode[GROUP:]
    row = lax.broadcasted_iota(jnp.int32, upper.shape, 0)
    left = lax.broadcasted_iota(jnp.int32, upper.shape, 1) < upper.shape[1] // 2
    spare = [
        jnp.where(left, pltpu.roll(upper, 6, 0), pltpu.roll(upper, 4, 0)),
        jnp.where(left, pltpu.roll(upper, 2, 0), pltpu.roll(lower, 6, 0)),
        jnp.where(left, pltpu.roll(lower, 4, 0), pltpu.roll(lower, 2, 0)),
        jnp.where(row == MODES, *scalars),
    ]
    rows = jnp.concatenate(blocks, axis=0)
    parts = [jnp.where(row < MODES, rows[at * GROUP : (at + 1) * GROUP], spare[at]) for at in range(4)]
    return jnp.concatenate(parts, axis=0)


def unpack(terms):
    parts = [terms[at * GROUP : (at + 1) * GROUP] for at in range(4)]
    row = lax.broadcasted_iota(jnp.int32, parts[0].shape, 0)
    lane = lax.broadcasted_iota(jnp.int32, parts[0].shape, 1)
    half = terms.shape[1] // 2
    turned = [pltpu.roll(part, half, 1) for part in parts[:3]]
    upper = jnp.where(
        row < 2, pltpu.roll(parts[0], 2, 0), jnp.where(row < 4, pltpu.roll(turned[0], 4, 0), pltpu.roll(parts[1], 6, 0))
    )
    lower = jnp.where(
        row < 2, pltpu.roll(turned[1], 2, 0), jnp.where(row < 4, pltpu.roll(parts[2], 4, 0), pltpu.roll(turned[2], 6, 0))
    )
    by_mode = [jnp.where((row < MODES) & (lane < half), part, 0.0) for part in (upper, lower)]
    blocks = [jnp.where(row < MODES, part, 0.0) for part in parts]
    scalars = parts[3][MODES : MODES + 1], parts[3][MODES + 1 : MODES + 2]
    return jnp.concatenate(by_mode, axis=0), scalars, [jnp.concatenate(blocks[at : at + 2], axis=0) for at in (0, 2)]


def powers(coarse, loads):
    lane = lax.broadcasted_iota(jnp.int32, (coarse, 4 * loads), 1)
    row = lax.broadcasted_iota(jnp.int32, (coarse, 4 * loads), 0)

    def choose(at, *values):
        return functools.reduce(lambda rest, pair: jnp.where(at == pair[0], pair[1], rest), enumerate(values), 0.0 * lane)

    strip, group = lane // coarse, lane // loads
    by_mode = choose(strip, jnp.where(lane > row, 2.0, 0.0), 1.0, 3.0, 2.0)
    scalars = choose(group, 0.0, 1.0, 2.0, 3.0), choose(group, 2.0, 2.0)
    blocks = [choose(group, 0.0, 2.0, 2.0, 1.0), choose(group, 2.0, 3.0, 3.0, 1.0)]
    return pack(by_mode, [line[:1] for line in scalars], blocks)


def magnitude(operator_ref):
    tall = 2 * GROUP
    largest = jnp.zeros((tall, operator_ref.shape[2]), operator_ref.dtype)
    for start in range(0, operator_ref.shape[1], tall):
        part = operator_ref[0, start : start + tall]
        largest = jnp.maximum(largest, jnp.maximum(part, -part))
    largest = jnp.max(largest.astype(jnp.float32), axis=0, keepdims=True)
    return jnp.clip(jnp.max(largest, axis=1, keepdims=True), 1e-30, 1e30)


def scale_of(terms):
    last = terms[-GROUP:]
    half = last.shape[1] // 2
    lane = lax.broadcasted_iota(jnp.int32, last.shape, 1)
    return jnp.where(lane < half, pltpu.roll(last, half, 1), last)[GROUP - 1 :]


def middle_kernel(
    edge_ref, slots_ref, operator_ref, straight_ref, handed_ref, image_ref,
    basis_ref, scale_ref, powers_ref, terms_ref, sums_ref, near_ref, back_ref, stay_ref,
):
    image = image_ref[...]
    send_near(image, edge_ref, near_ref, back_ref, stay_ref)
    coarse = terms_ref.shape[0] // 3
    loads = image.shape[0] - coarse
    basis = split_dot(straight_ref[...], slots_ref[0], NT) + split_dot(handed_ref[...], slots_ref[1], NT)
    basis_ref[...] = basis
    scale = magnitude(operator_ref)
    scale_ref[...] = jnp.broadcast_to(scale, scale_ref.shape)
    image = image * (1.0 / scale)
    residual, residual_image = basis[:loads], image[:loads]
    lanes = terms_ref.shape[1]
    powers_ref[...] = powers(coarse, loads)
    empty = jnp.zeros((lanes - 2 * loads - 2 * coarse, basis.shape[1]), jnp.float32)
    both = products_of(
        jnp.concatenate([basis[loads:], image[loads:]]),
        jnp.concatenate([residual, basis[loads:], image[loads:], empty, residual_image]),
    )
    by_g, by_h = both[:coarse], both[coarse:]
    lane = lax.broadcasted_iota(jnp.int32, (coarse, lanes), 1)
    first, last = lane < loads, lane >= lanes - loads
    terms_ref[:coarse] = jnp.where(first | last, by_g, 0.0)
    terms_ref[coarse : 2 * coarse] = jnp.where(last, pltpu.roll(by_h, lanes - loads, 1), 0.0)
    row = lax.broadcasted_iota(jnp.int32, (coarse, lanes), 0)
    by_mode = jnp.where((lane <= row) | ((lane >= coarse) & (lane < 2 * coarse)), pltpu.roll(by_g, lanes - loads, 1), 0.0)
    terms_ref[2 * coarse :] = by_mode
    sums_ref[...] = by_load([residual * residual, residual * residual_image])


def second_half_kernel(slots_ref, placed_ref, scale_ref, stay_ref, back_ref, *refs):
    *pair_refs, jump_ref, second_ref = refs
    sent_refs, got_refs = pair_refs[: len(pair_refs) // 2], pair_refs[len(pair_refs) // 2 :]
    jump = straight(stay_ref, sent_refs) - straight(back_ref, got_refs)
    jump = jump * (1.0 / scale_ref[:1, : jump.shape[1]])
    jump_ref[...] = split_dot(jump, slots_ref[0], NT)
    second_ref[...] = split_dot(jump, placed_ref[0], NT)


def second_kernel(
    slots_ref, placed_ref, basis_ref, half_jump_ref, half_second_ref, scale_ref, early_ref, sums_ref, got_ref,
    near_ref, *refs,
):
    *sent_refs, jump_ref, terms_ref, chip_ref = refs
    coarse = terms_ref.shape[0] // 2
    loads = basis_ref.shape[0] - coarse
    jump = for_other(near_ref, sent_refs) - handed(got_ref, loads + coarse, backwards=True)
    lanes = chip_ref.shape[1]
    chip = jnp.maximum(scale_ref[:1, :lanes], got_ref[got_ref.shape[0] - 1 :])
    chip_ref[...] = jnp.broadcast_to(chip, chip_ref.shape)
    inverse = 1.0 / chip
    ratio = scale_ref[:1, :lanes] * inverse
    wide_inverse, wide_ratio = (jnp.concatenate([line] * (basis_ref.shape[1] // lanes), axis=1) for line in (inverse, ratio))
    jump = jump * wide_inverse[:, : jump.shape[1]]
    second = (half_second_ref[...] * wide_ratio + split_dot(jump, placed_ref[1], NT)) * wide_inverse
    jump = half_jump_ref[...] * wide_ratio + split_dot(jump, slots_ref[1], NT)
    jump_ref[...] = jump
    basis = basis_ref[...]
    residual, jump_loads, second_loads = basis[:loads], jump[:loads], second[:loads]
    both = products_of(
        jnp.concatenate([basis[loads:], jump[loads:], second[loads:]]),
        jnp.concatenate([residual, jump_loads, second_loads, jump[loads:], second[loads:]]),
    )
    by_g, by_z, by_dz = (both[at * coarse : (at + 1) * coarse] for at in range(3))
    lanes = terms_ref.shape[1]
    lane = lax.broadcasted_iota(jnp.int32, (coarse, lanes), 1)
    group = lane // loads
    top = jnp.where(group == 1, by_z, jnp.where(group == 2, by_g, 0.0))
    low = jnp.where(group < 2, by_dz, jnp.where(group == 2, by_z, 0.0))
    row = lax.broadcasted_iota(jnp.int32, (coarse, lanes), 0)
    z_z = pltpu.roll(by_z, 2 * coarse, 1)
    strip = lane // coarse
    by_mode = jnp.where((lane > row) & (strip == 0), z_z, 0.0)
    by_mode = jnp.where(strip == 2, pltpu.roll(by_z, 3 * coarse, 1), by_mode)
    by_mode = jnp.where(strip == 3, pltpu.roll(by_g, 4 * coarse, 1), by_mode)
    diagonal = jnp.sum(jnp.where(lane == row, z_z, 0.0), axis=0, keepdims=True)
    sums = by_load([jump_loads * jump_loads, jump_loads * second_loads, residual * second_loads])
    scalars = (
        jnp.concatenate([sums_ref[0:1], sums_ref[1:2] * ratio[:, :loads], sums[0:1], sums[1:2]], axis=1),
        jnp.concatenate([sums[2:3], diagonal[:, :loads], chip[:, : 2 * loads]], axis=1),
    )
    blocks = [
        early_ref[at * coarse : (at + 1) * coarse] * jnp.where(group == 3, ratio, 1.0) + block
        for at, block in enumerate((top, low))
    ]
    by_mode = early_ref[2 * coarse :] * jnp.where(strip == 1, ratio, 1.0) + by_mode
    terms_ref[...] = pack(by_mode, scalars, blocks)


def chip_kernel(other_ref, own_ref, *sum_refs):
    own = own_ref[...]
    row = lax.broadcasted_iota(jnp.int32, own.shape, 0)
    lane = lax.broadcasted_iota(jnp.int32, own.shape, 1)
    total = jnp.where((row == own.shape[0] - 1) & (lane >= own.shape[1] // 2), own, own + other_ref[...])
    for ref in sum_refs:
        ref[...] = total


def summed(refs, power):
    parts = [ref[...] for ref in reversed(refs)]
    scales = [scale_of(part) for part in parts]
    largest = functools.reduce(jnp.maximum, scales)
    inverse = 1.0 / largest
    for at, scale in enumerate(scales):
        factor = scale * inverse
        square = factor * factor
        high = jnp.where(power > 2, square * factor, square)
        parts[at] = parts[at] * jnp.where(power > 1, high, jnp.where(power > 0, factor, 1.0))
    while len(parts) > 1:
        parts = [low + high for low, high in zip(parts[::2], parts[1::2])]
    return parts[0], largest


def sum_kernel(count, powers_ref, *refs):
    power = powers_ref[...]
    total, scale = summed(refs[:count], power)
    row = lax.broadcasted_iota(jnp.int32, power.shape, 0)
    lane = lax.broadcasted_iota(jnp.int32, power.shape, 1)
    total = jnp.where((row == power.shape[0] - 1) & (lane >= power.shape[1] // 2), scale, total)
    for ref in refs[count:]:
        ref[...] = total


def eliminate(work, coarse):
    row = lax.broadcasted_iota(jnp.int32, work.shape, 0)
    for start in range(0, coarse, GROUP):
        pivots = range(start, start + MODES)
        columns = [jnp.broadcast_to(work[:, pivot : pivot + 1], work.shape) for pivot in pivots]
        square = [[column[pivot : pivot + 1] for column in columns] for pivot in pivots]
        rows = [work[pivot : pivot + 1] for pivot in pivots]
        for at in range(MODES):
            scale = 1.0 / square[at][at]
            rows[at] = rows[at] * scale
            square[at] = [value * scale for value in square[at]]
            for other in range(MODES):
                if other != at:
                    factor = square[other][at]
                    rows[other] = rows[other] - factor * rows[at]
                    square[other] = [
                        value if to <= at else value - factor * square[at][to]
                        for to, value in enumerate(square[other])
                    ]
        for column, solved in zip(columns, rows):
            work = work - column * solved
        for pivot, solved in zip(pivots, rows):
            work = jnp.where(row == pivot, solved, work)
    return work


def thin_dot(left, right):
    high, right_high = (value.astype(jnp.bfloat16).astype(jnp.float32) for value in (left, right))
    return jnp.dot(
        jnp.concatenate([high, left - high, high], axis=1).astype(jnp.bfloat16),
        jnp.concatenate([right_high, right_high, right - right_high], axis=0).astype(jnp.bfloat16),
        preferred_element_type=jnp.float32,
    )


def final_kernel(powers_ref, *refs):
    *parts_refs, basis_ref, jump_ref, scale_ref, multipliers_ref, amplitudes_ref = refs
    terms, scale = summed(parts_refs, powers_ref[...])
    coarse = terms.shape[0] // 2
    loads = basis_ref.shape[0] - coarse
    groups = coarse // GROUP

    def total(values):
        return jnp.sum(values, axis=0, keepdims=True)

    ratio = scale_ref[:1, : scale.shape[1]] / scale
    jump = jump_ref[...] * jnp.concatenate([ratio] * (jump_ref.shape[1] // ratio.shape[1]), axis=1)
    by_mode, (sums, last_sums), (top, low) = unpack(terms)
    res_res, res_image, jump_jump, jump_second = (sums[:, at * loads : (at + 1) * loads] for at in range(4))
    res_second, diagonal = last_sums[:, :loads], last_sums[:, loads : loads + coarse]
    coarse_res, jump_z, second_g, image_g = (top[:, at * loads : (at + 1) * loads] for at in range(4))
    res_dz, jump_dz, second_z, res_h = (low[:, at * loads : (at + 1) * loads] for at in range(4))
    triangles, g_h, z_dz, g_dz = (by_mode[:, at * coarse : (at + 1) * coarse] for at in range(4))
    row = lax.broadcasted_iota(jnp.int32, (coarse, coarse), 0)
    column = lax.broadcasted_iota(jnp.int32, (coarse, coarse), 1)
    unit = jnp.where(row == column, 1.0, 0.0)
    other = triangles.T
    gram = jnp.where(row >= column, triangles, other)
    z_z = jnp.where(row < column, triangles, jnp.where(row == column, diagonal, other))
    empty = jnp.zeros((coarse, 5 * coarse - 2 * loads), jnp.float32)
    solved = eliminate(
        jnp.concatenate([gram, g_h, coarse_res, image_g, unit, empty], axis=1), coarse
    )
    inverse_h = solved[:, coarse : 2 * coarse]
    amounts = solved[:, 2 * coarse : 2 * coarse + loads]
    inverse_image = solved[:, 2 * coarse + loads : 2 * coarse + 2 * loads]
    inverse = solved[:, 2 * coarse + 2 * loads : 3 * coarse + 2 * loads]
    products = small_dot(jnp.concatenate([inverse_h, g_h, z_z, g_dz, z_dz], axis=0), amounts)
    inverse_h_amounts, h_amounts, z_amounts, g_dz_amounts, z_dz_amounts = (
        products[at * coarse : (at + 1) * coarse] for at in range(5)
    )
    shares = 2.0 * (inverse_image - inverse_h_amounts)
    both = jnp.concatenate([amounts, shares], axis=0).T
    basis_g, jump_z_rows = basis_ref[loads:], jump[loads:]
    d = basis_ref[:loads] - thin_dot(both[:, :coarse], basis_g)
    u = jump[:loads] - thin_dot(both, jnp.concatenate([jump_z_rows, basis_g], axis=0))
    products = small_dot(jnp.concatenate([g_h, z_z], axis=0), shares)
    image_d = image_g - h_amounts
    inner = res_res - total(amounts * coarse_res)
    curvature = 2.0 * (res_image - total(amounts * (res_h + image_d)))
    u_u = jump_jump - total(amounts * (2.0 * jump_z - z_amounts) + 2.0 * image_d * shares)
    second_u = second_g - g_dz_amounts - products[:coarse]
    jump_u = second_z - z_dz_amounts - 0.5 * products[coarse:]
    d_second = res_second - total(amounts * (res_dz + second_u) + shares * res_h)
    u_second = jump_second - total(amounts * (jump_dz + jump_u) + shares * (0.5 * jump_z + second_u))
    step = inner / curvature
    renewed = step * step * u_u - inner
    grown = 1.0 + renewed / inner
    curvature = grown * grown * curvature - grown * step * (2.0 * d_second + u_u) + 2.0 * step * step * u_second
    second_step = renewed / curvature
    on_d, on_u = step + second_step * grown, second_step * step
    amplitudes = amounts - on_d * shares + 2.0 * on_u * small_dot(inverse, second_u)
    amplitudes_ref[...] = jnp.concatenate(
        [amplitudes[label * GROUP : label * GROUP + MODES] for label in range(groups)], axis=0
    )
    inverse = 1.0 / scale[:, :loads]
    weights = jnp.concatenate([on_d * inverse, on_u * inverse, jnp.zeros((6, loads), jnp.float32)], axis=0).T
    multipliers_ref[...] = weights[:, 0:1] * d - weights[:, 1:2] * u


def call(kernel, shapes, in_specs, name, scratch=(), flops=0):
    return pl.pallas_call(
        kernel,
        out_shape=[jax.ShapeDtypeStruct(*shape) for shape in shapes],
        in_specs=in_specs,
        out_specs=[VMEM] * len(shapes),
        scratch_shapes=scratch,
        compiler_params=pltpu.CompilerParams(vmem_limit_bytes=24 * 1024 * 1024),
        cost_estimate=pl.CostEstimate(flops=flops, bytes_accessed=2**20, transcendentals=0),
        name=name,
    )


def permute(values, offset, plane_offset=0):
    peers, planes = lax.axis_size("sub"), lax.axis_size("rep")
    offset = offset * planes + plane_offset
    return lax.ppermute(values, ("sub", "rep"), [(at, at ^ offset) for at in range(peers * planes)])


def to_chips(*pairs):
    return [permute(pair, 2 * (len(pairs) - at) + 1) for at, pair in enumerate(pairs)]


def to_core(near, *pairs, extra=()):
    return permute(jnp.concatenate([near, *(pair[near.shape[0] :] for pair in pairs), *extra], axis=0), 1)


def last_parts(terms, powers):
    chips = [(offset + 1, 0) for offset in reversed(range(2, lax.axis_size("sub"), 2))]
    planes = [(1, offset) for offset in reversed(range(1, lax.axis_size("rep")))]
    shape = (terms.shape, terms.dtype)
    copies = call(chip_kernel, [shape] * len(chips), [VMEM] * 2, "chip")(permute(terms, 1), terms)
    parts = [permute(copy, *offset) for copy, offset in zip(copies, chips)]
    kernel = functools.partial(sum_kernel, len(parts) + 1)
    copies = call(kernel, [shape] * len(planes), [VMEM] * (len(parts) + 2), "sum")(powers, *parts, copies[0])
    return [*(permute(copy, *offset) for copy, offset in zip(copies, planes)), copies[0]]


def fused_body(dual_ops, mode_traces, route, mode_block, local_gap):
    peers = lax.axis_size("sub")
    loads, rows = local_gap.shape
    modes = mode_traces.shape[1]
    subs = mode_block.shape[0]
    groups = subs // AGG_SUBS
    per_peer = rows // peers
    height = loads + GROUP * groups
    f32, i32 = jnp.float32, jnp.int32
    tall = ((height, rows), f32)
    wide = ((3 * GROUP * groups, 4 * loads), f32)

    def pairs(height):
        return [((2 * height, per_peer), f32)] * (peers // 2 - 1)

    def singles(height):
        return [((height, per_peer), f32)] * 3

    def held(value):
        return pltpu.with_memory_space_constraint(value, pltpu.HBM)

    inputs = [route, mode_block.reshape(1, subs), local_gap, mode_traces.transpose(1, 0, 2), dual_ops]
    short = loads + GROUP
    far, values, operator, route, *send = call(
        place_kernel,
        [
            ((rows, rows - 2 * per_peer), jnp.bfloat16),
            ((short, rows), f32),
            (dual_ops.shape, dual_ops.dtype),
            (route.shape, i32),
            *pairs(short),
        ],
        [HBM] * 5,
        "place",
        [pltpu.VMEM((1, subs), i32), pltpu.VMEM((modes, 1, rows), f32), pltpu.SemaphoreType.DMA((5,))],
    )(*(held(value) for value in inputs))
    got = to_chips(*send)
    halves = ((2, rows, rows // 2), dual_ops.dtype)
    edge, slots, placed, near, back, stay = call(
        ready_kernel,
        [((rows, 3 * per_peer), jnp.bfloat16), halves, halves, *singles(short)],
        [VMEM] * 4,
        "ready",
        flops=2 * rows * rows * rows,
    )(route, far, values, operator)
    got_near = to_core(near, *got)
    half = ((height, rows // 2), f32)
    straight_jump, half_image = call(
        first_half_kernel, [half, tall], [VMEM] * (3 + 2 * len(got)), "first_half", flops=2 * rows * rows * height
    )(placed, stay, back, *send, *got)
    handed_jump, image, *image_send = call(
        first_kernel, [half, tall, *pairs(height)], [VMEM] * (5 + len(send)), "first"
    )(far, placed, half_image, got_near, near, *send)
    got = to_chips(*image_send)
    packed = ((2 * GROUP * groups, 4 * loads), f32)
    basis, scale, powers, terms, sums, near, back, stay = call(
        middle_kernel,
        [tall, ((GROUP, rows), f32), packed, wide, ((GROUP, loads), f32), *singles(height)],
        [VMEM] * 6,
        "middle",
        flops=4 * rows * rows * height,
    )(edge, slots, operator, straight_jump, handed_jump, image)
    got_near = to_core(near, *got[::-1], extra=[scale[:, :per_peer]])
    half_jump, half_second = call(
        second_half_kernel, [tall, tall], [VMEM] * (5 + 2 * len(got)), "second_half", flops=4 * rows * rows * height
    )(slots, placed, scale, stay, back, *image_send, *got)
    jump, terms, scale = call(second_kernel, [tall, packed, ((GROUP, 4 * loads), f32)], [VMEM] * (10 + len(got)), "second")(
        slots, placed, basis, half_jump, half_second, scale, terms, sums, got_near, near, *image_send
    )
    parts = last_parts(terms, powers)
    multipliers, amplitudes = call(
        final_kernel, [((loads, rows), f32), ((MODES * groups, loads), f32)], [VMEM] * (4 + len(parts)), "final"
    )(powers, *parts, basis, jump, scale)
    return multipliers, amplitudes.T


def general_body(dual_ops, mode_traces, route, mode_block, local_gap):
    own_index = lax.axis_index("sub")
    plane_index = lax.axis_index("rep")
    peer_count = lax.axis_size("sub")
    plane_count = lax.axis_size("rep")
    operator = dual_ops[0]
    traces = mode_traces[0]
    slot_rows = route[0]
    rows_here = operator.shape[0]
    load_cases = local_gap.shape[0]
    per_peer = rows_here // peer_count
    blocks = mode_block[:, 0]
    block_count = blocks.shape[0] // AGG_SUBS
    coarse = block_count * MODES
    positions = jnp.arange(rows_here, dtype=jnp.int32)
    inverse = jnp.zeros((rows_here,), jnp.int32).at[slot_rows].set(positions)
    slot_peer = positions // per_peer
    within = positions % per_peer
    flip_index = jnp.where(
        slot_peer == own_index, slot_peer * per_peer + per_peer - 1 - within, positions
    )
    peer_ids = jnp.arange(peer_count, dtype=jnp.int32)
    peer_blocks = blocks[peer_ids * plane_count + plane_index]
    own_block = blocks[own_index * plane_count + plane_index]
    labels = jnp.arange(block_count, dtype=jnp.int32)
    peer_onehot = (peer_blocks[:, None] == labels[None, :]).astype(jnp.float32)
    own_onehot = (labels == own_block).astype(jnp.float32)
    trace_slots = traces[:, slot_rows]
    receive_index = flip_index[inverse]

    def to_peers(values):
        return values[:, slot_rows]

    def from_peers(values):
        return values[:, inverse]

    gap_peers = to_peers(local_gap)
    got_traces = lax.all_to_all(trace_slots, "sub", split_axis=1, concat_axis=1, tiled=True)
    got_gap = lax.all_to_all(gap_peers, "sub", split_axis=1, concat_axis=1, tiled=True)
    partner_traces = got_traces[:, flip_index]
    residual = local_gap - got_gap[:, receive_index]
    own_gram = jnp.dot(traces, traces.T, precision=HIGHEST)
    paired = (trace_slots[:, None, :] * partner_traces[None, :, :]).reshape(
        MODES, MODES, peer_count, per_peer
    )
    cross_terms = jnp.sum(paired, axis=3)
    cross_blocks = jnp.einsum("klq,qb->kbl", cross_terms, peer_onehot, precision=HIGHEST)
    own_blocks = own_gram[:, None, :] * own_onehot[None, :, None]
    row_term = 2.0 * (own_blocks - cross_blocks).reshape(MODES, coarse)
    gram_term = (own_onehot[:, None, None] * row_term[None]).reshape(coarse, coarse)

    def coarse_term(values):
        own_part = 2.0 * jnp.dot(values, traces.T, precision=HIGHEST)
        return (own_part[:, None, :] * own_onehot[None, :, None]).reshape(load_cases, coarse)

    def expand(amounts):
        grouped = amounts.reshape(load_cases, block_count, MODES)
        own_amounts = lax.dynamic_index_in_dim(grouped, own_block, 1, keepdims=False)
        own_part = jnp.dot(own_amounts, traces, precision=HIGHEST)
        peer_amounts = jnp.einsum("qb,rbk->rkq", peer_onehot, grouped, precision=HIGHEST)
        spread = jnp.repeat(peer_amounts, per_peer, axis=2)
        peer_part = jnp.sum(spread * partner_traces[None, :, :], axis=1)
        return own_part - from_peers(peer_part)

    squares = jnp.sum(residual * residual, axis=1)
    gram_matrix, coarse_res, norm_res = lax.psum(
        (gram_term, coarse_term(residual), squares), ("sub", "rep")
    )
    factor = jnp.linalg.cholesky(gram_matrix)

    def solve_coarse(right):
        return jax.scipy.linalg.cho_solve((factor, True), right.T).T

    amplitudes = solve_coarse(coarse_res)
    projected = residual - expand(amplitudes)
    inner_sum = norm_res - jnp.sum(amplitudes * coarse_res, axis=1)
    direction = projected
    multipliers = jnp.zeros_like(residual)
    for iteration in range(ITERS):
        product = lax.dot_general(
            direction.astype(jnp.bfloat16),
            operator,
            (((1,), (1,)), ((), ())),
            preferred_element_type=jnp.float32,
        )
        got_product = lax.all_to_all(
            to_peers(product), "sub", split_axis=1, concat_axis=1, tiled=True
        )
        image_jump = product - got_product[:, receive_index]
        coarse_jump, jump_squares, residual_cross, curvature = lax.psum(
            (
                coarse_term(image_jump),
                jnp.sum(image_jump * image_jump, axis=1),
                jnp.sum(residual * image_jump, axis=1),
                jnp.sum(direction * image_jump, axis=1),
            ),
            ("sub", "rep"),
        )
        step_size = inner_sum / curvature
        multipliers = multipliers + step_size[:, None] * direction
        residual = residual - step_size[:, None] * image_jump
        coarse_res = coarse_res - step_size[:, None] * coarse_jump
        norm_res = (
            norm_res - 2.0 * step_size * residual_cross + step_size * step_size * jump_squares
        )
        amplitudes = solve_coarse(coarse_res)
        if iteration + 1 < ITERS:
            projected = residual - expand(amplitudes)
            renewed = norm_res - jnp.sum(amplitudes * coarse_res, axis=1)
            direction = projected + (renewed / inner_sum)[:, None] * direction
            inner_sum = renewed
    return (multipliers, amplitudes)


def fits(mesh, dual_ops, mode_block, local_gap):
    peers, planes = mesh.shape["sub"], mesh.shape["rep"]
    powers = all(size & (size - 1) == 0 for size in (peers, planes))
    whole = dual_ops.shape[1] % (128 * peers) == 0 and local_gap.shape[0] % 16 == 0
    coarse = GROUP * (mode_block.shape[0] // AGG_SUBS)
    return powers and whole and 4 * local_gap.shape[0] == 128 and 8 * coarse == 128


def solution(mesh):
    placed = (
        P(("sub", "rep"), None, None),
        P(("sub", "rep"), None, None),
        P(("sub", "rep"), None),
        P(),
        P(None, ("sub", "rep")),
    )

    def run(dual_ops, mode_traces, route, mode_block, local_gap):
        body = fused_body if fits(mesh, dual_ops, mode_block, local_gap) else general_body
        return jax.shard_map(
            body, mesh=mesh, in_specs=placed, out_specs=(P(None, ("sub", "rep")), P()), check_vma=False
        )(dual_ops, mode_traces, route, mode_block, local_gap)

    return run
```

```python
import functools

import jax
import jax.numpy as jnp
from jax import lax
from jax.experimental import pallas as pl
from jax.experimental.pallas import tpu as pltpu
from jax.sharding import PartitionSpec as P

MODES = 6
AGG_SUBS = 16
ITERS = 2
GROUP = 8

HIGHEST = lax.Precision.HIGHEST
VMEM = pl.BlockSpec(memory_space=pltpu.VMEM)
HBM = pl.BlockSpec(memory_space=pltpu.HBM)
NN = (((1,), (0,)), ((), ()))
NT = (((1,), (1,)), ((), ()))


def split(values):
    high = values.astype(jnp.bfloat16).astype(jnp.float32)
    return jnp.concatenate([high, values - high], axis=0).astype(jnp.bfloat16)


def split_dot(values, matrix, dims):
    rows = values.shape[0]
    both = lax.dot_general(split(values), matrix, dims, preferred_element_type=jnp.float32)
    return both[:rows] + both[rows:]


def small_dot(left, right):
    return jnp.dot(left, right, precision=HIGHEST, preferred_element_type=jnp.float32)


def send_far(values, far_ref, *pair_refs):
    height = values.shape[0]
    per_peer = pair_refs[0].shape[1]
    values = split(values)
    for at, ref in enumerate(pair_refs):
        columns = far_ref[:, 2 * at * per_peer : (2 * at + 2) * per_peer]
        slots = jnp.dot(values, columns, preferred_element_type=jnp.float32)
        slots = slots[:height] + slots[height:]
        ref[:height] = slots[:, :per_peer]
        ref[height:] = slots[:, per_peer:]


def send_near(values, edge_ref, near_ref, back_ref, stay_ref):
    per_peer = back_ref.shape[1]
    slots = split_dot(values, edge_ref[...], NN)
    for at, ref in enumerate((near_ref, back_ref, stay_ref)):
        ref[...] = slots[:, at * per_peer : (at + 1) * per_peer]


def straight(last_ref, pair_refs):
    height = last_ref.shape[0]
    return jnp.concatenate([*(ref[:height] for ref in pair_refs), last_ref[...]], axis=1)


def for_other(near_ref, pair_refs):
    height = near_ref.shape[0]
    return jnp.concatenate([near_ref[...], *(ref[height:] for ref in pair_refs)], axis=1)


def handed(got_ref, height, backwards=False):
    starts = list(range(height, got_ref.shape[0] - height + 1, height))
    starts = [0, *(starts[::-1] if backwards else starts)]
    return jnp.concatenate([got_ref[at : at + height] for at in starts], axis=1)


def spread(values, loads, groups):
    modes = values[loads:]
    label = modes[MODES : MODES + 1]
    used = lax.broadcasted_iota(jnp.int32, modes.shape, 0) < MODES
    parts = [jnp.where(used & (label == group), modes, 0.0) for group in range(groups)]
    return jnp.concatenate([values[:loads], *parts], axis=0)


def one_hot(route_ref, peer, per_peer):
    start = pl.multiple_of(peer * per_peer, per_peer)
    row_ids = lax.broadcasted_iota(jnp.int32, (route_ref.shape[1], per_peer), 0)
    return jnp.where(row_ids == route_ref[:, pl.ds(start, per_peer)], 1.0, 0.0).astype(jnp.bfloat16)


def place_kernel(
    route_hbm, block_hbm, gap_hbm, traces_hbm, operator_hbm,
    far_ref, values_ref, operator_ref, route_ref, *refs,
):
    *pair_refs, block_ref, traces_ref, sems = refs
    loads, rows = gap_hbm.shape
    per_peer = pair_refs[0].shape[1]
    peers = rows // per_peer
    copies = [
        pltpu.make_async_copy(source, target, sems.at[at])
        for at, (source, target) in enumerate(
            (
                (route_hbm, route_ref),
                (block_hbm, block_ref),
                (traces_hbm, traces_ref),
                (gap_hbm, values_ref.at[pl.ds(0, loads)]),
                (operator_hbm, operator_ref),
            )
        )
    ]

    def build(at):
        peer = own_index ^ (peers - 1 - at)
        far_ref[:, at * per_peer : (at + 1) * per_peer] = one_hot(route_ref, peer, per_peer)

    for copy in (copies[3], *copies[:3]):
        copy.start()
    own_index = lax.axis_index("sub")
    device = own_index * lax.axis_size("rep") + lax.axis_index("rep")
    copies[0].wait()
    for copy in copies[4:]:
        copy.start()
    for at in range(peers - 4):
        build(at)
    copies[1].wait()
    copies[2].wait()
    blocks = block_ref[...]
    lane = lax.broadcasted_iota(jnp.int32, blocks.shape, 1)
    own_block = jnp.sum(jnp.where(lane == device, blocks, 0), axis=1, keepdims=True)
    modes = traces_ref.shape[0]
    label = jnp.broadcast_to(own_block.astype(jnp.float32), (1, rows))
    for mode in range(modes):
        values_ref[loads + mode : loads + mode + 1] = traces_ref[mode]
    values_ref[loads + modes : loads + modes + 1] = label
    values_ref[loads + modes + 1 :] = jnp.zeros((GROUP - modes - 1, rows), jnp.float32)
    copies[3].wait()
    for at in range(peers - 4, peers - 2):
        build(at)
    send_far(values_ref[...], far_ref, *pair_refs)
    copies[4].wait()


def ready_kernel(
    route_ref, far_ref, values_ref, operator_ref,
    edge_ref, slots_ref, placed_ref, near_ref, back_ref, stay_ref,
):
    per_peer = back_ref.shape[1]
    peers = far_ref.shape[1] // per_peer + 2
    own_index = lax.axis_index("sub")
    low = lax.broadcasted_iota(jnp.int32, (per_peer, per_peer), 0)
    high = lax.broadcasted_iota(jnp.int32, (per_peer, per_peer), 1)
    reverse = jnp.where(low + high == per_peer - 1, 1.0, 0.0).astype(jnp.bfloat16)
    own_columns = one_hot(route_ref, own_index, per_peer)
    near_columns = one_hot(route_ref, own_index ^ 1, per_peer)
    reversed_columns = jnp.dot(own_columns, reverse, preferred_element_type=jnp.float32).astype(jnp.bfloat16)
    edge_ref[...] = jnp.concatenate([near_columns, reversed_columns, own_columns], axis=1)
    for at in range(peers // 2 - 1):
        start = 2 * at * per_peer
        slots_ref[0, :, at * per_peer : (at + 1) * per_peer] = far_ref[:, start : start + per_peer]
        slots_ref[1, :, (at + 1) * per_peer : (at + 2) * per_peer] = far_ref[:, start + per_peer : start + 2 * per_peer]
    slots_ref[0, :, (peers // 2 - 1) * per_peer :] = own_columns
    slots_ref[1, :, :per_peer] = near_columns
    send_near(values_ref[...], edge_ref, near_ref, back_ref, stay_ref)
    operator = operator_ref[0]
    for half in range(2):
        placed_ref[half] = jnp.dot(
            operator, slots_ref[half], preferred_element_type=jnp.float32
        ).astype(operator.dtype)


def first_half_kernel(placed_ref, stay_ref, back_ref, *refs):
    *pair_refs, jump_ref, image_ref = refs
    sent_refs, got_refs = pair_refs[: len(pair_refs) // 2], pair_refs[len(pair_refs) // 2 :]
    loads = stay_ref.shape[0] - GROUP
    groups = (jump_ref.shape[0] - loads) // GROUP
    own, got = (spread(straight(*refs), loads, groups) for refs in ((stay_ref, sent_refs), (back_ref, got_refs)))
    jump_ref[...] = own - got
    image_ref[...] = split_dot(own - got, placed_ref[0], NT)


def first_kernel(far_ref, placed_ref, half_ref, got_ref, near_ref, *refs):
    sent_refs, (jump_ref, image_ref, *pair_refs) = refs[: len(refs) // 2 - 1], refs[len(refs) // 2 - 1 :]
    height = near_ref.shape[0]
    loads = height - GROUP
    groups = (image_ref.shape[0] - loads) // GROUP
    own, got = (spread(value, loads, groups) for value in (for_other(near_ref, sent_refs), handed(got_ref, height)))
    jump_ref[...] = own - got
    image = half_ref[...] + split_dot(own - got, placed_ref[1], NT)
    image_ref[...] = image
    send_far(image, far_ref, *pair_refs)


def products_of(left, right):
    rows, columns = left.shape[0], right.shape[0]
    both = lax.dot_general(split(left), split(right), NT, preferred_element_type=jnp.float32)
    both = both[:rows] + both[rows:]
    return both[:, :columns] + both[:, columns:]


def by_load(products):
    sums = [jnp.sum(product, axis=1, keepdims=True) for product in products]
    empty = [jnp.zeros_like(sums[0])] * (GROUP - len(sums))
    return jnp.concatenate(sums + empty, axis=1).T


def pack(by_mode, scalars, blocks):
    by_mode = by_mode + pltpu.roll(by_mode, by_mode.shape[1] // 2, 1)
    upper, lower = by_mode[:GROUP], by_mode[GROUP:]
    row = lax.broadcasted_iota(jnp.int32, upper.shape, 0)
    left = lax.broadcasted_iota(jnp.int32, upper.shape, 1) < upper.shape[1] // 2
    spare = [
        jnp.where(left, pltpu.roll(upper, 6, 0), pltpu.roll(upper, 4, 0)),
        jnp.where(left, pltpu.roll(upper, 2, 0), pltpu.roll(lower, 6, 0)),
        jnp.where(left, pltpu.roll(lower, 4, 0), pltpu.roll(lower, 2, 0)),
        jnp.where(row == MODES, *scalars),
    ]
    rows = jnp.concatenate(blocks, axis=0)
    parts = [jnp.where(row < MODES, rows[at * GROUP : (at + 1) * GROUP], spare[at]) for at in range(4)]
    return jnp.concatenate(parts, axis=0)


def unpack(terms):
    parts = [terms[at * GROUP : (at + 1) * GROUP] for at in range(4)]
    row = lax.broadcasted_iota(jnp.int32, parts[0].shape, 0)
    lane = lax.broadcasted_iota(jnp.int32, parts[0].shape, 1)
    half = terms.shape[1] // 2
    turned = [pltpu.roll(part, half, 1) for part in parts[:3]]
    upper = jnp.where(
        row < 2, pltpu.roll(parts[0], 2, 0), jnp.where(row < 4, pltpu.roll(turned[0], 4, 0), pltpu.roll(parts[1], 6, 0))
    )
    lower = jnp.where(
        row < 2, pltpu.roll(turned[1], 2, 0), jnp.where(row < 4, pltpu.roll(parts[2], 4, 0), pltpu.roll(turned[2], 6, 0))
    )
    by_mode = [jnp.where((row < MODES) & (lane < half), part, 0.0) for part in (upper, lower)]
    blocks = [jnp.where(row < MODES, part, 0.0) for part in parts]
    scalars = parts[3][MODES : MODES + 1], parts[3][MODES + 1 : MODES + 2]
    return jnp.concatenate(by_mode, axis=0), scalars, [jnp.concatenate(blocks[at : at + 2], axis=0) for at in (0, 2)]


def powers(coarse, loads):
    lane = lax.broadcasted_iota(jnp.int32, (coarse, 4 * loads), 1)
    row = lax.broadcasted_iota(jnp.int32, (coarse, 4 * loads), 0)

    def choose(at, *values):
        return functools.reduce(lambda rest, pair: jnp.where(at == pair[0], pair[1], rest), enumerate(values), 0.0 * lane)

    strip, group = lane // coarse, lane // loads
    by_mode = choose(strip, jnp.where(lane > row, 2.0, 0.0), 1.0, 3.0, 2.0)
    scalars = choose(group, 0.0, 1.0, 2.0, 3.0), choose(group, 2.0, 2.0)
    blocks = [choose(group, 0.0, 2.0, 2.0, 1.0), choose(group, 2.0, 3.0, 3.0, 1.0)]
    return pack(by_mode, [line[:1] for line in scalars], blocks)


def magnitude(operator_ref):
    tall = 2 * GROUP
    largest = jnp.zeros((tall, operator_ref.shape[2]), operator_ref.dtype)
    for start in range(0, operator_ref.shape[1], tall):
        part = operator_ref[0, start : start + tall]
        largest = jnp.maximum(largest, jnp.maximum(part, -part))
    largest = jnp.max(largest.astype(jnp.float32), axis=0, keepdims=True)
    return jnp.clip(jnp.max(largest, axis=1, keepdims=True), 1e-30, 1e30)


def scale_of(terms):
    last = terms[-GROUP:]
    half = last.shape[1] // 2
    lane = lax.broadcasted_iota(jnp.int32, last.shape, 1)
    return jnp.where(lane < half, pltpu.roll(last, half, 1), last)[GROUP - 1 :]


def middle_kernel(
    edge_ref, slots_ref, operator_ref, straight_ref, handed_ref, image_ref,
    basis_ref, scale_ref, powers_ref, terms_ref, sums_ref, near_ref, back_ref, stay_ref,
):
    image = image_ref[...]
    send_near(image, edge_ref, near_ref, back_ref, stay_ref)
    coarse = terms_ref.shape[0] // 3
    loads = image.shape[0] - coarse
    basis = split_dot(straight_ref[...], slots_ref[0], NT) + split_dot(handed_ref[...], slots_ref[1], NT)
    basis_ref[...] = basis
    scale = magnitude(operator_ref)
    scale_ref[...] = jnp.broadcast_to(scale, scale_ref.shape)
    image = image * (1.0 / scale)
    residual, residual_image = basis[:loads], image[:loads]
    lanes = terms_ref.shape[1]
    powers_ref[...] = powers(coarse, loads)
    empty = jnp.zeros((lanes - 2 * loads - 2 * coarse, basis.shape[1]), jnp.float32)
    both = products_of(
        jnp.concatenate([basis[loads:], image[loads:]]),
        jnp.concatenate([residual, basis[loads:], image[loads:], empty, residual_image]),
    )
    by_g, by_h = both[:coarse], both[coarse:]
    lane = lax.broadcasted_iota(jnp.int32, (coarse, lanes), 1)
    first, last = lane < loads, lane >= lanes - loads
    terms_ref[:coarse] = jnp.where(first | last, by_g, 0.0)
    terms_ref[coarse : 2 * coarse] = jnp.where(last, pltpu.roll(by_h, lanes - loads, 1), 0.0)
    row = lax.broadcasted_iota(jnp.int32, (coarse, lanes), 0)
    by_mode = jnp.where((lane <= row) | ((lane >= coarse) & (lane < 2 * coarse)), pltpu.roll(by_g, lanes - loads, 1), 0.0)
    terms_ref[2 * coarse :] = by_mode
    sums_ref[...] = by_load([residual * residual, residual * residual_image])


def second_half_kernel(slots_ref, placed_ref, scale_ref, stay_ref, back_ref, *refs):
    *pair_refs, jump_ref, second_ref = refs
    sent_refs, got_refs = pair_refs[: len(pair_refs) // 2], pair_refs[len(pair_refs) // 2 :]
    jump = straight(stay_ref, sent_refs) - straight(back_ref, got_refs)
    jump = jump * (1.0 / scale_ref[:1, : jump.shape[1]])
    jump_ref[...] = split_dot(jump, slots_ref[0], NT)
    second_ref[...] = split_dot(jump, placed_ref[0], NT)


def second_kernel(
    slots_ref, placed_ref, basis_ref, half_jump_ref, half_second_ref, scale_ref, early_ref, sums_ref, got_ref,
    near_ref, *refs,
):
    *sent_refs, jump_ref, terms_ref, chip_ref = refs
    coarse = terms_ref.shape[0] // 2
    loads = basis_ref.shape[0] - coarse
    jump = for_other(near_ref, sent_refs) - handed(got_ref, loads + coarse, backwards=True)
    lanes = chip_ref.shape[1]
    chip = jnp.maximum(scale_ref[:1, :lanes], got_ref[got_ref.shape[0] - 1 :])
    chip_ref[...] = jnp.broadcast_to(chip, chip_ref.shape)
    inverse = 1.0 / chip
    ratio = scale_ref[:1, :lanes] * inverse
    wide_inverse, wide_ratio = (jnp.concatenate([line] * (basis_ref.shape[1] // lanes), axis=1) for line in (inverse, ratio))
    jump = jump * wide_inverse[:, : jump.shape[1]]
    second = (half_second_ref[...] * wide_ratio + split_dot(jump, placed_ref[1], NT)) * wide_inverse
    jump = half_jump_ref[...] * wide_ratio + split_dot(jump, slots_ref[1], NT)
    jump_ref[...] = jump
    basis = basis_ref[...]
    residual, jump_loads, second_loads = basis[:loads], jump[:loads], second[:loads]
    both = products_of(
        jnp.concatenate([basis[loads:], jump[loads:], second[loads:]]),
        jnp.concatenate([residual, jump_loads, second_loads, jump[loads:], second[loads:]]),
    )
    by_g, by_z, by_dz = (both[at * coarse : (at + 1) * coarse] for at in range(3))
    lanes = terms_ref.shape[1]
    lane = lax.broadcasted_iota(jnp.int32, (coarse, lanes), 1)
    group = lane // loads
    top = jnp.where(group == 1, by_z, jnp.where(group == 2, by_g, 0.0))
    low = jnp.where(group < 2, by_dz, jnp.where(group == 2, by_z, 0.0))
    row = lax.broadcasted_iota(jnp.int32, (coarse, lanes), 0)
    z_z = pltpu.roll(by_z, 2 * coarse, 1)
    strip = lane // coarse
    by_mode = jnp.where((lane > row) & (strip == 0), z_z, 0.0)
    by_mode = jnp.where(strip == 2, pltpu.roll(by_z, 3 * coarse, 1), by_mode)
    by_mode = jnp.where(strip == 3, pltpu.roll(by_g, 4 * coarse, 1), by_mode)
    diagonal = jnp.sum(jnp.where(lane == row, z_z, 0.0), axis=0, keepdims=True)
    sums = by_load([jump_loads * jump_loads, jump_loads * second_loads, residual * second_loads])
    scalars = (
        jnp.concatenate([sums_ref[0:1], sums_ref[1:2] * ratio[:, :loads], sums[0:1], sums[1:2]], axis=1),
        jnp.concatenate([sums[2:3], diagonal[:, :loads], chip[:, : 2 * loads]], axis=1),
    )
    blocks = [
        early_ref[at * coarse : (at + 1) * coarse] * jnp.where(group == 3, ratio, 1.0) + block
        for at, block in enumerate((top, low))
    ]
    by_mode = early_ref[2 * coarse :] * jnp.where(strip == 1, ratio, 1.0) + by_mode
    terms_ref[...] = pack(by_mode, scalars, blocks)


def chip_kernel(other_ref, own_ref, *sum_refs):
    own = own_ref[...]
    row = lax.broadcasted_iota(jnp.int32, own.shape, 0)
    lane = lax.broadcasted_iota(jnp.int32, own.shape, 1)
    total = jnp.where((row == own.shape[0] - 1) & (lane >= own.shape[1] // 2), own, own + other_ref[...])
    for ref in sum_refs:
        ref[...] = total


def summed(refs, power):
    parts = [ref[...] for ref in reversed(refs)]
    scales = [scale_of(part) for part in parts]
    largest = functools.reduce(jnp.maximum, scales)
    inverse = 1.0 / largest
    for at, scale in enumerate(scales):
        factor = scale * inverse
        square = factor * factor
        high = jnp.where(power > 2, square * factor, square)
        parts[at] = parts[at] * jnp.where(power > 1, high, jnp.where(power > 0, factor, 1.0))
    while len(parts) > 1:
        parts = [low + high for low, high in zip(parts[::2], parts[1::2])]
    return parts[0], largest


def sum_kernel(count, powers_ref, *refs):
    power = powers_ref[...]
    total, scale = summed(refs[:count], power)
    row = lax.broadcasted_iota(jnp.int32, power.shape, 0)
    lane = lax.broadcasted_iota(jnp.int32, power.shape, 1)
    total = jnp.where((row == power.shape[0] - 1) & (lane >= power.shape[1] // 2), scale, total)
    for ref in refs[count:]:
        ref[...] = total


def eliminate(work, coarse):
    row = lax.broadcasted_iota(jnp.int32, work.shape, 0)
    for start in range(0, coarse, GROUP):
        pivots = range(start, start + MODES)
        columns = [jnp.broadcast_to(work[:, pivot : pivot + 1], work.shape) for pivot in pivots]
        square = [[column[pivot : pivot + 1] for column in columns] for pivot in pivots]
        rows = [work[pivot : pivot + 1] for pivot in pivots]
        for at in range(MODES):
            scale = 1.0 / square[at][at]
            rows[at] = rows[at] * scale
            square[at] = [value * scale for value in square[at]]
            for other in range(MODES):
                if other != at:
                    factor = square[other][at]
                    rows[other] = rows[other] - factor * rows[at]
                    square[other] = [
                        value if to <= at else value - factor * square[at][to]
                        for to, value in enumerate(square[other])
                    ]
        for column, solved in zip(columns, rows):
            work = work - column * solved
        for pivot, solved in zip(pivots, rows):
            work = jnp.where(row == pivot, solved, work)
    return work


def thin_dot(left, right):
    high, right_high = (value.astype(jnp.bfloat16).astype(jnp.float32) for value in (left, right))
    return jnp.dot(
        jnp.concatenate([high, left - high, high], axis=1).astype(jnp.bfloat16),
        jnp.concatenate([right_high, right_high, right - right_high], axis=0).astype(jnp.bfloat16),
        preferred_element_type=jnp.float32,
    )


def final_kernel(powers_ref, *refs):
    *parts_refs, basis_ref, jump_ref, scale_ref, multipliers_ref, amplitudes_ref = refs
    terms, scale = summed(parts_refs, powers_ref[...])
    coarse = terms.shape[0] // 2
    loads = basis_ref.shape[0] - coarse
    groups = coarse // GROUP

    def total(values):
        return jnp.sum(values, axis=0, keepdims=True)

    ratio = scale_ref[:1, : scale.shape[1]] / scale
    jump = jump_ref[...] * jnp.concatenate([ratio] * (jump_ref.shape[1] // ratio.shape[1]), axis=1)
    by_mode, (sums, last_sums), (top, low) = unpack(terms)
    res_res, res_image, jump_jump, jump_second = (sums[:, at * loads : (at + 1) * loads] for at in range(4))
    res_second, diagonal = last_sums[:, :loads], last_sums[:, loads : loads + coarse]
    coarse_res, jump_z, second_g, image_g = (top[:, at * loads : (at + 1) * loads] for at in range(4))
    res_dz, jump_dz, second_z, res_h = (low[:, at * loads : (at + 1) * loads] for at in range(4))
    triangles, g_h, z_dz, g_dz = (by_mode[:, at * coarse : (at + 1) * coarse] for at in range(4))
    row = lax.broadcasted_iota(jnp.int32, (coarse, coarse), 0)
    column = lax.broadcasted_iota(jnp.int32, (coarse, coarse), 1)
    unit = jnp.where(row == column, 1.0, 0.0)
    other = triangles.T
    gram = jnp.where(row >= column, triangles, other)
    z_z = jnp.where(row < column, triangles, jnp.where(row == column, diagonal, other))
    empty = jnp.zeros((coarse, 5 * coarse - 2 * loads), jnp.float32)
    solved = eliminate(
        jnp.concatenate([gram, g_h, coarse_res, image_g, unit, empty], axis=1), coarse
    )
    inverse_h = solved[:, coarse : 2 * coarse]
    amounts = solved[:, 2 * coarse : 2 * coarse + loads]
    inverse_image = solved[:, 2 * coarse + loads : 2 * coarse + 2 * loads]
    inverse = solved[:, 2 * coarse + 2 * loads : 3 * coarse + 2 * loads]
    products = small_dot(jnp.concatenate([inverse_h, g_h, z_z, g_dz, z_dz], axis=0), amounts)
    inverse_h_amounts, h_amounts, z_amounts, g_dz_amounts, z_dz_amounts = (
        products[at * coarse : (at + 1) * coarse] for at in range(5)
    )
    shares = 2.0 * (inverse_image - inverse_h_amounts)
    both = jnp.concatenate([amounts, shares], axis=0).T
    basis_g, jump_z_rows = basis_ref[loads:], jump[loads:]
    d = basis_ref[:loads] - thin_dot(both[:, :coarse], basis_g)
    u = jump[:loads] - thin_dot(both, jnp.concatenate([jump_z_rows, basis_g], axis=0))
    products = small_dot(jnp.concatenate([g_h, z_z], axis=0), shares)
    image_d = image_g - h_amounts
    inner = res_res - total(amounts * coarse_res)
    curvature = 2.0 * (res_image - total(amounts * (res_h + image_d)))
    u_u = jump_jump - total(amounts * (2.0 * jump_z - z_amounts) + 2.0 * image_d * shares)
    second_u = second_g - g_dz_amounts - products[:coarse]
    jump_u = second_z - z_dz_amounts - 0.5 * products[coarse:]
    d_second = res_second - total(amounts * (res_dz + second_u) + shares * res_h)
    u_second = jump_second - total(amounts * (jump_dz + jump_u) + shares * (0.5 * jump_z + second_u))
    step = inner / curvature
    renewed = step * step * u_u - inner
    grown = 1.0 + renewed / inner
    curvature = grown * grown * curvature - grown * step * (2.0 * d_second + u_u) + 2.0 * step * step * u_second
    second_step = renewed / curvature
    on_d, on_u = step + second_step * grown, second_step * step
    amplitudes = amounts - on_d * shares + 2.0 * on_u * small_dot(inverse, second_u)
    amplitudes_ref[...] = jnp.concatenate(
        [amplitudes[label * GROUP : label * GROUP + MODES] for label in range(groups)], axis=0
    )
    inverse = 1.0 / scale[:, :loads]
    weights = jnp.concatenate([on_d * inverse, on_u * inverse, jnp.zeros((6, loads), jnp.float32)], axis=0).T
    multipliers_ref[...] = weights[:, 0:1] * d - weights[:, 1:2] * u


def call(kernel, shapes, in_specs, name, scratch=(), flops=0):
    return pl.pallas_call(
        kernel,
        out_shape=[jax.ShapeDtypeStruct(*shape) for shape in shapes],
        in_specs=in_specs,
        out_specs=[VMEM] * len(shapes),
        scratch_shapes=scratch,
        compiler_params=pltpu.CompilerParams(vmem_limit_bytes=24 * 1024 * 1024),
        cost_estimate=pl.CostEstimate(flops=flops, bytes_accessed=2**20, transcendentals=0),
        name=name,
    )


def permute(values, offset, plane_offset=0):
    peers, planes = lax.axis_size("sub"), lax.axis_size("rep")
    offset = offset * planes + plane_offset
    return lax.ppermute(values, ("sub", "rep"), [(at, at ^ offset) for at in range(peers * planes)])


def to_chips(*pairs):
    return [permute(pair, 2 * (len(pairs) - at) + 1) for at, pair in enumerate(pairs)]


def to_core(near, *pairs, extra=()):
    return permute(jnp.concatenate([near, *(pair[near.shape[0] :] for pair in pairs), *extra], axis=0), 1)


def last_parts(terms, powers):
    chips = [(offset + 1, 0) for offset in reversed(range(2, lax.axis_size("sub"), 2))]
    planes = [(1, offset) for offset in reversed(range(1, lax.axis_size("rep")))]
    shape = (terms.shape, terms.dtype)
    copies = call(chip_kernel, [shape] * len(chips), [VMEM] * 2, "chip")(permute(terms, 1), terms)
    parts = [permute(copy, *offset) for copy, offset in zip(copies, chips)]
    kernel = functools.partial(sum_kernel, len(parts) + 1)
    copies = call(kernel, [shape] * len(planes), [VMEM] * (len(parts) + 2), "sum")(powers, *parts, copies[0])
    return [*(permute(copy, *offset) for copy, offset in zip(copies, planes)), copies[0]]


def fused_body(dual_ops, mode_traces, route, mode_block, local_gap):
    peers = lax.axis_size("sub")
    loads, rows = local_gap.shape
    modes = mode_traces.shape[1]
    subs = mode_block.shape[0]
    groups = subs // AGG_SUBS
    per_peer = rows // peers
    height = loads + GROUP * groups
    f32, i32 = jnp.float32, jnp.int32
    tall = ((height, rows), f32)
    wide = ((3 * GROUP * groups, 4 * loads), f32)

    def pairs(height):
        return [((2 * height, per_peer), f32)] * (peers // 2 - 1)

    def singles(height):
        return [((height, per_peer), f32)] * 3

    def held(value):
        return pltpu.with_memory_space_constraint(value, pltpu.HBM)

    inputs = [route, mode_block.reshape(1, subs), local_gap, mode_traces.transpose(1, 0, 2), dual_ops]
    short = loads + GROUP
    far, values, operator, route, *send = call(
        place_kernel,
        [
            ((rows, rows - 2 * per_peer), jnp.bfloat16),
            ((short, rows), f32),
            (dual_ops.shape, dual_ops.dtype),
            (route.shape, i32),
            *pairs(short),
        ],
        [HBM] * 5,
        "place",
        [pltpu.VMEM((1, subs), i32), pltpu.VMEM((modes, 1, rows), f32), pltpu.SemaphoreType.DMA((5,))],
    )(*(held(value) for value in inputs))
    got = to_chips(*send)
    halves = ((2, rows, rows // 2), dual_ops.dtype)
    edge, slots, placed, near, back, stay = call(
        ready_kernel,
        [((rows, 3 * per_peer), jnp.bfloat16), halves, halves, *singles(short)],
        [VMEM] * 4,
        "ready",
        flops=2 * rows * rows * rows,
    )(route, far, values, operator)
    got_near = to_core(near, *got)
    half = ((height, rows // 2), f32)
    straight_jump, half_image = call(
        first_half_kernel, [half, tall], [VMEM] * (3 + 2 * len(got)), "first_half", flops=2 * rows * rows * height
    )(placed, stay, back, *send, *got)
    handed_jump, image, *image_send = call(
        first_kernel, [half, tall, *pairs(height)], [VMEM] * (5 + len(send)), "first"
    )(far, placed, half_image, got_near, near, *send)
    got = to_chips(*image_send)
    packed = ((2 * GROUP * groups, 4 * loads), f32)
    basis, scale, powers, terms, sums, near, back, stay = call(
        middle_kernel,
        [tall, ((GROUP, rows), f32), packed, wide, ((GROUP, loads), f32), *singles(height)],
        [VMEM] * 6,
        "middle",
        flops=4 * rows * rows * height,
    )(edge, slots, operator, straight_jump, handed_jump, image)
    got_near = to_core(near, *got[::-1], extra=[scale[:, :per_peer]])
    half_jump, half_second = call(
        second_half_kernel, [tall, tall], [VMEM] * (5 + 2 * len(got)), "second_half", flops=4 * rows * rows * height
    )(slots, placed, scale, stay, back, *image_send, *got)
    jump, terms, scale = call(second_kernel, [tall, packed, ((GROUP, 4 * loads), f32)], [VMEM] * (10 + len(got)), "second")(
        slots, placed, basis, half_jump, half_second, scale, terms, sums, got_near, near, *image_send
    )
    parts = last_parts(terms, powers)
    multipliers, amplitudes = call(
        final_kernel, [((loads, rows), f32), ((MODES * groups, loads), f32)], [VMEM] * (4 + len(parts)), "final"
    )(powers, *parts, basis, jump, scale)
    return multipliers, amplitudes.T


def general_body(dual_ops, mode_traces, route, mode_block, local_gap):
    own_index = lax.axis_index("sub")
    plane_index = lax.axis_index("rep")
    peer_count = lax.axis_size("sub")
    plane_count = lax.axis_size("rep")
    operator = dual_ops[0]
    traces = mode_traces[0]
    slot_rows = route[0]
    rows_here = operator.shape[0]
    load_cases = local_gap.shape[0]
    per_peer = rows_here // peer_count
    blocks = mode_block[:, 0]
    block_count = blocks.shape[0] // AGG_SUBS
    coarse = block_count * MODES
    positions = jnp.arange(rows_here, dtype=jnp.int32)
    inverse = jnp.zeros((rows_here,), jnp.int32).at[slot_rows].set(positions)
    slot_peer = positions // per_peer
    within = positions % per_peer
    flip_index = jnp.where(
        slot_peer == own_index, slot_peer * per_peer + per_peer - 1 - within, positions
    )
    peer_ids = jnp.arange(peer_count, dtype=jnp.int32)
    peer_blocks = blocks[peer_ids * plane_count + plane_index]
    own_block = blocks[own_index * plane_count + plane_index]
    labels = jnp.arange(block_count, dtype=jnp.int32)
    peer_onehot = (peer_blocks[:, None] == labels[None, :]).astype(jnp.float32)
    own_onehot = (labels == own_block).astype(jnp.float32)
    trace_slots = traces[:, slot_rows]
    receive_index = flip_index[inverse]

    def to_peers(values):
        return values[:, slot_rows]

    def from_peers(values):
        return values[:, inverse]

    gap_peers = to_peers(local_gap)
    got_traces = lax.all_to_all(trace_slots, "sub", split_axis=1, concat_axis=1, tiled=True)
    got_gap = lax.all_to_all(gap_peers, "sub", split_axis=1, concat_axis=1, tiled=True)
    partner_traces = got_traces[:, flip_index]
    residual = local_gap - got_gap[:, receive_index]
    own_gram = jnp.dot(traces, traces.T, precision=HIGHEST)
    paired = (trace_slots[:, None, :] * partner_traces[None, :, :]).reshape(
        MODES, MODES, peer_count, per_peer
    )
    cross_terms = jnp.sum(paired, axis=3)
    cross_blocks = jnp.einsum("klq,qb->kbl", cross_terms, peer_onehot, precision=HIGHEST)
    own_blocks = own_gram[:, None, :] * own_onehot[None, :, None]
    row_term = 2.0 * (own_blocks - cross_blocks).reshape(MODES, coarse)
    gram_term = (own_onehot[:, None, None] * row_term[None]).reshape(coarse, coarse)

    def coarse_term(values):
        own_part = 2.0 * jnp.dot(values, traces.T, precision=HIGHEST)
        return (own_part[:, None, :] * own_onehot[None, :, None]).reshape(load_cases, coarse)

    def expand(amounts):
        grouped = amounts.reshape(load_cases, block_count, MODES)
        own_amounts = lax.dynamic_index_in_dim(grouped, own_block, 1, keepdims=False)
        own_part = jnp.dot(own_amounts, traces, precision=HIGHEST)
        peer_amounts = jnp.einsum("qb,rbk->rkq", peer_onehot, grouped, precision=HIGHEST)
        spread = jnp.repeat(peer_amounts, per_peer, axis=2)
        peer_part = jnp.sum(spread * partner_traces[None, :, :], axis=1)
        return own_part - from_peers(peer_part)

    squares = jnp.sum(residual * residual, axis=1)
    gram_matrix, coarse_res, norm_res = lax.psum(
        (gram_term, coarse_term(residual), squares), ("sub", "rep")
    )
    factor = jnp.linalg.cholesky(gram_matrix)

    def solve_coarse(right):
        return jax.scipy.linalg.cho_solve((factor, True), right.T).T

    amplitudes = solve_coarse(coarse_res)
    projected = residual - expand(amplitudes)
    inner_sum = norm_res - jnp.sum(amplitudes * coarse_res, axis=1)
    direction = projected
    multipliers = jnp.zeros_like(residual)
    for iteration in range(ITERS):
        product = lax.dot_general(
            direction.astype(jnp.bfloat16),
            operator,
            (((1,), (1,)), ((), ())),
            preferred_element_type=jnp.float32,
        )
        got_product = lax.all_to_all(
            to_peers(product), "sub", split_axis=1, concat_axis=1, tiled=True
        )
        image_jump = product - got_product[:, receive_index]
        coarse_jump, jump_squares, residual_cross, curvature = lax.psum(
            (
                coarse_term(image_jump),
                jnp.sum(image_jump * image_jump, axis=1),
                jnp.sum(residual * image_jump, axis=1),
                jnp.sum(direction * image_jump, axis=1),
            ),
            ("sub", "rep"),
        )
        step_size = inner_sum / curvature
        multipliers = multipliers + step_size[:, None] * direction
        residual = residual - step_size[:, None] * image_jump
        coarse_res = coarse_res - step_size[:, None] * coarse_jump
        norm_res = (
            norm_res - 2.0 * step_size * residual_cross + step_size * step_size * jump_squares
        )
        amplitudes = solve_coarse(coarse_res)
        if iteration + 1 < ITERS:
            projected = residual - expand(amplitudes)
            renewed = norm_res - jnp.sum(amplitudes * coarse_res, axis=1)
            direction = projected + (renewed / inner_sum)[:, None] * direction
            inner_sum = renewed
    return (multipliers, amplitudes)


def fits(mesh, dual_ops, mode_block, local_gap):
    peers, planes = mesh.shape["sub"], mesh.shape["rep"]
    powers = all(size & (size - 1) == 0 for size in (peers, planes))
    whole = dual_ops.shape[1] % (128 * peers) == 0 and local_gap.shape[0] % 16 == 0
    coarse = GROUP * (mode_block.shape[0] // AGG_SUBS)
    return powers and whole and 4 * local_gap.shape[0] == 128 and 8 * coarse == 128


def solution(mesh):
    placed = (
        P(("sub", "rep"), None, None),
        P(("sub", "rep"), None, None),
        P(("sub", "rep"), None),
        P(),
        P(None, ("sub", "rep")),
    )

    def run(dual_ops, mode_traces, route, mode_block, local_gap):
        body = fused_body if fits(mesh, dual_ops, mode_block, local_gap) else general_body
        return jax.shard_map(
            body, mesh=mesh, in_specs=placed, out_specs=(P(None, ("sub", "rep")), P()), check_vma=False
        )(dual_ops, mode_traces, route, mode_block, local_gap)

    return run
```

```python
import functools

import jax
import jax.numpy as jnp
from jax import lax
from jax.experimental import pallas as pl
from jax.experimental.pallas import tpu as pltpu
from jax.sharding import PartitionSpec as P

MODES = 6
AGG_SUBS = 16
ITERS = 2
GROUP = 8

HIGHEST = lax.Precision.HIGHEST
VMEM = pl.BlockSpec(memory_space=pltpu.VMEM)
HBM = pl.BlockSpec(memory_space=pltpu.HBM)
NN = (((1,), (0,)), ((), ()))
NT = (((1,), (1,)), ((), ()))


def split(values):
    high = values.astype(jnp.bfloat16).astype(jnp.float32)
    return jnp.concatenate([high, values - high], axis=0).astype(jnp.bfloat16)


def split_dot(values, matrix, dims):
    rows = values.shape[0]
    both = lax.dot_general(split(values), matrix, dims, preferred_element_type=jnp.float32)
    return both[:rows] + both[rows:]


def small_dot(left, right):
    return jnp.dot(left, right, precision=HIGHEST, preferred_element_type=jnp.float32)


def send_far(values, far_ref, *pair_refs):
    height = values.shape[0]
    per_peer = pair_refs[0].shape[1]
    values = split(values)
    for at, ref in enumerate(pair_refs):
        columns = far_ref[:, 2 * at * per_peer : (2 * at + 2) * per_peer]
        slots = jnp.dot(values, columns, preferred_element_type=jnp.float32)
        slots = slots[:height] + slots[height:]
        ref[:height] = slots[:, :per_peer]
        ref[height:] = slots[:, per_peer:]


def send_near(values, edge_ref, near_ref, back_ref, stay_ref):
    per_peer = back_ref.shape[1]
    slots = split_dot(values, edge_ref[...], NN)
    for at, ref in enumerate((near_ref, back_ref, stay_ref)):
        ref[...] = slots[:, at * per_peer : (at + 1) * per_peer]


def straight(last_ref, pair_refs):
    height = last_ref.shape[0]
    return jnp.concatenate([*(ref[:height] for ref in pair_refs), last_ref[...]], axis=1)


def for_other(near_ref, pair_refs):
    height = near_ref.shape[0]
    return jnp.concatenate([near_ref[...], *(ref[height:] for ref in pair_refs)], axis=1)


def handed(got_ref, height, backwards=False):
    starts = list(range(height, got_ref.shape[0] - height + 1, height))
    starts = [0, *(starts[::-1] if backwards else starts)]
    return jnp.concatenate([got_ref[at : at + height] for at in starts], axis=1)


def spread(values, loads, groups):
    modes = values[loads:]
    label = modes[MODES : MODES + 1]
    used = lax.broadcasted_iota(jnp.int32, modes.shape, 0) < MODES
    parts = [jnp.where(used & (label == group), modes, 0.0) for group in range(groups)]
    return jnp.concatenate([values[:loads], *parts], axis=0)


def one_hot(route_ref, peer, per_peer):
    start = pl.multiple_of(peer * per_peer, per_peer)
    row_ids = lax.broadcasted_iota(jnp.int32, (route_ref.shape[1], per_peer), 0)
    return jnp.where(row_ids == route_ref[:, pl.ds(start, per_peer)], 1.0, 0.0).astype(jnp.bfloat16)


def place_kernel(
    route_hbm, block_hbm, gap_hbm, traces_hbm, operator_hbm,
    far_ref, values_ref, operator_ref, route_ref, *refs,
):
    *pair_refs, block_ref, traces_ref, sems = refs
    loads, rows = gap_hbm.shape
    per_peer = pair_refs[0].shape[1]
    peers = rows // per_peer
    copies = [
        pltpu.make_async_copy(source, target, sems.at[at])
        for at, (source, target) in enumerate(
            (
                (route_hbm, route_ref),
                (block_hbm, block_ref),
                (traces_hbm, traces_ref),
                (gap_hbm, values_ref.at[pl.ds(0, loads)]),
                (operator_hbm, operator_ref),
            )
        )
    ]

    def build(at):
        peer = own_index ^ (peers - 1 - at)
        far_ref[:, at * per_peer : (at + 1) * per_peer] = one_hot(route_ref, peer, per_peer)

    for copy in (copies[0], *copies[4:], *copies[1:4]):
        copy.start()
    own_index = lax.axis_index("sub")
    device = own_index * lax.axis_size("rep") + lax.axis_index("rep")
    copies[0].wait()
    for at in range(peers - 4):
        build(at)
    copies[1].wait()
    copies[2].wait()
    blocks = block_ref[...]
    lane = lax.broadcasted_iota(jnp.int32, blocks.shape, 1)
    own_block = jnp.sum(jnp.where(lane == device, blocks, 0), axis=1, keepdims=True)
    modes = traces_ref.shape[0]
    label = jnp.broadcast_to(own_block.astype(jnp.float32), (1, rows))
    for mode in range(modes):
        values_ref[loads + mode : loads + mode + 1] = traces_ref[mode]
    values_ref[loads + modes : loads + modes + 1] = label
    values_ref[loads + modes + 1 :] = jnp.zeros((GROUP - modes - 1, rows), jnp.float32)
    copies[3].wait()
    for at in range(peers - 4, peers - 2):
        build(at)
    send_far(values_ref[...], far_ref, *pair_refs)
    copies[4].wait()


def ready_kernel(
    route_ref, far_ref, values_ref, operator_ref,
    edge_ref, slots_ref, placed_ref, near_ref, back_ref, stay_ref,
):
    per_peer = back_ref.shape[1]
    peers = far_ref.shape[1] // per_peer + 2
    own_index = lax.axis_index("sub")
    low = lax.broadcasted_iota(jnp.int32, (per_peer, per_peer), 0)
    high = lax.broadcasted_iota(jnp.int32, (per_peer, per_peer), 1)
    reverse = jnp.where(low + high == per_peer - 1, 1.0, 0.0).astype(jnp.bfloat16)
    own_columns = one_hot(route_ref, own_index, per_peer)
    near_columns = one_hot(route_ref, own_index ^ 1, per_peer)
    reversed_columns = jnp.dot(own_columns, reverse, preferred_element_type=jnp.float32).astype(jnp.bfloat16)
    edge_ref[...] = jnp.concatenate([near_columns, reversed_columns, own_columns], axis=1)
    for at in range(peers // 2 - 1):
        start = 2 * at * per_peer
        slots_ref[0, :, at * per_peer : (at + 1) * per_peer] = far_ref[:, start : start + per_peer]
        slots_ref[1, :, (at + 1) * per_peer : (at + 2) * per_peer] = far_ref[:, start + per_peer : start + 2 * per_peer]
    slots_ref[0, :, (peers // 2 - 1) * per_peer :] = own_columns
    slots_ref[1, :, :per_peer] = near_columns
    send_near(values_ref[...], edge_ref, near_ref, back_ref, stay_ref)
    operator = operator_ref[0]
    for half in range(2):
        placed_ref[half] = jnp.dot(
            operator, slots_ref[half], preferred_element_type=jnp.float32
        ).astype(operator.dtype)


def first_half_kernel(placed_ref, stay_ref, back_ref, *refs):
    *pair_refs, jump_ref, image_ref = refs
    sent_refs, got_refs = pair_refs[: len(pair_refs) // 2], pair_refs[len(pair_refs) // 2 :]
    loads = stay_ref.shape[0] - GROUP
    groups = (jump_ref.shape[0] - loads) // GROUP
    own, got = (spread(straight(*refs), loads, groups) for refs in ((stay_ref, sent_refs), (back_ref, got_refs)))
    jump_ref[...] = own - got
    image_ref[...] = split_dot(own - got, placed_ref[0], NT)


def first_kernel(far_ref, placed_ref, half_ref, got_ref, near_ref, *refs):
    sent_refs, (jump_ref, image_ref, *pair_refs) = refs[: len(refs) // 2 - 1], refs[len(refs) // 2 - 1 :]
    height = near_ref.shape[0]
    loads = height - GROUP
    groups = (image_ref.shape[0] - loads) // GROUP
    own, got = (spread(value, loads, groups) for value in (for_other(near_ref, sent_refs), handed(got_ref, height)))
    jump_ref[...] = own - got
    image = half_ref[...] + split_dot(own - got, placed_ref[1], NT)
    image_ref[...] = image
    send_far(image, far_ref, *pair_refs)


def products_of(left, right):
    rows, columns = left.shape[0], right.shape[0]
    both = lax.dot_general(split(left), split(right), NT, preferred_element_type=jnp.float32)
    both = both[:rows] + both[rows:]
    return both[:, :columns] + both[:, columns:]


def by_load(products):
    sums = [jnp.sum(product, axis=1, keepdims=True) for product in products]
    empty = [jnp.zeros_like(sums[0])] * (GROUP - len(sums))
    return jnp.concatenate(sums + empty, axis=1).T


def pack(by_mode, scalars, blocks):
    by_mode = by_mode + pltpu.roll(by_mode, by_mode.shape[1] // 2, 1)
    upper, lower = by_mode[:GROUP], by_mode[GROUP:]
    row = lax.broadcasted_iota(jnp.int32, upper.shape, 0)
    left = lax.broadcasted_iota(jnp.int32, upper.shape, 1) < upper.shape[1] // 2
    spare = [
        jnp.where(left, pltpu.roll(upper, 6, 0), pltpu.roll(upper, 4, 0)),
        jnp.where(left, pltpu.roll(upper, 2, 0), pltpu.roll(lower, 6, 0)),
        jnp.where(left, pltpu.roll(lower, 4, 0), pltpu.roll(lower, 2, 0)),
        jnp.where(row == MODES, *scalars),
    ]
    rows = jnp.concatenate(blocks, axis=0)
    parts = [jnp.where(row < MODES, rows[at * GROUP : (at + 1) * GROUP], spare[at]) for at in range(4)]
    return jnp.concatenate(parts, axis=0)


def unpack(terms):
    parts = [terms[at * GROUP : (at + 1) * GROUP] for at in range(4)]
    row = lax.broadcasted_iota(jnp.int32, parts[0].shape, 0)
    lane = lax.broadcasted_iota(jnp.int32, parts[0].shape, 1)
    half = terms.shape[1] // 2
    turned = [pltpu.roll(part, half, 1) for part in parts[:3]]
    upper = jnp.where(
        row < 2, pltpu.roll(parts[0], 2, 0), jnp.where(row < 4, pltpu.roll(turned[0], 4, 0), pltpu.roll(parts[1], 6, 0))
    )
    lower = jnp.where(
        row < 2, pltpu.roll(turned[1], 2, 0), jnp.where(row < 4, pltpu.roll(parts[2], 4, 0), pltpu.roll(turned[2], 6, 0))
    )
    by_mode = [jnp.where((row < MODES) & (lane < half), part, 0.0) for part in (upper, lower)]
    blocks = [jnp.where(row < MODES, part, 0.0) for part in parts]
    scalars = parts[3][MODES : MODES + 1], parts[3][MODES + 1 : MODES + 2]
    return jnp.concatenate(by_mode, axis=0), scalars, [jnp.concatenate(blocks[at : at + 2], axis=0) for at in (0, 2)]


def powers(coarse, loads):
    lane = lax.broadcasted_iota(jnp.int32, (coarse, 4 * loads), 1)
    row = lax.broadcasted_iota(jnp.int32, (coarse, 4 * loads), 0)

    def choose(at, *values):
        return functools.reduce(lambda rest, pair: jnp.where(at == pair[0], pair[1], rest), enumerate(values), 0.0 * lane)

    strip, group = lane // coarse, lane // loads
    by_mode = choose(strip, jnp.where(lane > row, 2.0, 0.0), 1.0, 3.0, 2.0)
    scalars = choose(group, 0.0, 1.0, 2.0, 3.0), choose(group, 2.0, 2.0)
    blocks = [choose(group, 0.0, 2.0, 2.0, 1.0), choose(group, 2.0, 3.0, 3.0, 1.0)]
    return pack(by_mode, [line[:1] for line in scalars], blocks)


def magnitude(operator_ref):
    tall = 2 * GROUP
    largest = jnp.zeros((tall, operator_ref.shape[2]), operator_ref.dtype)
    for start in range(0, operator_ref.shape[1], tall):
        part = operator_ref[0, start : start + tall]
        largest = jnp.maximum(largest, jnp.maximum(part, -part))
    largest = jnp.max(largest.astype(jnp.float32), axis=0, keepdims=True)
    return jnp.clip(jnp.max(largest, axis=1, keepdims=True), 1e-30, 1e30)


def scale_of(terms):
    last = terms[-GROUP:]
    half = last.shape[1] // 2
    lane = lax.broadcasted_iota(jnp.int32, last.shape, 1)
    return jnp.where(lane < half, pltpu.roll(last, half, 1), last)[GROUP - 1 :]


def middle_kernel(
    edge_ref, slots_ref, operator_ref, straight_ref, handed_ref, image_ref,
    basis_ref, scale_ref, powers_ref, terms_ref, sums_ref, near_ref, back_ref, stay_ref,
):
    image = image_ref[...]
    send_near(image, edge_ref, near_ref, back_ref, stay_ref)
    coarse = terms_ref.shape[0] // 3
    loads = image.shape[0] - coarse
    basis = split_dot(straight_ref[...], slots_ref[0], NT) + split_dot(handed_ref[...], slots_ref[1], NT)
    basis_ref[...] = basis
    scale = magnitude(operator_ref)
    scale_ref[...] = jnp.broadcast_to(scale, scale_ref.shape)
    image = image * (1.0 / scale)
    residual, residual_image = basis[:loads], image[:loads]
    lanes = terms_ref.shape[1]
    powers_ref[...] = powers(coarse, loads)
    empty = jnp.zeros((lanes - 2 * loads - 2 * coarse, basis.shape[1]), jnp.float32)
    both = products_of(
        jnp.concatenate([basis[loads:], image[loads:]]),
        jnp.concatenate([residual, basis[loads:], image[loads:], empty, residual_image]),
    )
    by_g, by_h = both[:coarse], both[coarse:]
    lane = lax.broadcasted_iota(jnp.int32, (coarse, lanes), 1)
    first, last = lane < loads, lane >= lanes - loads
    terms_ref[:coarse] = jnp.where(first | last, by_g, 0.0)
    terms_ref[coarse : 2 * coarse] = jnp.where(last, pltpu.roll(by_h, lanes - loads, 1), 0.0)
    row = lax.broadcasted_iota(jnp.int32, (coarse, lanes), 0)
    by_mode = jnp.where((lane <= row) | ((lane >= coarse) & (lane < 2 * coarse)), pltpu.roll(by_g, lanes - loads, 1), 0.0)
    terms_ref[2 * coarse :] = by_mode
    sums_ref[...] = by_load([residual * residual, residual * residual_image])


def second_half_kernel(slots_ref, placed_ref, scale_ref, stay_ref, back_ref, *refs):
    *pair_refs, jump_ref, second_ref = refs
    sent_refs, got_refs = pair_refs[: len(pair_refs) // 2], pair_refs[len(pair_refs) // 2 :]
    jump = straight(stay_ref, sent_refs) - straight(back_ref, got_refs)
    jump = jump * (1.0 / scale_ref[:1, : jump.shape[1]])
    jump_ref[...] = split_dot(jump, slots_ref[0], NT)
    second_ref[...] = split_dot(jump, placed_ref[0], NT)


def second_kernel(
    slots_ref, placed_ref, basis_ref, half_jump_ref, half_second_ref, scale_ref, early_ref, sums_ref, got_ref,
    near_ref, *refs,
):
    *sent_refs, jump_ref, terms_ref, chip_ref = refs
    coarse = terms_ref.shape[0] // 2
    loads = basis_ref.shape[0] - coarse
    jump = for_other(near_ref, sent_refs) - handed(got_ref, loads + coarse, backwards=True)
    lanes = chip_ref.shape[1]
    chip = jnp.maximum(scale_ref[:1, :lanes], got_ref[got_ref.shape[0] - 1 :])
    chip_ref[...] = jnp.broadcast_to(chip, chip_ref.shape)
    inverse = 1.0 / chip
    ratio = scale_ref[:1, :lanes] * inverse
    wide_inverse, wide_ratio = (jnp.concatenate([line] * (basis_ref.shape[1] // lanes), axis=1) for line in (inverse, ratio))
    jump = jump * wide_inverse[:, : jump.shape[1]]
    second = (half_second_ref[...] * wide_ratio + split_dot(jump, placed_ref[1], NT)) * wide_inverse
    jump = half_jump_ref[...] * wide_ratio + split_dot(jump, slots_ref[1], NT)
    jump_ref[...] = jump
    basis = basis_ref[...]
    residual, jump_loads, second_loads = basis[:loads], jump[:loads], second[:loads]
    both = products_of(
        jnp.concatenate([basis[loads:], jump[loads:], second[loads:]]),
        jnp.concatenate([residual, jump_loads, second_loads, jump[loads:], second[loads:]]),
    )
    by_g, by_z, by_dz = (both[at * coarse : (at + 1) * coarse] for at in range(3))
    lanes = terms_ref.shape[1]
    lane = lax.broadcasted_iota(jnp.int32, (coarse, lanes), 1)
    group = lane // loads
    top = jnp.where(group == 1, by_z, jnp.where(group == 2, by_g, 0.0))
    low = jnp.where(group < 2, by_dz, jnp.where(group == 2, by_z, 0.0))
    row = lax.broadcasted_iota(jnp.int32, (coarse, lanes), 0)
    z_z = pltpu.roll(by_z, 2 * coarse, 1)
    strip = lane // coarse
    by_mode = jnp.where((lane > row) & (strip == 0), z_z, 0.0)
    by_mode = jnp.where(strip == 2, pltpu.roll(by_z, 3 * coarse, 1), by_mode)
    by_mode = jnp.where(strip == 3, pltpu.roll(by_g, 4 * coarse, 1), by_mode)
    diagonal = jnp.sum(jnp.where(lane == row, z_z, 0.0), axis=0, keepdims=True)
    sums = by_load([jump_loads * jump_loads, jump_loads * second_loads, residual * second_loads])
    scalars = (
        jnp.concatenate([sums_ref[0:1], sums_ref[1:2] * ratio[:, :loads], sums[0:1], sums[1:2]], axis=1),
        jnp.concatenate([sums[2:3], diagonal[:, :loads], chip[:, : 2 * loads]], axis=1),
    )
    blocks = [
        early_ref[at * coarse : (at + 1) * coarse] * jnp.where(group == 3, ratio, 1.0) + block
        for at, block in enumerate((top, low))
    ]
    by_mode = early_ref[2 * coarse :] * jnp.where(strip == 1, ratio, 1.0) + by_mode
    terms_ref[...] = pack(by_mode, scalars, blocks)


def chip_kernel(other_ref, own_ref, *sum_refs):
    own = own_ref[...]
    row = lax.broadcasted_iota(jnp.int32, own.shape, 0)
    lane = lax.broadcasted_iota(jnp.int32, own.shape, 1)
    total = jnp.where((row == own.shape[0] - 1) & (lane >= own.shape[1] // 2), own, own + other_ref[...])
    for ref in sum_refs:
        ref[...] = total


def summed(refs, power):
    parts = [ref[...] for ref in reversed(refs)]
    scales = [scale_of(part) for part in parts]
    largest = functools.reduce(jnp.maximum, scales)
    inverse = 1.0 / largest
    for at, scale in enumerate(scales):
        factor = scale * inverse
        square = factor * factor
        high = jnp.where(power > 2, square * factor, square)
        parts[at] = parts[at] * jnp.where(power > 1, high, jnp.where(power > 0, factor, 1.0))
    while len(parts) > 1:
        parts = [low + high for low, high in zip(parts[::2], parts[1::2])]
    return parts[0], largest


def sum_kernel(count, powers_ref, *refs):
    power = powers_ref[...]
    total, scale = summed(refs[:count], power)
    row = lax.broadcasted_iota(jnp.int32, power.shape, 0)
    lane = lax.broadcasted_iota(jnp.int32, power.shape, 1)
    total = jnp.where((row == power.shape[0] - 1) & (lane >= power.shape[1] // 2), scale, total)
    for ref in refs[count:]:
        ref[...] = total


def eliminate(work, coarse):
    row = lax.broadcasted_iota(jnp.int32, work.shape, 0)
    for start in range(0, coarse, GROUP):
        pivots = range(start, start + MODES)
        columns = [jnp.broadcast_to(work[:, pivot : pivot + 1], work.shape) for pivot in pivots]
        square = [[column[pivot : pivot + 1] for column in columns] for pivot in pivots]
        rows = [work[pivot : pivot + 1] for pivot in pivots]
        for at in range(MODES):
            scale = 1.0 / square[at][at]
            rows[at] = rows[at] * scale
            square[at] = [value * scale for value in square[at]]
            for other in range(MODES):
                if other != at:
                    factor = square[other][at]
                    rows[other] = rows[other] - factor * rows[at]
                    square[other] = [
                        value if to <= at else value - factor * square[at][to]
                        for to, value in enumerate(square[other])
                    ]
        for column, solved in zip(columns, rows):
            work = work - column * solved
        for pivot, solved in zip(pivots, rows):
            work = jnp.where(row == pivot, solved, work)
    return work


def thin_dot(left, right):
    high, right_high = (value.astype(jnp.bfloat16).astype(jnp.float32) for value in (left, right))
    return jnp.dot(
        jnp.concatenate([high, left - high, high], axis=1).astype(jnp.bfloat16),
        jnp.concatenate([right_high, right_high, right - right_high], axis=0).astype(jnp.bfloat16),
        preferred_element_type=jnp.float32,
    )


def final_kernel(powers_ref, *refs):
    *parts_refs, basis_ref, jump_ref, scale_ref, multipliers_ref, amplitudes_ref = refs
    terms, scale = summed(parts_refs, powers_ref[...])
    coarse = terms.shape[0] // 2
    loads = basis_ref.shape[0] - coarse
    groups = coarse // GROUP

    def total(values):
        return jnp.sum(values, axis=0, keepdims=True)

    ratio = scale_ref[:1, : scale.shape[1]] / scale
    jump = jump_ref[...] * jnp.concatenate([ratio] * (jump_ref.shape[1] // ratio.shape[1]), axis=1)
    by_mode, (sums, last_sums), (top, low) = unpack(terms)
    res_res, res_image, jump_jump, jump_second = (sums[:, at * loads : (at + 1) * loads] for at in range(4))
    res_second, diagonal = last_sums[:, :loads], last_sums[:, loads : loads + coarse]
    coarse_res, jump_z, second_g, image_g = (top[:, at * loads : (at + 1) * loads] for at in range(4))
    res_dz, jump_dz, second_z, res_h = (low[:, at * loads : (at + 1) * loads] for at in range(4))
    triangles, g_h, z_dz, g_dz = (by_mode[:, at * coarse : (at + 1) * coarse] for at in range(4))
    row = lax.broadcasted_iota(jnp.int32, (coarse, coarse), 0)
    column = lax.broadcasted_iota(jnp.int32, (coarse, coarse), 1)
    unit = jnp.where(row == column, 1.0, 0.0)
    other = triangles.T
    gram = jnp.where(row >= column, triangles, other)
    z_z = jnp.where(row < column, triangles, jnp.where(row == column, diagonal, other))
    empty = jnp.zeros((coarse, 5 * coarse - 2 * loads), jnp.float32)
    solved = eliminate(
        jnp.concatenate([gram, g_h, coarse_res, image_g, unit, empty], axis=1), coarse
    )
    inverse_h = solved[:, coarse : 2 * coarse]
    amounts = solved[:, 2 * coarse : 2 * coarse + loads]
    inverse_image = solved[:, 2 * coarse + loads : 2 * coarse + 2 * loads]
    inverse = solved[:, 2 * coarse + 2 * loads : 3 * coarse + 2 * loads]
    products = small_dot(jnp.concatenate([inverse_h, g_h, z_z, g_dz, z_dz], axis=0), amounts)
    inverse_h_amounts, h_amounts, z_amounts, g_dz_amounts, z_dz_amounts = (
        products[at * coarse : (at + 1) * coarse] for at in range(5)
    )
    shares = 2.0 * (inverse_image - inverse_h_amounts)
    both = jnp.concatenate([amounts, shares], axis=0).T
    basis_g, jump_z_rows = basis_ref[loads:], jump[loads:]
    d = basis_ref[:loads] - thin_dot(both[:, :coarse], basis_g)
    u = jump[:loads] - thin_dot(both, jnp.concatenate([jump_z_rows, basis_g], axis=0))
    products = small_dot(jnp.concatenate([g_h, z_z], axis=0), shares)
    image_d = image_g - h_amounts
    inner = res_res - total(amounts * coarse_res)
    curvature = 2.0 * (res_image - total(amounts * (res_h + image_d)))
    u_u = jump_jump - total(amounts * (2.0 * jump_z - z_amounts) + 2.0 * image_d * shares)
    second_u = second_g - g_dz_amounts - products[:coarse]
    jump_u = second_z - z_dz_amounts - 0.5 * products[coarse:]
    d_second = res_second - total(amounts * (res_dz + second_u) + shares * res_h)
    u_second = jump_second - total(amounts * (jump_dz + jump_u) + shares * (0.5 * jump_z + second_u))
    step = inner / curvature
    renewed = step * step * u_u - inner
    grown = 1.0 + renewed / inner
    curvature = grown * grown * curvature - grown * step * (2.0 * d_second + u_u) + 2.0 * step * step * u_second
    second_step = renewed / curvature
    on_d, on_u = step + second_step * grown, second_step * step
    amplitudes = amounts - on_d * shares + 2.0 * on_u * small_dot(inverse, second_u)
    amplitudes_ref[...] = jnp.concatenate(
        [amplitudes[label * GROUP : label * GROUP + MODES] for label in range(groups)], axis=0
    )
    inverse = 1.0 / scale[:, :loads]
    weights = jnp.concatenate([on_d * inverse, on_u * inverse, jnp.zeros((6, loads), jnp.float32)], axis=0).T
    multipliers_ref[...] = weights[:, 0:1] * d - weights[:, 1:2] * u


def call(kernel, shapes, in_specs, name, scratch=(), flops=0):
    return pl.pallas_call(
        kernel,
        out_shape=[jax.ShapeDtypeStruct(*shape) for shape in shapes],
        in_specs=in_specs,
        out_specs=[VMEM] * len(shapes),
        scratch_shapes=scratch,
        compiler_params=pltpu.CompilerParams(vmem_limit_bytes=24 * 1024 * 1024),
        cost_estimate=pl.CostEstimate(flops=flops, bytes_accessed=2**20, transcendentals=0),
        name=name,
    )


def permute(values, offset, plane_offset=0):
    peers, planes = lax.axis_size("sub"), lax.axis_size("rep")
    offset = offset * planes + plane_offset
    return lax.ppermute(values, ("sub", "rep"), [(at, at ^ offset) for at in range(peers * planes)])


def to_chips(*pairs):
    return [permute(pair, 2 * (len(pairs) - at) + 1) for at, pair in enumerate(pairs)]


def to_core(near, *pairs, extra=()):
    return permute(jnp.concatenate([near, *(pair[near.shape[0] :] for pair in pairs), *extra], axis=0), 1)


def last_parts(terms, powers):
    chips = [(offset + 1, 0) for offset in reversed(range(2, lax.axis_size("sub"), 2))]
    planes = [(1, offset) for offset in reversed(range(1, lax.axis_size("rep")))]
    shape = (terms.shape, terms.dtype)
    copies = call(chip_kernel, [shape] * len(chips), [VMEM] * 2, "chip")(permute(terms, 1), terms)
    parts = [permute(copy, *offset) for copy, offset in zip(copies, chips)]
    kernel = functools.partial(sum_kernel, len(parts) + 1)
    copies = call(kernel, [shape] * len(planes), [VMEM] * (len(parts) + 2), "sum")(powers, *parts, copies[0])
    return [*(permute(copy, *offset) for copy, offset in zip(copies, planes)), copies[0]]


def fused_body(dual_ops, mode_traces, route, mode_block, local_gap):
    peers = lax.axis_size("sub")
    loads, rows = local_gap.shape
    modes = mode_traces.shape[1]
    subs = mode_block.shape[0]
    groups = subs // AGG_SUBS
    per_peer = rows // peers
    height = loads + GROUP * groups
    f32, i32 = jnp.float32, jnp.int32
    tall = ((height, rows), f32)
    wide = ((3 * GROUP * groups, 4 * loads), f32)

    def pairs(height):
        return [((2 * height, per_peer), f32)] * (peers // 2 - 1)

    def singles(height):
        return [((height, per_peer), f32)] * 3

    def held(value):
        return pltpu.with_memory_space_constraint(value, pltpu.HBM)

    inputs = [route, mode_block.reshape(1, subs), local_gap, mode_traces.transpose(1, 0, 2), dual_ops]
    short = loads + GROUP
    far, values, operator, route, *send = call(
        place_kernel,
        [
            ((rows, rows - 2 * per_peer), jnp.bfloat16),
            ((short, rows), f32),
            (dual_ops.shape, dual_ops.dtype),
            (route.shape, i32),
            *pairs(short),
        ],
        [HBM] * 5,
        "place",
        [pltpu.VMEM((1, subs), i32), pltpu.VMEM((modes, 1, rows), f32), pltpu.SemaphoreType.DMA((5,))],
    )(*(held(value) for value in inputs))
    got = to_chips(*send)
    halves = ((2, rows, rows // 2), dual_ops.dtype)
    edge, slots, placed, near, back, stay = call(
        ready_kernel,
        [((rows, 3 * per_peer), jnp.bfloat16), halves, halves, *singles(short)],
        [VMEM] * 4,
        "ready",
        flops=2 * rows * rows * rows,
    )(route, far, values, operator)
    got_near = to_core(near, *got)
    half = ((height, rows // 2), f32)
    straight_jump, half_image = call(
        first_half_kernel, [half, tall], [VMEM] * (3 + 2 * len(got)), "first_half", flops=2 * rows * rows * height
    )(placed, stay, back, *send, *got)
    handed_jump, image, *image_send = call(
        first_kernel, [half, tall, *pairs(height)], [VMEM] * (5 + len(send)), "first"
    )(far, placed, half_image, got_near, near, *send)
    got = to_chips(*image_send)
    packed = ((2 * GROUP * groups, 4 * loads), f32)
    basis, scale, powers, terms, sums, near, back, stay = call(
        middle_kernel,
        [tall, ((GROUP, rows), f32), packed, wide, ((GROUP, loads), f32), *singles(height)],
        [VMEM] * 6,
        "middle",
        flops=4 * rows * rows * height,
    )(edge, slots, operator, straight_jump, handed_jump, image)
    got_near = to_core(near, *got[::-1], extra=[scale[:, :per_peer]])
    half_jump, half_second = call(
        second_half_kernel, [tall, tall], [VMEM] * (5 + 2 * len(got)), "second_half", flops=4 * rows * rows * height
    )(slots, placed, scale, stay, back, *image_send, *got)
    jump, terms, scale = call(second_kernel, [tall, packed, ((GROUP, 4 * loads), f32)], [VMEM] * (10 + len(got)), "second")(
        slots, placed, basis, half_jump, half_second, scale, terms, sums, got_near, near, *image_send
    )
    parts = last_parts(terms, powers)
    multipliers, amplitudes = call(
        final_kernel, [((loads, rows), f32), ((MODES * groups, loads), f32)], [VMEM] * (4 + len(parts)), "final"
    )(powers, *parts, basis, jump, scale)
    return multipliers, amplitudes.T


def general_body(dual_ops, mode_traces, route, mode_block, local_gap):
    own_index = lax.axis_index("sub")
    plane_index = lax.axis_index("rep")
    peer_count = lax.axis_size("sub")
    plane_count = lax.axis_size("rep")
    operator = dual_ops[0]
    traces = mode_traces[0]
    slot_rows = route[0]
    rows_here = operator.shape[0]
    load_cases = local_gap.shape[0]
    per_peer = rows_here // peer_count
    blocks = mode_block[:, 0]
    block_count = blocks.shape[0] // AGG_SUBS
    coarse = block_count * MODES
    positions = jnp.arange(rows_here, dtype=jnp.int32)
    inverse = jnp.zeros((rows_here,), jnp.int32).at[slot_rows].set(positions)
    slot_peer = positions // per_peer
    within = positions % per_peer
    flip_index = jnp.where(
        slot_peer == own_index, slot_peer * per_peer + per_peer - 1 - within, positions
    )
    peer_ids = jnp.arange(peer_count, dtype=jnp.int32)
    peer_blocks = blocks[peer_ids * plane_count + plane_index]
    own_block = blocks[own_index * plane_count + plane_index]
    labels = jnp.arange(block_count, dtype=jnp.int32)
    peer_onehot = (peer_blocks[:, None] == labels[None, :]).astype(jnp.float32)
    own_onehot = (labels == own_block).astype(jnp.float32)
    trace_slots = traces[:, slot_rows]
    receive_index = flip_index[inverse]

    def to_peers(values):
        return values[:, slot_rows]

    def from_peers(values):
        return values[:, inverse]

    gap_peers = to_peers(local_gap)
    got_traces = lax.all_to_all(trace_slots, "sub", split_axis=1, concat_axis=1, tiled=True)
    got_gap = lax.all_to_all(gap_peers, "sub", split_axis=1, concat_axis=1, tiled=True)
    partner_traces = got_traces[:, flip_index]
    residual = local_gap - got_gap[:, receive_index]
    own_gram = jnp.dot(traces, traces.T, precision=HIGHEST)
    paired = (trace_slots[:, None, :] * partner_traces[None, :, :]).reshape(
        MODES, MODES, peer_count, per_peer
    )
    cross_terms = jnp.sum(paired, axis=3)
    cross_blocks = jnp.einsum("klq,qb->kbl", cross_terms, peer_onehot, precision=HIGHEST)
    own_blocks = own_gram[:, None, :] * own_onehot[None, :, None]
    row_term = 2.0 * (own_blocks - cross_blocks).reshape(MODES, coarse)
    gram_term = (own_onehot[:, None, None] * row_term[None]).reshape(coarse, coarse)

    def coarse_term(values):
        own_part = 2.0 * jnp.dot(values, traces.T, precision=HIGHEST)
        return (own_part[:, None, :] * own_onehot[None, :, None]).reshape(load_cases, coarse)

    def expand(amounts):
        grouped = amounts.reshape(load_cases, block_count, MODES)
        own_amounts = lax.dynamic_index_in_dim(grouped, own_block, 1, keepdims=False)
        own_part = jnp.dot(own_amounts, traces, precision=HIGHEST)
        peer_amounts = jnp.einsum("qb,rbk->rkq", peer_onehot, grouped, precision=HIGHEST)
        spread = jnp.repeat(peer_amounts, per_peer, axis=2)
        peer_part = jnp.sum(spread * partner_traces[None, :, :], axis=1)
        return own_part - from_peers(peer_part)

    squares = jnp.sum(residual * residual, axis=1)
    gram_matrix, coarse_res, norm_res = lax.psum(
        (gram_term, coarse_term(residual), squares), ("sub", "rep")
    )
    factor = jnp.linalg.cholesky(gram_matrix)

    def solve_coarse(right):
        return jax.scipy.linalg.cho_solve((factor, True), right.T).T

    amplitudes = solve_coarse(coarse_res)
    projected = residual - expand(amplitudes)
    inner_sum = norm_res - jnp.sum(amplitudes * coarse_res, axis=1)
    direction = projected
    multipliers = jnp.zeros_like(residual)
    for iteration in range(ITERS):
        product = lax.dot_general(
            direction.astype(jnp.bfloat16),
            operator,
            (((1,), (1,)), ((), ())),
            preferred_element_type=jnp.float32,
        )
        got_product = lax.all_to_all(
            to_peers(product), "sub", split_axis=1, concat_axis=1, tiled=True
        )
        image_jump = product - got_product[:, receive_index]
        coarse_jump, jump_squares, residual_cross, curvature = lax.psum(
            (
                coarse_term(image_jump),
                jnp.sum(image_jump * image_jump, axis=1),
                jnp.sum(residual * image_jump, axis=1),
                jnp.sum(direction * image_jump, axis=1),
            ),
            ("sub", "rep"),
        )
        step_size = inner_sum / curvature
        multipliers = multipliers + step_size[:, None] * direction
        residual = residual - step_size[:, None] * image_jump
        coarse_res = coarse_res - step_size[:, None] * coarse_jump
        norm_res = (
            norm_res - 2.0 * step_size * residual_cross + step_size * step_size * jump_squares
        )
        amplitudes = solve_coarse(coarse_res)
        if iteration + 1 < ITERS:
            projected = residual - expand(amplitudes)
            renewed = norm_res - jnp.sum(amplitudes * coarse_res, axis=1)
            direction = projected + (renewed / inner_sum)[:, None] * direction
            inner_sum = renewed
    return (multipliers, amplitudes)


def fits(mesh, dual_ops, mode_block, local_gap):
    peers, planes = mesh.shape["sub"], mesh.shape["rep"]
    powers = all(size & (size - 1) == 0 for size in (peers, planes))
    whole = dual_ops.shape[1] % (128 * peers) == 0 and local_gap.shape[0] % 16 == 0
    coarse = GROUP * (mode_block.shape[0] // AGG_SUBS)
    return powers and whole and 4 * local_gap.shape[0] == 128 and 8 * coarse == 128


def solution(mesh):
    placed = (
        P(("sub", "rep"), None, None),
        P(("sub", "rep"), None, None),
        P(("sub", "rep"), None),
        P(),
        P(None, ("sub", "rep")),
    )

    def run(dual_ops, mode_traces, route, mode_block, local_gap):
        body = fused_body if fits(mesh, dual_ops, mode_block, local_gap) else general_body
        return jax.shard_map(
            body, mesh=mesh, in_specs=placed, out_specs=(P(None, ("sub", "rep")), P()), check_vma=False
        )(dual_ops, mode_traces, route, mode_block, local_gap)

    return run
```
